32 devices in a mesh: rep: 2 (over y), seq: 4 (over z), ch: 4 (over x, core).
Axes of the slice: x: 2, y: 2, z: 4, core: 2. Of those that a mesh axis runs over, the one named last changes fastest.
Arguments:
- key_proj: bfloat16 [4096, 4096], P(('rep', 'seq'), 'ch'), parts along dimension 0, may hold values from -6 to 6
- value_proj: bfloat16 [4096, 4096], P(('rep', 'seq'), 'ch'), parts along dimension 0, may hold values from -6 to 6
- query_proj: bfloat16 [4096, 4096], P(('rep', 'seq'), 'ch'), parts along dimension 0, may hold values from -6 to 6
- filters: bfloat16 [256, 2048], P('ch', 'seq'), may hold values from -3 to 3
- sources: int32 [8], P('rep'), parts along dimension 0, may hold values from 0 to 15, as said below
- owner: int32 [32], P('rep'), parts along dimension 0, may hold values from 0 to 3, as said below
Outputs:
- conv_out: bfloat16 [4096, 4096], P(('rep', 'seq'), 'ch'), parts along dimension 0
The draws below stay inside these ranges and needn't reach their ends.
There are 2 independent parts, one for each index of `rep`. The reference program is written for one: setup_inputs(seed, part) draws one part's arguments, and reference() takes and returns one part's arrays. A program takes and returns all parts, laid end to end along the dimension named above; an argument that names none is the same for every part. Nothing has to cross between parts.
Inputs may be any that keep to these rules, and one draw needn't show every extreme that they name: `sources`: four distinct stretch numbers in increasing order; the first is 0 and the last 15. owner[k] is the index along seq of the shard holding stretch k; every shard holds exactly 4 stretches, stored one after another in increasing stretch number.
All inputs are finite; a program needn't handle non-finite values.
Results may differ from the reference program's by a relative error of at most 0.0049.
Values may be sent and summed in bfloat16 or wider, within the bound.
No kernel may reach another device: no remote copies, remote signals or barrier semaphores. Data moves between devices by JAX's collectives and lax.ppermute only.
A program may use at most 64 MiB of HBM per device.

```python
import math
import jax
import jax.numpy as jnp
from jax import lax

D = 4096
GROUP_CH = 16
FILTER_GROUPS = 256
STRETCH = 128
WIN = 4
CH_DEV = 4
NCH = 16
SEQUENCE_LENGTH = 2048


def channel_offsets(key):
    sign_key, size_key = jax.random.split(jax.random.fold_in(key, 31))
    signs = jnp.where(jax.random.uniform(sign_key, (D,)) < 0.5, -1.0, 1.0)
    return signs * jax.random.uniform(size_key, (D,), minval=0.7, maxval=1.3)


def stretch_levels(key, salt):
    level_key = jax.random.fold_in(key, salt)
    return jnp.exp(jax.random.uniform(level_key, (NCH, 1, 1), minval=-4.0, maxval=1.0))


def draw_key_proj(key, part):
    offsets = channel_offsets(key)
    levels = stretch_levels(key, 41)
    noise_key = jax.random.fold_in(key, 43)
    noise = jax.random.normal(noise_key, (NCH, STRETCH, D))
    rows = jnp.clip(levels * (noise + offsets[None, None, :]), -6.0, 6.0)
    return rows.reshape(SEQUENCE_LENGTH, D).astype(jnp.bfloat16)


def draw_value_proj(key, part):
    offsets = channel_offsets(key)
    levels = stretch_levels(key, 47)
    noise_key = jax.random.fold_in(key, 53)
    noise = jax.random.normal(noise_key, (NCH, STRETCH, D))
    rows = jnp.clip(levels * (noise + offsets[None, None, :]), -6.0, 6.0)
    return rows.reshape(SEQUENCE_LENGTH, D).astype(jnp.bfloat16)


def draw_filters(key, part):
    first, second, third, fourth_random_key, fifth = jax.random.split(jax.random.fold_in(key, 7), 5)
    lag_dimension = jnp.arange(SEQUENCE_LENGTH, dtype=jnp.float32)
    quick = float(min(40, max(4, STRETCH // 2)))
    slow_share = 0.5
    slow_flag = jax.random.uniform(first, (FILTER_GROUPS, 1)) < slow_share
    fast_log = jax.random.uniform(second, (FILTER_GROUPS, 1), minval=math.log(quick), maxval=math.log(float(SEQUENCE_LENGTH)))
    slow_log = jax.random.uniform(third, (FILTER_GROUPS, 1), minval=math.log(float(SEQUENCE_LENGTH)), maxval=math.log(50.0 * SEQUENCE_LENGTH))
    decay_len = jnp.exp(jnp.where(slow_flag, slow_log, fast_log))
    spike_lag_offset = jax.random.randint(fourth_random_key, (FILTER_GROUPS, 3, 1), 1, SEQUENCE_LENGTH).astype(jnp.float32)
    retained_fraction = jax.random.uniform(fifth, (FILTER_GROUPS, 3, 1), minval=0.5, maxval=0.8)
    discarded_mask = jnp.prod(jnp.where(lag_dimension[None, None, :] >= spike_lag_offset, retained_fraction, 1.0), axis=1)
    scale = 1.0 / jnp.sqrt(jnp.minimum(decay_len, float(STRETCH)))
    noise_key = jax.random.fold_in(key, 13)
    rough = jnp.clip(jax.random.normal(noise_key, (FILTER_GROUPS, SEQUENCE_LENGTH)), -6.0, 6.0)
    near_part = rough * jnp.exp(-lag_dimension[None, :] / decay_len) * discarded_mask * scale
    sign_key = jax.random.fold_in(key, 17)
    tail_sign = jnp.where(jax.random.uniform(sign_key, (FILTER_GROUPS, 1)) < 0.5, -1.0, 1.0)
    tail_rough = 0.25 + 1.5 * jax.random.uniform(jax.random.fold_in(key, 19), (FILTER_GROUPS, SEQUENCE_LENGTH))
    tail_part = 0.015 * scale * tail_sign * tail_rough * jnp.exp(-lag_dimension[None, :] / (2.0 * SEQUENCE_LENGTH))
    return (near_part + tail_part).astype(jnp.bfloat16)


def draw_sources(key, part):
    inner = jax.random.permutation(jax.random.fold_in(key, 11), NCH - 2)[:2] + 1
    lower = jnp.minimum(inner[0], inner[1])
    upper = jnp.maximum(inner[0], inner[1])
    return jnp.stack([jnp.int32(0), lower.astype(jnp.int32), upper.astype(jnp.int32), jnp.int32(NCH - 1)]).astype(jnp.int32)


def draw_owner(key, part):
    shuffled = jax.random.permutation(jax.random.fold_in(key, 23), NCH)
    return (shuffled // CH_DEV).astype(jnp.int32)


def level_of(rng, dims, shards, smallest, largest):
    def one(dim, parts):
        draws = jax.random.uniform(jax.random.fold_in(jax.random.fold_in(rng, 6), dim), (parts,), jnp.float32, smallest / len(shards), largest / len(shards))
        return jnp.repeat(jnp.exp(draws), dims[dim] // parts).reshape((-1,) + (1,) * (len(dims) - dim - 1))

    factor_of = one(*shards[0])
    for cut in shards[1:]:
        factor_of = factor_of * one(*cut)
    return factor_of


def bell_draw(stream_key, extent, deviation, bound, shards=(), kind=jnp.bfloat16):
    array = deviation * jax.random.normal(stream_key, extent, jnp.float32)
    if shards:
        array = array * level_of(stream_key, extent, shards, -0.22, 0.18)
    return jnp.clip(array, -bound, bound).astype(kind)


def setup_inputs(seed: int = 0, part: int = 0) -> dict:
    seeds = jax.random.split(jax.random.key(seed), 7)
    part_keys = jax.random.split(jax.random.fold_in(seeds[6], part), 7)
    return {
        "key_proj": draw_key_proj(jax.random.fold_in(jax.random.fold_in(seeds[6], part), 71), part),
        "value_proj": draw_value_proj(jax.random.fold_in(jax.random.fold_in(seeds[6], part), 71), part),
        "query_proj": bell_draw(part_keys[2], (SEQUENCE_LENGTH, D), 1.0, 6.0, ((0, 4), (1, 4))),
        "filters": draw_filters(jax.random.fold_in(seeds[6], 71), part),
        "sources": draw_sources(jax.random.fold_in(jax.random.fold_in(seeds[6], part), 71), part),
        "owner": draw_owner(jax.random.fold_in(jax.random.fold_in(seeds[6], part), 71), part),
    }


def reference(key_proj, value_proj, query_proj, filters, sources, owner):
    stretch_total = owner.shape[0]
    channels = key_proj.shape[1]
    group_count = channels // GROUP_CH
    numbers = jnp.arange(stretch_total, dtype=jnp.int32)
    same_owner = (owner[:, None] == owner[None, :]).astype(jnp.int32)
    earlier = (numbers[None, :] < numbers[:, None]).astype(jnp.int32)
    position = (owner * CH_DEV + jnp.sum(same_owner * earlier, axis=1)).astype(jnp.int32)
    stretch_at = jnp.sum((position[None, :] == numbers[:, None]).astype(jnp.int32) * numbers[None, :], axis=1).astype(jnp.int32)
    source_at = jnp.sum((sources[:, None] == numbers[None, :]).astype(jnp.int32) * position[None, :], axis=1).astype(jnp.int32)
    gated = (key_proj.astype(jnp.float32) * value_proj.astype(jnp.float32)).astype(jnp.bfloat16)
    blocks = gated.reshape(stretch_total, STRETCH, group_count, GROUP_CH)
    window = jnp.take(blocks, source_at, axis=0).astype(jnp.float32)
    padded = jnp.concatenate([jnp.zeros((group_count, STRETCH), jnp.float32), filters.astype(jnp.float32)], axis=1)
    offsets = (STRETCH + jnp.arange(STRETCH, dtype=jnp.int32)[:, None] - jnp.arange(STRETCH, dtype=jnp.int32)[None, :]).astype(jnp.int32)

    def one_block(stored):
        target = stretch_at[stored]
        summed = jnp.zeros((STRETCH, group_count, GROUP_CH), jnp.float32)
        for window_slot in range(WIN):
            lag_block = target - sources[window_slot]
            lag_start = (jnp.maximum(lag_block, 0) * STRETCH).astype(jnp.int32)
            lag_span = lax.dynamic_slice_in_dim(padded, lag_start, 2 * STRETCH, 1)
            toeplitz = jnp.take(lag_span, offsets, axis=1)
            term = jnp.einsum("gij,jgc->igc", toeplitz, window[window_slot], precision=lax.Precision.HIGHEST)
            summed = summed + jnp.where(lag_block >= 0, term, 0.0)
        gate_rows = lax.dynamic_slice_in_dim(query_proj, (stored * STRETCH).astype(jnp.int32), STRETCH, 0).astype(jnp.float32)
        return (gate_rows * summed.reshape(STRETCH, channels)).astype(jnp.bfloat16)

    result = lax.map(one_block, numbers)
    return result.reshape(stretch_total * STRETCH, channels)
```

```python
import functools

import jax
import jax.numpy as jnp
from jax import lax
from jax.experimental import pallas as pl
from jax.experimental.pallas import tpu as pltpu
from jax.sharding import PartitionSpec as P

GROUP_CH = 16
STRETCH = 128
WIN = 4
SENT = WIN - 1
LANES = 128
BLOCKS = LANES // GROUP_CH
CHUNKS = 4
VMEM_LIMIT = 40 * 1024 * 1024

SMEM_SPEC = pl.BlockSpec(memory_space=pltpu.SMEM)
ANY_SPEC = pl.BlockSpec(memory_space=pl.ANY)


def params():
    return pltpu.CompilerParams(vmem_limit_bytes=VMEM_LIMIT)


def lane_block(shape):
    return lax.broadcasted_iota(jnp.int32, shape, 1) // GROUP_CH


def block_transpose(tiles):
    block = lane_block(tiles[0].shape)
    tiles = list(tiles)
    for distance in (4, 2, 1):
        low = (block & distance) == 0
        for first in range(BLOCKS):
            if first & distance:
                continue
            a, b = tiles[first], tiles[first + distance]
            shift = GROUP_CH * distance
            tiles[first] = jnp.where(low, a, pltpu.roll(b, shift, 1))
            tiles[first + distance] = jnp.where(low, pltpu.roll(a, LANES - shift, 1), b)
    return tiles


def gate_kernel(sources, owner, myself, key, value, own, meta, rows, sems):
    stretch_count = owner.shape[0]
    chunks, _, _, width = own.shape
    me = myself[0]
    slots = key.shape[0] // STRETCH
    for w in range(SENT):
        stretch = sources[w]
        holder = owner[stretch]
        meta[w] = holder

        def count(k, total, holder=holder, stretch=stretch):
            return total + jnp.where((owner[k] == holder) & (k < stretch), 1, 0)

        slot = lax.fori_loop(0, stretch_count, count, 0)

        @pl.when(holder == me)
        def _(w=w, slot=slot):
            start = pl.multiple_of(slot * STRETCH, STRETCH)
            pltpu.make_async_copy(key.at[pl.ds(start, STRETCH)], rows.at[w, 0], sems.at[w, 0]).start()
            pltpu.make_async_copy(value.at[pl.ds(start, STRETCH)], rows.at[w, 1], sems.at[w, 1]).start()

    def target(k, slot):
        mine = owner[k] == me

        @pl.when(mine)
        def _():
            for w in range(WIN):
                lag_block = jnp.maximum(k - sources[w], -1)
                meta[SENT + slot * WIN + w] = (stretch_count - 1 - lag_block) * STRETCH

        return slot + jnp.where(mine, 1, 0)

    lax.fori_loop(0, stretch_count, target, 0)
    meta[SENT + slots * WIN] = me

    for w in range(SENT):

        @pl.when(owner[sources[w]] == me)
        def _(w=w):
            pltpu.make_async_copy(key.at[pl.ds(0, STRETCH)], rows.at[w, 0], sems.at[w, 0]).wait()
            pltpu.make_async_copy(value.at[pl.ds(0, STRETCH)], rows.at[w, 1], sems.at[w, 1]).wait()
            for chunk in range(chunks):
                columns = pl.ds(chunk * width, width)
                product = rows[w, 0, :, columns].astype(jnp.float32) * rows[w, 1, :, columns].astype(
                    jnp.float32
                )
                own[chunk, w] = product.astype(jnp.bfloat16)


def gate(sources, owner, myself, key_proj, value_proj):
    channels = key_proj.shape[1]
    slots = key_proj.shape[0] // STRETCH
    width = channels // CHUNKS
    return pl.pallas_call(
        gate_kernel,
        in_specs=[SMEM_SPEC] * 3 + [ANY_SPEC] * 2,
        out_specs=[pl.BlockSpec(memory_space=pltpu.VMEM), SMEM_SPEC],
        out_shape=[
            jax.ShapeDtypeStruct((CHUNKS, SENT, STRETCH, width), jnp.bfloat16),
            jax.ShapeDtypeStruct((SENT + slots * WIN + 1,), jnp.int32),
        ],
        scratch_shapes=[
            pltpu.VMEM((SENT, 2, STRETCH, channels), jnp.bfloat16),
            pltpu.SemaphoreType.DMA((SENT, 2)),
        ],
        compiler_params=params(),
        name="gate",
    )(sources, owner, myself, key_proj, value_proj)


def relay_kernel(step, first, size, meta, own, *refs):
    out_up, out_down, sems = refs[-3:]
    chunks = own.shape[0]
    me = meta[meta.shape[0] - 1]
    for out, chunk, lane in ((out_up, step - me, 0), (out_down, step - (size - 1 - me), 1)):
        valid = (chunk >= 0) & (chunk < chunks)
        for phase in range(2):
            for w in range(SENT):

                @pl.when(valid & (meta[w] == me))
                def _(w=w, out=out, chunk=chunk, lane=lane, phase=phase):
                    copy = pltpu.make_async_copy(own.at[chunk, w], out.at[w], sems.at[lane, w])
                    if phase == 0:
                        copy.start()
                    else:
                        copy.wait()


def relay(step, size, meta, own, received):
    shape = jax.ShapeDtypeStruct(own.shape[1:], own.dtype)
    first = received is None
    received = () if first else received
    return pl.pallas_call(
        functools.partial(relay_kernel, step, first, size),
        in_specs=[SMEM_SPEC, ANY_SPEC] + [ANY_SPEC] * len(received),
        out_specs=[ANY_SPEC] * 2,
        out_shape=[shape, shape],
        input_output_aliases={} if first else {2: 0, 3: 1},
        scratch_shapes=[pltpu.SemaphoreType.DMA((2, SENT))],
        compiler_params=params(),
        name="relay",
    )(meta, own, *received)


def lags_kernel(size, myself, own, *refs):
    ups, downs = refs[: size - 1], refs[size - 1 : 2 * (size - 1)]
    out, blocks, reverse, sems = refs[2 * (size - 1) :]
    group_count, part = own.shape
    lag_count = size * part
    padded = out.shape[2]
    step = pl.program_id(0)

    @pl.when(step == 0)
    def _():
        me = myself[0]
        for phase in range(2):
            for shard in range(size):
                for source, where in (
                    [(own, me == shard)]
                    + [(ups[hop], me - shard == hop + 1) for hop in range(size - 1)]
                    + [(downs[hop], shard - me == hop + 1) for hop in range(size - 1)]
                ):

                    @pl.when(where)
                    def _(source=source, shard=shard, phase=phase):
                        copy = pltpu.make_async_copy(source, blocks.at[shard], sems.at[shard])
                        if phase == 0:
                            copy.start()
                        else:
                            copy.wait()

        row = lax.broadcasted_iota(jnp.int32, (LANES, LANES), 0)
        column = lax.broadcasted_iota(jnp.int32, (LANES, LANES), 1)
        flip = jnp.where(row + column == LANES - 1, 1.0, 0.0).astype(jnp.bfloat16)
        for start in range(0, lag_count, LANES):
            piece = blocks[start // part, :, pl.ds(start % part, LANES)]
            reverse[:, pl.ds(lag_count - LANES - start, LANES)] = jnp.dot(
                piece, flip, preferred_element_type=jnp.float32
            )
        reverse[:, pl.ds(lag_count, padded - lag_count)] = jnp.zeros(
            (group_count, padded - lag_count), jnp.float32
        )

    row = lax.broadcasted_iota(jnp.int32, (GROUP_CH, LANES), 0)
    column = lax.broadcasted_iota(jnp.int32, (GROUP_CH, LANES), 1)
    inside = column > row
    tile_rows = pl.ds(pl.multiple_of(step * BLOCKS, BLOCKS), BLOCKS)
    before = [jnp.zeros((GROUP_CH, LANES), jnp.float32)] * BLOCKS
    for start in range(0, padded, LANES):
        tile = reverse[tile_rows, pl.ds(start, LANES)]
        for g in range(BLOCKS):
            spread = jnp.broadcast_to(tile[g : g + 1, :], (GROUP_CH, LANES))
            rolled = pltpu.roll(spread, 1, 1, stride=1, stride_axis=0)
            out[g, :, pl.ds(start, LANES)] = jnp.where(inside, rolled, before[g]).astype(jnp.bfloat16)
            before[g] = rolled


def lags(size, myself, own, ups, downs):
    group_count, part = own.shape
    padded = size * part + 2 * STRETCH
    return pl.pallas_call(
        functools.partial(lags_kernel, size),
        grid=(group_count // BLOCKS,),
        in_specs=[SMEM_SPEC] + [ANY_SPEC] * (2 * size - 1),
        out_specs=pl.BlockSpec((BLOCKS, GROUP_CH, padded), lambda i: (i, 0, 0)),
        out_shape=jax.ShapeDtypeStruct((group_count, GROUP_CH, padded), jnp.bfloat16),
        scratch_shapes=[
            pltpu.VMEM((size, group_count, part), jnp.bfloat16),
            pltpu.VMEM((group_count, padded), jnp.float32),
            pltpu.SemaphoreType.DMA((size,)),
        ],
        compiler_params=params(),
        name="lags",
    )(myself, own, *ups, *downs)


def conv_kernel(size, chunk, meta, own, key, value, query, shifted, *refs):
    ups, downs = refs[: size - 1], refs[size - 1 : 2 * (size - 1)]
    out, pieces, spans, sems = refs[-4:]
    slots = query.shape[0] // STRETCH
    step = pl.program_id(0)

    @pl.when(step == 0)
    def _():
        me = meta[meta.shape[0] - 1]
        for phase in range(2):
            for w in range(SENT):
                holder = meta[w]
                for source, where in (
                    [(own.at[chunk], me == holder)]
                    + [(ups[hop], (holder < me) & (me == hop + 1)) for hop in range(size - 1)]
                    + [
                        (downs[hop], (holder > me) & (size - 1 - me == hop + 1))
                        for hop in range(size - 1)
                    ]
                ):

                    @pl.when(where)
                    def _(source=source, w=w, phase=phase):
                        copy = pltpu.make_async_copy(source.at[w], pieces.at[w], sems.at[w])
                        if phase == 0:
                            copy.start()
                        else:
                            copy.wait()

    columns = pl.ds(pl.multiple_of(step * LANES, LANES), LANES)
    block = lane_block((GROUP_CH, LANES))
    zero = jnp.zeros((GROUP_CH, LANES), jnp.bfloat16)
    for w in range(WIN):
        if w < SENT:
            rows = [pieces[w, pl.ds(GROUP_CH * m, GROUP_CH), columns] for m in range(BLOCKS)]
        else:
            rows = [
                (
                    key[pl.ds(GROUP_CH * m, GROUP_CH), :].astype(jnp.float32)
                    * value[pl.ds(GROUP_CH * m, GROUP_CH), :].astype(jnp.float32)
                ).astype(jnp.bfloat16)
                for m in range(BLOCKS)
            ]
        base = w * 2 * STRETCH
        for g, tile in enumerate(block_transpose(rows)):
            spans[g, pl.ds(base, GROUP_CH), :] = zero
            for lead in range(1 - BLOCKS, BLOCKS):
                if lead == 0:
                    moved = tile
                else:
                    moved = pltpu.roll(tile, (-lead * GROUP_CH) % LANES, 1)
                    kept = block < BLOCKS - lead if lead > 0 else block >= -lead
                    moved = jnp.where(kept, moved, zero)
                spans[g, pl.ds(base + (lead + BLOCKS) * GROUP_CH, GROUP_CH), :] = moved

    results = []
    for g in range(BLOCKS):
        filter_rows = []
        for slot in range(slots):
            filter_rows.append(
                jnp.concatenate(
                    [
                        shifted[
                            g,
                            :,
                            pl.ds(pl.multiple_of(meta[SENT + slot * WIN + w], STRETCH), 2 * STRETCH),
                        ]
                        for w in range(WIN)
                    ],
                    axis=1,
                )
            )
        results.append(
            jnp.dot(jnp.concatenate(filter_rows, axis=0), spans[g], preferred_element_type=jnp.float32)
        )
    for slot in range(slots):
        tiles = [result[slot * GROUP_CH : (slot + 1) * GROUP_CH] for result in results]
        for m, tile in enumerate(block_transpose(tiles)):
            place = pl.ds(slot * STRETCH + m * GROUP_CH, GROUP_CH)
            out[place, :] = (query[place, :].astype(jnp.float32) * tile).astype(jnp.bfloat16)


def conv(size, chunk, meta, own, key_proj, value_proj, query_proj, shifted, ups, downs, before):
    row_count, channels = query_proj.shape
    width = channels // CHUNKS
    steps = width // LANES
    last = row_count // STRETCH - 1
    padded = shifted.shape[2]
    operands = [meta, own, key_proj, value_proj, query_proj, shifted, *ups, *downs]
    in_specs = [
        SMEM_SPEC,
        ANY_SPEC,
        pl.BlockSpec((STRETCH, LANES), lambda i: (last, chunk * steps + i)),
        pl.BlockSpec((STRETCH, LANES), lambda i: (last, chunk * steps + i)),
        pl.BlockSpec((row_count, LANES), lambda i: (0, chunk * steps + i)),
        pl.BlockSpec((BLOCKS, GROUP_CH, padded), lambda i: (chunk * steps + i, 0, 0)),
    ] + [ANY_SPEC] * (2 * size - 2)
    aliases = {}
    if before is not None:
        aliases = {len(operands): 0}
        operands.append(before)
        in_specs.append(ANY_SPEC)
    return pl.pallas_call(
        functools.partial(conv_kernel, size, chunk),
        grid=(steps,),
        in_specs=in_specs,
        out_specs=pl.BlockSpec((row_count, LANES), lambda i: (0, chunk * steps + i)),
        out_shape=jax.ShapeDtypeStruct((row_count, channels), jnp.bfloat16),
        input_output_aliases=aliases,
        scratch_shapes=[
            pltpu.VMEM((SENT, STRETCH, width), jnp.bfloat16),
            pltpu.VMEM((BLOCKS, WIN * 2 * STRETCH, LANES), jnp.bfloat16),
            pltpu.SemaphoreType.DMA((SENT,)),
        ],
        compiler_params=params(),
        name="conv",
    )(*operands)


def shards(size, key_proj, value_proj, query_proj, filters, sources, owner):
    up = [(z, z + 1) for z in range(size - 1)]
    down = [(z + 1, z) for z in range(size - 1)]
    myself = lax.axis_index("seq").astype(jnp.int32).reshape(1)
    own, meta = gate(sources, owner, myself, key_proj, value_proj)

    sent = [relay(0, size, meta, own, None)]
    for step in range(CHUNKS + size - 2):
        received = (
            lax.ppermute(sent[step][0], "seq", up),
            lax.ppermute(sent[step][1], "seq", down),
        )
        if step < CHUNKS + size - 3:
            received = relay(step + 1, size, meta, own, received)
        sent.append(received)

    filter_ups, filter_downs = [filters], [filters]
    for _ in range(size - 1):
        filter_ups.append(lax.ppermute(filter_ups[-1], "seq", up))
        filter_downs.append(lax.ppermute(filter_downs[-1], "seq", down))
    shifted = lags(size, myself, filters, filter_ups[1:], filter_downs[1:])

    out = None
    for chunk in range(CHUNKS):
        ups = [sent[chunk + hop][0] for hop in range(1, size)]
        downs = [sent[chunk + hop][1] for hop in range(1, size)]
        out = conv(
            size, chunk, meta, own, key_proj, value_proj, query_proj, shifted, ups, downs, out
        )
    return out


def solution(mesh):
    return jax.shard_map(
        functools.partial(shards, mesh.shape["seq"]),
        mesh=mesh,
        in_specs=(
            P(("rep", "seq"), "ch"),
            P(("rep", "seq"), "ch"),
            P(("rep", "seq"), "ch"),
            P("ch", "seq"),
            P("rep"),
            P("rep"),
        ),
        out_specs=P(("rep", "seq"), "ch"),
        check_vma=False,
    )
```

```python
import functools

import jax
import jax.numpy as jnp
from jax import lax
from jax.experimental import pallas as pl
from jax.experimental.pallas import tpu as pltpu
from jax.sharding import PartitionSpec as P

GROUP_CH = 16
STRETCH = 128
WIN = 4
SENT = WIN - 1
LANES = 128
BLOCKS = LANES // GROUP_CH
SPAN = 2 * STRETCH
VMEM_LIMIT = 40 * 1024 * 1024
GATE_LIMIT = 62 * 1024 * 1024

SMEM_SPEC = pl.BlockSpec(memory_space=pltpu.SMEM)
ANY_SPEC = pl.BlockSpec(memory_space=pl.ANY)
HBM_SPEC = pl.BlockSpec(memory_space=pltpu.HBM)
VMEM_SPEC = pl.BlockSpec(memory_space=pltpu.VMEM)
NT = (((1,), (1,)), ((), ()))


def params(limit=VMEM_LIMIT):
    return pltpu.CompilerParams(vmem_limit_bytes=limit)


def lane_block(shape):
    return lax.broadcasted_iota(jnp.int32, shape, 1) // GROUP_CH


def block_transpose(tiles):
    block = lane_block(tiles[0].shape)
    tiles = list(tiles)
    for distance in (4, 2, 1):
        low = (block & distance) == 0
        for first in range(BLOCKS):
            if first & distance:
                continue
            a, b = tiles[first], tiles[first + distance]
            shift = GROUP_CH * distance
            tiles[first] = jnp.where(low, a, pltpu.roll(b, shift, 1))
            tiles[first + distance] = jnp.where(low, pltpu.roll(a, LANES - shift, 1), b)
    return tiles


def gate_kernel(size, parts, fill, sources_in, owner_in, key, value, *refs):
    sends = refs[:parts]
    last, meta, sources, owner, rows, sems, small = refs[parts:]
    stretch_count = owner.shape[0]
    slots = key.shape[0] // STRETCH
    channels = key.shape[1]
    width = channels // parts
    me = lax.axis_index("seq")
    copies = [
        pltpu.make_async_copy(sources_in, sources, small.at[0]),
        pltpu.make_async_copy(owner_in, owner, small.at[1]),
    ]
    for copy in copies:
        copy.start()

    def fetch(w, start):
        span = pl.ds(start, STRETCH)
        return (
            pltpu.make_async_copy(key.at[span], rows.at[w, 0], sems.at[w, 0]),
            pltpu.make_async_copy(value.at[span], rows.at[w, 1], sems.at[w, 1]),
        )

    for copy in fetch(SENT, (slots - 1) * STRETCH):
        copy.start()
    for copy in copies:
        copy.wait()
    for w in range(SENT):
        stretch = sources[w]
        holder = owner[stretch]
        meta[w] = holder

        @pl.when(holder == me)
        def _(w=w, stretch=stretch, holder=holder):
            def count(k, total):
                return total + jnp.where((owner[k] == holder) & (k < stretch), 1, 0)

            slot = lax.fori_loop(0, stretch_count, count, 0)
            for copy in fetch(w, pl.multiple_of(slot * STRETCH, STRETCH)):
                copy.start()

    def target(k, slot):
        mine = owner[k] == me

        @pl.when(mine)
        def _():
            for w in range(WIN):
                lag_block = jnp.maximum(k - sources[w], -1)
                meta[SENT + slot * WIN + w] = (stretch_count - 1 - lag_block) * STRETCH

        return slot + jnp.where(mine, 1, 0)

    lax.fori_loop(0, stretch_count, target, 0)
    tail = SENT + slots * WIN
    meta[tail] = me
    for shift in range(parts):
        meta[tail + 1 + shift] = lax.rem(me + size - shift, size) if parts > 1 else 0

    def product(w, columns):
        rows_k = rows[w, 0, :, columns].astype(jnp.float32)
        rows_v = rows[w, 1, :, columns].astype(jnp.float32)
        return (rows_k * rows_v).astype(jnp.bfloat16).T

    for copy in fetch(SENT, 0):
        copy.wait()
    for start in range(0, channels, LANES):
        last[pl.ds(start, LANES), :] = product(SENT, pl.ds(start, LANES))
    for w in range(SENT):
        mine = owner[sources[w]] == me

        @pl.when(mine)
        def _(w=w):
            for copy in fetch(w, 0):
                copy.wait()
            for shift in range(parts):
                base = lax.rem(me + shift, parts) * width
                for start in range(0, width, LANES):
                    columns = pl.ds(pl.multiple_of(base + start, LANES), LANES)
                    sends[shift][w, pl.ds(start, LANES), :] = product(w, columns)

        if fill:

            @pl.when(jnp.logical_not(mine))
            def _(w=w):
                for send in sends:
                    send[w] = jnp.zeros(send.shape[1:], send.dtype)


def gate(size, parts, fill, sources, owner, key_proj, value_proj):
    row_count, channels = key_proj.shape
    slots = row_count // STRETCH
    send = jax.ShapeDtypeStruct((SENT, channels // parts, STRETCH), jnp.bfloat16)
    *sends, last, meta = pl.pallas_call(
        functools.partial(gate_kernel, size, parts, fill),
        in_specs=[HBM_SPEC] * 4,
        out_specs=[VMEM_SPEC] * (parts + 1) + [SMEM_SPEC],
        out_shape=[send] * parts
        + [
            jax.ShapeDtypeStruct((channels, STRETCH), jnp.bfloat16),
            jax.ShapeDtypeStruct((SENT + slots * WIN + 1 + parts,), jnp.int32),
        ],
        scratch_shapes=[
            pltpu.SMEM(sources.shape, jnp.int32),
            pltpu.SMEM(owner.shape, jnp.int32),
            pltpu.VMEM((WIN, 2, STRETCH, channels), jnp.bfloat16),
            pltpu.SemaphoreType.DMA((WIN, 2)),
            pltpu.SemaphoreType.DMA((2,)),
        ],
        compiler_params=params(GATE_LIMIT),
        name="gate",
    )(sources, owner, key_proj, value_proj)
    return sends, last, meta


def merge_kernel(size, slots, meta, *refs):
    parts, out = refs[:-1], refs[-1]
    me = meta[SENT + slots * WIN]
    for w in range(SENT):
        shift = lax.rem(me + size - meta[w], size)
        for k in range(size):

            @pl.when(shift == k)
            def _(w=w, k=k):
                out[w] = parts[k][w]


def merge(size, slots, meta, parts):
    return pl.pallas_call(
        functools.partial(merge_kernel, size, slots),
        in_specs=[SMEM_SPEC] + [VMEM_SPEC] * size,
        out_specs=VMEM_SPEC,
        out_shape=jax.ShapeDtypeStruct(parts[0].shape, parts[0].dtype),
        compiler_params=params(),
        name="merge",
    )(meta, *parts)


def lags_kernel(size, *refs):
    received = refs[:size]
    out, blocks, reverse, sems = refs[size:]
    group_count, part = received[0].shape
    lag_count = size * part
    padded = out.shape[2]
    step = pl.program_id(0)

    @pl.when(step == 0)
    def _():
        me = lax.axis_index("seq")
        copies = [
            pltpu.make_async_copy(
                received[shift], blocks.at[lax.rem(me + size - shift, size)], sems.at[shift]
            )
            for shift in range(size)
        ]
        for copy in copies:
            copy.start()
        for copy in copies:
            copy.wait()
        row = lax.broadcasted_iota(jnp.int32, (LANES, LANES), 0)
        column = lax.broadcasted_iota(jnp.int32, (LANES, LANES), 1)
        flip = jnp.where(row + column == LANES - 1, 1.0, 0.0).astype(jnp.bfloat16)
        for start in range(0, lag_count, LANES):
            piece = blocks[start // part, :, pl.ds(start % part, LANES)]
            reverse[:, pl.ds(lag_count - LANES - start, LANES)] = jnp.dot(
                piece, flip, preferred_element_type=jnp.float32
            )
        reverse[:, pl.ds(lag_count, padded - lag_count)] = jnp.zeros(
            (group_count, padded - lag_count), jnp.float32
        )

    row = lax.broadcasted_iota(jnp.int32, (GROUP_CH, LANES), 0)
    column = lax.broadcasted_iota(jnp.int32, (GROUP_CH, LANES), 1)
    inside = column > row
    tile_rows = pl.ds(pl.multiple_of(step * BLOCKS, BLOCKS), BLOCKS)
    before = [jnp.zeros((GROUP_CH, LANES), jnp.float32)] * BLOCKS
    for start in range(0, padded, LANES):
        tile = reverse[tile_rows, pl.ds(start, LANES)]
        for g in range(BLOCKS):
            spread = jnp.broadcast_to(tile[g : g + 1, :], (GROUP_CH, LANES))
            rolled = pltpu.roll(spread, 1, 1, stride=1, stride_axis=0)
            out[g, :, pl.ds(start, LANES)] = jnp.where(inside, rolled, before[g]).astype(jnp.bfloat16)
            before[g] = rolled


def lags(size, received):
    group_count, part = received[0].shape
    padded = size * part + SPAN
    return pl.pallas_call(
        functools.partial(lags_kernel, size),
        grid=(group_count // BLOCKS,),
        in_specs=[ANY_SPEC] * size,
        out_specs=pl.BlockSpec((BLOCKS, GROUP_CH, padded), lambda i: (i, 0, 0)),
        out_shape=jax.ShapeDtypeStruct((group_count, GROUP_CH, padded), jnp.bfloat16),
        scratch_shapes=[
            pltpu.VMEM((size, group_count, part), jnp.bfloat16),
            pltpu.VMEM((group_count, padded), jnp.float32),
            pltpu.SemaphoreType.DMA((size,)),
        ],
        compiler_params=params(),
        name="lags",
    )(*received)


def spread_rows(tile, spans, base):
    lane = lax.broadcasted_iota(jnp.int32, tile.shape, 1)
    zero = jnp.zeros(tile.shape, tile.dtype)
    for i1 in range(BLOCKS):
        shift = GROUP_CH * i1
        if i1 == 0:
            low, high = zero, tile
        else:
            moved = pltpu.roll(tile, LANES - shift, 1)
            early = lane < LANES - shift
            low, high = jnp.where(early, zero, moved), jnp.where(early, moved, zero)
        rows = pl.ds(shift, GROUP_CH)
        for g in range(BLOCKS):
            part = slice(g * GROUP_CH, (g + 1) * GROUP_CH)
            spans[g, rows, pl.ds(base, LANES)] = low[part]
            spans[g, rows, pl.ds(base + LANES, LANES)] = high[part]


def window(meta, shifted, group, slot, w):
    start = pl.multiple_of(meta[SENT + slot * WIN + w], STRETCH)
    return shifted[group, :, pl.ds(start, SPAN)]


def last_kernel(slots, meta, last, shifted, out, spans):
    for start in range(0, last.shape[0], LANES):
        spread_rows(last[pl.ds(start, LANES), :], spans, 0)
        results = [
            lax.dot_general(
                window(meta, shifted, start // GROUP_CH + g, slots - 1, SENT),
                spans[g],
                NT,
                preferred_element_type=jnp.float32,
            )
            for g in range(BLOCKS)
        ]
        for m, tile in enumerate(block_transpose(results)):
            out[pl.ds(m * GROUP_CH, GROUP_CH), pl.ds(start, LANES)] = tile


def last_term(slots, meta, last, shifted):
    return pl.pallas_call(
        functools.partial(last_kernel, slots),
        in_specs=[SMEM_SPEC, VMEM_SPEC, VMEM_SPEC],
        out_specs=VMEM_SPEC,
        out_shape=jax.ShapeDtypeStruct((STRETCH, last.shape[0]), jnp.float32),
        scratch_shapes=[pltpu.VMEM((BLOCKS, LANES, SPAN), jnp.bfloat16)],
        compiler_params=params(),
        name="last_term",
    )(meta, last, shifted)


def conv_kernel(shift, slots, meta, pieces, shifted, term, query, *refs):
    out, gates, result, spans, sems = refs[-5:]
    width = pieces.shape[1]
    row_count = query.shape[0]
    base = pl.multiple_of(meta[SENT + slots * WIN + 1 + shift] * width, width)
    fetch = pltpu.make_async_copy(query.at[:, pl.ds(base, width)], gates, sems.at[0])
    fetch.start()
    for start in range(0, width, LANES):
        columns = pl.ds(start, LANES)
        for w in range(SENT):
            spread_rows(pieces[w, columns, :], spans, w * SPAN)
        results = []
        for g in range(BLOCKS):
            group = base // GROUP_CH + (start // GROUP_CH + g)
            filter_rows = jnp.concatenate(
                [
                    jnp.concatenate([window(meta, shifted, group, slot, w) for w in range(SENT)], axis=1)
                    for slot in range(slots)
                ],
                axis=0,
            )
            results.append(
                lax.dot_general(filter_rows, spans[g], NT, preferred_element_type=jnp.float32)
            )
        if start == 0:
            fetch.wait()
        for slot in range(slots):
            tiles = [value[slot * GROUP_CH : (slot + 1) * GROUP_CH] for value in results]
            for m, tile in enumerate(block_transpose(tiles)):
                place = pl.ds(slot * STRETCH + m * GROUP_CH, GROUP_CH)
                if slot == slots - 1:
                    tile = tile + term[
                        pl.ds(m * GROUP_CH, GROUP_CH), pl.ds(pl.multiple_of(base + start, LANES), LANES)
                    ]
                result[place, columns] = (gates[place, columns].astype(jnp.float32) * tile).astype(
                    jnp.bfloat16
                )
    store = pltpu.make_async_copy(result, out.at[:, pl.ds(base, width)], sems.at[1])
    store.start()
    store.wait()


def conv(shift, meta, pieces, shifted, term, query_proj, before):
    row_count = query_proj.shape[0]
    slots = row_count // STRETCH
    width = pieces.shape[1]
    operands = [meta, pieces, shifted, term, query_proj]
    in_specs = [SMEM_SPEC, VMEM_SPEC, VMEM_SPEC, VMEM_SPEC, HBM_SPEC]
    aliases = {}
    if before is not None:
        aliases = {len(operands): 0}
        operands.append(before)
        in_specs.append(HBM_SPEC)
    return pl.pallas_call(
        functools.partial(conv_kernel, shift, slots),
        in_specs=in_specs,
        out_specs=HBM_SPEC,
        out_shape=jax.ShapeDtypeStruct(query_proj.shape, jnp.bfloat16),
        input_output_aliases=aliases,
        scratch_shapes=[
            pltpu.VMEM((row_count, width), jnp.bfloat16),
            pltpu.VMEM((row_count, width), jnp.bfloat16),
            pltpu.VMEM((BLOCKS, LANES, SENT * SPAN), jnp.bfloat16),
            pltpu.SemaphoreType.DMA((2,)),
        ],
        compiler_params=params(),
        name="conv",
    )(*operands)


def shards(size, key_proj, value_proj, query_proj, filters, sources, owner):
    row_count, channels = key_proj.shape
    slots = row_count // STRETCH
    by_parts = channels % (size * LANES) == 0
    parts = size if by_parts else 1

    def shifted_by(value, shift):
        return lax.ppermute(value, "seq", [(z, (z + shift) % size) for z in range(size)])

    filter_parts = [filters] + [shifted_by(filters, shift) for shift in range(1, size)]
    sends, last, meta = gate(size, parts, not by_parts, sources, owner, key_proj, value_proj)
    shifted = lags(size, filter_parts)
    term = last_term(slots, meta, last, shifted)
    if by_parts:
        scattered = [sends[0]] + [shifted_by(sends[shift], shift) for shift in range(1, size)]
        term, *scattered = lax.optimization_barrier((term, *scattered))
        merged = merge(size, slots, meta, scattered)
        gathered = [merged] + [shifted_by(merged, shift) for shift in range(1, size)]
    else:
        gathered = [lax.psum(sends[0], "seq")]
    out = None
    for shift, pieces in enumerate(gathered):
        out = conv(shift, meta, pieces, shifted, term, query_proj, out)
    return out


def solution(mesh):
    return jax.shard_map(
        functools.partial(shards, mesh.shape["seq"]),
        mesh=mesh,
        in_specs=(
            P(("rep", "seq"), "ch"),
            P(("rep", "seq"), "ch"),
            P(("rep", "seq"), "ch"),
            P("ch", "seq"),
            P("rep"),
            P("rep"),
        ),
        out_specs=P(("rep", "seq"), "ch"),
        check_vma=False,
    )
```

```python
import functools

import jax
import jax.numpy as jnp
from jax import lax
from jax.experimental import pallas as pl
from jax.experimental.pallas import tpu as pltpu
from jax.sharding import PartitionSpec as P

GROUP_CH = 16
STRETCH = 128
WIN = 4
SENT = WIN - 1
LANES = 128
BLOCKS = LANES // GROUP_CH
SPAN = 2 * STRETCH
VMEM_LIMIT = 40 * 1024 * 1024

SMEM_SPEC = pl.BlockSpec(memory_space=pltpu.SMEM)
ANY_SPEC = pl.BlockSpec(memory_space=pl.ANY)
HBM_SPEC = pl.BlockSpec(memory_space=pltpu.HBM)
VMEM_SPEC = pl.BlockSpec(memory_space=pltpu.VMEM)
NT = (((1,), (1,)), ((), ()))


def params():
    return pltpu.CompilerParams(vmem_limit_bytes=VMEM_LIMIT)


def lane_block(shape):
    return lax.broadcasted_iota(jnp.int32, shape, 1) // GROUP_CH


def block_transpose(tiles):
    block = lane_block(tiles[0].shape)
    tiles = list(tiles)
    for distance in (4, 2, 1):
        low = (block & distance) == 0
        for first in range(BLOCKS):
            if first & distance:
                continue
            a, b = tiles[first], tiles[first + distance]
            shift = GROUP_CH * distance
            tiles[first] = jnp.where(low, a, pltpu.roll(b, shift, 1))
            tiles[first + distance] = jnp.where(low, pltpu.roll(a, LANES - shift, 1), b)
    return tiles


def gate_kernel(size, parts, fill, sources_in, owner_in, key_in, value_in, *refs):
    sends = refs[:parts]
    last, meta, sources, owner, key, value, sems = refs[parts:]
    stretch_count = owner.shape[0]
    slots = key.shape[0] // STRETCH
    channels = key.shape[1]
    width = channels // parts
    me = lax.axis_index("seq")
    copies = [
        pltpu.make_async_copy(sources_in, sources, sems.at[0]),
        pltpu.make_async_copy(owner_in, owner, sems.at[1]),
        pltpu.make_async_copy(key_in, key, sems.at[2]),
        pltpu.make_async_copy(value_in, value, sems.at[3]),
    ]
    for copy in copies:
        copy.start()

    def product(start, columns):
        rows = pl.ds(start, STRETCH)
        rows_k = key[rows, columns].astype(jnp.float32)
        rows_v = value[rows, columns].astype(jnp.float32)
        return (rows_k * rows_v).astype(jnp.bfloat16).T

    for copy in copies[:2]:
        copy.wait()

    def target(k, slot):
        mine = owner[k] == me

        @pl.when(mine)
        def _():
            for w in range(WIN):
                lag_block = jnp.maximum(k - sources[w], -1)
                meta[SENT + slot * WIN + w] = (stretch_count - 1 - lag_block) * STRETCH

        return slot + jnp.where(mine, 1, 0)

    lax.fori_loop(0, stretch_count, target, 0)
    tail = SENT + slots * WIN
    meta[tail] = me
    for shift in range(parts):
        meta[tail + 1 + shift] = lax.rem(me + size - shift, size) if parts > 1 else 0

    for copy in copies[2:]:
        copy.wait()
    for start in range(0, channels, LANES):
        last[pl.ds(start, LANES), :] = product((slots - 1) * STRETCH, pl.ds(start, LANES))
    for w in range(SENT):
        stretch = sources[w]
        holder = owner[stretch]
        mine = holder == me
        meta[w] = holder

        @pl.when(mine)
        def _(w=w, stretch=stretch, holder=holder):
            def count(k, total):
                return total + jnp.where(owner[k] == holder, 1, 0)

            slot = lax.fori_loop(0, stretch, count, 0)
            first = pl.multiple_of(slot * STRETCH, STRETCH)
            for shift in range(parts):
                base = lax.rem(me + shift, parts) * width
                for start in range(0, width, LANES):
                    columns = pl.ds(pl.multiple_of(base + start, LANES), LANES)
                    sends[shift][w, pl.ds(start, LANES), :] = product(first, columns)

        if fill:

            @pl.when(jnp.logical_not(mine))
            def _(w=w):
                for send in sends:
                    send[w] = jnp.zeros(send.shape[1:], send.dtype)


def gate(size, parts, fill, sources, owner, key_proj, value_proj):
    row_count, channels = key_proj.shape
    slots = row_count // STRETCH
    operands = [
        pltpu.with_memory_space_constraint(operand, pltpu.HBM)
        for operand in (sources, owner, key_proj, value_proj)
    ]
    send = jax.ShapeDtypeStruct((SENT, channels // parts, STRETCH), jnp.bfloat16)
    *sends, last, meta = pl.pallas_call(
        functools.partial(gate_kernel, size, parts, fill),
        in_specs=[HBM_SPEC] * 4,
        out_specs=[VMEM_SPEC] * (parts + 1) + [SMEM_SPEC],
        out_shape=[send] * parts
        + [
            jax.ShapeDtypeStruct((channels, STRETCH), jnp.bfloat16),
            jax.ShapeDtypeStruct((SENT + slots * WIN + 1 + parts,), jnp.int32),
        ],
        scratch_shapes=[
            pltpu.SMEM(sources.shape, jnp.int32),
            pltpu.SMEM(owner.shape, jnp.int32),
            pltpu.VMEM(key_proj.shape, key_proj.dtype),
            pltpu.VMEM(value_proj.shape, value_proj.dtype),
            pltpu.SemaphoreType.DMA((4,)),
        ],
        compiler_params=params(),
        name="gate",
    )(*operands)
    return sends, last, meta


def merge_kernel(size, slots, meta, *refs):
    parts, out = refs[:-1], refs[-1]
    me = meta[SENT + slots * WIN]
    for w in range(SENT):
        shift = lax.rem(me + size - meta[w], size)
        for k in range(size):

            @pl.when(shift == k)
            def _(w=w, k=k):
                out[w] = parts[k][w]


def merge(size, slots, meta, parts):
    return pl.pallas_call(
        functools.partial(merge_kernel, size, slots),
        in_specs=[SMEM_SPEC] + [VMEM_SPEC] * size,
        out_specs=VMEM_SPEC,
        out_shape=jax.ShapeDtypeStruct(parts[0].shape, parts[0].dtype),
        compiler_params=params(),
        name="merge",
    )(meta, *parts)


def lags_kernel(size, *refs):
    received = refs[:size]
    out, blocks, reverse, sems = refs[size:]
    group_count, part = received[0].shape
    lag_count = size * part
    padded = out.shape[2]
    step = pl.program_id(0)

    @pl.when(step == 0)
    def _():
        me = lax.axis_index("seq")
        copies = [
            pltpu.make_async_copy(
                received[shift], blocks.at[lax.rem(me + size - shift, size)], sems.at[shift]
            )
            for shift in range(size)
        ]
        for copy in copies:
            copy.start()
        for copy in copies:
            copy.wait()
        row = lax.broadcasted_iota(jnp.int32, (LANES, LANES), 0)
        column = lax.broadcasted_iota(jnp.int32, (LANES, LANES), 1)
        flip = jnp.where(row + column == LANES - 1, 1.0, 0.0).astype(jnp.bfloat16)
        for start in range(0, lag_count, LANES):
            piece = blocks[start // part, :, pl.ds(start % part, LANES)]
            reverse[:, pl.ds(lag_count - LANES - start, LANES)] = jnp.dot(
                piece, flip, preferred_element_type=jnp.float32
            )
        reverse[:, pl.ds(lag_count, padded - lag_count)] = jnp.zeros(
            (group_count, padded - lag_count), jnp.float32
        )

    row = lax.broadcasted_iota(jnp.int32, (GROUP_CH, LANES), 0)
    column = lax.broadcasted_iota(jnp.int32, (GROUP_CH, LANES), 1)
    inside = column > row
    tile_rows = pl.ds(pl.multiple_of(step * BLOCKS, BLOCKS), BLOCKS)
    before = [jnp.zeros((GROUP_CH, LANES), jnp.float32)] * BLOCKS
    for start in range(0, padded, LANES):
        tile = reverse[tile_rows, pl.ds(start, LANES)]
        for g in range(BLOCKS):
            spread = jnp.broadcast_to(tile[g : g + 1, :], (GROUP_CH, LANES))
            rolled = pltpu.roll(spread, 1, 1, stride=1, stride_axis=0)
            out[g, :, pl.ds(start, LANES)] = jnp.where(inside, rolled, before[g]).astype(jnp.bfloat16)
            before[g] = rolled


def lags(size, received):
    group_count, part = received[0].shape
    padded = size * part + SPAN
    return pl.pallas_call(
        functools.partial(lags_kernel, size),
        grid=(group_count // BLOCKS,),
        in_specs=[ANY_SPEC] * size,
        out_specs=pl.BlockSpec((BLOCKS, GROUP_CH, padded), lambda i: (i, 0, 0)),
        out_shape=jax.ShapeDtypeStruct((group_count, GROUP_CH, padded), jnp.bfloat16),
        scratch_shapes=[
            pltpu.VMEM((size, group_count, part), jnp.bfloat16),
            pltpu.VMEM((group_count, padded), jnp.float32),
            pltpu.SemaphoreType.DMA((size,)),
        ],
        compiler_params=params(),
        name="lags",
    )(*received)


def spread_rows(tile, spans, base):
    lane = lax.broadcasted_iota(jnp.int32, tile.shape, 1)
    zero = jnp.zeros(tile.shape, tile.dtype)
    for i1 in range(BLOCKS):
        shift = GROUP_CH * i1
        if i1 == 0:
            low, high = zero, tile
        else:
            moved = pltpu.roll(tile, LANES - shift, 1)
            early = lane < LANES - shift
            low, high = jnp.where(early, zero, moved), jnp.where(early, moved, zero)
        rows = pl.ds(shift, GROUP_CH)
        for g in range(BLOCKS):
            part = slice(g * GROUP_CH, (g + 1) * GROUP_CH)
            spans[g, rows, pl.ds(base, LANES)] = low[part]
            spans[g, rows, pl.ds(base + LANES, LANES)] = high[part]


def window(meta, shifted, group, slot, w):
    start = pl.multiple_of(meta[SENT + slot * WIN + w], STRETCH)
    return shifted[group, :, pl.ds(start, SPAN)]


def last_kernel(slots, meta, last, shifted, out, spans):
    for start in range(0, last.shape[0], LANES):
        spread_rows(last[pl.ds(start, LANES), :], spans, 0)
        results = [
            lax.dot_general(
                window(meta, shifted, start // GROUP_CH + g, slots - 1, SENT),
                spans[g],
                NT,
                preferred_element_type=jnp.float32,
            )
            for g in range(BLOCKS)
        ]
        for m, tile in enumerate(block_transpose(results)):
            out[pl.ds(m * GROUP_CH, GROUP_CH), pl.ds(start, LANES)] = tile


def last_term(slots, meta, last, shifted):
    return pl.pallas_call(
        functools.partial(last_kernel, slots),
        in_specs=[SMEM_SPEC, VMEM_SPEC, VMEM_SPEC],
        out_specs=VMEM_SPEC,
        out_shape=jax.ShapeDtypeStruct((STRETCH, last.shape[0]), jnp.float32),
        scratch_shapes=[pltpu.VMEM((BLOCKS, LANES, SPAN), jnp.bfloat16)],
        compiler_params=params(),
        name="last_term",
    )(meta, last, shifted)


def conv_kernel(shift, slots, meta, pieces, shifted, term, query, *refs):
    out, gates, result, spans, sems = refs[-5:]
    width = pieces.shape[1]
    row_count = query.shape[0]
    base = pl.multiple_of(meta[SENT + slots * WIN + 1 + shift] * width, width)
    fetch = pltpu.make_async_copy(query.at[:, pl.ds(base, width)], gates, sems.at[0])
    fetch.start()
    for start in range(0, width, LANES):
        columns = pl.ds(start, LANES)
        for w in range(SENT):
            spread_rows(pieces[w, columns, :], spans, w * SPAN)
        results = []
        for g in range(BLOCKS):
            group = base // GROUP_CH + (start // GROUP_CH + g)
            filter_rows = jnp.concatenate(
                [
                    jnp.concatenate([window(meta, shifted, group, slot, w) for w in range(SENT)], axis=1)
                    for slot in range(slots)
                ],
                axis=0,
            )
            results.append(
                lax.dot_general(filter_rows, spans[g], NT, preferred_element_type=jnp.float32)
            )
        if start == 0:
            fetch.wait()
        for slot in range(slots):
            tiles = [value[slot * GROUP_CH : (slot + 1) * GROUP_CH] for value in results]
            for m, tile in enumerate(block_transpose(tiles)):
                place = pl.ds(slot * STRETCH + m * GROUP_CH, GROUP_CH)
                if slot == slots - 1:
                    tile = tile + term[
                        pl.ds(m * GROUP_CH, GROUP_CH), pl.ds(pl.multiple_of(base + start, LANES), LANES)
                    ]
                result[place, columns] = (gates[place, columns].astype(jnp.float32) * tile).astype(
                    jnp.bfloat16
                )
    store = pltpu.make_async_copy(result, out.at[:, pl.ds(base, width)], sems.at[1])
    store.start()
    store.wait()


def conv(shift, meta, pieces, shifted, term, query_proj, before):
    row_count = query_proj.shape[0]
    slots = row_count // STRETCH
    width = pieces.shape[1]
    operands = [meta, pieces, shifted, term, query_proj]
    in_specs = [SMEM_SPEC, VMEM_SPEC, VMEM_SPEC, VMEM_SPEC, HBM_SPEC]
    aliases = {}
    if before is not None:
        aliases = {len(operands): 0}
        operands.append(before)
        in_specs.append(HBM_SPEC)
    return pl.pallas_call(
        functools.partial(conv_kernel, shift, slots),
        in_specs=in_specs,
        out_specs=HBM_SPEC,
        out_shape=jax.ShapeDtypeStruct(query_proj.shape, jnp.bfloat16),
        input_output_aliases=aliases,
        scratch_shapes=[
            pltpu.VMEM((row_count, width), jnp.bfloat16),
            pltpu.VMEM((row_count, width), jnp.bfloat16),
            pltpu.VMEM((BLOCKS, LANES, SENT * SPAN), jnp.bfloat16),
            pltpu.SemaphoreType.DMA((2,)),
        ],
        compiler_params=params(),
        name="conv",
    )(*operands)


def shards(size, key_proj, value_proj, query_proj, filters, sources, owner):
    row_count, channels = key_proj.shape
    slots = row_count // STRETCH
    by_parts = channels % (size * LANES) == 0
    parts = size if by_parts else 1

    def shifted_by(value, shift):
        return lax.ppermute(value, "seq", [(z, (z + shift) % size) for z in range(size)])

    filter_parts = [filters] + [shifted_by(filters, shift) for shift in range(1, size)]
    sends, last, meta = gate(size, parts, not by_parts, sources, owner, key_proj, value_proj)
    sends, filter_parts = lax.optimization_barrier((sends, filter_parts))
    shifted = lags(size, filter_parts)
    term = last_term(slots, meta, last, shifted)
    if by_parts:
        scattered = [sends[0]] + [shifted_by(sends[shift], shift) for shift in range(1, size)]
        term, *scattered = lax.optimization_barrier((term, *scattered))
        merged = merge(size, slots, meta, scattered)
        order = sorted(range(1, size), key=lambda shift: min(shift, size - shift))
        gathered = [(0, merged)]
        for shift in order[:-1]:
            gathered.append((shift, shifted_by(merged, shift)))
        out = conv(0, meta, merged, shifted, term, query_proj, None)
        if len(order) > 1:
            shift, first = gathered[1]
            merged, first, out = lax.optimization_barrier((merged, first, out))
            gathered[1] = (shift, first)
        for shift in order[-1:]:
            gathered.append((shift, shifted_by(merged, shift)))
        gathered = gathered[1:]
    else:
        gathered = [(0, lax.psum(sends[0], "seq"))]
        out = None
    for shift, pieces in gathered:
        out = conv(shift, meta, pieces, shifted, term, query_proj, out)
    return out


def solution(mesh):
    return jax.shard_map(
        functools.partial(shards, mesh.shape["seq"]),
        mesh=mesh,
        in_specs=(
            P(("rep", "seq"), "ch"),
            P(("rep", "seq"), "ch"),
            P(("rep", "seq"), "ch"),
            P("ch", "seq"),
            P("rep"),
            P("rep"),
        ),
        out_specs=P(("rep", "seq"), "ch"),
        check_vma=False,
    )
```

```python
import functools

import jax
import jax.numpy as jnp
from jax import lax
from jax.experimental import pallas as pl
from jax.experimental.pallas import tpu as pltpu
from jax.sharding import PartitionSpec as P

GROUP_CH = 16
STRETCH = 128
WIN = 4
SENT = WIN - 1
LANES = 128
BLOCKS = LANES // GROUP_CH
SPAN = 2 * STRETCH
VMEM_LIMIT = 40 * 1024 * 1024

SMEM_SPEC = pl.BlockSpec(memory_space=pltpu.SMEM)
ANY_SPEC = pl.BlockSpec(memory_space=pl.ANY)
HBM_SPEC = pl.BlockSpec(memory_space=pltpu.HBM)
VMEM_SPEC = pl.BlockSpec(memory_space=pltpu.VMEM)
NT = (((1,), (1,)), ((), ()))


def params():
    return pltpu.CompilerParams(vmem_limit_bytes=VMEM_LIMIT)


def partner(me, step, size):
    return me ^ step if size & (size - 1) == 0 else lax.rem(me + step, size)


def sender(me, step, size):
    return me ^ step if size & (size - 1) == 0 else lax.rem(me + size - step, size)


def lane_block(shape):
    return lax.broadcasted_iota(jnp.int32, shape, 1) // GROUP_CH


def block_transpose(tiles):
    block = lane_block(tiles[0].shape)
    tiles = list(tiles)
    for distance in (4, 2, 1):
        low = (block & distance) == 0
        for first in range(BLOCKS):
            if first & distance:
                continue
            a, b = tiles[first], tiles[first + distance]
            shift = GROUP_CH * distance
            tiles[first] = jnp.where(low, a, pltpu.roll(b, shift, 1))
            tiles[first + distance] = jnp.where(low, pltpu.roll(a, LANES - shift, 1), b)
    return tiles


def gate_kernel(size, parts, fill, sources_in, owner_in, key_in, value_in, *refs):
    sends = refs[:parts]
    last, meta, sources, owner, key, value, sems = refs[parts:]
    stretch_count = owner.shape[0]
    slots = key.shape[0] // STRETCH
    channels = key.shape[1]
    width = channels // parts
    me = lax.axis_index("seq")
    copies = [
        pltpu.make_async_copy(sources_in, sources, sems.at[0]),
        pltpu.make_async_copy(owner_in, owner, sems.at[1]),
        pltpu.make_async_copy(key_in, key, sems.at[2]),
        pltpu.make_async_copy(value_in, value, sems.at[3]),
    ]
    for copy in copies:
        copy.start()

    def product(start, columns):
        rows = pl.ds(start, STRETCH)
        rows_k = key[rows, columns].astype(jnp.float32)
        rows_v = value[rows, columns].astype(jnp.float32)
        return (rows_k * rows_v).astype(jnp.bfloat16).T

    for copy in copies[:2]:
        copy.wait()

    def target(k, slot):
        mine = owner[k] == me

        @pl.when(mine)
        def _():
            for w in range(WIN):
                lag_block = jnp.maximum(k - sources[w], -1)
                meta[SENT + slot * WIN + w] = (stretch_count - 1 - lag_block) * STRETCH

        return slot + jnp.where(mine, 1, 0)

    lax.fori_loop(0, stretch_count, target, 0)
    for copy in copies[2:]:
        copy.wait()
    for start in range(0, channels, LANES):
        last[pl.ds(start, LANES), :] = product((slots - 1) * STRETCH, pl.ds(start, LANES))
    for w in range(SENT):
        stretch = sources[w]
        holder = owner[stretch]
        mine = holder == me
        meta[w] = holder

        @pl.when(mine)
        def _(w=w, stretch=stretch, holder=holder):
            def count(k, total):
                return total + jnp.where(owner[k] == holder, 1, 0)

            slot = lax.fori_loop(0, stretch, count, 0)
            first = pl.multiple_of(slot * STRETCH, STRETCH)
            for step in range(parts):
                base = (partner(me, step, size) if parts > 1 else 0) * width
                for start in range(0, width, LANES):
                    columns = pl.ds(pl.multiple_of(base + start, LANES), LANES)
                    sends[step][w, pl.ds(start, LANES), :] = product(first, columns)

        if fill:

            @pl.when(jnp.logical_not(mine))
            def _(w=w):
                for send in sends:
                    send[w] = jnp.zeros(send.shape[1:], send.dtype)


def gate(size, parts, fill, sources, owner, key_proj, value_proj):
    row_count, channels = key_proj.shape
    slots = row_count // STRETCH
    operands = [
        pltpu.with_memory_space_constraint(operand, pltpu.HBM)
        for operand in (sources, owner, key_proj, value_proj)
    ]
    send = jax.ShapeDtypeStruct((SENT, channels // parts, STRETCH), jnp.bfloat16)
    *sends, last, meta = pl.pallas_call(
        functools.partial(gate_kernel, size, parts, fill),
        in_specs=[HBM_SPEC] * 4,
        out_specs=[VMEM_SPEC] * (parts + 1) + [SMEM_SPEC],
        out_shape=[send] * parts
        + [
            jax.ShapeDtypeStruct((channels, STRETCH), jnp.bfloat16),
            jax.ShapeDtypeStruct((SENT + slots * WIN,), jnp.int32),
        ],
        scratch_shapes=[
            pltpu.SMEM(sources.shape, jnp.int32),
            pltpu.SMEM(owner.shape, jnp.int32),
            pltpu.VMEM(key_proj.shape, key_proj.dtype),
            pltpu.VMEM(value_proj.shape, value_proj.dtype),
            pltpu.SemaphoreType.DMA((4,)),
        ],
        compiler_params=params(),
        name="gate",
    )(*operands)
    return sends, last, meta


def merge_kernel(size, meta, *refs):
    parts, out = refs[:-1], refs[-1]
    me = lax.axis_index("seq")
    for w in range(SENT):
        for step in range(size):

            @pl.when(sender(me, step, size) == meta[w])
            def _(w=w, step=step):
                out[w] = parts[step][w]


def merge(size, meta, parts):
    return pl.pallas_call(
        functools.partial(merge_kernel, size),
        in_specs=[SMEM_SPEC] + [VMEM_SPEC] * size,
        out_specs=VMEM_SPEC,
        out_shape=jax.ShapeDtypeStruct(parts[0].shape, parts[0].dtype),
        compiler_params=params(),
        name="merge",
    )(meta, *parts)


def lags_kernel(size, *refs):
    received = refs[:size]
    out, blocks, reverse, sems = refs[size:]
    group_count, part = received[0].shape
    lag_count = size * part
    padded = out.shape[2]
    tile_step = pl.program_id(0)

    @pl.when(tile_step == 0)
    def _():
        me = lax.axis_index("seq")
        copies = [
            pltpu.make_async_copy(
                received[step], blocks.at[sender(me, step, size)], sems.at[step]
            )
            for step in range(size)
        ]
        for copy in copies:
            copy.start()
        for copy in copies:
            copy.wait()
        row = lax.broadcasted_iota(jnp.int32, (LANES, LANES), 0)
        column = lax.broadcasted_iota(jnp.int32, (LANES, LANES), 1)
        flip = jnp.where(row + column == LANES - 1, 1.0, 0.0).astype(jnp.bfloat16)
        for start in range(0, lag_count, LANES):
            piece = blocks[start // part, :, pl.ds(start % part, LANES)]
            reverse[:, pl.ds(lag_count - LANES - start, LANES)] = jnp.dot(
                piece, flip, preferred_element_type=jnp.float32
            )
        reverse[:, pl.ds(lag_count, padded - lag_count)] = jnp.zeros(
            (group_count, padded - lag_count), jnp.float32
        )

    row = lax.broadcasted_iota(jnp.int32, (GROUP_CH, LANES), 0)
    column = lax.broadcasted_iota(jnp.int32, (GROUP_CH, LANES), 1)
    inside = column > row
    tile_rows = pl.ds(pl.multiple_of(tile_step * BLOCKS, BLOCKS), BLOCKS)
    before = [jnp.zeros((GROUP_CH, LANES), jnp.float32)] * BLOCKS
    for start in range(0, padded, LANES):
        tile = reverse[tile_rows, pl.ds(start, LANES)]
        for g in range(BLOCKS):
            spread = jnp.broadcast_to(tile[g : g + 1, :], (GROUP_CH, LANES))
            rolled = pltpu.roll(spread, 1, 1, stride=1, stride_axis=0)
            out[g, :, pl.ds(start, LANES)] = jnp.where(inside, rolled, before[g]).astype(jnp.bfloat16)
            before[g] = rolled


def lags(size, received):
    group_count, part = received[0].shape
    padded = size * part + SPAN
    return pl.pallas_call(
        functools.partial(lags_kernel, size),
        grid=(group_count // BLOCKS,),
        in_specs=[ANY_SPEC] * size,
        out_specs=pl.BlockSpec((BLOCKS, GROUP_CH, padded), lambda i: (i, 0, 0)),
        out_shape=jax.ShapeDtypeStruct((group_count, GROUP_CH, padded), jnp.bfloat16),
        scratch_shapes=[
            pltpu.VMEM((size, group_count, part), jnp.bfloat16),
            pltpu.VMEM((group_count, padded), jnp.float32),
            pltpu.SemaphoreType.DMA((size,)),
        ],
        compiler_params=params(),
        name="lags",
    )(*received)


def spread_rows(tile, spans, base):
    lane = lax.broadcasted_iota(jnp.int16, tile.shape, 1)
    zero = jnp.zeros(tile.shape, tile.dtype)
    for i1 in range(BLOCKS):
        shift = GROUP_CH * i1
        if i1 == 0:
            low, high = zero, tile
        else:
            moved = pltpu.roll(tile, LANES - shift, 1)
            early = lane < LANES - shift
            low, high = jnp.where(early, zero, moved), jnp.where(early, moved, zero)
        rows = pl.ds(shift, GROUP_CH)
        for g in range(BLOCKS):
            part = slice(g * GROUP_CH, (g + 1) * GROUP_CH)
            spans[g, rows, pl.ds(base, LANES)] = low[part]
            spans[g, rows, pl.ds(base + LANES, LANES)] = high[part]


def window(meta, shifted, group, slot, w):
    start = pl.multiple_of(meta[SENT + slot * WIN + w], STRETCH)
    return shifted[group, :, pl.ds(start, SPAN)]


def last_kernel(slots, meta, last, shifted, out, spans):
    for start in range(0, last.shape[0], LANES):
        spread_rows(last[pl.ds(start, LANES), :], spans, 0)
        results = [
            lax.dot_general(
                window(meta, shifted, start // GROUP_CH + g, slots - 1, SENT),
                spans[g],
                NT,
                preferred_element_type=jnp.float32,
            )
            for g in range(BLOCKS)
        ]
        for m, tile in enumerate(block_transpose(results)):
            out[pl.ds(m * GROUP_CH, GROUP_CH), pl.ds(start, LANES)] = tile


def last_term(slots, meta, last, shifted):
    return pl.pallas_call(
        functools.partial(last_kernel, slots),
        in_specs=[SMEM_SPEC, VMEM_SPEC, VMEM_SPEC],
        out_specs=VMEM_SPEC,
        out_shape=jax.ShapeDtypeStruct((STRETCH, last.shape[0]), jnp.float32),
        scratch_shapes=[pltpu.VMEM((BLOCKS, LANES, SPAN), jnp.bfloat16)],
        compiler_params=params(),
        name="last_term",
    )(meta, last, shifted)


def conv_kernel(step, slots, meta_in, pieces, shifted, term, query, *refs):
    others, (out, meta, gates, result, spans, sems) = refs[:-6], refs[-6:]
    width = pieces.shape[1]
    size = out.shape[1] // width
    me = lax.axis_index("seq")
    base = pl.multiple_of((me ^ step) * width if size > 1 else 0, width)
    copies = [
        pltpu.make_async_copy(meta_in, meta, sems.at[0]),
        pltpu.make_async_copy(query.at[:, pl.ds(base, width)], gates, sems.at[1]),
    ]
    for copy in copies:
        copy.start()
    starts = range(0, width, LANES)

    def spread(start):
        for w in range(SENT):
            tile = pieces[w, pl.ds(start, LANES), :]
            if len(others) > 1:
                end = (me == 0) | (me == size - 1)
                tile = jnp.where(end, tile, others[0][w, pl.ds(start, LANES), :])
            spread_rows(tile, spans.at[start // LANES], w * SPAN)

    spread(0)
    for copy in copies:
        copy.wait()
    for start in starts:
        columns = pl.ds(start, LANES)
        results = []
        for g in range(BLOCKS):
            group = base // GROUP_CH + (start // GROUP_CH + g)
            filter_rows = jnp.concatenate(
                [
                    jnp.concatenate([window(meta, shifted, group, slot, w) for w in range(SENT)], axis=1)
                    for slot in range(slots)
                ],
                axis=0,
            )
            results.append(
                lax.dot_general(
                    filter_rows, spans[start // LANES, g], NT, preferred_element_type=jnp.float32
                )
            )
        if start + LANES < width:
            spread(start + LANES)
        for slot in range(slots):
            tiles = [value[slot * GROUP_CH : (slot + 1) * GROUP_CH] for value in results]
            for m, tile in enumerate(block_transpose(tiles)):
                place = pl.ds(slot * STRETCH + m * GROUP_CH, GROUP_CH)
                if slot == slots - 1:
                    tile = tile + term[
                        pl.ds(m * GROUP_CH, GROUP_CH), pl.ds(pl.multiple_of(base + start, LANES), LANES)
                    ]
                result[place, columns] = (gates[place, columns].astype(jnp.float32) * tile).astype(
                    jnp.bfloat16
                )
    store = pltpu.make_async_copy(result, out.at[:, pl.ds(base, width)], sems.at[2])
    store.start()
    store.wait()


def conv(step, meta, pieces, shifted, term, query_proj, before, other=None):
    row_count = query_proj.shape[0]
    slots = row_count // STRETCH
    width = pieces.shape[1]
    operands = [meta, pieces, shifted, term, query_proj]
    in_specs = [ANY_SPEC, VMEM_SPEC, VMEM_SPEC, VMEM_SPEC, HBM_SPEC]
    if other is not None:
        operands.append(other)
        in_specs.append(VMEM_SPEC)
    aliases = {}
    if before is not None:
        aliases = {len(operands): 0}
        operands.append(before)
        in_specs.append(HBM_SPEC)
    return pl.pallas_call(
        functools.partial(conv_kernel, step, slots),
        in_specs=in_specs,
        out_specs=HBM_SPEC,
        out_shape=jax.ShapeDtypeStruct(query_proj.shape, jnp.bfloat16),
        input_output_aliases=aliases,
        scratch_shapes=[
            pltpu.SMEM(meta.shape, jnp.int32),
            pltpu.VMEM((row_count, width), jnp.bfloat16),
            pltpu.VMEM((row_count, width), jnp.bfloat16),
            pltpu.VMEM((width // LANES, BLOCKS, LANES, SENT * SPAN), jnp.bfloat16),
            pltpu.SemaphoreType.DMA((3,)),
        ],
        compiler_params=params(),
        name="conv",
    )(*operands)


def shards(size, key_proj, value_proj, query_proj, filters, sources, owner):
    row_count, channels = key_proj.shape
    slots = row_count // STRETCH
    by_parts = size == 4 and channels % (size * LANES) == 0
    parts = size if by_parts else 1

    def to_partner(value, step):
        return lax.ppermute(value, "seq", [(z, z ^ step if size & (size - 1) == 0 else (z + step) % size) for z in range(size)])

    filter_parts = [filters] + [to_partner(filters, step) for step in range(1, size)]
    sends, last, meta = gate(size, parts, not by_parts, sources, owner, key_proj, value_proj)
    sends, filter_parts = lax.optimization_barrier((sends, filter_parts))
    shifted = lags(size, filter_parts)
    term = last_term(slots, meta, last, shifted)
    if not by_parts:
        pieces = lax.psum(sends[0], "seq")
        return conv(0, meta, pieces, shifted, term, query_proj, None)

    scattered = [sends[0]] + [to_partner(sends[step], step) for step in range(1, size)]
    term, *scattered = lax.optimization_barrier((term, *scattered))
    merged = merge(size, meta, scattered)
    near = lax.ppermute(merged, "seq", [(0, 1), (1, 0), (2, 3), (3, 2)])
    far = lax.ppermute(merged, "seq", [(0, 2), (2, 0), (1, 3), (3, 1)])
    out = conv(0, meta, merged, shifted, term, query_proj, None)
    merged, far, out = lax.optimization_barrier((merged, far, out))
    onward = lax.ppermute(far, "seq", [(2, 3), (1, 0)])
    middle = lax.ppermute(merged, "seq", [(1, 2), (2, 1)])
    out = conv(1, meta, near, shifted, term, query_proj, out)
    out = conv(2, meta, far, shifted, term, query_proj, out)
    return conv(3, meta, onward, shifted, term, query_proj, out, middle)


def solution(mesh):
    return jax.shard_map(
        functools.partial(shards, mesh.shape["seq"]),
        mesh=mesh,
        in_specs=(
            P(("rep", "seq"), "ch"),
            P(("rep", "seq"), "ch"),
            P(("rep", "seq"), "ch"),
            P("ch", "seq"),
            P("rep"),
            P("rep"),
        ),
        out_specs=P(("rep", "seq"), "ch"),
        check_vma=False,
    )
```

```python
import functools

import jax
import jax.numpy as jnp
from jax import lax
from jax.experimental import pallas as pl
from jax.experimental.pallas import tpu as pltpu
from jax.sharding import PartitionSpec as P

GROUP_CH = 16
STRETCH = 128
WIN = 4
SENT = WIN - 1
LANES = 128
BLOCKS = LANES // GROUP_CH
SPAN = 2 * STRETCH
VMEM_LIMIT = 40 * 1024 * 1024

SMEM_SPEC = pl.BlockSpec(memory_space=pltpu.SMEM)
ANY_SPEC = pl.BlockSpec(memory_space=pl.ANY)
HBM_SPEC = pl.BlockSpec(memory_space=pltpu.HBM)
VMEM_SPEC = pl.BlockSpec(memory_space=pltpu.VMEM)
NT = (((1,), (1,)), ((), ()))


def params():
    return pltpu.CompilerParams(vmem_limit_bytes=VMEM_LIMIT)


def partner(me, step, size):
    return me ^ step if size & (size - 1) == 0 else lax.rem(me + step, size)


def sender(me, step, size):
    return me ^ step if size & (size - 1) == 0 else lax.rem(me + size - step, size)


def lane_block(shape):
    return lax.broadcasted_iota(jnp.int32, shape, 1) // GROUP_CH


def block_transpose(tiles):
    block = lane_block(tiles[0].shape)
    tiles = list(tiles)
    for distance in (4, 2, 1):
        low = (block & distance) == 0
        for first in range(BLOCKS):
            if first & distance:
                continue
            a, b = tiles[first], tiles[first + distance]
            shift = GROUP_CH * distance
            tiles[first] = jnp.where(low, a, pltpu.roll(b, shift, 1))
            tiles[first + distance] = jnp.where(low, pltpu.roll(a, LANES - shift, 1), b)
    return tiles


PLACE = SENT
MANY = 2 * SENT
WINDOWS = MANY + 1
SLOTS = 2


def gate_kernel(size, parts, sources_in, owner_in, key_in, value_in, *refs):
    sends, extras = refs[:parts], refs[parts : 2 * parts]
    last, meta, sources, owner, key, value, sems = refs[2 * parts :]
    stretch_count = owner.shape[0]
    slots = key.shape[0] // STRETCH
    channels = key.shape[1]
    width = channels // parts
    me = lax.axis_index("seq")
    copies = [
        pltpu.make_async_copy(sources_in, sources, sems.at[0]),
        pltpu.make_async_copy(owner_in, owner, sems.at[1]),
        pltpu.make_async_copy(key_in, key, sems.at[2]),
        pltpu.make_async_copy(value_in, value, sems.at[3]),
    ]
    for copy in copies:
        copy.start()

    def product(start, columns):
        rows = pl.ds(start, STRETCH)
        rows_k = key[rows, columns].astype(jnp.float32)
        rows_v = value[rows, columns].astype(jnp.float32)
        return (rows_k * rows_v).astype(jnp.bfloat16).T

    for copy in copies[:2]:
        copy.wait()

    def target(k, slot):
        mine = owner[k] == me

        @pl.when(mine)
        def _():
            for w in range(WIN):
                lag_block = jnp.maximum(k - sources[w], -1)
                meta[WINDOWS + slot * WIN + w] = (stretch_count - 1 - lag_block) * STRETCH

        return slot + jnp.where(mine, 1, 0)

    lax.fori_loop(0, stretch_count, target, 0)
    for copy in copies[2:]:
        copy.wait()
    for start in range(0, channels, LANES):
        last[pl.ds(start, LANES), :] = product((slots - 1) * STRETCH, pl.ds(start, LANES))
    holders = [owner[sources[w]] for w in range(SENT)]
    many = 0
    for w, holder in enumerate(holders):
        place = sum([jnp.where(other == holder, 1, 0) for other in holders[:w]], 0)
        meta[w] = holder
        meta[PLACE + w] = place
        many = many + jnp.where(place >= SLOTS, 1, 0)

        @pl.when(holder == me)
        def _(w=w, holder=holder, place=place):
            def count(k, total):
                return total + jnp.where(owner[k] == holder, 1, 0)

            slot = lax.fori_loop(0, sources[w], count, 0)
            first = pl.multiple_of(slot * STRETCH, STRETCH)
            for step in range(parts):
                base = (partner(me, step, size) if parts > 1 else 0) * width

                def fill(target, step=step, base=base):
                    for start in range(0, width, LANES):
                        columns = pl.ds(pl.multiple_of(base + start, LANES), LANES)
                        target[pl.ds(start, LANES), :] = product(first, columns)

                if w < SLOTS:
                    fill(sends[step].at[place])
                else:

                    @pl.when(place < SLOTS)
                    def _(step=step, fill=fill):
                        fill(sends[step].at[jnp.minimum(place, SLOTS - 1)])

                    @pl.when(place >= SLOTS)
                    def _(step=step, fill=fill):
                        fill(extras[step].at[0])

    meta[MANY] = many


def gate(size, parts, sources, owner, key_proj, value_proj):
    row_count, channels = key_proj.shape
    slots = row_count // STRETCH
    operands = [
        pltpu.with_memory_space_constraint(operand, pltpu.HBM)
        for operand in (sources, owner, key_proj, value_proj)
    ]
    send = jax.ShapeDtypeStruct((SLOTS, channels // parts, STRETCH), jnp.bfloat16)
    extra = jax.ShapeDtypeStruct((SENT - SLOTS, channels // parts, STRETCH), jnp.bfloat16)
    *sends, last, meta = pl.pallas_call(
        functools.partial(gate_kernel, size, parts),
        in_specs=[HBM_SPEC] * 4,
        out_specs=[VMEM_SPEC] * (2 * parts + 1) + [SMEM_SPEC],
        out_shape=[send] * parts
        + [extra] * parts
        + [
            jax.ShapeDtypeStruct((channels, STRETCH), jnp.bfloat16),
            jax.ShapeDtypeStruct((WINDOWS + slots * WIN,), jnp.int32),
        ],
        scratch_shapes=[
            pltpu.SMEM(sources.shape, jnp.int32),
            pltpu.SMEM(owner.shape, jnp.int32),
            pltpu.VMEM(key_proj.shape, key_proj.dtype),
            pltpu.VMEM(value_proj.shape, value_proj.dtype),
            pltpu.SemaphoreType.DMA((4,)),
        ],
        compiler_params=params(),
        name="gate",
    )(*operands)
    return sends[:parts], sends[parts:], last, meta


def merge_kernel(size, meta, *refs):
    parts, extras, out = refs[:size], refs[size:-1], refs[-1]
    me = lax.axis_index("seq")
    for w in range(SENT):
        place = meta[PLACE + w]
        for step in range(size):
            here = sender(me, step, size) == meta[w]

            @pl.when(here & (place < SLOTS))
            def _(w=w, step=step, place=place):
                out[w] = parts[step][jnp.minimum(place, SLOTS - 1)]

            if extras and w >= SLOTS:

                @pl.when(here & (place >= SLOTS))
                def _(w=w, step=step):
                    out[w] = extras[step][0]


def merge(size, meta, parts, extras=()):
    return pl.pallas_call(
        functools.partial(merge_kernel, size),
        in_specs=[SMEM_SPEC] + [VMEM_SPEC] * (size + len(extras)),
        out_specs=VMEM_SPEC,
        out_shape=jax.ShapeDtypeStruct((SENT,) + parts[0].shape[1:], parts[0].dtype),
        compiler_params=params(),
        name="merge",
    )(meta, *parts, *extras)


def lags_kernel(size, *refs):
    received = refs[:size]
    out, blocks, reverse, sems = refs[size:]
    group_count, part = received[0].shape
    lag_count = size * part
    padded = out.shape[2]
    tile_step = pl.program_id(0)

    @pl.when(tile_step == 0)
    def _():
        me = lax.axis_index("seq")
        copies = [
            pltpu.make_async_copy(
                received[step], blocks.at[sender(me, step, size)], sems.at[step]
            )
            for step in range(size)
        ]
        for copy in copies:
            copy.start()
        for copy in copies:
            copy.wait()
        row = lax.broadcasted_iota(jnp.int32, (LANES, LANES), 0)
        column = lax.broadcasted_iota(jnp.int32, (LANES, LANES), 1)
        flip = jnp.where(row + column == LANES - 1, 1.0, 0.0).astype(jnp.bfloat16)
        for start in range(0, lag_count, LANES):
            piece = blocks[start // part, :, pl.ds(start % part, LANES)]
            reverse[:, pl.ds(lag_count - LANES - start, LANES)] = jnp.dot(
                piece, flip, preferred_element_type=jnp.float32
            )
        reverse[:, pl.ds(lag_count, padded - lag_count)] = jnp.zeros(
            (group_count, padded - lag_count), jnp.float32
        )

    row = lax.broadcasted_iota(jnp.int32, (GROUP_CH, LANES), 0)
    column = lax.broadcasted_iota(jnp.int32, (GROUP_CH, LANES), 1)
    inside = column > row
    tile_rows = pl.ds(pl.multiple_of(tile_step * BLOCKS, BLOCKS), BLOCKS)
    before = [jnp.zeros((GROUP_CH, LANES), jnp.float32)] * BLOCKS
    for start in range(0, padded, LANES):
        tile = reverse[tile_rows, pl.ds(start, LANES)]
        for g in range(BLOCKS):
            spread = jnp.broadcast_to(tile[g : g + 1, :], (GROUP_CH, LANES))
            rolled = pltpu.roll(spread, 1, 1, stride=1, stride_axis=0)
            out[g, :, pl.ds(start, LANES)] = jnp.where(inside, rolled, before[g]).astype(jnp.bfloat16)
            before[g] = rolled


def lags(size, received):
    group_count, part = received[0].shape
    padded = size * part + SPAN
    return pl.pallas_call(
        functools.partial(lags_kernel, size),
        grid=(group_count // BLOCKS,),
        in_specs=[ANY_SPEC] * size,
        out_specs=pl.BlockSpec((BLOCKS, GROUP_CH, padded), lambda i: (i, 0, 0)),
        out_shape=jax.ShapeDtypeStruct((group_count, GROUP_CH, padded), jnp.bfloat16),
        scratch_shapes=[
            pltpu.VMEM((size, group_count, part), jnp.bfloat16),
            pltpu.VMEM((group_count, padded), jnp.float32),
            pltpu.SemaphoreType.DMA((size,)),
        ],
        compiler_params=params(),
        name="lags",
    )(*received)


def spread_rows(tile, spans, base):
    lane = lax.broadcasted_iota(jnp.int16, tile.shape, 1)
    zero = jnp.zeros(tile.shape, tile.dtype)
    for i1 in range(BLOCKS):
        shift = GROUP_CH * i1
        if i1 == 0:
            low, high = zero, tile
        else:
            moved = pltpu.roll(tile, LANES - shift, 1)
            early = lane < LANES - shift
            low, high = jnp.where(early, zero, moved), jnp.where(early, moved, zero)
        rows = pl.ds(shift, GROUP_CH)
        for g in range(BLOCKS):
            part = slice(g * GROUP_CH, (g + 1) * GROUP_CH)
            spans[g, rows, pl.ds(base, LANES)] = low[part]
            spans[g, rows, pl.ds(base + LANES, LANES)] = high[part]


def window(meta, shifted, group, slot, w):
    start = pl.multiple_of(meta[WINDOWS + slot * WIN + w], STRETCH)
    return shifted[group, :, pl.ds(start, SPAN)]


def last_kernel(slots, meta, last, shifted, out, spans):
    for start in range(0, last.shape[0], LANES):
        spread_rows(last[pl.ds(start, LANES), :], spans, 0)
        results = [
            lax.dot_general(
                window(meta, shifted, start // GROUP_CH + g, slots - 1, SENT),
                spans[g],
                NT,
                preferred_element_type=jnp.float32,
            )
            for g in range(BLOCKS)
        ]
        for m, tile in enumerate(block_transpose(results)):
            out[pl.ds(m * GROUP_CH, GROUP_CH), pl.ds(start, LANES)] = tile


def last_term(slots, meta, last, shifted):
    return pl.pallas_call(
        functools.partial(last_kernel, slots),
        in_specs=[SMEM_SPEC, VMEM_SPEC, VMEM_SPEC],
        out_specs=VMEM_SPEC,
        out_shape=jax.ShapeDtypeStruct((STRETCH, last.shape[0]), jnp.float32),
        scratch_shapes=[pltpu.VMEM((BLOCKS, LANES, SPAN), jnp.bfloat16)],
        compiler_params=params(),
        name="last_term",
    )(meta, last, shifted)


def conv_kernel(step, slots, meta_in, pieces, shifted, term, query, *refs):
    others, (out, meta, gates, result, spans, sems) = refs[:-6], refs[-6:]
    width = pieces.shape[1]
    size = out.shape[1] // width
    me = lax.axis_index("seq")
    base = pl.multiple_of((me ^ step) * width if size > 1 else 0, width)
    copies = [
        pltpu.make_async_copy(meta_in, meta, sems.at[0]),
        pltpu.make_async_copy(query.at[:, pl.ds(base, width)], gates, sems.at[1]),
    ]
    for copy in copies:
        copy.start()
    starts = range(0, width, LANES)

    def spread(start):
        for w in range(SENT):
            tile = pieces[w, pl.ds(start, LANES), :]
            if len(others) > 1:
                end = (me == 0) | (me == size - 1)
                tile = jnp.where(end, tile, others[0][w, pl.ds(start, LANES), :])
            spread_rows(tile, spans.at[start // LANES], w * SPAN)

    spread(0)
    for copy in copies:
        copy.wait()
    for start in starts:
        columns = pl.ds(start, LANES)
        results = []
        for g in range(BLOCKS):
            group = base // GROUP_CH + (start // GROUP_CH + g)
            filter_rows = jnp.concatenate(
                [
                    jnp.concatenate([window(meta, shifted, group, slot, w) for w in range(SENT)], axis=1)
                    for slot in range(slots)
                ],
                axis=0,
            )
            results.append(
                lax.dot_general(
                    filter_rows, spans[start // LANES, g], NT, preferred_element_type=jnp.float32
                )
            )
        if start + LANES < width:
            spread(start + LANES)
        for slot in range(slots):
            tiles = [value[slot * GROUP_CH : (slot + 1) * GROUP_CH] for value in results]
            for m, tile in enumerate(block_transpose(tiles)):
                place = pl.ds(slot * STRETCH + m * GROUP_CH, GROUP_CH)
                if slot == slots - 1:
                    tile = tile + term[
                        pl.ds(m * GROUP_CH, GROUP_CH), pl.ds(pl.multiple_of(base + start, LANES), LANES)
                    ]
                result[place, columns] = (gates[place, columns].astype(jnp.float32) * tile).astype(
                    jnp.bfloat16
                )
    store = pltpu.make_async_copy(result, out.at[:, pl.ds(base, width)], sems.at[2])
    store.start()
    store.wait()


def conv(step, meta, pieces, shifted, term, query_proj, before, other=None):
    row_count = query_proj.shape[0]
    slots = row_count // STRETCH
    width = pieces.shape[1]
    operands = [meta, pieces, shifted, term, query_proj]
    in_specs = [ANY_SPEC, VMEM_SPEC, VMEM_SPEC, VMEM_SPEC, HBM_SPEC]
    if other is not None:
        operands.append(other)
        in_specs.append(VMEM_SPEC)
    aliases = {}
    if before is not None:
        aliases = {len(operands): 0}
        operands.append(before)
        in_specs.append(HBM_SPEC)
    return pl.pallas_call(
        functools.partial(conv_kernel, step, slots),
        in_specs=in_specs,
        out_specs=HBM_SPEC,
        out_shape=jax.ShapeDtypeStruct(query_proj.shape, jnp.bfloat16),
        input_output_aliases=aliases,
        scratch_shapes=[
            pltpu.SMEM(meta.shape, jnp.int32),
            pltpu.VMEM((row_count, width), jnp.bfloat16),
            pltpu.VMEM((row_count, width), jnp.bfloat16),
            pltpu.VMEM((width // LANES, BLOCKS, LANES, SENT * SPAN), jnp.bfloat16),
            pltpu.SemaphoreType.DMA((3,)),
        ],
        compiler_params=params(),
        name="conv",
    )(*operands)


def shards(size, key_proj, value_proj, query_proj, filters, sources, owner):
    row_count, channels = key_proj.shape
    slots = row_count // STRETCH
    by_parts = size == 4 and channels % (size * LANES) == 0
    parts = size if by_parts else 1

    def to_partner(value, step):
        return lax.ppermute(value, "seq", [(z, z ^ step if size & (size - 1) == 0 else (z + step) % size) for z in range(size)])

    filter_parts = [filters] + [to_partner(filters, step) for step in range(1, size)]
    sends, extras, last, meta = gate(size, parts, sources, owner, key_proj, value_proj)
    sends, filter_parts = lax.optimization_barrier((sends, filter_parts))
    shifted = lags(size, filter_parts)
    term = last_term(slots, meta, last, shifted)
    if not by_parts:
        me = lax.axis_index("seq")
        held = jnp.concatenate([sends[0], extras[0]])
        places = meta[PLACE:MANY]
        mine = (meta[:SENT] == me)[:, None, None]
        pieces = lax.psum(jnp.where(mine, held[places], jnp.zeros_like(held)), "seq")
        return conv(0, meta, pieces, shifted, term, query_proj, None)

    scattered = [sends[0]] + [to_partner(sends[step], step) for step in range(1, size)]
    term, *scattered = lax.optimization_barrier((term, *scattered))

    def merge_more(meta, scattered, extras):
        more = [extras[0]] + [to_partner(extras[step], step) for step in range(1, size)]
        return merge(size, meta, scattered, more)

    def merge_plain(meta, scattered, extras):
        return merge(size, meta, scattered)

    merged = lax.cond(meta[MANY] > 0, merge_more, merge_plain, meta, scattered, extras)
    far = lax.ppermute(merged, "seq", [(0, 2), (2, 0), (1, 3), (3, 1)])
    near = lax.ppermute(merged, "seq", [(0, 1), (1, 0), (2, 3), (3, 2)])
    out = conv(0, meta, merged, shifted, term, query_proj, None)
    out = conv(1, meta, near, shifted, term, query_proj, out)
    merged, far, out = lax.optimization_barrier((merged, far, out))
    onward = lax.ppermute(far, "seq", [(2, 3), (1, 0)])
    middle = lax.ppermute(merged, "seq", [(1, 2), (2, 1)])
    out = conv(2, meta, far, shifted, term, query_proj, out)
    return conv(3, meta, onward, shifted, term, query_proj, out, middle)


def solution(mesh):
    return jax.shard_map(
        functools.partial(shards, mesh.shape["seq"]),
        mesh=mesh,
        in_specs=(
            P(("rep", "seq"), "ch"),
            P(("rep", "seq"), "ch"),
            P(("rep", "seq"), "ch"),
            P("ch", "seq"),
            P("rep"),
            P("rep"),
        ),
        out_specs=P(("rep", "seq"), "ch"),
        check_vma=False,
    )
```

```python
import functools

import jax
import jax.numpy as jnp
from jax import lax
from jax.experimental import pallas as pl
from jax.experimental.pallas import tpu as pltpu
from jax.sharding import PartitionSpec as P

GROUP_CH = 16
STRETCH = 128
WIN = 4
SENT = WIN - 1
LANES = 128
BLOCKS = LANES // GROUP_CH
SPAN = 2 * STRETCH
VMEM_LIMIT = 16 * 1024 * 1024

SMEM_SPEC = pl.BlockSpec(memory_space=pltpu.SMEM)
ANY_SPEC = pl.BlockSpec(memory_space=pl.ANY)
HBM_SPEC = pl.BlockSpec(memory_space=pltpu.HBM)
VMEM_SPEC = pl.BlockSpec(memory_space=pltpu.VMEM)
NT = (((1,), (1,)), ((), ()))


def params():
    return pltpu.CompilerParams(vmem_limit_bytes=VMEM_LIMIT)


def partner(me, step, size):
    return me ^ step if size & (size - 1) == 0 else lax.rem(me + step, size)


def sender(me, step, size):
    return me ^ step if size & (size - 1) == 0 else lax.rem(me + size - step, size)


def lane_block(shape):
    return lax.broadcasted_iota(jnp.int32, shape, 1) // GROUP_CH


def block_transpose(tiles):
    block = lane_block(tiles[0].shape)
    tiles = list(tiles)
    for distance in (4, 2, 1):
        low = (block & distance) == 0
        for first in range(BLOCKS):
            if first & distance:
                continue
            a, b = tiles[first], tiles[first + distance]
            shift = GROUP_CH * distance
            tiles[first] = jnp.where(low, a, pltpu.roll(b, shift, 1))
            tiles[first + distance] = jnp.where(low, pltpu.roll(a, LANES - shift, 1), b)
    return tiles


PLACE = SENT
MANY = 2 * SENT
WINDOWS = MANY + 1
SLOTS = 2


def gate_kernel(size, parts, sources_in, owner_in, key_in, value_in, filters_in, *refs):
    send, extra, last, meta, sources, owner, key, value, filters, sems = refs
    stretch_count = owner.shape[0]
    slots = key.shape[0] // STRETCH
    channels = key.shape[1]
    width = channels // parts
    me = lax.axis_index("seq")
    copies = [
        pltpu.make_async_copy(sources_in, sources, sems.at[0]),
        pltpu.make_async_copy(owner_in, owner, sems.at[1]),
        pltpu.make_async_copy(key_in, key, sems.at[2]),
        pltpu.make_async_copy(value_in, value, sems.at[3]),
        pltpu.make_async_copy(filters_in, filters, sems.at[4]),
    ]
    for copy in copies:
        copy.start()

    def product(start, columns):
        rows = pl.ds(start, STRETCH)
        rows_k = key[rows, columns].astype(jnp.float32)
        rows_v = value[rows, columns].astype(jnp.float32)
        return (rows_k * rows_v).astype(jnp.bfloat16).T

    for copy in copies[:2]:
        copy.wait()

    def target(k, slot):
        mine = owner[k] == me

        @pl.when(mine)
        def _():
            for w in range(WIN):
                lag_block = jnp.maximum(k - sources[w], -1)
                meta[WINDOWS + slot * WIN + w] = (stretch_count - 1 - lag_block) * STRETCH

        return slot + jnp.where(mine, 1, 0)

    lax.fori_loop(0, stretch_count, target, 0)
    for copy in copies[2:]:
        copy.wait()
    for start in range(0, channels, LANES):
        last[pl.ds(start, LANES), :] = product((slots - 1) * STRETCH, pl.ds(start, LANES))
    holders = [owner[sources[w]] for w in range(SENT)]
    many = 0
    for w, holder in enumerate(holders):
        place = sum([jnp.where(other == holder, 1, 0) for other in holders[:w]], 0)
        meta[w] = holder
        meta[PLACE + w] = place
        many = many + jnp.where(place >= SLOTS, 1, 0)

        @pl.when(holder == me)
        def _(w=w, holder=holder, place=place):
            def count(k, total):
                return total + jnp.where(owner[k] == holder, 1, 0)

            slot = lax.fori_loop(0, sources[w], count, 0)
            first = pl.multiple_of(slot * STRETCH, STRETCH)
            for step in range(parts):
                part = partner(me, step, size) if parts > 1 else 0
                base = part * width

                def fill(target, offset, base=base):
                    for start in range(0, width, LANES):
                        columns = pl.ds(pl.multiple_of(base + start, LANES), LANES)
                        target[pl.ds(offset + start, LANES), :] = product(first, columns)

                if w < SLOTS:
                    fill(send.at[part], pl.multiple_of(place * width, LANES))
                else:

                    @pl.when(place < SLOTS)
                    def _(part=part, fill=fill):
                        fill(send.at[part], pl.multiple_of(place * width, LANES))

                    @pl.when(place >= SLOTS)
                    def _(step=step, fill=fill):
                        fill(extra.at[step], 0)

    meta[MANY] = many
    group_count = filters.shape[0]
    for tile in range(filters.shape[1] // LANES):
        rows = pl.ds(SLOTS * width + tile * group_count, group_count)
        for part in range(parts):
            send[part, rows, :] = filters[:, pl.ds(tile * LANES, LANES)]


def gate(size, parts, sources, owner, key_proj, value_proj, filters):
    row_count, channels = key_proj.shape
    slots = row_count // STRETCH
    width = channels // parts
    operands = [
        pltpu.with_memory_space_constraint(operand, pltpu.HBM)
        for operand in (sources, owner, key_proj, value_proj, filters)
    ]
    rows = SLOTS * width + filters.size // LANES
    return pl.pallas_call(
        functools.partial(gate_kernel, size, parts),
        in_specs=[HBM_SPEC] * 5,
        out_specs=[VMEM_SPEC] * 3 + [SMEM_SPEC],
        out_shape=[
            jax.ShapeDtypeStruct((parts, rows, LANES), jnp.bfloat16),
            jax.ShapeDtypeStruct((parts, width, LANES), jnp.bfloat16),
            jax.ShapeDtypeStruct((channels, STRETCH), jnp.bfloat16),
            jax.ShapeDtypeStruct((WINDOWS + slots * WIN,), jnp.int32),
        ],
        scratch_shapes=[
            pltpu.SMEM(sources.shape, jnp.int32),
            pltpu.SMEM(owner.shape, jnp.int32),
            pltpu.VMEM(key_proj.shape, key_proj.dtype),
            pltpu.VMEM(value_proj.shape, value_proj.dtype),
            pltpu.VMEM(filters.shape, filters.dtype),
            pltpu.SemaphoreType.DMA((5,)),
        ],
        compiler_params=params(),
        name="gate",
    )(*operands)


def merge_kernel(size, width, meta, received, *refs):
    extras, out = refs[:-1], refs[-1]
    me = lax.axis_index("seq")
    for w in range(SENT):
        place = meta[PLACE + w]
        rows = pl.ds(pl.multiple_of(jnp.minimum(place, SLOTS - 1) * width, LANES), width)
        out[w] = received[meta[w], rows, :]
    for w in range(SLOTS, SENT):
        for step, extra in enumerate(extras):

            @pl.when((sender(me, step, size) == meta[w]) & (meta[PLACE + w] >= SLOTS))
            def _(w=w, extra=extra):
                out[w] = extra[...]


def merge(size, width, meta, received, extras=()):
    return pl.pallas_call(
        functools.partial(merge_kernel, size, width),
        in_specs=[SMEM_SPEC] + [VMEM_SPEC] * (1 + len(extras)),
        out_specs=VMEM_SPEC,
        out_shape=jax.ShapeDtypeStruct((SENT, width, LANES), received.dtype),
        compiler_params=params(),
        name="merge",
    )(meta, received, *extras)


def lags_kernel(first, blocks, out, reverse):
    group_count, padded = reverse.shape
    tiles = (blocks.shape[1] - first) // group_count
    lag_count = blocks.shape[0] * tiles * LANES
    tile_step = pl.program_id(0)

    @pl.when(tile_step == 0)
    def _():
        row = lax.broadcasted_iota(jnp.int32, (LANES, LANES), 0)
        column = lax.broadcasted_iota(jnp.int32, (LANES, LANES), 1)
        flip = jnp.where(row + column == LANES - 1, 1.0, 0.0).astype(jnp.bfloat16)
        for tile in range(lag_count // LANES):
            piece = blocks[tile // tiles, pl.ds(first + tile % tiles * group_count, group_count), :]
            reverse[:, pl.ds(lag_count - LANES * (tile + 1), LANES)] = jnp.dot(
                piece, flip, preferred_element_type=jnp.float32
            )
        reverse[:, pl.ds(lag_count, padded - lag_count)] = jnp.zeros(
            (group_count, padded - lag_count), jnp.float32
        )

    row = lax.broadcasted_iota(jnp.int32, (GROUP_CH, LANES), 0)
    column = lax.broadcasted_iota(jnp.int32, (GROUP_CH, LANES), 1)
    inside = column > row
    tile_rows = pl.ds(pl.multiple_of(tile_step * BLOCKS, BLOCKS), BLOCKS)
    before = [jnp.zeros((GROUP_CH, LANES), jnp.float32)] * BLOCKS
    for start in range(0, padded, LANES):
        tile = reverse[tile_rows, pl.ds(start, LANES)]
        for g in range(BLOCKS):
            spread = jnp.broadcast_to(tile[g : g + 1, :], (GROUP_CH, LANES))
            rolled = pltpu.roll(spread, 1, 1, stride=1, stride_axis=0)
            out[g, :, pl.ds(start, LANES)] = jnp.where(inside, rolled, before[g]).astype(jnp.bfloat16)
            before[g] = rolled


def lags(blocks, first, group_count):
    size, rows, _ = blocks.shape
    padded = size * (rows - first) // group_count * LANES + SPAN
    return pl.pallas_call(
        functools.partial(lags_kernel, first),
        grid=(group_count // BLOCKS,),
        in_specs=[VMEM_SPEC],
        out_specs=pl.BlockSpec((BLOCKS, GROUP_CH, padded), lambda i: (i, 0, 0)),
        out_shape=jax.ShapeDtypeStruct((group_count, GROUP_CH, padded), jnp.bfloat16),
        scratch_shapes=[pltpu.VMEM((group_count, padded), jnp.float32)],
        compiler_params=params(),
        name="lags",
    )(blocks)


def spread_rows(tile, spans, base):
    lane = lax.broadcasted_iota(jnp.int16, tile.shape, 1)
    zero = jnp.zeros(tile.shape, tile.dtype)
    for i1 in range(BLOCKS):
        shift = GROUP_CH * i1
        if i1 == 0:
            low, high = zero, tile
        else:
            moved = pltpu.roll(tile, LANES - shift, 1)
            early = lane < LANES - shift
            low, high = jnp.where(early, zero, moved), jnp.where(early, moved, zero)
        rows = pl.ds(shift, GROUP_CH)
        for g in range(BLOCKS):
            part = slice(g * GROUP_CH, (g + 1) * GROUP_CH)
            spans[g, rows, pl.ds(base, LANES)] = low[part]
            spans[g, rows, pl.ds(base + LANES, LANES)] = high[part]


def window(meta, shifted, group, slot, w):
    start = pl.multiple_of(meta[WINDOWS + slot * WIN + w], STRETCH)
    return shifted[group, :, pl.ds(start, SPAN)]


def last_kernel(slots, meta, last, shifted, out, spans):
    for start in range(0, last.shape[0], LANES):
        spread_rows(last[pl.ds(start, LANES), :], spans, 0)
        results = [
            lax.dot_general(
                window(meta, shifted, start // GROUP_CH + g, slots - 1, SENT),
                spans[g],
                NT,
                preferred_element_type=jnp.float32,
            )
            for g in range(BLOCKS)
        ]
        for m, tile in enumerate(block_transpose(results)):
            out[pl.ds(m * GROUP_CH, GROUP_CH), pl.ds(start, LANES)] = tile


def last_term(slots, meta, last, shifted):
    return pl.pallas_call(
        functools.partial(last_kernel, slots),
        in_specs=[SMEM_SPEC, VMEM_SPEC, VMEM_SPEC],
        out_specs=VMEM_SPEC,
        out_shape=jax.ShapeDtypeStruct((STRETCH, last.shape[0]), jnp.float32),
        scratch_shapes=[pltpu.VMEM((BLOCKS, LANES, SPAN), jnp.bfloat16)],
        compiler_params=params(),
        name="last_term",
    )(meta, last, shifted)


def conv_kernel(step, slots, meta_in, pieces, shifted, term, query, *refs):
    out, meta, gates, result, spans, sems = refs[-6:]
    width = pieces.shape[1]
    size = out.shape[1] // width
    me = lax.axis_index("seq")
    base = pl.multiple_of(lax.rem(me + size - step, size) * width, width)
    copies = [
        pltpu.make_async_copy(meta_in, meta, sems.at[0]),
        pltpu.make_async_copy(query.at[:, pl.ds(base, width)], gates, sems.at[1]),
    ]
    for copy in copies:
        copy.start()
    starts = range(0, width, LANES)

    def spread(start):
        for w in range(SENT):
            tile = pieces[w, pl.ds(start, LANES), :]
            spread_rows(tile, spans.at[start // LANES], w * SPAN)

    spread(0)
    for copy in copies:
        copy.wait()
    for start in starts:
        columns = pl.ds(start, LANES)
        results = []
        for g in range(BLOCKS):
            group = base // GROUP_CH + (start // GROUP_CH + g)
            filter_rows = jnp.concatenate(
                [
                    jnp.concatenate([window(meta, shifted, group, slot, w) for w in range(SENT)], axis=1)
                    for slot in range(slots)
                ],
                axis=0,
            )
            results.append(
                lax.dot_general(
                    filter_rows, spans[start // LANES, g], NT, preferred_element_type=jnp.float32
                )
            )
        if start + LANES < width:
            spread(start + LANES)
        for slot in range(slots):
            tiles = [value[slot * GROUP_CH : (slot + 1) * GROUP_CH] for value in results]
            for m, tile in enumerate(block_transpose(tiles)):
                place = pl.ds(slot * STRETCH + m * GROUP_CH, GROUP_CH)
                if slot == slots - 1:
                    tile = tile + term[
                        pl.ds(m * GROUP_CH, GROUP_CH), pl.ds(pl.multiple_of(base + start, LANES), LANES)
                    ]
                result[place, columns] = (gates[place, columns].astype(jnp.float32) * tile).astype(
                    jnp.bfloat16
                )
    store = pltpu.make_async_copy(result, out.at[:, pl.ds(base, width)], sems.at[2])
    store.start()
    store.wait()


def conv(step, meta, pieces, shifted, term, query_proj, before):
    row_count = query_proj.shape[0]
    slots = row_count // STRETCH
    width = pieces.shape[1]
    operands = [meta, pieces, shifted, term, query_proj]
    in_specs = [ANY_SPEC, VMEM_SPEC, VMEM_SPEC, VMEM_SPEC, HBM_SPEC]
    aliases = {}
    if before is not None:
        aliases = {len(operands): 0}
        operands.append(before)
        in_specs.append(HBM_SPEC)
    return pl.pallas_call(
        functools.partial(conv_kernel, step, slots),
        in_specs=in_specs,
        out_specs=HBM_SPEC,
        out_shape=jax.ShapeDtypeStruct(query_proj.shape, jnp.bfloat16),
        input_output_aliases=aliases,
        scratch_shapes=[
            pltpu.SMEM(meta.shape, jnp.int32),
            pltpu.VMEM((row_count, width), jnp.bfloat16),
            pltpu.VMEM((row_count, width), jnp.bfloat16),
            pltpu.VMEM((width // LANES, BLOCKS, LANES, SENT * SPAN), jnp.bfloat16),
            pltpu.SemaphoreType.DMA((3,)),
        ],
        compiler_params=params(),
        name="conv",
    )(*operands)


def shards(size, key_proj, value_proj, query_proj, filters, sources, owner):
    row_count, channels = key_proj.shape
    slots = row_count // STRETCH
    by_parts = size == 4 and channels % (size * LANES) == 0
    parts = size if by_parts else 1

    width = channels // parts
    send, extra, last, meta = gate(size, parts, sources, owner, key_proj, value_proj, filters)
    first = SLOTS * width
    group_count = filters.shape[0]
    if not by_parts:
        shifted = lags(lax.all_gather(send[0, first:], "seq"), 0, group_count)
        term = last_term(slots, meta, last, shifted)
        held = jnp.concatenate([send[0, :first].reshape(SLOTS, width, LANES), extra])
        mine = (meta[:SENT] == lax.axis_index("seq"))[:, None, None]
        pieces = lax.psum(jnp.where(mine, held[meta[PLACE:MANY]], jnp.zeros_like(held)), "seq")
        return conv(0, meta, pieces, shifted, term, query_proj, None)

    received = lax.all_to_all(send, "seq", 0, 0, tiled=True)

    def merge_more(meta, received, extra):
        more = [extra[0]] + [
            lax.ppermute(extra[step], "seq", [(z, z ^ step) for z in range(size)])
            for step in range(1, size)
        ]
        return merge(size, width, meta, received, more)

    def merge_plain(meta, received, extra):
        return merge(size, width, meta, received)

    merged = lax.cond(meta[MANY] > 0, merge_more, merge_plain, meta, received, extra)
    gathered = [(0, merged)]
    for step in (1, 3, 2):
        moved = lax.ppermute(merged, "seq", [(z, (z + step) % size) for z in range(size)])
        gathered.append((step, moved))
    shifted = lags(received, first, group_count)
    term = last_term(slots, meta, last, shifted)
    out = None
    for step, pieces in gathered:
        out = conv(step, meta, pieces, shifted, term, query_proj, out)
    return out


def solution(mesh):
    return jax.shard_map(
        functools.partial(shards, mesh.shape["seq"]),
        mesh=mesh,
        in_specs=(
            P(("rep", "seq"), "ch"),
            P(("rep", "seq"), "ch"),
            P(("rep", "seq"), "ch"),
            P("ch", "seq"),
            P("rep"),
            P("rep"),
        ),
        out_specs=P(("rep", "seq"), "ch"),
        check_vma=False,
    )
```

```python
import functools

import jax
import jax.numpy as jnp
from jax import lax
from jax.experimental import pallas as pl
from jax.experimental.pallas import tpu as pltpu
from jax.sharding import PartitionSpec as P

GROUP_CH = 16
STRETCH = 128
WIN = 4
SENT = WIN - 1
LANES = 128
BLOCKS = LANES // GROUP_CH
SPAN = 2 * STRETCH
VMEM_LIMIT = 16 * 1024 * 1024

SMEM_SPEC = pl.BlockSpec(memory_space=pltpu.SMEM)
ANY_SPEC = pl.BlockSpec(memory_space=pl.ANY)
HBM_SPEC = pl.BlockSpec(memory_space=pltpu.HBM)
VMEM_SPEC = pl.BlockSpec(memory_space=pltpu.VMEM)
NT = (((1,), (1,)), ((), ()))


def params():
    return pltpu.CompilerParams(vmem_limit_bytes=VMEM_LIMIT)


def partner(me, step, size):
    return me ^ step if size & (size - 1) == 0 else lax.rem(me + step, size)


def sender(me, step, size):
    return me ^ step if size & (size - 1) == 0 else lax.rem(me + size - step, size)


PLACE = SENT
MANY = 2 * SENT
WINDOWS = MANY + 1
SLOTS = 2


def gate_kernel(size, parts, sources_in, owner_in, key_in, value_in, filters_in, *refs):
    sends = refs[:parts]
    extra, last, meta, sources, owner, key, value, filters, sems = refs[parts:]
    stretch_count = owner.shape[0]
    slots = key.shape[0] // STRETCH
    channels = key.shape[1]
    width = channels // parts
    me = lax.axis_index("seq")
    copies = [
        pltpu.make_async_copy(sources_in, sources, sems.at[0]),
        pltpu.make_async_copy(owner_in, owner, sems.at[1]),
        pltpu.make_async_copy(key_in, key, sems.at[2]),
        pltpu.make_async_copy(value_in, value, sems.at[3]),
        pltpu.make_async_copy(filters_in, filters, sems.at[4]),
    ]
    for copy in copies:
        copy.start()

    def product(start, columns):
        rows = pl.ds(start, STRETCH)
        rows_k = key[rows, columns].astype(jnp.float32)
        rows_v = value[rows, columns].astype(jnp.float32)
        return (rows_k * rows_v).astype(jnp.bfloat16).T

    for copy in copies[:2]:
        copy.wait()

    def target(k, slot):
        mine = owner[k] == me

        @pl.when(mine)
        def _():
            for w in range(WIN):
                lag_block = jnp.maximum(k - sources[w], -1)
                meta[WINDOWS + slot * WIN + w] = (stretch_count - 1 - lag_block) * STRETCH

        return slot + jnp.where(mine, 1, 0)

    lax.fori_loop(0, stretch_count, target, 0)
    for copy in copies[2:]:
        copy.wait()
    for start in range(0, channels, LANES):
        last[pl.ds(start, LANES), :] = product((slots - 1) * STRETCH, pl.ds(start, LANES))
    holders = [owner[sources[w]] for w in range(SENT)]
    many = 0
    for w, holder in enumerate(holders):
        place = sum([jnp.where(other == holder, 1, 0) for other in holders[:w]], 0)
        meta[w] = holder
        meta[PLACE + w] = place
        many = many + jnp.where(place >= SLOTS, 1, 0)

        @pl.when(holder == me)
        def _(w=w, holder=holder, place=place):
            def count(k, total):
                return total + jnp.where(owner[k] == holder, 1, 0)

            slot = lax.fori_loop(0, sources[w], count, 0)
            first = pl.multiple_of(slot * STRETCH, STRETCH)
            for step in range(parts):
                part = partner(me, step, size) if parts > 1 else 0
                base = part * width

                def fill(target, offset, base=base):
                    for start in range(0, width, LANES):
                        columns = pl.ds(pl.multiple_of(base + start, LANES), LANES)
                        target[pl.ds(offset + start, LANES), :] = product(first, columns)

                if w < SLOTS:
                    fill(sends[step], pl.multiple_of(place * width, LANES))
                else:

                    @pl.when(place < SLOTS)
                    def _(step=step, fill=fill):
                        fill(sends[step], pl.multiple_of(place * width, LANES))

                    @pl.when(place >= SLOTS)
                    def _(step=step, fill=fill):
                        fill(extra.at[step], 0)

    meta[MANY] = many
    group_count = filters.shape[0]
    for tile in range(filters.shape[1] // LANES):
        rows = pl.ds(SLOTS * width + tile * group_count, group_count)
        for send in sends:
            send[rows, :] = filters[:, pl.ds(tile * LANES, LANES)]


def gate(size, parts, sources, owner, key_proj, value_proj, filters):
    row_count, channels = key_proj.shape
    slots = row_count // STRETCH
    width = channels // parts
    operands = [
        pltpu.with_memory_space_constraint(operand, pltpu.HBM)
        for operand in (sources, owner, key_proj, value_proj, filters)
    ]
    rows = SLOTS * width + filters.size // LANES
    *sends, extra, last, meta = pl.pallas_call(
        functools.partial(gate_kernel, size, parts),
        in_specs=[HBM_SPEC] * 5,
        out_specs=[VMEM_SPEC] * (parts + 2) + [SMEM_SPEC],
        out_shape=[jax.ShapeDtypeStruct((rows, LANES), jnp.bfloat16)] * parts
        + [
            jax.ShapeDtypeStruct((parts, width, LANES), jnp.bfloat16),
            jax.ShapeDtypeStruct((channels, STRETCH), jnp.bfloat16),
            jax.ShapeDtypeStruct((WINDOWS + slots * WIN,), jnp.int32),
        ],
        scratch_shapes=[
            pltpu.SMEM(sources.shape, jnp.int32),
            pltpu.SMEM(owner.shape, jnp.int32),
            pltpu.VMEM(key_proj.shape, key_proj.dtype),
            pltpu.VMEM(value_proj.shape, value_proj.dtype),
            pltpu.VMEM(filters.shape, filters.dtype),
            pltpu.SemaphoreType.DMA((5,)),
        ],
        compiler_params=params(),
        name="gate",
    )(*operands)
    return sends, extra, last, meta


def merge_kernel(size, width, meta, *refs):
    received, extras, out = refs[:size], refs[size:-1], refs[-1]
    me = lax.axis_index("seq")
    for w in range(SENT):
        place = meta[PLACE + w]
        rows = pl.ds(pl.multiple_of(jnp.minimum(place, SLOTS - 1) * width, LANES), width)
        for step in range(size):

            @pl.when(sender(me, step, size) == meta[w])
            def _(w=w, step=step, rows=rows):
                out[w] = received[step][rows, :]

    for w in range(SLOTS, SENT):
        for step, extra in enumerate(extras):

            @pl.when((sender(me, step, size) == meta[w]) & (meta[PLACE + w] >= SLOTS))
            def _(w=w, extra=extra):
                out[w] = extra[...]


def merge(size, width, meta, received, extras=()):
    return pl.pallas_call(
        functools.partial(merge_kernel, size, width),
        in_specs=[SMEM_SPEC] + [VMEM_SPEC] * (size + len(extras)),
        out_specs=VMEM_SPEC,
        out_shape=jax.ShapeDtypeStruct((SENT, width, LANES), received[0].dtype),
        compiler_params=params(),
        name="merge",
    )(meta, *received, *extras)


def lags_kernel(first, *refs):
    received, (out, reverse) = refs[:-2], refs[-2:]
    size = len(received)
    group_count, padded = reverse.shape
    tiles = (received[0].shape[0] - first) // group_count
    lag_count = size * tiles * LANES
    tile_step = pl.program_id(0)

    @pl.when(tile_step == 0)
    def _():
        me = lax.axis_index("seq")
        row = lax.broadcasted_iota(jnp.int32, (LANES, LANES), 0)
        column = lax.broadcasted_iota(jnp.int32, (LANES, LANES), 1)
        flip = jnp.where(row + column == LANES - 1, 1.0, 0.0).astype(jnp.bfloat16)
        for step in range(size):
            shard = sender(me, step, size)
            for tile in range(tiles):
                piece = received[step][pl.ds(first + tile * group_count, group_count), :]
                start = lag_count - LANES * (shard * tiles + tile + 1)
                reverse[:, pl.ds(pl.multiple_of(start, LANES), LANES)] = jnp.dot(
                    piece, flip, preferred_element_type=jnp.float32
                )
        reverse[:, pl.ds(lag_count, padded - lag_count)] = jnp.zeros(
            (group_count, padded - lag_count), jnp.float32
        )

    row = lax.broadcasted_iota(jnp.int32, (GROUP_CH, LANES), 0)
    column = lax.broadcasted_iota(jnp.int32, (GROUP_CH, LANES), 1)
    inside = column > row
    tile_rows = pl.ds(pl.multiple_of(tile_step * BLOCKS, BLOCKS), BLOCKS)
    before = [jnp.zeros((GROUP_CH, LANES), jnp.float32)] * BLOCKS
    for start in range(0, padded, LANES):
        tile = reverse[tile_rows, pl.ds(start, LANES)]
        for g in range(BLOCKS):
            spread = jnp.broadcast_to(tile[g : g + 1, :], (GROUP_CH, LANES))
            rolled = pltpu.roll(spread, 1, 1, stride=1, stride_axis=0)
            out[g, :, pl.ds(start, LANES)] = jnp.where(inside, rolled, before[g]).astype(jnp.bfloat16)
            before[g] = rolled


def lags(received, first, group_count):
    size = len(received)
    padded = size * (received[0].shape[0] - first) // group_count * LANES + SPAN
    return pl.pallas_call(
        functools.partial(lags_kernel, first),
        grid=(group_count // BLOCKS,),
        in_specs=[VMEM_SPEC] * size,
        out_specs=pl.BlockSpec((BLOCKS, GROUP_CH, padded), lambda i: (i, 0, 0)),
        out_shape=jax.ShapeDtypeStruct((group_count, GROUP_CH, padded), jnp.bfloat16),
        scratch_shapes=[pltpu.VMEM((group_count, padded), jnp.float32)],
        compiler_params=params(),
        name="lags",
    )(*received)


def spread_rows(tile, spans, base):
    lane = lax.broadcasted_iota(jnp.int16, tile.shape, 1)
    zero = jnp.zeros(tile.shape, tile.dtype)
    for i1 in range(BLOCKS):
        shift = GROUP_CH * i1
        if i1 == 0:
            low, high = zero, tile
        else:
            moved = pltpu.roll(tile, LANES - shift, 1)
            early = lane < LANES - shift
            low, high = jnp.where(early, zero, moved), jnp.where(early, moved, zero)
        rows = pl.ds(shift, GROUP_CH)
        for g in range(BLOCKS):
            part = slice(g * GROUP_CH, (g + 1) * GROUP_CH)
            spans[g, rows, pl.ds(base, LANES)] = low[part]
            spans[g, rows, pl.ds(base + LANES, LANES)] = high[part]


def window(meta, shifted, group, slot, w):
    start = pl.multiple_of(meta[WINDOWS + slot * WIN + w], STRETCH)
    return shifted[group, :, pl.ds(start, SPAN)]


def rows_of(results, block):
    part = slice(block * GROUP_CH, (block + 1) * GROUP_CH)
    return jnp.concatenate([result[part] for result in results], axis=0).T


def last_kernel(slots, meta, last, shifted, out, spans):
    for start in range(0, last.shape[0], LANES):
        spread_rows(last[pl.ds(start, LANES), :], spans, 0)
        results = [
            lax.dot_general(
                spans[g],
                window(meta, shifted, start // GROUP_CH + g, slots - 1, SENT),
                NT,
                preferred_element_type=jnp.float32,
            )
            for g in range(BLOCKS)
        ]
        for m in range(BLOCKS):
            out[pl.ds(m * GROUP_CH, GROUP_CH), pl.ds(start, LANES)] = rows_of(results, m)


def last_term(slots, meta, last, shifted):
    return pl.pallas_call(
        functools.partial(last_kernel, slots),
        in_specs=[SMEM_SPEC, VMEM_SPEC, VMEM_SPEC],
        out_specs=VMEM_SPEC,
        out_shape=jax.ShapeDtypeStruct((STRETCH, last.shape[0]), jnp.float32),
        scratch_shapes=[pltpu.VMEM((BLOCKS, LANES, SPAN), jnp.bfloat16)],
        compiler_params=params(),
        name="last_term",
    )(meta, last, shifted)


def conv_kernel(step, slots, meta_in, pieces, shifted, term, query, *refs):
    out, meta, gates, result, spans, sems = refs[-6:]
    width = pieces.shape[1]
    size = out.shape[1] // width
    me = lax.axis_index("seq")
    base = pl.multiple_of(lax.rem(me + size - step, size) * width, width)
    copies = [
        pltpu.make_async_copy(meta_in, meta, sems.at[0]),
        pltpu.make_async_copy(query.at[:, pl.ds(base, width)], gates, sems.at[1]),
    ]
    for copy in copies:
        copy.start()
    starts = range(0, width, LANES)

    def spread(start):
        for w in range(SENT):
            tile = pieces[w, pl.ds(start, LANES), :]
            spread_rows(tile, spans.at[start // LANES], w * SPAN)

    spread(0)
    for copy in copies:
        copy.wait()
    for start in starts:
        columns = pl.ds(start, LANES)
        results = []
        for g in range(BLOCKS):
            group = base // GROUP_CH + (start // GROUP_CH + g)
            filter_rows = jnp.concatenate(
                [
                    jnp.concatenate([window(meta, shifted, group, slot, w) for w in range(SENT)], axis=1)
                    for slot in range(slots)
                ],
                axis=0,
            )
            results.append(
                lax.dot_general(
                    spans[start // LANES, g], filter_rows, NT, preferred_element_type=jnp.float32
                )
            )
        if start + LANES < width:
            spread(start + LANES)
        for m in range(BLOCKS):
            rows = rows_of(results, m)
            for slot in range(slots):
                place = pl.ds(slot * STRETCH + m * GROUP_CH, GROUP_CH)
                tile = rows[slot * GROUP_CH : (slot + 1) * GROUP_CH]
                if slot == slots - 1:
                    tile = tile + term[
                        pl.ds(m * GROUP_CH, GROUP_CH), pl.ds(pl.multiple_of(base + start, LANES), LANES)
                    ]
                result[place, columns] = (gates[place, columns].astype(jnp.float32) * tile).astype(
                    jnp.bfloat16
                )
    store = pltpu.make_async_copy(result, out.at[:, pl.ds(base, width)], sems.at[2])
    store.start()
    store.wait()


def conv(step, meta, pieces, shifted, term, query_proj, before):
    row_count = query_proj.shape[0]
    slots = row_count // STRETCH
    width = pieces.shape[1]
    operands = [meta, pieces, shifted, term, query_proj]
    in_specs = [ANY_SPEC, VMEM_SPEC, VMEM_SPEC, VMEM_SPEC, HBM_SPEC]
    aliases = {}
    if before is not None:
        aliases = {len(operands): 0}
        operands.append(before)
        in_specs.append(HBM_SPEC)
    return pl.pallas_call(
        functools.partial(conv_kernel, step, slots),
        in_specs=in_specs,
        out_specs=HBM_SPEC,
        out_shape=jax.ShapeDtypeStruct(query_proj.shape, jnp.bfloat16),
        input_output_aliases=aliases,
        scratch_shapes=[
            pltpu.SMEM(meta.shape, jnp.int32),
            pltpu.VMEM((row_count, width), jnp.bfloat16),
            pltpu.VMEM((row_count, width), jnp.bfloat16),
            pltpu.VMEM((width // LANES, BLOCKS, LANES, SENT * SPAN), jnp.bfloat16),
            pltpu.SemaphoreType.DMA((3,)),
        ],
        compiler_params=params(),
        name="conv",
    )(*operands)


def shards(size, key_proj, value_proj, query_proj, filters, sources, owner):
    row_count, channels = key_proj.shape
    slots = row_count // STRETCH
    by_parts = size == 4 and channels % (size * LANES) == 0
    parts = size if by_parts else 1

    width = channels // parts
    sends, extra, last, meta = gate(
        size, parts, sources, owner, key_proj, value_proj, filters
    )
    first = SLOTS * width
    group_count = filters.shape[0]
    if not by_parts:
        blocks = lax.all_gather(sends[0][first:], "seq")
        steps = sender(lax.axis_index("seq"), jnp.arange(size, dtype=jnp.int32), size)
        blocks = jnp.take(blocks, steps, axis=0)
        shifted = lags([blocks[step] for step in range(size)], 0, group_count)
        term = last_term(slots, meta, last, shifted)
        held = jnp.concatenate([sends[0][:first].reshape(SLOTS, width, LANES), extra])
        mine = (meta[:SENT] == lax.axis_index("seq"))[:, None, None]
        pieces = lax.psum(jnp.where(mine, held[meta[PLACE:MANY]], jnp.zeros_like(held)), "seq")
        return conv(0, meta, pieces, shifted, term, query_proj, None)

    def exchange(value, step):
        return lax.ppermute(value, "seq", [(z, z ^ step) for z in range(size)])

    received = [sends[0]] + [exchange(sends[step], step) for step in range(1, size)]

    def merge_more(meta, received, extra):
        more = [extra[0]] + [exchange(extra[step], step) for step in range(1, size)]
        return merge(size, width, meta, received, more)

    def merge_plain(meta, received, extra):
        return merge(size, width, meta, received)

    merged = lax.cond(meta[MANY] > 0, merge_more, merge_plain, meta, received, extra)

    def shift(value, step):
        return lax.ppermute(value, "seq", [(z, (z + step) % size) for z in range(size)])

    up, down = shift(merged, 1), shift(merged, size - 1)
    shifted = lags(received, first, group_count)
    far_part, shifted = lax.optimization_barrier((merged, shifted))
    far = shift(far_part, 2)
    term = last_term(slots, meta, last, shifted)
    out = None
    for step, pieces in ((0, merged), (1, up), (size - 1, down), (2, far)):
        out = conv(step, meta, pieces, shifted, term, query_proj, out)
    return out


def solution(mesh):
    return jax.shard_map(
        functools.partial(shards, mesh.shape["seq"]),
        mesh=mesh,
        in_specs=(
            P(("rep", "seq"), "ch"),
            P(("rep", "seq"), "ch"),
            P(("rep", "seq"), "ch"),
            P("ch", "seq"),
            P("rep"),
            P("rep"),
        ),
        out_specs=P(("rep", "seq"), "ch"),
        check_vma=False,
    )
```

```python
import functools

import jax
import jax.numpy as jnp
from jax import lax
from jax.experimental import pallas as pl
from jax.experimental.pallas import tpu as pltpu
from jax.sharding import PartitionSpec as P

GROUP_CH = 16
STRETCH = 128
WIN = 4
SENT = WIN - 1
LANES = 128
BLOCKS = LANES // GROUP_CH
SPAN = 2 * STRETCH
VMEM_LIMIT = 16 * 1024 * 1024

SMEM_SPEC = pl.BlockSpec(memory_space=pltpu.SMEM)
ANY_SPEC = pl.BlockSpec(memory_space=pl.ANY)
HBM_SPEC = pl.BlockSpec(memory_space=pltpu.HBM)
VMEM_SPEC = pl.BlockSpec(memory_space=pltpu.VMEM)
NT = (((1,), (1,)), ((), ()))


def params():
    return pltpu.CompilerParams(vmem_limit_bytes=VMEM_LIMIT)


def steps_of(size):
    return sorted(range(size), key=lambda step: (min(step, size - step), step))


def partner(me, step, size):
    return lax.rem(me + step, size)


def sender(me, step, size):
    return lax.rem(me + size - step, size)


PLACE = SENT
MANY = 2 * SENT
WINDOWS = MANY + 1
SLOTS = 2


def product(key, value, start, columns):
    rows = pl.ds(start, STRETCH)
    rows_k = key[rows, columns].astype(jnp.float32)
    rows_v = value[rows, columns].astype(jnp.float32)
    return (rows_k * rows_v).astype(jnp.bfloat16).T


def gate_kernel(size, parts, sources_in, owner_in, key_in, value_in, filters_in, *refs):
    sends = refs[:parts]
    extra, meta, sources, owner, key, value, filters, sems = refs[parts:]
    stretch_count = owner.shape[0]
    channels = key.shape[1]
    width = channels // parts
    me = lax.axis_index("seq")
    copies = [
        pltpu.make_async_copy(sources_in, sources, sems.at[0]),
        pltpu.make_async_copy(owner_in, owner, sems.at[1]),
        pltpu.make_async_copy(key_in, key, sems.at[2]),
        pltpu.make_async_copy(value_in, value, sems.at[3]),
        pltpu.make_async_copy(filters_in, filters, sems.at[4]),
    ]
    for copy in copies:
        copy.start()

    for copy in copies[:2]:
        copy.wait()

    def target(k, slot):
        mine = owner[k] == me

        @pl.when(mine)
        def _():
            for w in range(WIN):
                lag_block = jnp.maximum(k - sources[w], -1)
                meta[WINDOWS + slot * WIN + w] = (stretch_count - 1 - lag_block) * STRETCH

        return slot + jnp.where(mine, 1, 0)

    lax.fori_loop(0, stretch_count, target, 0)
    for copy in copies[2:]:
        copy.wait()
    holders = [owner[sources[w]] for w in range(SENT)]
    many = 0
    for w, holder in enumerate(holders):
        place = sum([jnp.where(other == holder, 1, 0) for other in holders[:w]], 0)
        meta[w] = holder
        meta[PLACE + w] = place
        many = many + jnp.where(place >= SLOTS, 1, 0)

        @pl.when(holder == me)
        def _(w=w, holder=holder, place=place):
            def count(k, total):
                return total + jnp.where(owner[k] == holder, 1, 0)

            slot = lax.fori_loop(0, sources[w], count, 0)
            first = pl.multiple_of(slot * STRETCH, STRETCH)
            for step in range(parts):
                part = partner(me, step, size) if parts > 1 else 0
                base = part * width

                def fill(target, offset, base=base):
                    for start in range(0, width, LANES):
                        columns = pl.ds(pl.multiple_of(base + start, LANES), LANES)
                        target[pl.ds(offset + start, LANES), :] = product(key, value, first, columns)

                if w < SLOTS:
                    fill(sends[step], pl.multiple_of(place * width, LANES))
                else:

                    @pl.when(place < SLOTS)
                    def _(step=step, fill=fill):
                        fill(sends[step], pl.multiple_of(place * width, LANES))

                    @pl.when(place >= SLOTS)
                    def _(step=step, fill=fill):
                        fill(extra.at[step], 0)

    meta[MANY] = many
    group_count = filters.shape[0]
    for tile in range(filters.shape[1] // LANES):
        rows = pl.ds(SLOTS * width + tile * group_count, group_count)
        for send in sends:
            send[rows, :] = filters[:, pl.ds(tile * LANES, LANES)]


def gate(size, parts, sources, owner, key_proj, value_proj, filters):
    row_count, channels = key_proj.shape
    slots = row_count // STRETCH
    width = channels // parts
    operands = [
        pltpu.with_memory_space_constraint(operand, pltpu.HBM)
        for operand in (sources, owner, key_proj, value_proj, filters)
    ]
    rows = SLOTS * width + filters.size // LANES
    *sends, extra, meta = pl.pallas_call(
        functools.partial(gate_kernel, size, parts),
        in_specs=[HBM_SPEC] * 5,
        out_specs=[VMEM_SPEC] * (parts + 1) + [SMEM_SPEC],
        out_shape=[jax.ShapeDtypeStruct((rows, LANES), jnp.bfloat16)] * parts
        + [
            jax.ShapeDtypeStruct((parts, width, LANES), jnp.bfloat16),
            jax.ShapeDtypeStruct((WINDOWS + slots * WIN,), jnp.int32),
        ],
        scratch_shapes=[
            pltpu.SMEM(sources.shape, jnp.int32),
            pltpu.SMEM(owner.shape, jnp.int32),
            pltpu.VMEM(key_proj.shape, key_proj.dtype),
            pltpu.VMEM(value_proj.shape, value_proj.dtype),
            pltpu.VMEM(filters.shape, filters.dtype),
            pltpu.SemaphoreType.DMA((5,)),
        ],
        compiler_params=params(),
        name="gate",
    )(*operands)
    return sends, extra, meta


def merge_kernel(size, width, meta, *refs):
    received, extras, out = refs[:size], refs[size:-1], refs[-1]
    me = lax.axis_index("seq")
    for w in range(SENT):
        place = meta[PLACE + w]
        rows = pl.ds(pl.multiple_of(jnp.minimum(place, SLOTS - 1) * width, LANES), width)
        for block, step in zip(received, steps_of(size)):

            @pl.when(sender(me, step, size) == meta[w])
            def _(w=w, block=block, rows=rows):
                out[w] = block[rows, :]

    for w in range(SLOTS, SENT):
        for step, extra in enumerate(extras):

            @pl.when((sender(me, step, size) == meta[w]) & (meta[PLACE + w] >= SLOTS))
            def _(w=w, extra=extra):
                out[w] = extra[...]


def merge(size, width, meta, received, extras=()):
    return pl.pallas_call(
        functools.partial(merge_kernel, size, width),
        in_specs=[SMEM_SPEC] + [VMEM_SPEC] * (size + len(extras)),
        out_specs=VMEM_SPEC,
        out_shape=jax.ShapeDtypeStruct((SENT, width, LANES), received[0].dtype),
        compiler_params=params(),
        name="merge",
    )(meta, *received, *extras)


def lags_kernel(first, *refs):
    received, (out, reverse) = refs[:-2], refs[-2:]
    size = len(received)
    group_count, padded = reverse.shape
    tiles = (received[0].shape[0] - first) // group_count
    lag_count = size * tiles * LANES
    tile_step = pl.program_id(0)

    @pl.when(tile_step == 0)
    def _():
        me = lax.axis_index("seq")
        row = lax.broadcasted_iota(jnp.int32, (LANES, LANES), 0)
        column = lax.broadcasted_iota(jnp.int32, (LANES, LANES), 1)
        flip = jnp.where(row + column == LANES - 1, 1.0, 0.0).astype(jnp.bfloat16)
        for block, step in zip(received, steps_of(size)):
            shard = sender(me, step, size)
            for tile in range(tiles):
                piece = block[pl.ds(first + tile * group_count, group_count), :]
                start = lag_count - LANES * (shard * tiles + tile + 1)
                reverse[:, pl.ds(pl.multiple_of(start, LANES), LANES)] = jnp.dot(
                    piece, flip, preferred_element_type=jnp.float32
                )
        reverse[:, pl.ds(lag_count, padded - lag_count)] = jnp.zeros(
            (group_count, padded - lag_count), jnp.float32
        )

    row = lax.broadcasted_iota(jnp.int32, (GROUP_CH, LANES), 0)
    column = lax.broadcasted_iota(jnp.int32, (GROUP_CH, LANES), 1)
    inside = column > row
    tile_rows = pl.ds(pl.multiple_of(tile_step * BLOCKS, BLOCKS), BLOCKS)
    before = [jnp.zeros((GROUP_CH, LANES), jnp.float32)] * BLOCKS
    for start in range(0, padded, LANES):
        tile = reverse[tile_rows, pl.ds(start, LANES)]
        for g in range(BLOCKS):
            spread = jnp.broadcast_to(tile[g : g + 1, :], (GROUP_CH, LANES))
            rolled = pltpu.roll(spread, 1, 1, stride=1, stride_axis=0)
            out[g, :, pl.ds(start, LANES)] = jnp.where(inside, rolled, before[g]).astype(jnp.bfloat16)
            before[g] = rolled


def lags(received, first, group_count):
    size = len(received)
    padded = size * (received[0].shape[0] - first) // group_count * LANES + SPAN
    return pl.pallas_call(
        functools.partial(lags_kernel, first),
        grid=(group_count // BLOCKS,),
        in_specs=[VMEM_SPEC] * size,
        out_specs=pl.BlockSpec((BLOCKS, GROUP_CH, padded), lambda i: (i, 0, 0)),
        out_shape=jax.ShapeDtypeStruct((group_count, GROUP_CH, padded), jnp.bfloat16),
        scratch_shapes=[pltpu.VMEM((group_count, padded), jnp.float32)],
        compiler_params=params(),
        name="lags",
    )(*received)


def spread_rows(tile, spans, base):
    lane = lax.broadcasted_iota(jnp.int16, tile.shape, 1)
    zero = jnp.zeros(tile.shape, tile.dtype)
    for i1 in range(BLOCKS):
        shift = GROUP_CH * i1
        if i1 == 0:
            low, high = zero, tile
        else:
            moved = pltpu.roll(tile, LANES - shift, 1)
            early = lane < LANES - shift
            low, high = jnp.where(early, zero, moved), jnp.where(early, moved, zero)
        rows = pl.ds(shift, GROUP_CH)
        for g in range(BLOCKS):
            part = slice(g * GROUP_CH, (g + 1) * GROUP_CH)
            spans[g, rows, pl.ds(base, LANES)] = low[part]
            spans[g, rows, pl.ds(base + LANES, LANES)] = high[part]


def window(meta, shifted, group, slot, w):
    start = pl.multiple_of(meta[WINDOWS + slot * WIN + w], STRETCH)
    return shifted[group, :, pl.ds(start, SPAN)]


def last_rows_kernel(key, value, out):
    for start in range(0, out.shape[0], LANES):
        out[pl.ds(start, LANES), :] = product(key, value, 0, pl.ds(start, LANES))


def last_rows(key_proj, value_proj):
    row_count, channels = key_proj.shape
    block = pl.BlockSpec((STRETCH, channels), lambda i: (row_count // STRETCH - 1, 0))
    operands = [pltpu.with_memory_space_constraint(x, pltpu.HBM) for x in (key_proj, value_proj)]
    return pl.pallas_call(
        last_rows_kernel,
        grid=(1,),
        in_specs=[block, block],
        out_specs=pl.BlockSpec((channels, STRETCH), lambda i: (0, 0)),
        out_shape=jax.ShapeDtypeStruct((channels, STRETCH), jnp.bfloat16),
        compiler_params=params(),
        name="last_rows",
    )(*operands)


def rows_of(results, block):
    part = slice(block * GROUP_CH, (block + 1) * GROUP_CH)
    return jnp.concatenate([result[part] for result in results], axis=0).T


def last_kernel(slots, meta, last, shifted, out, spans):
    for start in range(0, last.shape[0], LANES):
        spread_rows(last[pl.ds(start, LANES), :], spans, 0)
        results = [
            lax.dot_general(
                spans[g],
                window(meta, shifted, start // GROUP_CH + g, slots - 1, SENT),
                NT,
                preferred_element_type=jnp.float32,
            )
            for g in range(BLOCKS)
        ]
        for m in range(BLOCKS):
            out[pl.ds(m * GROUP_CH, GROUP_CH), pl.ds(start, LANES)] = rows_of(results, m)


def last_term(slots, meta, last, shifted):
    return pl.pallas_call(
        functools.partial(last_kernel, slots),
        in_specs=[SMEM_SPEC, VMEM_SPEC, VMEM_SPEC],
        out_specs=VMEM_SPEC,
        out_shape=jax.ShapeDtypeStruct((STRETCH, last.shape[0]), jnp.float32),
        scratch_shapes=[pltpu.VMEM((BLOCKS, LANES, SPAN), jnp.bfloat16)],
        compiler_params=params(),
        name="last_term",
    )(meta, last, shifted)


def conv_kernel(step, slots, meta_in, pieces, shifted, term, query, *refs):
    out, meta, result, spans, sems = refs[-5:]
    width = pieces.shape[1]
    size = out.shape[1] // width
    me = lax.axis_index("seq")
    base = pl.multiple_of(lax.rem(me + size - step, size) * width, width)
    scalars = pltpu.make_async_copy(meta_in, meta, sems.at[0])
    scalars.start()
    starts = range(0, width, LANES)

    def spread(start):
        for w in range(SENT):
            tile = pieces[w, pl.ds(start, LANES), :]
            spread_rows(tile, spans.at[start // LANES], w * SPAN)

    spread(0)
    scalars.wait()
    stores = []
    for start in starts:
        columns = pl.ds(start, LANES)
        results = []
        for g in range(BLOCKS):
            group = base // GROUP_CH + (start // GROUP_CH + g)
            filter_rows = jnp.concatenate(
                [
                    jnp.concatenate([window(meta, shifted, group, slot, w) for w in range(SENT)], axis=1)
                    for slot in range(slots)
                ],
                axis=0,
            )
            results.append(
                lax.dot_general(
                    spans[start // LANES, g], filter_rows, NT, preferred_element_type=jnp.float32
                )
            )
        if start + LANES < width:
            spread(start + LANES)
        for m in range(BLOCKS):
            rows = rows_of(results, m)
            for slot in range(slots):
                place = pl.ds(slot * STRETCH + m * GROUP_CH, GROUP_CH)
                tile = rows[slot * GROUP_CH : (slot + 1) * GROUP_CH]
                if slot == slots - 1:
                    tile = tile + term[
                        pl.ds(m * GROUP_CH, GROUP_CH), pl.ds(pl.multiple_of(base + start, LANES), LANES)
                    ]
                gates = query[place, pl.ds(pl.multiple_of(base + start, LANES), LANES)]
                result[place, columns] = (gates.astype(jnp.float32) * tile).astype(jnp.bfloat16)
        store = pltpu.make_async_copy(
            result.at[:, columns],
            out.at[:, pl.ds(pl.multiple_of(base + start, LANES), LANES)],
            sems.at[1 + start // LANES],
        )
        store.start()
        stores.append(store)
    for store in stores:
        store.wait()


def conv(step, meta, pieces, shifted, term, query_proj, before):
    row_count = query_proj.shape[0]
    slots = row_count // STRETCH
    width = pieces.shape[1]
    operands = [meta, pieces, shifted, term, query_proj]
    in_specs = [ANY_SPEC] + [VMEM_SPEC] * 4
    aliases = {}
    if before is not None:
        aliases = {len(operands): 0}
        operands.append(before)
        in_specs.append(HBM_SPEC)
    return pl.pallas_call(
        functools.partial(conv_kernel, step, slots),
        in_specs=in_specs,
        out_specs=HBM_SPEC,
        out_shape=jax.ShapeDtypeStruct(query_proj.shape, jnp.bfloat16),
        input_output_aliases=aliases,
        scratch_shapes=[
            pltpu.SMEM(meta.shape, jnp.int32),
            pltpu.VMEM((row_count, width), jnp.bfloat16),
            pltpu.VMEM((width // LANES, BLOCKS, LANES, SENT * SPAN), jnp.bfloat16),
            pltpu.SemaphoreType.DMA((1 + width // LANES,)),
        ],
        compiler_params=params(),
        name="conv",
    )(*operands)


def shards(size, key_proj, value_proj, query_proj, filters, sources, owner):
    row_count, channels = key_proj.shape
    slots = row_count // STRETCH
    by_parts = size == 4 and channels % (size * LANES) == 0
    parts = size if by_parts else 1

    width = channels // parts
    sends, extra, meta = gate(size, parts, sources, owner, key_proj, value_proj, filters)
    last = last_rows(key_proj, value_proj)
    first = SLOTS * width
    group_count = filters.shape[0]
    if not by_parts:
        blocks = lax.all_gather(sends[0][first:], "seq")
        steps = sender(lax.axis_index("seq"), jnp.arange(size, dtype=jnp.int32), size)
        blocks = jnp.take(blocks, steps, axis=0)
        shifted = lags([blocks[step] for step in steps_of(size)], 0, group_count)
        term = last_term(slots, meta, last, shifted)
        held = jnp.concatenate([sends[0][:first].reshape(SLOTS, width, LANES), extra])
        mine = (meta[:SENT] == lax.axis_index("seq"))[:, None, None]
        pieces = lax.psum(jnp.where(mine, held[meta[PLACE:MANY]], jnp.zeros_like(held)), "seq")
        return conv(0, meta, pieces, shifted, term, query_proj, None)

    def shift(value, step):
        return lax.ppermute(value, "seq", [(z, (z + step) % size) for z in range(size)])

    up, down, far = (shift(sends[step], step) for step in (1, size - 1, 2))
    last, up = lax.optimization_barrier((last, up))
    received = [sends[0], up, down, far]

    def merge_more(meta, received, extra):
        more = [extra[0]] + [shift(extra[step], step) for step in range(1, size)]
        return merge(size, width, meta, received, more)

    def merge_plain(meta, received, extra):
        return merge(size, width, meta, received)

    merged = lax.cond(meta[MANY] > 0, merge_more, merge_plain, meta, received, extra)

    up, down = shift(merged, 1), shift(merged, size - 1)
    shifted = lags(received, first, group_count)
    far_part, shifted = lax.optimization_barrier((merged, shifted))
    far = shift(far_part, 2)
    term = last_term(slots, meta, last, shifted)
    out = None
    for step, pieces in ((0, merged), (1, up), (size - 1, down), (2, far)):
        out = conv(step, meta, pieces, shifted, term, query_proj, out)
    return out


def solution(mesh):
    return jax.shard_map(
        functools.partial(shards, mesh.shape["seq"]),
        mesh=mesh,
        in_specs=(
            P(("rep", "seq"), "ch"),
            P(("rep", "seq"), "ch"),
            P(("rep", "seq"), "ch"),
            P("ch", "seq"),
            P("rep"),
            P("rep"),
        ),
        out_specs=P(("rep", "seq"), "ch"),
        check_vma=False,
    )
```

```python
import functools

import jax
import jax.numpy as jnp
from jax import lax
from jax.experimental import pallas as pl
from jax.experimental.pallas import tpu as pltpu
from jax.sharding import PartitionSpec as P

GROUP_CH = 16
STRETCH = 128
WIN = 4
SENT = WIN - 1
LANES = 128
BLOCKS = LANES // GROUP_CH
SPAN = 2 * STRETCH
VMEM_LIMIT = 16 * 1024 * 1024

SMEM_SPEC = pl.BlockSpec(memory_space=pltpu.SMEM)
ANY_SPEC = pl.BlockSpec(memory_space=pl.ANY)
HBM_SPEC = pl.BlockSpec(memory_space=pltpu.HBM)
VMEM_SPEC = pl.BlockSpec(memory_space=pltpu.VMEM)
NT = (((1,), (1,)), ((), ()))


def params():
    return pltpu.CompilerParams(vmem_limit_bytes=VMEM_LIMIT)


def steps_of(size):
    return sorted(range(size), key=lambda step: (min(step, size - step), step))


def partner(me, step, size):
    return lax.rem(me + step, size)


def sender(me, step, size):
    return lax.rem(me + size - step, size)


PLACE = SENT
MANY = 2 * SENT
WINDOWS = MANY + 1
SLOTS = 2


def product(key, value, start, columns):
    rows = pl.ds(start, STRETCH)
    rows_k = key[rows, columns].astype(jnp.float32)
    rows_v = value[rows, columns].astype(jnp.float32)
    return (rows_k * rows_v).astype(jnp.bfloat16).T


def gate_kernel(size, parts, shares, sources_in, owner_in, key_in, value_in, filters_in, *refs):
    sends = refs[:parts]
    extra, meta, sources, owner, key, value, filters, sems = refs[parts:]
    stretch_count = owner.shape[0]
    channels = key.shape[1]
    width = channels // parts
    me = lax.axis_index("seq")
    copies = [
        pltpu.make_async_copy(sources_in, sources, sems.at[0]),
        pltpu.make_async_copy(owner_in, owner, sems.at[1]),
        pltpu.make_async_copy(key_in, key, sems.at[2]),
        pltpu.make_async_copy(value_in, value, sems.at[3]),
        pltpu.make_async_copy(filters_in, filters, sems.at[4]),
    ]
    for copy in copies:
        copy.start()

    for copy in copies[:2]:
        copy.wait()

    def target(k, slot):
        mine = owner[k] == me

        @pl.when(mine)
        def _():
            for w in range(WIN):
                lag_block = jnp.maximum(k - sources[w], -1)
                meta[WINDOWS + slot * WIN + w] = (stretch_count - 1 - lag_block) * STRETCH

        return slot + jnp.where(mine, 1, 0)

    lax.fori_loop(0, stretch_count, target, 0)
    for copy in copies[2:]:
        copy.wait()
    holders = [owner[sources[w]] for w in range(SENT)]
    many = 0
    for w, holder in enumerate(holders):
        place = sum([jnp.where(other == holder, 1, 0) for other in holders[:w]], 0)
        meta[w] = holder
        meta[PLACE + w] = place
        many = many + jnp.where(place >= SLOTS, 1, 0)

        @pl.when(holder == me)
        def _(w=w, holder=holder, place=place):
            def count(k, total):
                return total + jnp.where(owner[k] == holder, 1, 0)

            slot = lax.fori_loop(0, sources[w], count, 0)
            first = pl.multiple_of(slot * STRETCH, STRETCH)
            for step in range(parts):
                part = partner(me, step, size) if parts > 1 else 0
                base = part * width

                def fill(target, offset, base=base):
                    for start in range(0, width, LANES):
                        columns = pl.ds(pl.multiple_of(base + start, LANES), LANES)
                        target[pl.ds(offset + start, LANES), :] = product(key, value, first, columns)

                if w < SLOTS:
                    fill(sends[step], pl.multiple_of(place * width, LANES))
                else:

                    @pl.when(place < SLOTS)
                    def _(step=step, fill=fill):
                        fill(sends[step], pl.multiple_of(place * width, LANES))

                    @pl.when(place >= SLOTS)
                    def _(step=step, fill=fill):
                        fill(extra.at[step], 0)

    meta[MANY] = many
    share = filters.shape[0] // shares
    groups = pl.ds(0, share)
    if shares > 1:
        groups = pl.ds(pl.multiple_of(lax.axis_index("rep") * share, share), share)
    for tile in range(filters.shape[1] // LANES):
        piece = filters[groups, pl.ds(tile * LANES, LANES)]
        for send in sends:
            send[pl.ds(SLOTS * width + tile * share, share), :] = piece


def gate(size, parts, shares, sources, owner, key_proj, value_proj, filters):
    row_count, channels = key_proj.shape
    slots = row_count // STRETCH
    width = channels // parts
    operands = [
        pltpu.with_memory_space_constraint(operand, pltpu.HBM)
        for operand in (sources, owner, key_proj, value_proj, filters)
    ]
    rows = SLOTS * width + filters.size // (shares * LANES)
    *sends, extra, meta = pl.pallas_call(
        functools.partial(gate_kernel, size, parts, shares),
        in_specs=[HBM_SPEC] * 5,
        out_specs=[VMEM_SPEC] * (parts + 1) + [SMEM_SPEC],
        out_shape=[jax.ShapeDtypeStruct((rows, LANES), jnp.bfloat16)] * parts
        + [
            jax.ShapeDtypeStruct((parts, width, LANES), jnp.bfloat16),
            jax.ShapeDtypeStruct((WINDOWS + slots * WIN,), jnp.int32),
        ],
        scratch_shapes=[
            pltpu.SMEM(sources.shape, jnp.int32),
            pltpu.SMEM(owner.shape, jnp.int32),
            pltpu.VMEM(key_proj.shape, key_proj.dtype),
            pltpu.VMEM(value_proj.shape, value_proj.dtype),
            pltpu.VMEM(filters.shape, filters.dtype),
            pltpu.SemaphoreType.DMA((5,)),
        ],
        compiler_params=params(),
        name="gate",
    )(*operands)
    return sends, extra, meta


def merge_kernel(size, width, meta, *refs):
    received, extras = refs[:size], refs[size:-4]
    out, low, high, filters = refs[-4:]
    me = lax.axis_index("seq")

    def write(w, piece):
        out[w] = piece
        low[w] = piece[: width // 2]
        high[w] = piece[width // 2 :]

    for w in range(SENT):
        place = meta[PLACE + w]
        rows = pl.ds(pl.multiple_of(jnp.minimum(place, SLOTS - 1) * width, LANES), width)
        for block, step in zip(received, steps_of(size)):

            @pl.when(sender(me, step, size) == meta[w])
            def _(w=w, block=block, rows=rows):
                write(w, block[rows, :])

    for w in range(SLOTS, SENT):
        for step, extra in enumerate(extras):

            @pl.when((sender(me, step, size) == meta[w]) & (meta[PLACE + w] >= SLOTS))
            def _(w=w, extra=extra):
                write(w, extra[...])

    for block, step in zip(received, steps_of(size)):
        filters[sender(me, step, size)] = block[pl.ds(SLOTS * width, filters.shape[1]), :]


def merge(size, width, meta, received, extras=()):
    return pl.pallas_call(
        functools.partial(merge_kernel, size, width),
        in_specs=[SMEM_SPEC] + [VMEM_SPEC] * (size + len(extras)),
        out_specs=[VMEM_SPEC] * 4,
        out_shape=[
            jax.ShapeDtypeStruct(shape, received[0].dtype)
            for shape in (
                (SENT, width, LANES),
                (SENT, width // 2, LANES),
                (SENT, width // 2, LANES),
                (size, received[0].shape[0] - SLOTS * width, LANES),
            )
        ],
        compiler_params=params(),
        name="merge",
    )(meta, *received, *extras)


def lags_kernel(*refs):
    shares, (out, reverse) = refs[:-2], refs[-2:]
    size = shares[0].shape[0]
    group_count, padded = reverse.shape
    share = group_count // len(shares)
    tiles = shares[0].shape[1] // share
    lag_count = size * tiles * LANES
    tile_step = pl.program_id(0)

    @pl.when(tile_step == 0)
    def _():
        row = lax.broadcasted_iota(jnp.int32, (LANES, LANES), 0)
        column = lax.broadcasted_iota(jnp.int32, (LANES, LANES), 1)
        flip = jnp.where(row + column == LANES - 1, 1.0, 0.0).astype(jnp.bfloat16)
        for index, blocks in enumerate(shares):
            groups = pl.ds(0, share)
            if len(shares) > 1:
                place = lax.axis_index("rep") if index == 0 else 1 - lax.axis_index("rep")
                groups = pl.ds(pl.multiple_of(place * share, share), share)
            for tile in range(size * tiles):
                piece = blocks[tile // tiles, pl.ds(tile % tiles * share, share), :]
                reverse[groups, pl.ds(lag_count - LANES * (tile + 1), LANES)] = jnp.dot(
                    piece, flip, preferred_element_type=jnp.float32
                )
        reverse[:, pl.ds(lag_count, padded - lag_count)] = jnp.zeros(
            (group_count, padded - lag_count), jnp.float32
        )

    row = lax.broadcasted_iota(jnp.int32, (GROUP_CH, LANES), 0)
    column = lax.broadcasted_iota(jnp.int32, (GROUP_CH, LANES), 1)
    inside = column > row
    tile_rows = pl.ds(pl.multiple_of(tile_step * BLOCKS, BLOCKS), BLOCKS)
    before = [jnp.zeros((GROUP_CH, LANES), jnp.float32)] * BLOCKS
    for start in range(0, padded, LANES):
        tile = reverse[tile_rows, pl.ds(start, LANES)]
        for g in range(BLOCKS):
            spread = jnp.broadcast_to(tile[g : g + 1, :], (GROUP_CH, LANES))
            rolled = pltpu.roll(spread, 1, 1, stride=1, stride_axis=0)
            out[g, :, pl.ds(start, LANES)] = jnp.where(inside, rolled, before[g]).astype(jnp.bfloat16)
            before[g] = rolled


def lags(shares, group_count):
    padded = sum(blocks.size for blocks in shares) // group_count + SPAN
    return pl.pallas_call(
        lags_kernel,
        grid=(group_count // BLOCKS,),
        in_specs=[VMEM_SPEC] * len(shares),
        out_specs=pl.BlockSpec((BLOCKS, GROUP_CH, padded), lambda i: (i, 0, 0)),
        out_shape=jax.ShapeDtypeStruct((group_count, GROUP_CH, padded), jnp.bfloat16),
        scratch_shapes=[pltpu.VMEM((group_count, padded), jnp.float32)],
        compiler_params=params(),
        name="lags",
    )(*shares)


def spread_rows(tile, spans, base):
    lane = lax.broadcasted_iota(jnp.int16, tile.shape, 1)
    zero = jnp.zeros(tile.shape, tile.dtype)
    for i1 in range(BLOCKS):
        shift = GROUP_CH * i1
        if i1 == 0:
            low, high = zero, tile
        else:
            moved = pltpu.roll(tile, LANES - shift, 1)
            early = lane < LANES - shift
            low, high = jnp.where(early, zero, moved), jnp.where(early, moved, zero)
        rows = pl.ds(shift, GROUP_CH)
        for g in range(BLOCKS):
            part = slice(g * GROUP_CH, (g + 1) * GROUP_CH)
            spans[g, rows, pl.ds(base, LANES)] = low[part]
            spans[g, rows, pl.ds(base + LANES, LANES)] = high[part]


def window(meta, shifted, group, slot, w):
    start = pl.multiple_of(meta[WINDOWS + slot * WIN + w], STRETCH)
    return shifted[group, :, pl.ds(start, SPAN)]


def last_rows_kernel(key, value, out):
    for start in range(0, out.shape[0], LANES):
        out[pl.ds(start, LANES), :] = product(key, value, 0, pl.ds(start, LANES))


def last_rows(key_proj, value_proj):
    row_count, channels = key_proj.shape
    block = pl.BlockSpec((STRETCH, channels), lambda i: (row_count // STRETCH - 1, 0))
    operands = [pltpu.with_memory_space_constraint(x, pltpu.HBM) for x in (key_proj, value_proj)]
    return pl.pallas_call(
        last_rows_kernel,
        grid=(1,),
        in_specs=[block, block],
        out_specs=pl.BlockSpec((channels, STRETCH), lambda i: (0, 0)),
        out_shape=jax.ShapeDtypeStruct((channels, STRETCH), jnp.bfloat16),
        compiler_params=params(),
        name="last_rows",
    )(*operands)


def rows_of(results, block):
    part = slice(block * GROUP_CH, (block + 1) * GROUP_CH)
    return jnp.concatenate([result[part] for result in results], axis=0).T


def last_kernel(slots, meta, last, shifted, out, spans):
    for start in range(0, last.shape[0], LANES):
        spread_rows(last[pl.ds(start, LANES), :], spans, 0)
        results = [
            lax.dot_general(
                spans[g],
                window(meta, shifted, start // GROUP_CH + g, slots - 1, SENT),
                NT,
                preferred_element_type=jnp.float32,
            )
            for g in range(BLOCKS)
        ]
        for m in range(BLOCKS):
            out[pl.ds(m * GROUP_CH, GROUP_CH), pl.ds(start, LANES)] = rows_of(results, m)


def last_term(slots, meta, last, shifted):
    return pl.pallas_call(
        functools.partial(last_kernel, slots),
        in_specs=[SMEM_SPEC, VMEM_SPEC, VMEM_SPEC],
        out_specs=VMEM_SPEC,
        out_shape=jax.ShapeDtypeStruct((STRETCH, last.shape[0]), jnp.float32),
        scratch_shapes=[pltpu.VMEM((BLOCKS, LANES, SPAN), jnp.bfloat16)],
        compiler_params=params(),
        name="last_term",
    )(meta, last, shifted)


def conv_kernel(step, slots, part, offset, meta_in, pieces, shifted, term, query, *refs):
    out, meta, result, spans, sems = refs[-5:]
    width = pieces.shape[1]
    size = out.shape[1] // part
    me = lax.axis_index("seq")
    base = pl.multiple_of(lax.rem(me + size - step, size) * part + offset, width)
    scalars = pltpu.make_async_copy(meta_in, meta, sems.at[0])
    scalars.start()
    starts = range(0, width, LANES)

    def spread(start):
        for w in range(SENT):
            tile = pieces[w, pl.ds(start, LANES), :]
            spread_rows(tile, spans.at[start // LANES], w * SPAN)

    spread(0)
    scalars.wait()
    stores = []
    for start in starts:
        columns = pl.ds(start, LANES)
        results = []
        for g in range(BLOCKS):
            group = base // GROUP_CH + (start // GROUP_CH + g)
            filter_rows = jnp.concatenate(
                [
                    jnp.concatenate([window(meta, shifted, group, slot, w) for w in range(SENT)], axis=1)
                    for slot in range(slots)
                ],
                axis=0,
            )
            results.append(
                lax.dot_general(
                    spans[start // LANES, g], filter_rows, NT, preferred_element_type=jnp.float32
                )
            )
        if start + LANES < width:
            spread(start + LANES)
        for m in range(BLOCKS):
            rows = rows_of(results, m)
            for slot in range(slots):
                place = pl.ds(slot * STRETCH + m * GROUP_CH, GROUP_CH)
                tile = rows[slot * GROUP_CH : (slot + 1) * GROUP_CH]
                if slot == slots - 1:
                    tile = tile + term[
                        pl.ds(m * GROUP_CH, GROUP_CH), pl.ds(pl.multiple_of(base + start, LANES), LANES)
                    ]
                gates = query[place, pl.ds(pl.multiple_of(base + start, LANES), LANES)]
                result[place, columns] = (gates.astype(jnp.float32) * tile).astype(jnp.bfloat16)
        store = pltpu.make_async_copy(
            result.at[:, columns],
            out.at[:, pl.ds(pl.multiple_of(base + start, LANES), LANES)],
            sems.at[1 + start // LANES],
        )
        store.start()
        stores.append(store)
    for store in stores:
        store.wait()


def conv(step, meta, pieces, shifted, term, query_proj, before, part=None, offset=0):
    row_count = query_proj.shape[0]
    slots = row_count // STRETCH
    width = pieces.shape[1]
    operands = [meta, pieces, shifted, term, query_proj]
    in_specs = [ANY_SPEC] + [VMEM_SPEC] * 4
    aliases = {}
    if before is not None:
        aliases = {len(operands): 0}
        operands.append(before)
        in_specs.append(HBM_SPEC)
    return pl.pallas_call(
        functools.partial(conv_kernel, step, slots, part or width, offset),
        in_specs=in_specs,
        out_specs=HBM_SPEC,
        out_shape=jax.ShapeDtypeStruct(query_proj.shape, jnp.bfloat16),
        input_output_aliases=aliases,
        scratch_shapes=[
            pltpu.SMEM(meta.shape, jnp.int32),
            pltpu.VMEM((row_count, width), jnp.bfloat16),
            pltpu.VMEM((width // LANES, BLOCKS, LANES, SENT * SPAN), jnp.bfloat16),
            pltpu.SemaphoreType.DMA((1 + width // LANES,)),
        ],
        compiler_params=params(),
        name="conv",
    )(*operands)


def shards(size, reps, key_proj, value_proj, query_proj, filters, sources, owner):
    row_count, channels = key_proj.shape
    slots = row_count // STRETCH
    by_parts = (size, reps) == (4, 2) and channels % (2 * size * LANES) == 0
    shares = reps if by_parts else 1
    parts = size if by_parts else 1

    width = channels // parts
    sends, extra, meta = gate(size, parts, shares, sources, owner, key_proj, value_proj, filters)
    last = last_rows(key_proj, value_proj)
    first = SLOTS * width
    group_count = filters.shape[0]
    if not by_parts:
        shifted = lags([lax.all_gather(sends[0][first:], "seq")], group_count)
        term = last_term(slots, meta, last, shifted)
        held = jnp.concatenate([sends[0][:first].reshape(SLOTS, width, LANES), extra])
        mine = (meta[:SENT] == lax.axis_index("seq"))[:, None, None]
        pieces = lax.psum(jnp.where(mine, held[meta[PLACE:MANY]], jnp.zeros_like(held)), "seq")
        return conv(0, meta, pieces, shifted, term, query_proj, None)

    def shift(value, step):
        return lax.ppermute(value, "seq", [(z, (z + step) % size) for z in range(size)])

    up, down, far = (shift(sends[step], step) for step in (1, size - 1, 2))
    last, up = lax.optimization_barrier((last, up))
    received = [sends[0], up, down, far]

    def merge_more(meta, received, extra):
        more = [extra[0]] + [shift(extra[step], step) for step in range(1, size)]
        return merge(size, width, meta, received, more)

    def merge_plain(meta, received, extra):
        return merge(size, width, meta, received)

    merged, low, high, share = lax.cond(
        meta[MANY] > 0, merge_more, merge_plain, meta, received, extra
    )
    up = shift(merged, 1)
    other = lax.ppermute(share, "rep", [(0, 1), (1, 0)])
    down = shift(merged, size - 1)
    shifted = lags([share, other], group_count)
    low, high, shifted = lax.optimization_barrier((low, high, shifted))
    far = [shift(half, 2) for half in (low, high)]
    term = last_term(slots, meta, last, shifted)
    out = None
    for step, pieces in ((0, merged), (1, up), (size - 1, down)):
        out = conv(step, meta, pieces, shifted, term, query_proj, out)
    for index, pieces in enumerate(far):
        out = conv(
            2, meta, pieces, shifted, term, query_proj, out, width, index * (width // len(far))
        )
    return out


def solution(mesh):
    return jax.shard_map(
        functools.partial(shards, mesh.shape["seq"], mesh.shape["rep"]),
        mesh=mesh,
        in_specs=(
            P(("rep", "seq"), "ch"),
            P(("rep", "seq"), "ch"),
            P(("rep", "seq"), "ch"),
            P("ch", "seq"),
            P("rep"),
            P("rep"),
        ),
        out_specs=P(("rep", "seq"), "ch"),
        check_vma=False,
    )
```

```python
import functools

import jax
import jax.numpy as jnp
from jax import lax
from jax.experimental import pallas as pl
from jax.experimental.pallas import tpu as pltpu
from jax.sharding import PartitionSpec as P

GROUP_CH = 16
STRETCH = 128
WIN = 4
SENT = WIN - 1
LANES = 128
BLOCKS = LANES // GROUP_CH
SPAN = 2 * STRETCH
VMEM_LIMIT = 16 * 1024 * 1024

SMEM_SPEC = pl.BlockSpec(memory_space=pltpu.SMEM)
ANY_SPEC = pl.BlockSpec(memory_space=pl.ANY)
HBM_SPEC = pl.BlockSpec(memory_space=pltpu.HBM)
VMEM_SPEC = pl.BlockSpec(memory_space=pltpu.VMEM)
NT = (((1,), (1,)), ((), ()))


def params():
    return pltpu.CompilerParams(vmem_limit_bytes=VMEM_LIMIT)


def steps_of(size):
    return sorted(range(size), key=lambda step: (min(step, size - step), step))


def partner(me, step, size):
    return lax.rem(me + step, size)


def sender(me, step, size):
    return lax.rem(me + size - step, size)


PLACE = SENT
MANY = 2 * SENT
WINDOWS = MANY + 1
SLOTS = 2


def product(key, value, start, columns):
    rows = pl.ds(start, STRETCH)
    rows_k = key[rows, columns].astype(jnp.float32)
    rows_v = value[rows, columns].astype(jnp.float32)
    return (rows_k * rows_v).astype(jnp.bfloat16).T


def gate_kernel(size, parts, sources_in, owner_in, key_in, value_in, filters_in, *refs):
    sends = refs[:parts]
    extra, meta, sources, owner, key, value, filters, sems = refs[parts:]
    stretch_count = owner.shape[0]
    channels = key.shape[1]
    width = channels // parts
    me = lax.axis_index("seq")
    copies = [
        pltpu.make_async_copy(sources_in, sources, sems.at[0]),
        pltpu.make_async_copy(owner_in, owner, sems.at[1]),
        pltpu.make_async_copy(key_in, key, sems.at[2]),
        pltpu.make_async_copy(value_in, value, sems.at[3]),
        pltpu.make_async_copy(filters_in, filters, sems.at[4]),
    ]
    for copy in copies:
        copy.start()

    for copy in copies[:2]:
        copy.wait()

    def target(k, slot):
        mine = owner[k] == me

        @pl.when(mine)
        def _():
            for w in range(WIN):
                lag_block = jnp.maximum(k - sources[w], -1)
                meta[WINDOWS + slot * WIN + w] = (stretch_count - 1 - lag_block) * STRETCH

        return slot + jnp.where(mine, 1, 0)

    lax.fori_loop(0, stretch_count, target, 0)
    for copy in copies[2:]:
        copy.wait()
    holders = [owner[sources[w]] for w in range(SENT)]
    many = 0
    for w, holder in enumerate(holders):
        place = sum([jnp.where(other == holder, 1, 0) for other in holders[:w]], 0)
        meta[w] = holder
        meta[PLACE + w] = place
        many = many + jnp.where(place >= SLOTS, 1, 0)

        @pl.when(holder == me)
        def _(w=w, holder=holder, place=place):
            def count(k, total):
                return total + jnp.where(owner[k] == holder, 1, 0)

            slot = lax.fori_loop(0, sources[w], count, 0)
            first = pl.multiple_of(slot * STRETCH, STRETCH)
            for step in range(parts):
                part = partner(me, step, size) if parts > 1 else 0
                base = part * width

                def fill(target, offset, base=base):
                    for start in range(0, width, LANES):
                        columns = pl.ds(pl.multiple_of(base + start, LANES), LANES)
                        target[pl.ds(offset + start, LANES), :] = product(key, value, first, columns)

                if w < SLOTS:
                    fill(sends[step], pl.multiple_of(place * width, LANES))
                else:

                    @pl.when(place < SLOTS)
                    def _(step=step, fill=fill):
                        fill(sends[step], pl.multiple_of(place * width, LANES))

                    @pl.when(place >= SLOTS)
                    def _(step=step, fill=fill):
                        fill(extra.at[step], 0)

    meta[MANY] = many
    group_count = filters.shape[0]
    for send in sends:
        rows = (send.shape[0] - SLOTS * width) * LANES // filters.shape[1]
        groups = pl.ds(0, rows)
        if 0 < rows < group_count:
            groups = pl.ds(pl.multiple_of(lax.axis_index("rep") * rows, rows), rows)
        for tile in range(filters.shape[1] // LANES if rows else 0):
            send[pl.ds(SLOTS * width + tile * rows, rows), :] = filters[
                groups, pl.ds(tile * LANES, LANES)
            ]


def gate(size, filter_rows, sources, owner, key_proj, value_proj, filters):
    row_count, channels = key_proj.shape
    slots = row_count // STRETCH
    parts = len(filter_rows)
    width = channels // parts
    operands = [
        pltpu.with_memory_space_constraint(operand, pltpu.HBM)
        for operand in (sources, owner, key_proj, value_proj, filters)
    ]
    *sends, extra, meta = pl.pallas_call(
        functools.partial(gate_kernel, size, parts),
        in_specs=[HBM_SPEC] * 5,
        out_specs=[VMEM_SPEC] * (parts + 1) + [SMEM_SPEC],
        out_shape=[
            jax.ShapeDtypeStruct((SLOTS * width + rows, LANES), jnp.bfloat16) for rows in filter_rows
        ]
        + [
            jax.ShapeDtypeStruct((parts, width, LANES), jnp.bfloat16),
            jax.ShapeDtypeStruct((WINDOWS + slots * WIN,), jnp.int32),
        ],
        scratch_shapes=[
            pltpu.SMEM(sources.shape, jnp.int32),
            pltpu.SMEM(owner.shape, jnp.int32),
            pltpu.VMEM(key_proj.shape, key_proj.dtype),
            pltpu.VMEM(value_proj.shape, value_proj.dtype),
            pltpu.VMEM(filters.shape, filters.dtype),
            pltpu.SemaphoreType.DMA((5,)),
        ],
        compiler_params=params(),
        name="gate",
    )(*operands)
    return sends, extra, meta


def merge_kernel(size, width, meta, *refs):
    received, extras, out = refs[:size], refs[size:-1], refs[-1]
    me = lax.axis_index("seq")

    for w in range(SENT):
        place = meta[PLACE + w]
        rows = pl.ds(pl.multiple_of(jnp.minimum(place, SLOTS - 1) * width, LANES), width)
        for block, step in zip(received, steps_of(size)):

            @pl.when(sender(me, step, size) == meta[w])
            def _(w=w, block=block, rows=rows):
                out[w] = block[rows, :]

    for w in range(SLOTS, SENT):
        for step, extra in enumerate(extras):

            @pl.when((sender(me, step, size) == meta[w]) & (meta[PLACE + w] >= SLOTS))
            def _(w=w, extra=extra):
                out[w] = extra[...]


def merge(size, width, meta, received, extras=()):
    return pl.pallas_call(
        functools.partial(merge_kernel, size, width),
        in_specs=[SMEM_SPEC] + [VMEM_SPEC] * (size + len(extras)),
        out_specs=VMEM_SPEC,
        out_shape=jax.ShapeDtypeStruct((SENT, width, LANES), received[0].dtype),
        compiler_params=params(),
        name="merge",
    )(meta, *received, *extras)


def pick_kernel(first, *refs):
    received, out = refs[:-1], refs[-1]
    for index, block in enumerate(received):
        out[index] = block[pl.ds(first, out.shape[1]), :]


def pick(first, received):
    rows = received[0].shape[0] - first
    return pl.pallas_call(
        functools.partial(pick_kernel, first),
        in_specs=[VMEM_SPEC] * len(received),
        out_specs=VMEM_SPEC,
        out_shape=jax.ShapeDtypeStruct((len(received), rows, LANES), received[0].dtype),
        compiler_params=params(),
        name="pick",
    )(*received)


def lag_tiles(size, first, filters):
    if len(filters) == 1:
        blocks = filters[0]
        group_count = blocks.shape[1] // first
        for shard in range(size):
            for tile in range(first):
                rows = pl.ds(tile * group_count, group_count)
                yield pl.ds(0, group_count), shard * first + tile, blocks[shard, rows, :]
        return
    own, far, mine, other = filters
    me, rep = lax.axis_index("seq"), lax.axis_index("rep")
    group_count = own.shape[0]
    tiles = own.shape[1] // LANES
    half = group_count // 2
    for tile in range(tiles):
        whole = pl.ds(0, group_count)
        yield whole, me * tiles + tile, own[:, pl.ds(tile * LANES, LANES)]
        rows = pl.ds(first + tile * group_count, group_count)
        yield whole, sender(me, 2, size) * tiles + tile, far[rows, :]
        for index, step in enumerate((1, size - 1)):
            number = sender(me, step, size) * tiles + tile
            for place, halves in ((rep, mine), (1 - rep, other)):
                groups = pl.ds(pl.multiple_of(place * half, half), half)
                yield groups, number, halves[index, pl.ds(tile * half, half), :]


def build_shifted(size, first, filters, reverse, shifted):
    group_count, padded = reverse.shape
    lag_count = padded - SPAN
    row = lax.broadcasted_iota(jnp.int32, (LANES, LANES), 0)
    column = lax.broadcasted_iota(jnp.int32, (LANES, LANES), 1)
    flip = jnp.where(row + column == LANES - 1, 1.0, 0.0).astype(jnp.bfloat16)
    for groups, number, values in lag_tiles(size, first, filters):
        start = lag_count - LANES - number * LANES
        if not isinstance(start, int):
            start = pl.multiple_of(start, LANES)
        reverse[groups, pl.ds(start, LANES)] = jnp.dot(
            values, flip, preferred_element_type=jnp.float32
        )
    reverse[:, pl.ds(lag_count, SPAN)] = jnp.zeros((group_count, SPAN), jnp.float32)
    inside = (
        lax.broadcasted_iota(jnp.int32, (GROUP_CH, LANES), 1)
        > lax.broadcasted_iota(jnp.int32, (GROUP_CH, LANES), 0)
    )

    @pl.loop(0, group_count // BLOCKS)
    def _(block):
        tile_rows = pl.ds(pl.multiple_of(block * BLOCKS, BLOCKS), BLOCKS)
        before = [jnp.zeros((GROUP_CH, LANES), jnp.float32)] * BLOCKS
        for start in range(0, padded, LANES):
            tile = reverse[tile_rows, pl.ds(start, LANES)]
            for g in range(BLOCKS):
                spread = jnp.broadcast_to(tile[g : g + 1, :], (GROUP_CH, LANES))
                rolled = pltpu.roll(spread, 1, 1, stride=1, stride_axis=0)
                shifted[block * BLOCKS + g, :, pl.ds(start, LANES)] = jnp.where(
                    inside, rolled, before[g]
                ).astype(jnp.bfloat16)
                before[g] = rolled


def spread_rows(tile, spans, base):
    lane = lax.broadcasted_iota(jnp.int16, tile.shape, 1)
    zero = jnp.zeros(tile.shape, tile.dtype)
    for i1 in range(BLOCKS):
        shift = GROUP_CH * i1
        if i1 == 0:
            low, high = zero, tile
        else:
            moved = pltpu.roll(tile, LANES - shift, 1)
            early = lane < LANES - shift
            low, high = jnp.where(early, zero, moved), jnp.where(early, moved, zero)
        rows = pl.ds(shift, GROUP_CH)
        for g in range(BLOCKS):
            part = slice(g * GROUP_CH, (g + 1) * GROUP_CH)
            spans[g, rows, pl.ds(base, LANES)] = low[part]
            spans[g, rows, pl.ds(base + LANES, LANES)] = high[part]


def window(meta, shifted, group, slot, w):
    start = pl.multiple_of(meta[WINDOWS + slot * WIN + w], STRETCH)
    return shifted[group, :, pl.ds(start, SPAN)]


def filter_rows(meta, shifted, group, slots):
    return jnp.concatenate(
        [
            jnp.concatenate([window(meta, shifted, group, slot, w) for w in range(SENT)], axis=1)
            for slot in range(slots)
        ],
        axis=0,
    )


def rows_of(results, block):
    part = slice(block * GROUP_CH, (block + 1) * GROUP_CH)
    return jnp.concatenate([result[part] for result in results], axis=0).T


def last_rows_kernel(key, value, out):
    for start in range(0, out.shape[0], LANES):
        out[pl.ds(start, LANES), :] = product(key, value, 0, pl.ds(start, LANES))


def last_rows(key_proj, value_proj):
    row_count, channels = key_proj.shape
    block = pl.BlockSpec((STRETCH, channels), lambda i: (row_count // STRETCH - 1, 0))
    operands = [pltpu.with_memory_space_constraint(x, pltpu.HBM) for x in (key_proj, value_proj)]
    return pl.pallas_call(
        last_rows_kernel,
        grid=(1,),
        in_specs=[block, block],
        out_specs=pl.BlockSpec((channels, STRETCH), lambda i: (0, 0)),
        out_shape=jax.ShapeDtypeStruct((channels, STRETCH), jnp.bfloat16),
        compiler_params=params(),
        name="last_rows",
    )(*operands)


def last_term(slots, meta, last, shifted, term, spans):
    for start in range(0, last.shape[0], LANES):
        held = spans.at[start // LANES % 2]
        spread_rows(last[pl.ds(start, LANES), :], held, 0)
        results = [
            lax.dot_general(
                held[g],
                window(meta, shifted, start // GROUP_CH + g, slots - 1, SENT),
                NT,
                preferred_element_type=jnp.float32,
            )
            for g in range(BLOCKS)
        ]
        for m in range(BLOCKS):
            term[pl.ds(m * GROUP_CH, GROUP_CH), pl.ds(start, LANES)] = rows_of(results, m)


def spread_part(pieces, start, spans):
    for w in range(SENT):
        spread_rows(pieces[w, pl.ds(start, LANES), :], spans, w * SPAN)


def conv_part(filter_rows_of, base, start, term, query, out, result, spans, sem):
    slots = query.shape[0] // STRETCH
    columns = pl.ds(pl.multiple_of(base + start, LANES), LANES)
    results = [
        lax.dot_general(
            spans[g],
            filter_rows_of(start // GROUP_CH + g),
            NT,
            preferred_element_type=jnp.float32,
        )
        for g in range(BLOCKS)
    ]
    for m in range(BLOCKS):
        rows = rows_of(results, m)
        for slot in range(slots):
            place = pl.ds(slot * STRETCH + m * GROUP_CH, GROUP_CH)
            tile = rows[slot * GROUP_CH : (slot + 1) * GROUP_CH]
            if slot == slots - 1:
                tile = tile + term[pl.ds(m * GROUP_CH, GROUP_CH), columns]
            gates = query[place, columns].astype(jnp.float32)
            result[place, :] = (gates * tile).astype(jnp.bfloat16)
    store = pltpu.make_async_copy(result, out.at[:, columns], sem)
    store.start()
    return store


def part_base(step, size, width):
    me = lax.axis_index("seq")
    return pl.multiple_of(sender(me, step, size) * width, width)


def scratch(count, row_count):
    return [
        pltpu.VMEM((count, row_count, LANES), jnp.bfloat16),
        pltpu.VMEM((count, BLOCKS, LANES, SENT * SPAN), jnp.bfloat16),
        pltpu.SemaphoreType.DMA((count + 1,)),
    ]


def open_kernel(size, first, meta_in, last, pieces, query, *refs):
    filters = refs[:-9]
    shifted, term, out, reverse, meta, last_spans, result, spans, sems = refs[-9:]
    slots = query.shape[0] // STRETCH
    width = pieces.shape[1]
    scalars = pltpu.make_async_copy(meta_in, meta, sems.at[width // LANES])
    scalars.start()
    build_shifted(size, first, filters, reverse, shifted)
    scalars.wait()
    last_term(slots, meta, last, shifted, term, last_spans)
    base = part_base(0, out.shape[1] // width, width)
    stores = []
    for index, start in enumerate(range(0, width, LANES)):
        spread_part(pieces, start, spans.at[index])
        stores.append(
            conv_part(
                lambda group: filter_rows(meta, shifted, base // GROUP_CH + group, slots),
                base,
                start,
                term,
                query,
                out,
                result.at[index],
                spans.at[index],
                sems.at[index],
            )
        )
    for store in stores:
        store.wait()


def open_conv(size, first, meta, last, pieces, query_proj, group_count, lag_count, filters):
    row_count, channels = query_proj.shape
    padded = lag_count + SPAN
    return pl.pallas_call(
        functools.partial(open_kernel, size, first),
        in_specs=[ANY_SPEC] + [VMEM_SPEC] * (3 + len(filters)),
        out_specs=[VMEM_SPEC, VMEM_SPEC, HBM_SPEC],
        out_shape=[
            jax.ShapeDtypeStruct((group_count, GROUP_CH, padded), jnp.bfloat16),
            jax.ShapeDtypeStruct((STRETCH, channels), jnp.float32),
            jax.ShapeDtypeStruct((row_count, channels), jnp.bfloat16),
        ],
        scratch_shapes=[
            pltpu.VMEM((group_count, padded), jnp.float32),
            pltpu.SMEM(meta.shape, jnp.int32),
            pltpu.VMEM((2, BLOCKS, LANES, SPAN), jnp.bfloat16),
            *scratch(pieces.shape[1] // LANES, row_count),
        ],
        compiler_params=params(),
        name="open_conv",
    )(meta, last, pieces, query_proj, *filters)


def near_kernel(size, steps, next_step, meta_in, shifted, term, query, before, *refs):
    parts = refs[: len(steps)]
    out, ready, meta, result, spans, sems = refs[len(steps) :]
    slots = query.shape[0] // STRETCH
    width = parts[0].shape[1]
    places = [(index, start) for index in range(len(steps)) for start in range(0, width, LANES)]
    scalars = pltpu.make_async_copy(meta_in, meta, sems.at[len(places)])
    scalars.start()
    for number, (index, start) in enumerate(places[: len(places) // 2]):
        spread_part(parts[index], start, spans.at[number])
    scalars.wait()
    stores = []
    for number, (index, start) in enumerate(places):
        if number >= len(places) // 2:
            spread_part(parts[index], start, spans.at[number])
        base = part_base(steps[index], size, width)
        stores.append(
            conv_part(
                lambda group, base=base: filter_rows(meta, shifted, base // GROUP_CH + group, slots),
                base,
                start,
                term,
                query,
                out,
                result.at[number],
                spans.at[number],
                sems.at[number],
            )
        )
    base = part_base(next_step, size, width)
    for group in range(width // GROUP_CH):
        ready[group] = filter_rows(meta, shifted, base // GROUP_CH + group, slots)
    for store in stores:
        store.wait()


def near_conv(size, steps, next_step, meta, parts, shifted, term, query_proj, before):
    row_count, channels = query_proj.shape
    width = channels // size
    slots = row_count // STRETCH
    return pl.pallas_call(
        functools.partial(near_kernel, size, steps, next_step),
        in_specs=[ANY_SPEC] + [VMEM_SPEC] * 3 + [HBM_SPEC] + [VMEM_SPEC] * len(parts),
        out_specs=[HBM_SPEC, VMEM_SPEC],
        out_shape=[
            jax.ShapeDtypeStruct((row_count, channels), jnp.bfloat16),
            jax.ShapeDtypeStruct((width // GROUP_CH, slots * GROUP_CH, SENT * SPAN), jnp.bfloat16),
        ],
        input_output_aliases={4: 0},
        scratch_shapes=[
            pltpu.SMEM(meta.shape, jnp.int32),
            *scratch(len(parts) * width // LANES, row_count),
        ],
        compiler_params=params(),
        name="near_conv",
    )(meta, shifted, term, query_proj, before, *parts)


def far_kernel(size, step, pieces, ready, term, query, before, out, result, spans, sems):
    width = pieces.shape[1]
    base = part_base(step, size, width)
    stores = []
    for index, start in enumerate(range(0, width, LANES)):
        spread_part(pieces, start, spans.at[index])
        stores.append(
            conv_part(
                lambda group: ready[group],
                base,
                start,
                term,
                query,
                out,
                result.at[index],
                spans.at[index],
                sems.at[index],
            )
        )
    for store in stores:
        store.wait()


def far_conv(size, step, pieces, ready, term, query_proj, before):
    row_count, channels = query_proj.shape
    return pl.pallas_call(
        functools.partial(far_kernel, size, step),
        in_specs=[VMEM_SPEC] * 4 + [HBM_SPEC],
        out_specs=HBM_SPEC,
        out_shape=jax.ShapeDtypeStruct((row_count, channels), jnp.bfloat16),
        input_output_aliases={4: 0},
        scratch_shapes=scratch(pieces.shape[1] // LANES, row_count),
        compiler_params=params(),
        name="far_conv",
    )(pieces, ready, term, query_proj, before)


def shards(size, reps, key_proj, value_proj, query_proj, filters, sources, owner):
    row_count, channels = key_proj.shape
    group_count, part = filters.shape
    lag_count = size * part
    tiles = part // LANES
    by_parts = (size, reps) == (4, 2) and channels % (size * LANES) == 0
    half = group_count // 2 * tiles
    filter_rows = [0, half, 2 * half, half] if by_parts else [2 * half]
    parts = len(filter_rows)
    width = channels // parts
    sends, extra, meta = gate(size, filter_rows, sources, owner, key_proj, value_proj, filters)
    last = last_rows(key_proj, value_proj)
    first = SLOTS * width
    if not by_parts:
        blocks = lax.all_gather(sends[0][first:], "seq")
        held = jnp.concatenate([sends[0][:first].reshape(SLOTS, width, LANES), extra])
        mine = (meta[:SENT] == lax.axis_index("seq"))[:, None, None]
        pieces = lax.psum(jnp.where(mine, held[meta[PLACE:MANY]], jnp.zeros_like(held)), "seq")
        return open_conv(
            size, tiles, meta, last, pieces, query_proj, group_count, lag_count, [blocks]
        )[2]

    def shift(value, step):
        return lax.ppermute(value, "seq", [(z, (z + step) % size) for z in range(size)])

    up, down, far = (shift(sends[step], step) for step in (1, size - 1, 2))
    mine = pick(first, [up, down])
    other = lax.ppermute(mine, "rep", [(0, 1), (1, 0)])
    last, other, far = lax.optimization_barrier((last, other, far))
    received = [sends[0], up, down, far]

    def merge_more(meta, received, extra):
        more = [extra[0]] + [shift(extra[step], step) for step in range(1, size)]
        return merge(size, width, meta, received, more)

    def merge_plain(meta, received, extra):
        return merge(size, width, meta, received)

    merged = lax.cond(meta[MANY] > 0, merge_more, merge_plain, meta, received, extra)
    up, down, far_part = shift(merged, 1), shift(merged, size - 1), shift(merged, 2)
    shifted, term, out = open_conv(
        size,
        first,
        meta,
        last,
        merged,
        query_proj,
        group_count,
        lag_count,
        [filters, far, mine, other],
    )
    out, ready = near_conv(
        size, (1, size - 1), 2, meta, [up, down], shifted, term, query_proj, out
    )
    return far_conv(size, 2, far_part, ready, term, query_proj, out)


def solution(mesh):
    return jax.shard_map(
        functools.partial(shards, mesh.shape["seq"], mesh.shape["rep"]),
        mesh=mesh,
        in_specs=(
            P(("rep", "seq"), "ch"),
            P(("rep", "seq"), "ch"),
            P(("rep", "seq"), "ch"),
            P("ch", "seq"),
            P("rep"),
            P("rep"),
        ),
        out_specs=P(("rep", "seq"), "ch"),
        check_vma=False,
    )
```

```python
import functools

import jax
import jax.numpy as jnp
from jax import lax
from jax.experimental import pallas as pl
from jax.experimental.pallas import tpu as pltpu
from jax.sharding import PartitionSpec as P

GROUP_CH = 16
STRETCH = 128
WIN = 4
SENT = WIN - 1
LANES = 128
BLOCKS = LANES // GROUP_CH
SPAN = 2 * STRETCH
VMEM_LIMIT = 16 * 1024 * 1024

SMEM_SPEC = pl.BlockSpec(memory_space=pltpu.SMEM)
ANY_SPEC = pl.BlockSpec(memory_space=pl.ANY)
HBM_SPEC = pl.BlockSpec(memory_space=pltpu.HBM)
VMEM_SPEC = pl.BlockSpec(memory_space=pltpu.VMEM)
NT = (((1,), (1,)), ((), ()))


def params():
    return pltpu.CompilerParams(vmem_limit_bytes=VMEM_LIMIT)


def steps_of(size):
    return sorted(range(size), key=lambda step: (min(step, size - step), step))


def partner(me, step, size):
    return lax.rem(me + step, size)


def sender(me, step, size):
    return lax.rem(me + size - step, size)


PLACE = SENT
MANY = 2 * SENT
WINDOWS = MANY + 1
SLOTS = 2


def product(key, value, start, columns):
    rows = pl.ds(start, STRETCH)
    rows_k = key[rows, columns].astype(jnp.float32)
    rows_v = value[rows, columns].astype(jnp.float32)
    return (rows_k * rows_v).astype(jnp.bfloat16).T


def gate_kernel(size, parts, sources_in, owner_in, key_in, value_in, filters_in, *refs):
    sends = refs[:parts]
    extra, meta, sources, owner, key, value, filters, sems = refs[parts:]
    stretch_count = owner.shape[0]
    channels = key.shape[1]
    width = channels // parts
    me = lax.axis_index("seq")
    copies = [
        pltpu.make_async_copy(sources_in, sources, sems.at[0]),
        pltpu.make_async_copy(owner_in, owner, sems.at[1]),
        pltpu.make_async_copy(key_in, key, sems.at[2]),
        pltpu.make_async_copy(value_in, value, sems.at[3]),
        pltpu.make_async_copy(filters_in, filters, sems.at[4]),
    ]
    for copy in copies:
        copy.start()

    for copy in copies[:2]:
        copy.wait()

    def target(k, slot):
        mine = owner[k] == me

        @pl.when(mine)
        def _():
            for w in range(WIN):
                lag_block = jnp.maximum(k - sources[w], -1)
                meta[WINDOWS + slot * WIN + w] = (stretch_count - 1 - lag_block) * STRETCH

        return slot + jnp.where(mine, 1, 0)

    lax.fori_loop(0, stretch_count, target, 0)
    for copy in copies[2:]:
        copy.wait()
    holders = [owner[sources[w]] for w in range(SENT)]
    many = 0
    for w, holder in enumerate(holders):
        place = sum([jnp.where(other == holder, 1, 0) for other in holders[:w]], 0)
        meta[w] = holder
        meta[PLACE + w] = place
        many = many + jnp.where(place >= SLOTS, 1, 0)

        @pl.when(holder == me)
        def _(w=w, holder=holder, place=place):
            def count(k, total):
                return total + jnp.where(owner[k] == holder, 1, 0)

            slot = lax.fori_loop(0, sources[w], count, 0)
            first = pl.multiple_of(slot * STRETCH, STRETCH)
            for step in range(parts):
                part = partner(me, step, size) if parts > 1 else 0
                base = part * width

                def fill(target, offset, base=base):
                    for start in range(0, width, LANES):
                        columns = pl.ds(pl.multiple_of(base + start, LANES), LANES)
                        target[pl.ds(offset + start, LANES), :] = product(key, value, first, columns)

                if w < SLOTS:
                    fill(sends[step], pl.multiple_of(place * width, LANES))
                else:

                    @pl.when(place < SLOTS)
                    def _(step=step, fill=fill):
                        fill(sends[step], pl.multiple_of(place * width, LANES))

                    @pl.when(place >= SLOTS)
                    def _(step=step, fill=fill):
                        fill(extra.at[step], 0)

    meta[MANY] = many
    group_count = filters.shape[0]
    for send in sends:
        rows = (send.shape[0] - SLOTS * width) * LANES // filters.shape[1]
        groups = pl.ds(0, rows)
        if 0 < rows < group_count:
            groups = pl.ds(pl.multiple_of(lax.axis_index("rep") * rows, rows), rows)
        for tile in range(filters.shape[1] // LANES if rows else 0):
            send[pl.ds(SLOTS * width + tile * rows, rows), :] = filters[
                groups, pl.ds(tile * LANES, LANES)
            ]


def gate(size, filter_rows, sources, owner, key_proj, value_proj, filters):
    row_count, channels = key_proj.shape
    slots = row_count // STRETCH
    parts = len(filter_rows)
    width = channels // parts
    operands = [
        pltpu.with_memory_space_constraint(operand, pltpu.HBM)
        for operand in (sources, owner, key_proj, value_proj, filters)
    ]
    *sends, extra, meta = pl.pallas_call(
        functools.partial(gate_kernel, size, parts),
        in_specs=[HBM_SPEC] * 5,
        out_specs=[VMEM_SPEC] * (parts + 1) + [SMEM_SPEC],
        out_shape=[
            jax.ShapeDtypeStruct((SLOTS * width + rows, LANES), jnp.bfloat16) for rows in filter_rows
        ]
        + [
            jax.ShapeDtypeStruct((parts, width, LANES), jnp.bfloat16),
            jax.ShapeDtypeStruct((WINDOWS + slots * WIN,), jnp.int32),
        ],
        scratch_shapes=[
            pltpu.SMEM(sources.shape, jnp.int32),
            pltpu.SMEM(owner.shape, jnp.int32),
            pltpu.VMEM(key_proj.shape, key_proj.dtype),
            pltpu.VMEM(value_proj.shape, value_proj.dtype),
            pltpu.VMEM(filters.shape, filters.dtype),
            pltpu.SemaphoreType.DMA((5,)),
        ],
        compiler_params=params(),
        name="gate",
    )(*operands)
    return sends, extra, meta


def merge_kernel(size, width, meta, *refs):
    received, extras, out = refs[:size], refs[size:-1], refs[-1]
    me = lax.axis_index("seq")

    for w in range(SENT):
        place = meta[PLACE + w]
        rows = pl.ds(pl.multiple_of(jnp.minimum(place, SLOTS - 1) * width, LANES), width)
        for block, step in zip(received, steps_of(size)):

            @pl.when(sender(me, step, size) == meta[w])
            def _(w=w, block=block, rows=rows):
                out[w] = block[rows, :]

    for w in range(SLOTS, SENT):
        for step, extra in enumerate(extras):

            @pl.when((sender(me, step, size) == meta[w]) & (meta[PLACE + w] >= SLOTS))
            def _(w=w, extra=extra):
                out[w] = extra[...]


def merge(size, width, meta, received, extras=()):
    return pl.pallas_call(
        functools.partial(merge_kernel, size, width),
        in_specs=[SMEM_SPEC] + [VMEM_SPEC] * (size + len(extras)),
        out_specs=VMEM_SPEC,
        out_shape=jax.ShapeDtypeStruct((SENT, width, LANES), received[0].dtype),
        compiler_params=params(),
        name="merge",
    )(meta, *received, *extras)


def pick_kernel(first, *refs):
    received, out = refs[:-1], refs[-1]
    for index, block in enumerate(received):
        out[index] = block[pl.ds(first, out.shape[1]), :]


def pick(first, received):
    rows = received[0].shape[0] - first
    return pl.pallas_call(
        functools.partial(pick_kernel, first),
        in_specs=[VMEM_SPEC] * len(received),
        out_specs=VMEM_SPEC,
        out_shape=jax.ShapeDtypeStruct((len(received), rows, LANES), received[0].dtype),
        compiler_params=params(),
        name="pick",
    )(*received)


def lag_tiles(size, first, filters):
    if len(filters) == 1:
        blocks = filters[0]
        group_count = blocks.shape[1] // first
        for shard in range(size):
            for tile in range(first):
                rows = pl.ds(tile * group_count, group_count)
                yield pl.ds(0, group_count), shard * first + tile, blocks[shard, rows, :]
        return
    own, far, mine, other = filters
    me, rep = lax.axis_index("seq"), lax.axis_index("rep")
    group_count = own.shape[0]
    tiles = own.shape[1] // LANES
    half = group_count // 2
    for tile in range(tiles):
        whole = pl.ds(0, group_count)
        yield whole, me * tiles + tile, own[:, pl.ds(tile * LANES, LANES)]
        yield whole, sender(me, 2, size) * tiles + tile, far[:, pl.ds(tile * LANES, LANES)]
        for index, step in enumerate((1, size - 1)):
            number = sender(me, step, size) * tiles + tile
            for place, halves in ((rep, mine), (1 - rep, other)):
                groups = pl.ds(pl.multiple_of(place * half, half), half)
                yield groups, number, halves[index, pl.ds(tile * half, half), :]


def build_shifted(size, first, filters, reverse, shifted):
    group_count, padded = reverse.shape
    lag_count = padded - SPAN
    row = lax.broadcasted_iota(jnp.int32, (LANES, LANES), 0)
    column = lax.broadcasted_iota(jnp.int32, (LANES, LANES), 1)
    flip = jnp.where(row + column == LANES - 1, 1.0, 0.0).astype(jnp.bfloat16)
    for groups, number, values in lag_tiles(size, first, filters):
        start = lag_count - LANES - number * LANES
        if not isinstance(start, int):
            start = pl.multiple_of(start, LANES)
        reverse[groups, pl.ds(start, LANES)] = jnp.dot(
            values, flip, preferred_element_type=jnp.float32
        )
    reverse[:, pl.ds(lag_count, SPAN)] = jnp.zeros((group_count, SPAN), jnp.float32)
    inside = (
        lax.broadcasted_iota(jnp.int32, (GROUP_CH, LANES), 1)
        > lax.broadcasted_iota(jnp.int32, (GROUP_CH, LANES), 0)
    )

    @pl.loop(0, group_count // BLOCKS)
    def _(block):
        tile_rows = pl.ds(pl.multiple_of(block * BLOCKS, BLOCKS), BLOCKS)
        before = [jnp.zeros((GROUP_CH, LANES), jnp.float32)] * BLOCKS
        for start in range(0, padded, LANES):
            tile = reverse[tile_rows, pl.ds(start, LANES)]
            for g in range(BLOCKS):
                spread = jnp.broadcast_to(tile[g : g + 1, :], (GROUP_CH, LANES))
                rolled = pltpu.roll(spread, 1, 1, stride=1, stride_axis=0)
                shifted[block * BLOCKS + g, :, pl.ds(start, LANES)] = jnp.where(
                    inside, rolled, before[g]
                ).astype(jnp.bfloat16)
                before[g] = rolled


def spread_rows(tile, spans, base):
    lane = lax.broadcasted_iota(jnp.int16, tile.shape, 1)
    zero = jnp.zeros(tile.shape, tile.dtype)
    for i1 in range(BLOCKS):
        shift = GROUP_CH * i1
        if i1 == 0:
            low, high = zero, tile
        else:
            moved = pltpu.roll(tile, LANES - shift, 1)
            early = lane < LANES - shift
            low, high = jnp.where(early, zero, moved), jnp.where(early, moved, zero)
        rows = pl.ds(shift, GROUP_CH)
        for g in range(BLOCKS):
            part = slice(g * GROUP_CH, (g + 1) * GROUP_CH)
            spans[g, rows, pl.ds(base, LANES)] = low[part]
            spans[g, rows, pl.ds(base + LANES, LANES)] = high[part]


def window(meta, shifted, group, slot, w):
    start = pl.multiple_of(meta[WINDOWS + slot * WIN + w], STRETCH)
    return shifted[group, :, pl.ds(start, SPAN)]


def filter_rows(meta, shifted, group, slots):
    return jnp.concatenate(
        [
            jnp.concatenate([window(meta, shifted, group, slot, w) for w in range(SENT)], axis=1)
            for slot in range(slots)
        ],
        axis=0,
    )


def rows_of(results, block):
    part = slice(block * GROUP_CH, (block + 1) * GROUP_CH)
    return jnp.concatenate([result[part] for result in results], axis=0).T


def last_rows_kernel(key, value, out):
    for start in range(0, out.shape[0], LANES):
        out[pl.ds(start, LANES), :] = product(key, value, 0, pl.ds(start, LANES))


def last_rows(key_proj, value_proj):
    row_count, channels = key_proj.shape
    block = pl.BlockSpec((STRETCH, channels), lambda i: (row_count // STRETCH - 1, 0))
    operands = [pltpu.with_memory_space_constraint(x, pltpu.HBM) for x in (key_proj, value_proj)]
    return pl.pallas_call(
        last_rows_kernel,
        grid=(1,),
        in_specs=[block, block],
        out_specs=pl.BlockSpec((channels, STRETCH), lambda i: (0, 0)),
        out_shape=jax.ShapeDtypeStruct((channels, STRETCH), jnp.bfloat16),
        compiler_params=params(),
        name="last_rows",
    )(*operands)


def last_term(slots, meta, last, shifted, term, spans):
    for start in range(0, last.shape[0], LANES):
        held = spans.at[start // LANES % 2]
        spread_rows(last[pl.ds(start, LANES), :], held, 0)
        results = [
            lax.dot_general(
                held[g],
                window(meta, shifted, start // GROUP_CH + g, slots - 1, SENT),
                NT,
                preferred_element_type=jnp.float32,
            )
            for g in range(BLOCKS)
        ]
        for m in range(BLOCKS):
            term[pl.ds(m * GROUP_CH, GROUP_CH), pl.ds(start, LANES)] = rows_of(results, m)


def spread_part(pieces, start, spans):
    for w in range(SENT):
        spread_rows(pieces[w, pl.ds(start, LANES), :], spans, w * SPAN)


def conv_part(filter_rows_of, base, start, term, query, out, result, spans, sem):
    slots = query.shape[0] // STRETCH
    columns = pl.ds(pl.multiple_of(base + start, LANES), LANES)
    results = [
        lax.dot_general(
            spans[g],
            filter_rows_of(start // GROUP_CH + g),
            NT,
            preferred_element_type=jnp.float32,
        )
        for g in range(BLOCKS)
    ]
    for m in range(BLOCKS):
        rows = rows_of(results, m)
        for slot in range(slots):
            place = pl.ds(slot * STRETCH + m * GROUP_CH, GROUP_CH)
            tile = rows[slot * GROUP_CH : (slot + 1) * GROUP_CH]
            if slot == slots - 1:
                tile = tile + term[pl.ds(m * GROUP_CH, GROUP_CH), columns]
            gates = query[place, columns].astype(jnp.float32)
            result[place, :] = (gates * tile).astype(jnp.bfloat16)
    store = pltpu.make_async_copy(result, out.at[:, columns], sem)
    store.start()
    return store


def part_base(step, size, width):
    me = lax.axis_index("seq")
    return pl.multiple_of(sender(me, step, size) * width, width)


def scratch(count, row_count):
    return [
        pltpu.VMEM((count, row_count, LANES), jnp.bfloat16),
        pltpu.VMEM((count, BLOCKS, LANES, SENT * SPAN), jnp.bfloat16),
        pltpu.SemaphoreType.DMA((count + 1,)),
    ]


def open_kernel(size, first, meta_in, last, pieces, query, *refs):
    filters = refs[:-9]
    shifted, term, out, reverse, meta, last_spans, result, spans, sems = refs[-9:]
    slots = query.shape[0] // STRETCH
    width = pieces.shape[1]
    scalars = pltpu.make_async_copy(meta_in, meta, sems.at[width // LANES])
    scalars.start()
    build_shifted(size, first, filters, reverse, shifted)
    scalars.wait()
    last_term(slots, meta, last, shifted, term, last_spans)
    base = part_base(0, out.shape[1] // width, width)
    stores = []
    for index, start in enumerate(range(0, width, LANES)):
        spread_part(pieces, start, spans.at[index])
        stores.append(
            conv_part(
                lambda group: filter_rows(meta, shifted, base // GROUP_CH + group, slots),
                base,
                start,
                term,
                query,
                out,
                result.at[index],
                spans.at[index],
                sems.at[index],
            )
        )
    for store in stores:
        store.wait()


def open_conv(size, first, meta, last, pieces, query_proj, group_count, lag_count, filters):
    row_count, channels = query_proj.shape
    padded = lag_count + SPAN
    return pl.pallas_call(
        functools.partial(open_kernel, size, first),
        in_specs=[ANY_SPEC] + [VMEM_SPEC] * (3 + len(filters)),
        out_specs=[VMEM_SPEC, VMEM_SPEC, HBM_SPEC],
        out_shape=[
            jax.ShapeDtypeStruct((group_count, GROUP_CH, padded), jnp.bfloat16),
            jax.ShapeDtypeStruct((STRETCH, channels), jnp.float32),
            jax.ShapeDtypeStruct((row_count, channels), jnp.bfloat16),
        ],
        scratch_shapes=[
            pltpu.VMEM((group_count, padded), jnp.float32),
            pltpu.SMEM(meta.shape, jnp.int32),
            pltpu.VMEM((2, BLOCKS, LANES, SPAN), jnp.bfloat16),
            *scratch(pieces.shape[1] // LANES, row_count),
        ],
        compiler_params=params(),
        name="open_conv",
    )(meta, last, pieces, query_proj, *filters)


def near_kernel(size, steps, next_step, meta_in, shifted, term, query, before, *refs):
    parts = refs[: len(steps)]
    out, ready, meta, result, spans, sems = refs[len(steps) :]
    slots = query.shape[0] // STRETCH
    width = parts[0].shape[1]
    places = [(index, start) for index in range(len(steps)) for start in range(0, width, LANES)]
    scalars = pltpu.make_async_copy(meta_in, meta, sems.at[len(places)])
    scalars.start()
    for number, (index, start) in enumerate(places[: len(places) // 2]):
        spread_part(parts[index], start, spans.at[number])
    scalars.wait()
    stores = []
    for number, (index, start) in enumerate(places):
        if number >= len(places) // 2:
            spread_part(parts[index], start, spans.at[number])
        base = part_base(steps[index], size, width)
        stores.append(
            conv_part(
                lambda group, base=base: filter_rows(meta, shifted, base // GROUP_CH + group, slots),
                base,
                start,
                term,
                query,
                out,
                result.at[number],
                spans.at[number],
                sems.at[number],
            )
        )
    base = part_base(next_step, size, width)
    for group in range(width // GROUP_CH):
        ready[group] = filter_rows(meta, shifted, base // GROUP_CH + group, slots)
    for store in stores:
        store.wait()


def near_conv(size, steps, next_step, meta, parts, shifted, term, query_proj, before):
    row_count, channels = query_proj.shape
    width = channels // size
    slots = row_count // STRETCH
    return pl.pallas_call(
        functools.partial(near_kernel, size, steps, next_step),
        in_specs=[ANY_SPEC] + [VMEM_SPEC] * 3 + [HBM_SPEC] + [VMEM_SPEC] * len(parts),
        out_specs=[HBM_SPEC, VMEM_SPEC],
        out_shape=[
            jax.ShapeDtypeStruct((row_count, channels), jnp.bfloat16),
            jax.ShapeDtypeStruct((width // GROUP_CH, slots * GROUP_CH, SENT * SPAN), jnp.bfloat16),
        ],
        input_output_aliases={4: 0},
        scratch_shapes=[
            pltpu.SMEM(meta.shape, jnp.int32),
            *scratch(len(parts) * width // LANES, row_count),
        ],
        compiler_params=params(),
        name="near_conv",
    )(meta, shifted, term, query_proj, before, *parts)


def far_kernel(size, step, pieces, ready, term, query, before, out, result, spans, sems):
    width = pieces.shape[1]
    base = part_base(step, size, width)
    stores = []
    for index, start in enumerate(range(0, width, LANES)):
        spread_part(pieces, start, spans.at[index])
        stores.append(
            conv_part(
                lambda group: ready[group],
                base,
                start,
                term,
                query,
                out,
                result.at[index],
                spans.at[index],
                sems.at[index],
            )
        )
    for store in stores:
        store.wait()


def far_conv(size, step, pieces, ready, term, query_proj, before):
    row_count, channels = query_proj.shape
    return pl.pallas_call(
        functools.partial(far_kernel, size, step),
        in_specs=[VMEM_SPEC] * 4 + [HBM_SPEC],
        out_specs=HBM_SPEC,
        out_shape=jax.ShapeDtypeStruct((row_count, channels), jnp.bfloat16),
        input_output_aliases={4: 0},
        scratch_shapes=scratch(pieces.shape[1] // LANES, row_count),
        compiler_params=params(),
        name="far_conv",
    )(pieces, ready, term, query_proj, before)


def shards(size, reps, key_proj, value_proj, query_proj, filters, sources, owner):
    row_count, channels = key_proj.shape
    group_count, part = filters.shape
    lag_count = size * part
    tiles = part // LANES
    by_parts = (size, reps) == (4, 2) and channels % (size * LANES) == 0
    half = group_count // 2 * tiles
    filter_rows = [0, half, 0, half] if by_parts else [2 * half]
    parts = len(filter_rows)
    width = channels // parts
    sends, extra, meta = gate(size, filter_rows, sources, owner, key_proj, value_proj, filters)
    last = last_rows(key_proj, value_proj)
    first = SLOTS * width
    if not by_parts:
        blocks = lax.all_gather(sends[0][first:], "seq")
        held = jnp.concatenate([sends[0][:first].reshape(SLOTS, width, LANES), extra])
        mine = (meta[:SENT] == lax.axis_index("seq"))[:, None, None]
        pieces = lax.psum(jnp.where(mine, held[meta[PLACE:MANY]], jnp.zeros_like(held)), "seq")
        return open_conv(
            size, tiles, meta, last, pieces, query_proj, group_count, lag_count, [blocks]
        )[2]

    def shift(value, step):
        return lax.ppermute(value, "seq", [(z, (z + step) % size) for z in range(size)])

    far_filters = shift(filters, 2)
    sends, far_filters = lax.optimization_barrier((sends, far_filters))
    up, down, far = (shift(sends[step], step) for step in (1, size - 1, 2))
    mine = pick(first, [up, down])
    other = lax.ppermute(mine, "rep", [(0, 1), (1, 0)])
    last, other, far = lax.optimization_barrier((last, other, far))
    received = [sends[0], up, down, far]

    def merge_more(meta, received, extra):
        more = [extra[0]] + [shift(extra[step], step) for step in range(1, size)]
        return merge(size, width, meta, received, more)

    def merge_plain(meta, received, extra):
        return merge(size, width, meta, received)

    merged = lax.cond(meta[MANY] > 0, merge_more, merge_plain, meta, received, extra)
    up, down, far_part = shift(merged, 1), shift(merged, size - 1), shift(merged, 2)
    shifted, term, out = open_conv(
        size,
        first,
        meta,
        last,
        merged,
        query_proj,
        group_count,
        lag_count,
        [filters, far_filters, mine, other],
    )
    out, ready = near_conv(
        size, (1, size - 1), 2, meta, [up, down], shifted, term, query_proj, out
    )
    return far_conv(size, 2, far_part, ready, term, query_proj, out)


def solution(mesh):
    return jax.shard_map(
        functools.partial(shards, mesh.shape["seq"], mesh.shape["rep"]),
        mesh=mesh,
        in_specs=(
            P(("rep", "seq"), "ch"),
            P(("rep", "seq"), "ch"),
            P(("rep", "seq"), "ch"),
            P("ch", "seq"),
            P("rep"),
            P("rep"),
        ),
        out_specs=P(("rep", "seq"), "ch"),
        check_vma=False,
    )
```

```python
import functools

import jax
import jax.numpy as jnp
from jax import lax
from jax.experimental import pallas as pl
from jax.experimental.pallas import tpu as pltpu
from jax.sharding import PartitionSpec as P

GROUP_CH = 16
STRETCH = 128
WIN = 4
SENT = WIN - 1
LANES = 128
BLOCKS = LANES // GROUP_CH
SPAN = 2 * STRETCH
VMEM_LIMIT = 16 * 1024 * 1024

SMEM_SPEC = pl.BlockSpec(memory_space=pltpu.SMEM)
ANY_SPEC = pl.BlockSpec(memory_space=pl.ANY)
HBM_SPEC = pl.BlockSpec(memory_space=pltpu.HBM)
VMEM_SPEC = pl.BlockSpec(memory_space=pltpu.VMEM)
NT = (((1,), (1,)), ((), ()))


def params():
    return pltpu.CompilerParams(vmem_limit_bytes=VMEM_LIMIT)


def steps_of(size):
    return sorted(range(size), key=lambda step: (min(step, size - step), step))


def partner(me, step, size):
    return lax.rem(me + step, size)


def sender(me, step, size):
    return lax.rem(me + size - step, size)


PLACE = SENT
MANY = 2 * SENT
WINDOWS = MANY + 1
SLOTS = 2


def product(key, value, start, columns):
    rows = pl.ds(start, STRETCH)
    rows_k = key[rows, columns].astype(jnp.float32)
    rows_v = value[rows, columns].astype(jnp.float32)
    return (rows_k * rows_v).astype(jnp.bfloat16).T


def gate_kernel(size, parts, sources_in, owner_in, key_in, value_in, filters_in, *refs):
    sends = refs[:parts]
    extra, meta, sources, owner, key, value, filters, sems = refs[parts:]
    stretch_count = owner.shape[0]
    channels = key.shape[1]
    width = channels // parts
    me = lax.axis_index("seq")
    copies = [
        pltpu.make_async_copy(sources_in, sources, sems.at[0]),
        pltpu.make_async_copy(owner_in, owner, sems.at[1]),
        pltpu.make_async_copy(key_in, key, sems.at[2]),
        pltpu.make_async_copy(value_in, value, sems.at[3]),
        pltpu.make_async_copy(filters_in, filters, sems.at[4]),
    ]
    for copy in copies:
        copy.start()

    for copy in copies[:2]:
        copy.wait()

    def target(k, slot):
        mine = owner[k] == me

        @pl.when(mine)
        def _():
            for w in range(WIN):
                lag_block = jnp.maximum(k - sources[w], -1)
                meta[WINDOWS + slot * WIN + w] = (stretch_count - 1 - lag_block) * STRETCH

        return slot + jnp.where(mine, 1, 0)

    lax.fori_loop(0, stretch_count, target, 0)
    for copy in copies[2:]:
        copy.wait()
    holders = [owner[sources[w]] for w in range(SENT)]
    many = 0
    for w, holder in enumerate(holders):
        place = sum([jnp.where(other == holder, 1, 0) for other in holders[:w]], 0)
        meta[w] = holder
        meta[PLACE + w] = place
        many = many + jnp.where(place >= SLOTS, 1, 0)

        @pl.when(holder == me)
        def _(w=w, holder=holder, place=place):
            def count(k, total):
                return total + jnp.where(owner[k] == holder, 1, 0)

            slot = lax.fori_loop(0, sources[w], count, 0)
            first = pl.multiple_of(slot * STRETCH, STRETCH)
            for step in range(parts):
                part = partner(me, step, size) if parts > 1 else 0
                base = part * width

                def fill(target, offset, base=base):
                    for start in range(0, width, LANES):
                        columns = pl.ds(pl.multiple_of(base + start, LANES), LANES)
                        target[pl.ds(offset + start, LANES), :] = product(key, value, first, columns)

                if w < SLOTS:
                    fill(sends[step], pl.multiple_of(place * width, LANES))
                else:

                    @pl.when(place < SLOTS)
                    def _(step=step, fill=fill):
                        fill(sends[step], pl.multiple_of(place * width, LANES))

                    @pl.when(place >= SLOTS)
                    def _(step=step, fill=fill):
                        fill(extra.at[step], 0)

    meta[MANY] = many
    group_count = filters.shape[0]
    for send in sends:
        rows = (send.shape[0] - SLOTS * width) * LANES // filters.shape[1]
        groups = pl.ds(0, rows)
        if 0 < rows < group_count:
            groups = pl.ds(pl.multiple_of(lax.axis_index("rep") * rows, rows), rows)
        for tile in range(filters.shape[1] // LANES if rows else 0):
            send[pl.ds(SLOTS * width + tile * rows, rows), :] = filters[
                groups, pl.ds(tile * LANES, LANES)
            ]


def gate(size, filter_rows, sources, owner, key_proj, value_proj, filters):
    row_count, channels = key_proj.shape
    slots = row_count // STRETCH
    parts = len(filter_rows)
    width = channels // parts
    operands = [
        pltpu.with_memory_space_constraint(operand, pltpu.HBM)
        for operand in (sources, owner, key_proj, value_proj, filters)
    ]
    *sends, extra, meta = pl.pallas_call(
        functools.partial(gate_kernel, size, parts),
        in_specs=[HBM_SPEC] * 5,
        out_specs=[VMEM_SPEC] * (parts + 1) + [SMEM_SPEC],
        out_shape=[
            jax.ShapeDtypeStruct((SLOTS * width + rows, LANES), jnp.bfloat16) for rows in filter_rows
        ]
        + [
            jax.ShapeDtypeStruct((parts, width, LANES), jnp.bfloat16),
            jax.ShapeDtypeStruct((WINDOWS + slots * WIN,), jnp.int32),
        ],
        scratch_shapes=[
            pltpu.SMEM(sources.shape, jnp.int32),
            pltpu.SMEM(owner.shape, jnp.int32),
            pltpu.VMEM(key_proj.shape, key_proj.dtype),
            pltpu.VMEM(value_proj.shape, value_proj.dtype),
            pltpu.VMEM(filters.shape, filters.dtype),
            pltpu.SemaphoreType.DMA((5,)),
        ],
        compiler_params=params(),
        name="gate",
    )(*operands)
    return sends, extra, meta


def merge_kernel(size, width, meta, *refs):
    received, extras, out = refs[:size], refs[size:-1], refs[-1]
    me = lax.axis_index("seq")

    for w in range(SENT):
        place = meta[PLACE + w]
        rows = pl.ds(pl.multiple_of(jnp.minimum(place, SLOTS - 1) * width, LANES), width)
        for block, step in zip(received, steps_of(size)):

            @pl.when(sender(me, step, size) == meta[w])
            def _(w=w, block=block, rows=rows):
                out[w] = block[rows, :]

    for w in range(SLOTS, SENT):
        for step, extra in enumerate(extras):

            @pl.when((sender(me, step, size) == meta[w]) & (meta[PLACE + w] >= SLOTS))
            def _(w=w, extra=extra):
                out[w] = extra[...]


def merge(size, width, meta, received, extras=()):
    return pl.pallas_call(
        functools.partial(merge_kernel, size, width),
        in_specs=[SMEM_SPEC] + [VMEM_SPEC] * (size + len(extras)),
        out_specs=VMEM_SPEC,
        out_shape=jax.ShapeDtypeStruct((SENT, width, LANES), received[0].dtype),
        compiler_params=params(),
        name="merge",
    )(meta, *received, *extras)


def pick_kernel(first, *refs):
    received, out = refs[:-1], refs[-1]
    for index, block in enumerate(received):
        out[index] = block[pl.ds(first, out.shape[1]), :]


def pick(first, received):
    rows = received[0].shape[0] - first
    return pl.pallas_call(
        functools.partial(pick_kernel, first),
        in_specs=[VMEM_SPEC] * len(received),
        out_specs=VMEM_SPEC,
        out_shape=jax.ShapeDtypeStruct((len(received), rows, LANES), received[0].dtype),
        compiler_params=params(),
        name="pick",
    )(*received)


def lag_tiles(size, first, filters):
    if len(filters) == 1:
        blocks = filters[0]
        group_count = blocks.shape[1] // first
        for shard in range(size):
            for tile in range(first):
                rows = pl.ds(tile * group_count, group_count)
                yield pl.ds(0, group_count), shard * first + tile, blocks[shard, rows, :]
        return
    own, far, mine, other = filters
    me, rep = lax.axis_index("seq"), lax.axis_index("rep")
    group_count = own.shape[0]
    tiles = own.shape[1] // LANES
    half = group_count // 2
    for tile in range(tiles):
        whole = pl.ds(0, group_count)
        yield whole, me * tiles + tile, own[:, pl.ds(tile * LANES, LANES)]
        rows = pl.ds(first + tile * group_count, group_count)
        yield whole, sender(me, 2, size) * tiles + tile, far[rows, :]
        for index, step in enumerate((1, size - 1)):
            number = sender(me, step, size) * tiles + tile
            for place, halves in ((rep, mine), (1 - rep, other)):
                groups = pl.ds(pl.multiple_of(place * half, half), half)
                yield groups, number, halves[index, pl.ds(tile * half, half), :]


def build_shifted(size, first, filters, reverse, shifted):
    group_count, padded = reverse.shape
    lag_count = padded - SPAN
    row = lax.broadcasted_iota(jnp.int32, (LANES, LANES), 0)
    column = lax.broadcasted_iota(jnp.int32, (LANES, LANES), 1)
    flip = jnp.where(row + column == LANES - 1, 1.0, 0.0).astype(jnp.bfloat16)
    for groups, number, values in lag_tiles(size, first, filters):
        start = lag_count - LANES - number * LANES
        if not isinstance(start, int):
            start = pl.multiple_of(start, LANES)
        reverse[groups, pl.ds(start, LANES)] = jnp.dot(
            values, flip, preferred_element_type=jnp.float32
        )
    reverse[:, pl.ds(lag_count, SPAN)] = jnp.zeros((group_count, SPAN), jnp.float32)
    inside = (
        lax.broadcasted_iota(jnp.int32, (GROUP_CH, LANES), 1)
        > lax.broadcasted_iota(jnp.int32, (GROUP_CH, LANES), 0)
    )

    @pl.loop(0, group_count // BLOCKS)
    def _(block):
        tile_rows = pl.ds(pl.multiple_of(block * BLOCKS, BLOCKS), BLOCKS)
        before = [jnp.zeros((GROUP_CH, LANES), jnp.float32)] * BLOCKS
        for start in range(0, padded, LANES):
            tile = reverse[tile_rows, pl.ds(start, LANES)]
            for g in range(BLOCKS):
                spread = jnp.broadcast_to(tile[g : g + 1, :], (GROUP_CH, LANES))
                rolled = pltpu.roll(spread, 1, 1, stride=1, stride_axis=0)
                shifted[block * BLOCKS + g, :, pl.ds(start, LANES)] = jnp.where(
                    inside, rolled, before[g]
                ).astype(jnp.bfloat16)
                before[g] = rolled


def spread_rows(tile, spans, base):
    lane = lax.broadcasted_iota(jnp.int16, tile.shape, 1)
    zero = jnp.zeros(tile.shape, tile.dtype)
    for i1 in range(BLOCKS):
        shift = GROUP_CH * i1
        if i1 == 0:
            low, high = zero, tile
        else:
            moved = pltpu.roll(tile, LANES - shift, 1)
            early = lane < LANES - shift
            low, high = jnp.where(early, zero, moved), jnp.where(early, moved, zero)
        rows = pl.ds(shift, GROUP_CH)
        for g in range(BLOCKS):
            part = slice(g * GROUP_CH, (g + 1) * GROUP_CH)
            spans[g, rows, pl.ds(base, LANES)] = low[part]
            spans[g, rows, pl.ds(base + LANES, LANES)] = high[part]


def window(meta, shifted, group, slot, w):
    start = pl.multiple_of(meta[WINDOWS + slot * WIN + w], STRETCH)
    return shifted[group, :, pl.ds(start, SPAN)]


def filter_rows(meta, shifted, group, slots):
    return jnp.concatenate(
        [
            jnp.concatenate([window(meta, shifted, group, slot, w) for w in range(SENT)], axis=1)
            for slot in range(slots)
        ],
        axis=0,
    )


def rows_of(results, block):
    part = slice(block * GROUP_CH, (block + 1) * GROUP_CH)
    return jnp.concatenate([result[part] for result in results], axis=0).T


def last_rows_kernel(key, value, out):
    for start in range(0, out.shape[0], LANES):
        out[pl.ds(start, LANES), :] = product(key, value, 0, pl.ds(start, LANES))


def last_rows(key_proj, value_proj):
    row_count, channels = key_proj.shape
    block = pl.BlockSpec((STRETCH, channels), lambda i: (row_count // STRETCH - 1, 0))
    operands = [pltpu.with_memory_space_constraint(x, pltpu.HBM) for x in (key_proj, value_proj)]
    return pl.pallas_call(
        last_rows_kernel,
        grid=(1,),
        in_specs=[block, block],
        out_specs=pl.BlockSpec((channels, STRETCH), lambda i: (0, 0)),
        out_shape=jax.ShapeDtypeStruct((channels, STRETCH), jnp.bfloat16),
        compiler_params=params(),
        name="last_rows",
    )(*operands)


def last_term(slots, meta, last, shifted, term, spans):
    for start in range(0, last.shape[0], LANES):
        held = spans.at[start // LANES % 2]
        spread_rows(last[pl.ds(start, LANES), :], held, 0)
        results = [
            lax.dot_general(
                held[g],
                window(meta, shifted, start // GROUP_CH + g, slots - 1, SENT),
                NT,
                preferred_element_type=jnp.float32,
            )
            for g in range(BLOCKS)
        ]
        for m in range(BLOCKS):
            term[pl.ds(m * GROUP_CH, GROUP_CH), pl.ds(start, LANES)] = rows_of(results, m)


def spread_part(pieces, start, spans):
    for w in range(SENT):
        spread_rows(pieces[w, pl.ds(start, LANES), :], spans, w * SPAN)


def conv_part(filter_rows_of, base, start, term, query, out, result, spans, sem):
    slots = query.shape[0] // STRETCH
    columns = pl.ds(pl.multiple_of(base + start, LANES), LANES)
    results = [
        lax.dot_general(
            spans[g],
            filter_rows_of(start // GROUP_CH + g),
            NT,
            preferred_element_type=jnp.float32,
        )
        for g in range(BLOCKS)
    ]
    for m in range(BLOCKS):
        rows = rows_of(results, m)
        for slot in range(slots):
            place = pl.ds(slot * STRETCH + m * GROUP_CH, GROUP_CH)
            tile = rows[slot * GROUP_CH : (slot + 1) * GROUP_CH]
            if slot == slots - 1:
                tile = tile + term[pl.ds(m * GROUP_CH, GROUP_CH), columns]
            gates = query[place, columns].astype(jnp.float32)
            result[place, :] = (gates * tile).astype(jnp.bfloat16)
    store = pltpu.make_async_copy(result, out.at[:, columns], sem)
    store.start()
    return store


def part_base(step, size, width):
    me = lax.axis_index("seq")
    return pl.multiple_of((me ^ step if size > 1 else 0) * width, width)


def scratch(count, row_count):
    return [
        pltpu.VMEM((count, row_count, LANES), jnp.bfloat16),
        pltpu.VMEM((count, BLOCKS, LANES, SENT * SPAN), jnp.bfloat16),
        pltpu.SemaphoreType.DMA((count + 1,)),
    ]


def open_kernel(size, first, meta_in, last, pieces, query, *refs):
    filters = refs[:-9]
    shifted, term, out, reverse, meta, last_spans, result, spans, sems = refs[-9:]
    slots = query.shape[0] // STRETCH
    width = pieces.shape[1]
    scalars = pltpu.make_async_copy(meta_in, meta, sems.at[width // LANES])
    scalars.start()
    build_shifted(size, first, filters, reverse, shifted)
    scalars.wait()
    last_term(slots, meta, last, shifted, term, last_spans)
    base = part_base(0, out.shape[1] // width, width)
    stores = []
    for index, start in enumerate(range(0, width, LANES)):
        spread_part(pieces, start, spans.at[index])
        stores.append(
            conv_part(
                lambda group: filter_rows(meta, shifted, base // GROUP_CH + group, slots),
                base,
                start,
                term,
                query,
                out,
                result.at[index],
                spans.at[index],
                sems.at[index],
            )
        )
    for store in stores:
        store.wait()


def open_conv(size, first, meta, last, pieces, query_proj, group_count, lag_count, filters):
    row_count, channels = query_proj.shape
    padded = lag_count + SPAN
    return pl.pallas_call(
        functools.partial(open_kernel, size, first),
        in_specs=[ANY_SPEC] + [VMEM_SPEC] * (3 + len(filters)),
        out_specs=[VMEM_SPEC, VMEM_SPEC, HBM_SPEC],
        out_shape=[
            jax.ShapeDtypeStruct((group_count, GROUP_CH, padded), jnp.bfloat16),
            jax.ShapeDtypeStruct((STRETCH, channels), jnp.float32),
            jax.ShapeDtypeStruct((row_count, channels), jnp.bfloat16),
        ],
        scratch_shapes=[
            pltpu.VMEM((group_count, padded), jnp.float32),
            pltpu.SMEM(meta.shape, jnp.int32),
            pltpu.VMEM((2, BLOCKS, LANES, SPAN), jnp.bfloat16),
            *scratch(pieces.shape[1] // LANES, row_count),
        ],
        compiler_params=params(),
        name="open_conv",
    )(meta, last, pieces, query_proj, *filters)


def near_kernel(size, steps, next_step, meta_in, shifted, term, query, before, *refs):
    parts = refs[: len(steps)]
    out, ready, meta, result, spans, sems = refs[len(steps) :]
    slots = query.shape[0] // STRETCH
    width = parts[0].shape[1]
    places = [(index, start) for index in range(len(steps)) for start in range(0, width, LANES)]
    scalars = pltpu.make_async_copy(meta_in, meta, sems.at[len(places)])
    scalars.start()
    for number, (index, start) in enumerate(places[: len(places) // 2]):
        spread_part(parts[index], start, spans.at[number])
    scalars.wait()
    stores = []
    for number, (index, start) in enumerate(places):
        if number >= len(places) // 2:
            spread_part(parts[index], start, spans.at[number])
        base = part_base(steps[index], size, width)
        stores.append(
            conv_part(
                lambda group, base=base: filter_rows(meta, shifted, base // GROUP_CH + group, slots),
                base,
                start,
                term,
                query,
                out,
                result.at[number],
                spans.at[number],
                sems.at[number],
            )
        )
    base = part_base(next_step, size, width)
    for group in range(width // GROUP_CH):
        ready[group] = filter_rows(meta, shifted, base // GROUP_CH + group, slots)
    for store in stores:
        store.wait()


def near_conv(size, steps, next_step, meta, parts, shifted, term, query_proj, before):
    row_count, channels = query_proj.shape
    width = channels // size
    slots = row_count // STRETCH
    return pl.pallas_call(
        functools.partial(near_kernel, size, steps, next_step),
        in_specs=[ANY_SPEC] + [VMEM_SPEC] * 3 + [HBM_SPEC] + [VMEM_SPEC] * len(parts),
        out_specs=[HBM_SPEC, VMEM_SPEC],
        out_shape=[
            jax.ShapeDtypeStruct((row_count, channels), jnp.bfloat16),
            jax.ShapeDtypeStruct((width // GROUP_CH, slots * GROUP_CH, SENT * SPAN), jnp.bfloat16),
        ],
        input_output_aliases={4: 0},
        scratch_shapes=[
            pltpu.SMEM(meta.shape, jnp.int32),
            *scratch(len(parts) * width // LANES, row_count),
        ],
        compiler_params=params(),
        name="near_conv",
    )(meta, shifted, term, query_proj, before, *parts)


def far_kernel(size, step, pieces, ready, term, query, before, out, result, spans, sems):
    width = pieces.shape[1]
    base = part_base(step, size, width)
    stores = []
    for index, start in enumerate(range(0, width, LANES)):
        spread_part(pieces, start, spans.at[index])
        stores.append(
            conv_part(
                lambda group: ready[group],
                base,
                start,
                term,
                query,
                out,
                result.at[index],
                spans.at[index],
                sems.at[index],
            )
        )
    for store in stores:
        store.wait()


def far_conv(size, step, pieces, ready, term, query_proj, before):
    row_count, channels = query_proj.shape
    return pl.pallas_call(
        functools.partial(far_kernel, size, step),
        in_specs=[VMEM_SPEC] * 4 + [HBM_SPEC],
        out_specs=HBM_SPEC,
        out_shape=jax.ShapeDtypeStruct((row_count, channels), jnp.bfloat16),
        input_output_aliases={4: 0},
        scratch_shapes=scratch(pieces.shape[1] // LANES, row_count),
        compiler_params=params(),
        name="far_conv",
    )(pieces, ready, term, query_proj, before)


def shards(size, reps, key_proj, value_proj, query_proj, filters, sources, owner):
    row_count, channels = key_proj.shape
    group_count, part = filters.shape
    lag_count = size * part
    tiles = part // LANES
    by_parts = (size, reps) == (4, 2) and channels % (size * LANES) == 0
    half = group_count // 2 * tiles
    filter_rows = [0, half, 2 * half, half] if by_parts else [2 * half]
    parts = len(filter_rows)
    width = channels // parts
    sends, extra, meta = gate(size, filter_rows, sources, owner, key_proj, value_proj, filters)
    last = last_rows(key_proj, value_proj)
    first = SLOTS * width
    if not by_parts:
        blocks = lax.all_gather(sends[0][first:], "seq")
        held = jnp.concatenate([sends[0][:first].reshape(SLOTS, width, LANES), extra])
        mine = (meta[:SENT] == lax.axis_index("seq"))[:, None, None]
        pieces = lax.psum(jnp.where(mine, held[meta[PLACE:MANY]], jnp.zeros_like(held)), "seq")
        return open_conv(
            size, tiles, meta, last, pieces, query_proj, group_count, lag_count, [blocks]
        )[2]

    def shift(value, step):
        return lax.ppermute(value, "seq", [(z, (z + step) % size) for z in range(size)])

    up, down, far = (shift(sends[step], step) for step in (1, size - 1, 2))
    mine = pick(first, [up, down])
    other = lax.ppermute(mine, "rep", [(0, 1), (1, 0)])
    last, other, far = lax.optimization_barrier((last, other, far))
    received = [sends[0], up, down, far]

    def merge_more(meta, received, extra):
        more = [extra[0]] + [shift(extra[step], step) for step in range(1, size)]
        return merge(size, width, meta, received, more)

    def merge_plain(meta, received, extra):
        return merge(size, width, meta, received)

    merged = lax.cond(meta[MANY] > 0, merge_more, merge_plain, meta, received, extra)
    far_part = lax.ppermute(merged, "seq", [(0, 2), (2, 0), (1, 3), (3, 1)])
    near_part = lax.ppermute(merged, "seq", [(0, 1), (1, 0), (2, 3), (3, 2)])
    shifted, term, out = open_conv(
        size,
        first,
        meta,
        last,
        merged,
        query_proj,
        group_count,
        lag_count,
        [filters, far, mine, other],
    )
    far_part, out = lax.optimization_barrier((far_part, out))
    last_part = lax.ppermute(far_part, "seq", [(0, 1), (1, 0), (2, 3), (3, 2)])
    out, ready = near_conv(
        size, (1, 2), 3, meta, [near_part, far_part], shifted, term, query_proj, out
    )
    return far_conv(size, 3, last_part, ready, term, query_proj, out)


def solution(mesh):
    return jax.shard_map(
        functools.partial(shards, mesh.shape["seq"], mesh.shape["rep"]),
        mesh=mesh,
        in_specs=(
            P(("rep", "seq"), "ch"),
            P(("rep", "seq"), "ch"),
            P(("rep", "seq"), "ch"),
            P("ch", "seq"),
            P("rep"),
            P("rep"),
        ),
        out_specs=P(("rep", "seq"), "ch"),
        check_vma=False,
    )
```

```python
import functools

import jax
import jax.numpy as jnp
from jax import lax
from jax.experimental import pallas as pl
from jax.experimental.pallas import tpu as pltpu
from jax.sharding import PartitionSpec as P

GROUP_CH = 16
STRETCH = 128
WIN = 4
SENT = WIN - 1
LANES = 128
BLOCKS = LANES // GROUP_CH
SPAN = 2 * STRETCH
VMEM_LIMIT = 16 * 1024 * 1024

SMEM_SPEC = pl.BlockSpec(memory_space=pltpu.SMEM)
ANY_SPEC = pl.BlockSpec(memory_space=pl.ANY)
HBM_SPEC = pl.BlockSpec(memory_space=pltpu.HBM)
VMEM_SPEC = pl.BlockSpec(memory_space=pltpu.VMEM)
NT = (((1,), (1,)), ((), ()))


def params():
    return pltpu.CompilerParams(vmem_limit_bytes=VMEM_LIMIT)


STEPS = (0, 2, 1, 3)


PLACE = SENT
MANY = 2 * SENT
WINDOWS = MANY + 1
SLOTS = 2


def product(key, value, start, columns):
    rows = pl.ds(start, STRETCH)
    rows_k = key[rows, columns].astype(jnp.float32)
    rows_v = value[rows, columns].astype(jnp.float32)
    return (rows_k * rows_v).astype(jnp.bfloat16).T


def gate_kernel(parts, sources_in, owner_in, key_in, value_in, filters_in, *refs):
    sends = refs[:parts]
    extra, meta, sources, owner, key, value, filters, sems = refs[parts:]
    stretch_count = owner.shape[0]
    channels = key.shape[1]
    width = channels // parts
    me = lax.axis_index("seq")
    copies = [
        pltpu.make_async_copy(sources_in, sources, sems.at[0]),
        pltpu.make_async_copy(owner_in, owner, sems.at[1]),
        pltpu.make_async_copy(key_in, key, sems.at[2]),
        pltpu.make_async_copy(value_in, value, sems.at[3]),
        pltpu.make_async_copy(filters_in, filters, sems.at[4]),
    ]
    for copy in copies:
        copy.start()

    for copy in copies[:2]:
        copy.wait()

    def target(k, slot):
        mine = owner[k] == me

        @pl.when(mine)
        def _():
            for w in range(WIN):
                lag_block = jnp.maximum(k - sources[w], -1)
                meta[WINDOWS + slot * WIN + w] = (stretch_count - 1 - lag_block) * STRETCH

        return slot + jnp.where(mine, 1, 0)

    lax.fori_loop(0, stretch_count, target, 0)
    for copy in copies[2:]:
        copy.wait()
    holders = [owner[sources[w]] for w in range(SENT)]
    many = 0
    for w, holder in enumerate(holders):
        place = sum([jnp.where(other == holder, 1, 0) for other in holders[:w]], 0)
        meta[w] = holder
        meta[PLACE + w] = place
        many = many + jnp.where(place >= SLOTS, 1, 0)

        @pl.when(holder == me)
        def _(w=w, holder=holder, place=place):
            def count(k, total):
                return total + jnp.where(owner[k] == holder, 1, 0)

            slot = lax.fori_loop(0, sources[w], count, 0)
            first = pl.multiple_of(slot * STRETCH, STRETCH)
            for step in range(parts):
                part = me ^ step if parts > 1 else 0
                base = part * width

                def fill(target, offset, base=base):
                    for start in range(0, width, LANES):
                        columns = pl.ds(pl.multiple_of(base + start, LANES), LANES)
                        target[pl.ds(offset + start, LANES), :] = product(key, value, first, columns)

                if w < SLOTS:
                    fill(sends[step], pl.multiple_of(place * width, LANES))
                else:

                    @pl.when(place < SLOTS)
                    def _(step=step, fill=fill):
                        fill(sends[step], pl.multiple_of(place * width, LANES))

                    @pl.when(place >= SLOTS)
                    def _(step=step, fill=fill):
                        fill(extra.at[step], 0)

    meta[MANY] = many
    group_count = filters.shape[0]
    for tile in range(filters.shape[1] // LANES):
        piece = filters[:, pl.ds(tile * LANES, LANES)]
        for send in sends:
            if send.shape[0] > SLOTS * width:
                send[pl.ds(SLOTS * width + tile * group_count, group_count), :] = piece


def gate(filter_rows, sources, owner, key_proj, value_proj, filters):
    row_count, channels = key_proj.shape
    slots = row_count // STRETCH
    parts = len(filter_rows)
    width = channels // parts
    operands = [
        pltpu.with_memory_space_constraint(operand, pltpu.HBM)
        for operand in (sources, owner, key_proj, value_proj, filters)
    ]
    *sends, extra, meta = pl.pallas_call(
        functools.partial(gate_kernel, parts),
        in_specs=[HBM_SPEC] * 5,
        out_specs=[VMEM_SPEC] * (parts + 1) + [SMEM_SPEC],
        out_shape=[
            jax.ShapeDtypeStruct((SLOTS * width + rows, LANES), jnp.bfloat16) for rows in filter_rows
        ]
        + [
            jax.ShapeDtypeStruct((parts, width, LANES), jnp.bfloat16),
            jax.ShapeDtypeStruct((WINDOWS + slots * WIN,), jnp.int32),
        ],
        scratch_shapes=[
            pltpu.SMEM(sources.shape, jnp.int32),
            pltpu.SMEM(owner.shape, jnp.int32),
            pltpu.VMEM(key_proj.shape, key_proj.dtype),
            pltpu.VMEM(value_proj.shape, value_proj.dtype),
            pltpu.VMEM(filters.shape, filters.dtype),
            pltpu.SemaphoreType.DMA((5,)),
        ],
        compiler_params=params(),
        name="gate",
    )(*operands)
    return sends, extra, meta


def merge_kernel(width, meta, *refs):
    received, extras, out = refs[: len(STEPS)], refs[len(STEPS) : -1], refs[-1]
    me = lax.axis_index("seq")

    for w in range(SENT):
        place = meta[PLACE + w]
        rows = pl.ds(pl.multiple_of(jnp.minimum(place, SLOTS - 1) * width, LANES), width)
        for block, step in zip(received, STEPS):

            @pl.when(me ^ step == meta[w])
            def _(w=w, block=block, rows=rows):
                out[w] = block[rows, :]

    for w in range(SLOTS, SENT):
        for extra, step in zip(extras, STEPS):

            @pl.when((me ^ step == meta[w]) & (meta[PLACE + w] >= SLOTS))
            def _(w=w, extra=extra):
                out[w] = extra[...]


def merge(width, meta, received, extras=()):
    return pl.pallas_call(
        functools.partial(merge_kernel, width),
        in_specs=[SMEM_SPEC] + [VMEM_SPEC] * (len(received) + len(extras)),
        out_specs=VMEM_SPEC,
        out_shape=jax.ShapeDtypeStruct((SENT, width, LANES), received[0].dtype),
        compiler_params=params(),
        name="merge",
    )(meta, *received, *extras)


def pick_kernel(first, received, out):
    out[...] = received[pl.ds(first, out.shape[0]), :]


def pick(first, received):
    return pl.pallas_call(
        functools.partial(pick_kernel, first),
        in_specs=[VMEM_SPEC],
        out_specs=VMEM_SPEC,
        out_shape=jax.ShapeDtypeStruct((received.shape[0] - first, LANES), received.dtype),
        compiler_params=params(),
        name="pick",
    )(received)


def lag_tiles(size, first, filters):
    if len(filters) == 1:
        blocks = filters[0]
        group_count = blocks.shape[1] // first
        for shard in range(size):
            for tile in range(first):
                rows = pl.ds(tile * group_count, group_count)
                yield shard * first + tile, blocks[shard, rows, :]
        return
    own, far, near, cross = filters
    me = lax.axis_index("seq")
    group_count = own.shape[0]
    tiles = own.shape[1] // LANES
    for tile in range(tiles):
        yield me * tiles + tile, own[:, pl.ds(tile * LANES, LANES)]
        for block, start, step in ((far, first, 2), (near, first, 1), (cross, 0, 3)):
            rows = pl.ds(start + tile * group_count, group_count)
            yield (me ^ step) * tiles + tile, block[rows, :]


def build_shifted(size, first, filters, reverse, shifted):
    group_count, padded = reverse.shape
    lag_count = padded - SPAN
    row = lax.broadcasted_iota(jnp.int32, (LANES, LANES), 0)
    column = lax.broadcasted_iota(jnp.int32, (LANES, LANES), 1)
    flip = jnp.where(row + column == LANES - 1, 1.0, 0.0).astype(jnp.bfloat16)
    for number, values in lag_tiles(size, first, filters):
        start = lag_count - LANES - number * LANES
        if not isinstance(start, int):
            start = pl.multiple_of(start, LANES)
        reverse[:, pl.ds(start, LANES)] = jnp.dot(
            values, flip, preferred_element_type=jnp.float32
        )
    reverse[:, pl.ds(lag_count, SPAN)] = jnp.zeros((group_count, SPAN), jnp.float32)
    inside = (
        lax.broadcasted_iota(jnp.int32, (GROUP_CH, LANES), 1)
        > lax.broadcasted_iota(jnp.int32, (GROUP_CH, LANES), 0)
    )

    @pl.loop(0, group_count // BLOCKS)
    def _(block):
        tile_rows = pl.ds(pl.multiple_of(block * BLOCKS, BLOCKS), BLOCKS)
        before = [jnp.zeros((GROUP_CH, LANES), jnp.float32)] * BLOCKS
        for start in range(0, padded, LANES):
            tile = reverse[tile_rows, pl.ds(start, LANES)]
            for g in range(BLOCKS):
                spread = jnp.broadcast_to(tile[g : g + 1, :], (GROUP_CH, LANES))
                rolled = pltpu.roll(spread, 1, 1, stride=1, stride_axis=0)
                shifted[block * BLOCKS + g, :, pl.ds(start, LANES)] = jnp.where(
                    inside, rolled, before[g]
                ).astype(jnp.bfloat16)
                before[g] = rolled


def spread_rows(tile, spans, base):
    lane = lax.broadcasted_iota(jnp.int16, tile.shape, 1)
    zero = jnp.zeros(tile.shape, tile.dtype)
    for i1 in range(BLOCKS):
        shift = GROUP_CH * i1
        if i1 == 0:
            low, high = zero, tile
        else:
            moved = pltpu.roll(tile, LANES - shift, 1)
            early = lane < LANES - shift
            low, high = jnp.where(early, zero, moved), jnp.where(early, moved, zero)
        rows = pl.ds(shift, GROUP_CH)
        for g in range(BLOCKS):
            part = slice(g * GROUP_CH, (g + 1) * GROUP_CH)
            spans[g, rows, pl.ds(base, LANES)] = low[part]
            spans[g, rows, pl.ds(base + LANES, LANES)] = high[part]


def window(meta, shifted, group, slot, w):
    start = pl.multiple_of(meta[WINDOWS + slot * WIN + w], STRETCH)
    return shifted[group, :, pl.ds(start, SPAN)]


def filter_rows(meta, shifted, group, slots):
    return jnp.concatenate(
        [
            jnp.concatenate([window(meta, shifted, group, slot, w) for w in range(SENT)], axis=1)
            for slot in range(slots)
        ],
        axis=0,
    )


def rows_of(results, block):
    part = slice(block * GROUP_CH, (block + 1) * GROUP_CH)
    return jnp.concatenate([result[part] for result in results], axis=0).T


def last_rows_kernel(key, value, out):
    for start in range(0, out.shape[0], LANES):
        out[pl.ds(start, LANES), :] = product(key, value, 0, pl.ds(start, LANES))


def last_rows(key_proj, value_proj):
    row_count, channels = key_proj.shape
    block = pl.BlockSpec((STRETCH, channels), lambda i: (row_count // STRETCH - 1, 0))
    operands = [pltpu.with_memory_space_constraint(x, pltpu.HBM) for x in (key_proj, value_proj)]
    return pl.pallas_call(
        last_rows_kernel,
        grid=(1,),
        in_specs=[block, block],
        out_specs=pl.BlockSpec((channels, STRETCH), lambda i: (0, 0)),
        out_shape=jax.ShapeDtypeStruct((channels, STRETCH), jnp.bfloat16),
        compiler_params=params(),
        name="last_rows",
    )(*operands)


def last_term(slots, meta, last, shifted, term, spans):
    for start in range(0, last.shape[0], LANES):
        held = spans.at[start // LANES % 2]
        spread_rows(last[pl.ds(start, LANES), :], held, 0)
        results = [
            lax.dot_general(
                held[g],
                window(meta, shifted, start // GROUP_CH + g, slots - 1, SENT),
                NT,
                preferred_element_type=jnp.float32,
            )
            for g in range(BLOCKS)
        ]
        for m in range(BLOCKS):
            term[pl.ds(m * GROUP_CH, GROUP_CH), pl.ds(start, LANES)] = rows_of(results, m)


def spread_part(pieces, start, spans):
    for w in range(SENT):
        spread_rows(pieces[w, pl.ds(start, LANES), :], spans, w * SPAN)


def conv_part(filter_rows_of, base, start, term, query, out, result, spans, sem):
    slots = query.shape[0] // STRETCH
    columns = pl.ds(pl.multiple_of(base + start, LANES), LANES)
    results = [
        lax.dot_general(
            spans[g],
            filter_rows_of(start // GROUP_CH + g),
            NT,
            preferred_element_type=jnp.float32,
        )
        for g in range(BLOCKS)
    ]
    for m in range(BLOCKS):
        rows = rows_of(results, m)
        for slot in range(slots):
            place = pl.ds(slot * STRETCH + m * GROUP_CH, GROUP_CH)
            tile = rows[slot * GROUP_CH : (slot + 1) * GROUP_CH]
            if slot == slots - 1:
                tile = tile + term[pl.ds(m * GROUP_CH, GROUP_CH), columns]
            gates = query[place, columns].astype(jnp.float32)
            result[place, :] = (gates * tile).astype(jnp.bfloat16)
    store = pltpu.make_async_copy(result, out.at[:, columns], sem)
    store.start()
    return store


def part_base(step, size, width):
    me = lax.axis_index("seq")
    return pl.multiple_of((me ^ step if size > 1 else 0) * width, width)


def scratch(count, row_count):
    return [
        pltpu.VMEM((count, row_count, LANES), jnp.bfloat16),
        pltpu.VMEM((count, BLOCKS, LANES, SENT * SPAN), jnp.bfloat16),
        pltpu.SemaphoreType.DMA((count + 1,)),
    ]


def open_kernel(size, first, meta_in, last, pieces, query, *refs):
    filters = refs[:-9]
    shifted, term, out, reverse, meta, last_spans, result, spans, sems = refs[-9:]
    slots = query.shape[0] // STRETCH
    width = pieces.shape[1]
    scalars = pltpu.make_async_copy(meta_in, meta, sems.at[width // LANES])
    scalars.start()
    build_shifted(size, first, filters, reverse, shifted)
    scalars.wait()
    last_term(slots, meta, last, shifted, term, last_spans)
    base = part_base(0, out.shape[1] // width, width)
    stores = []
    for index, start in enumerate(range(0, width, LANES)):
        spread_part(pieces, start, spans.at[index])
        stores.append(
            conv_part(
                lambda group: filter_rows(meta, shifted, base // GROUP_CH + group, slots),
                base,
                start,
                term,
                query,
                out,
                result.at[index],
                spans.at[index],
                sems.at[index],
            )
        )
    for store in stores:
        store.wait()


def open_conv(size, first, meta, last, pieces, query_proj, group_count, lag_count, filters):
    row_count, channels = query_proj.shape
    padded = lag_count + SPAN
    return pl.pallas_call(
        functools.partial(open_kernel, size, first),
        in_specs=[ANY_SPEC] + [VMEM_SPEC] * (3 + len(filters)),
        out_specs=[VMEM_SPEC, VMEM_SPEC, HBM_SPEC],
        out_shape=[
            jax.ShapeDtypeStruct((group_count, GROUP_CH, padded), jnp.bfloat16),
            jax.ShapeDtypeStruct((STRETCH, channels), jnp.float32),
            jax.ShapeDtypeStruct((row_count, channels), jnp.bfloat16),
        ],
        scratch_shapes=[
            pltpu.VMEM((group_count, padded), jnp.float32),
            pltpu.SMEM(meta.shape, jnp.int32),
            pltpu.VMEM((2, BLOCKS, LANES, SPAN), jnp.bfloat16),
            *scratch(pieces.shape[1] // LANES, row_count),
        ],
        compiler_params=params(),
        name="open_conv",
    )(meta, last, pieces, query_proj, *filters)


def near_kernel(size, steps, next_step, meta_in, shifted, term, query, before, *refs):
    parts = refs[: len(steps)]
    out, ready, meta, result, spans, sems = refs[len(steps) :]
    slots = query.shape[0] // STRETCH
    width = parts[0].shape[1]
    places = [(index, start) for index in range(len(steps)) for start in range(0, width, LANES)]
    scalars = pltpu.make_async_copy(meta_in, meta, sems.at[len(places)])
    scalars.start()
    for number, (index, start) in enumerate(places[: len(places) // 2]):
        spread_part(parts[index], start, spans.at[number])
    scalars.wait()
    stores = []
    for number, (index, start) in enumerate(places):
        if number >= len(places) // 2:
            spread_part(parts[index], start, spans.at[number])
        base = part_base(steps[index], size, width)
        stores.append(
            conv_part(
                lambda group, base=base: filter_rows(meta, shifted, base // GROUP_CH + group, slots),
                base,
                start,
                term,
                query,
                out,
                result.at[number],
                spans.at[number],
                sems.at[number],
            )
        )
    base = part_base(next_step, size, width)
    for group in range(width // GROUP_CH):
        ready[group] = filter_rows(meta, shifted, base // GROUP_CH + group, slots)
    for store in stores:
        store.wait()


def near_conv(size, steps, next_step, meta, parts, shifted, term, query_proj, before):
    row_count, channels = query_proj.shape
    width = channels // size
    slots = row_count // STRETCH
    return pl.pallas_call(
        functools.partial(near_kernel, size, steps, next_step),
        in_specs=[ANY_SPEC] + [VMEM_SPEC] * 3 + [HBM_SPEC] + [VMEM_SPEC] * len(parts),
        out_specs=[HBM_SPEC, VMEM_SPEC],
        out_shape=[
            jax.ShapeDtypeStruct((row_count, channels), jnp.bfloat16),
            jax.ShapeDtypeStruct((width // GROUP_CH, slots * GROUP_CH, SENT * SPAN), jnp.bfloat16),
        ],
        input_output_aliases={4: 0},
        scratch_shapes=[
            pltpu.SMEM(meta.shape, jnp.int32),
            *scratch(len(parts) * width // LANES, row_count),
        ],
        compiler_params=params(),
        name="near_conv",
    )(meta, shifted, term, query_proj, before, *parts)


def far_kernel(size, step, pieces, ready, term, query, before, out, result, spans, sems):
    width = pieces.shape[1]
    base = part_base(step, size, width)
    stores = []
    for index, start in enumerate(range(0, width, LANES)):
        spread_part(pieces, start, spans.at[index])
        stores.append(
            conv_part(
                lambda group: ready[group],
                base,
                start,
                term,
                query,
                out,
                result.at[index],
                spans.at[index],
                sems.at[index],
            )
        )
    for store in stores:
        store.wait()


def far_conv(size, step, pieces, ready, term, query_proj, before):
    row_count, channels = query_proj.shape
    return pl.pallas_call(
        functools.partial(far_kernel, size, step),
        in_specs=[VMEM_SPEC] * 4 + [HBM_SPEC],
        out_specs=HBM_SPEC,
        out_shape=jax.ShapeDtypeStruct((row_count, channels), jnp.bfloat16),
        input_output_aliases={4: 0},
        scratch_shapes=scratch(pieces.shape[1] // LANES, row_count),
        compiler_params=params(),
        name="far_conv",
    )(pieces, ready, term, query_proj, before)


def shards(size, key_proj, value_proj, query_proj, filters, sources, owner):
    row_count, channels = key_proj.shape
    group_count, part = filters.shape
    lag_count = size * part
    tiles = part // LANES
    by_parts = size == 4 and channels % (size * LANES) == 0
    block = group_count * tiles
    filter_rows = [0, block, block, 0] if by_parts else [block]
    parts = len(filter_rows)
    width = channels // parts
    operands = [
        pltpu.with_memory_space_constraint(operand, pltpu.HBM)
        for operand in (sources, owner, key_proj, value_proj, filters)
    ]
    *sends, extra, meta = pl.pallas_call(
        functools.partial(gate_kernel, parts),
        in_specs=[HBM_SPEC] * 5,
        out_specs=[VMEM_SPEC] * (parts + 1) + [SMEM_SPEC],
        out_shape=[
            jax.ShapeDtypeStruct((SLOTS * width + rows, LANES), jnp.bfloat16) for rows in filter_rows
        ]
        + [
            jax.ShapeDtypeStruct((parts, width, LANES), jnp.bfloat16),
            jax.ShapeDtypeStruct((WINDOWS + slots * WIN,), jnp.int32),
        ],
        scratch_shapes=[
            pltpu.SMEM(sources.shape, jnp.int32),
            pltpu.SMEM(owner.shape, jnp.int32),
            pltpu.VMEM(key_proj.shape, key_proj.dtype),
            pltpu.VMEM(value_proj.shape, value_proj.dtype),
            pltpu.VMEM(filters.shape, filters.dtype),
            pltpu.SemaphoreType.DMA((5,)),
        ],
        compiler_params=params(),
        name="gate",
    )(*operands)
    return sends, extra, meta


def merge_kernel(width, meta, *refs):
    received, extras, out = refs[: len(STEPS)], refs[len(STEPS) : -1], refs[-1]
    me = lax.axis_index("seq")

    for w in range(SENT):
        place = meta[PLACE + w]
        rows = pl.ds(pl.multiple_of(jnp.minimum(place, SLOTS - 1) * width, LANES), width)
        for block, step in zip(received, STEPS):

            @pl.when(me ^ step == meta[w])
            def _(w=w, block=block, rows=rows):
                out[w] = block[rows, :]

    for w in range(SLOTS, SENT):
        for extra, step in zip(extras, STEPS):

            @pl.when((me ^ step == meta[w]) & (meta[PLACE + w] >= SLOTS))
            def _(w=w, extra=extra):
                out[w] = extra[...]


def merge(width, meta, received, extras=()):
    return pl.pallas_call(
        functools.partial(merge_kernel, width),
        in_specs=[SMEM_SPEC] + [VMEM_SPEC] * (len(received) + len(extras)),
        out_specs=VMEM_SPEC,
        out_shape=jax.ShapeDtypeStruct((SENT, width, LANES), received[0].dtype),
        compiler_params=params(),
        name="merge",
    )(meta, *received, *extras)


def pick_kernel(first, received, out):
    out[...] = received[pl.ds(first, out.shape[0]), :]


def pick(first, received):
    return pl.pallas_call(
        functools.partial(pick_kernel, first),
        in_specs=[VMEM_SPEC],
        out_specs=VMEM_SPEC,
        out_shape=jax.ShapeDtypeStruct((received.shape[0] - first, LANES), received.dtype),
        compiler_params=params(),
        name="pick",
    )(received)


def lag_tiles(size, first, filters):
    if len(filters) == 1:
        blocks = filters[0]
        group_count = blocks.shape[1] // first
        for shard in range(size):
            for tile in range(first):
                rows = pl.ds(tile * group_count, group_count)
                yield shard * first + tile, blocks[shard, rows, :]
        return
    own, far, near, cross = filters
    me = lax.axis_index("seq")
    group_count = own.shape[0]
    tiles = own.shape[1] // LANES
    for tile in range(tiles):
        yield me * tiles + tile, own[:, pl.ds(tile * LANES, LANES)]
        for block, start, step in ((far, first, 2), (near, first, 1), (cross, 0, 3)):
            rows = pl.ds(start + tile * group_count, group_count)
            yield (me ^ step) * tiles + tile, block[rows, :]


def build_shifted(size, first, filters, reverse, shifted):
    group_count, padded = reverse.shape
    lag_count = padded - SPAN
    row = lax.broadcasted_iota(jnp.int32, (LANES, LANES), 0)
    column = lax.broadcasted_iota(jnp.int32, (LANES, LANES), 1)
    flip = jnp.where(row + column == LANES - 1, 1.0, 0.0).astype(jnp.bfloat16)
    for number, values in lag_tiles(size, first, filters):
        start = lag_count - LANES - number * LANES
        if not isinstance(start, int):
            start = pl.multiple_of(start, LANES)
        reverse[:, pl.ds(start, LANES)] = jnp.dot(
            values, flip, preferred_element_type=jnp.float32
        )
    reverse[:, pl.ds(lag_count, SPAN)] = jnp.zeros((group_count, SPAN), jnp.float32)
    inside = (
        lax.broadcasted_iota(jnp.int32, (GROUP_CH, LANES), 1)
        > lax.broadcasted_iota(jnp.int32, (GROUP_CH, LANES), 0)
    )

    @pl.loop(0, group_count // BLOCKS)
    def _(block):
        tile_rows = pl.ds(pl.multiple_of(block * BLOCKS, BLOCKS), BLOCKS)
        before = [jnp.zeros((GROUP_CH, LANES), jnp.float32)] * BLOCKS
        for start in range(0, padded, LANES):
            tile = reverse[tile_rows, pl.ds(start, LANES)]
            for g in range(BLOCKS):
                spread = jnp.broadcast_to(tile[g : g + 1, :], (GROUP_CH, LANES))
                rolled = pltpu.roll(spread, 1, 1, stride=1, stride_axis=0)
                shifted[block * BLOCKS + g, :, pl.ds(start, LANES)] = jnp.where(
                    inside, rolled, before[g]
                ).astype(jnp.bfloat16)
                before[g] = rolled


def spread_rows(tile, spans, base):
    lane = lax.broadcasted_iota(jnp.int16, tile.shape, 1)
    zero = jnp.zeros(tile.shape, tile.dtype)
    for i1 in range(BLOCKS):
        shift = GROUP_CH * i1
        if i1 == 0:
            low, high = zero, tile
        else:
            moved = pltpu.roll(tile, LANES - shift, 1)
            early = lane < LANES - shift
            low, high = jnp.where(early, zero, moved), jnp.where(early, moved, zero)
        rows = pl.ds(shift, GROUP_CH)
        for g in range(BLOCKS):
            part = slice(g * GROUP_CH, (g + 1) * GROUP_CH)
            spans[g, rows, pl.ds(base, LANES)] = low[part]
            spans[g, rows, pl.ds(base + LANES, LANES)] = high[part]


def window(meta, shifted, group, slot, w):
    start = pl.multiple_of(meta[WINDOWS + slot * WIN + w], STRETCH)
    return shifted[group, :, pl.ds(start, SPAN)]


def filter_rows(meta, shifted, group, slots):
    return jnp.concatenate(
        [
            jnp.concatenate([window(meta, shifted, group, slot, w) for w in range(SENT)], axis=1)
            for slot in range(slots)
        ],
        axis=0,
    )


def rows_of(results, block):
    part = slice(block * GROUP_CH, (block + 1) * GROUP_CH)
    return jnp.concatenate([result[part] for result in results], axis=0).T


def last_rows_kernel(key, value, out):
    for start in range(0, out.shape[0], LANES):
        out[pl.ds(start, LANES), :] = product(key, value, 0, pl.ds(start, LANES))


def last_rows(key_proj, value_proj):
    row_count, channels = key_proj.shape
    block = pl.BlockSpec((STRETCH, channels), lambda i: (row_count // STRETCH - 1, 0))
    operands = [pltpu.with_memory_space_constraint(x, pltpu.HBM) for x in (key_proj, value_proj)]
    return pl.pallas_call(
        last_rows_kernel,
        grid=(1,),
        in_specs=[block, block],
        out_specs=pl.BlockSpec((channels, STRETCH), lambda i: (0, 0)),
        out_shape=jax.ShapeDtypeStruct((channels, STRETCH), jnp.bfloat16),
        compiler_params=params(),
        name="last_rows",
    )(*operands)


def last_term(slots, meta, last, shifted, term, spans):
    for start in range(0, last.shape[0], LANES):
        held = spans.at[start // LANES % 2]
        spread_rows(last[pl.ds(start, LANES), :], held, 0)
        results = [
            lax.dot_general(
                held[g],
                window(meta, shifted, start // GROUP_CH + g, slots - 1, SENT),
                NT,
                preferred_element_type=jnp.float32,
            )
            for g in range(BLOCKS)
        ]
        for m in range(BLOCKS):
            term[pl.ds(m * GROUP_CH, GROUP_CH), pl.ds(start, LANES)] = rows_of(results, m)


def spread_part(pieces, start, spans):
    for w in range(SENT):
        spread_rows(pieces[w, pl.ds(start, LANES), :], spans, w * SPAN)


def conv_part(filter_rows_of, base, start, term, query, out, result, spans, sem):
    slots = query.shape[0] // STRETCH
    columns = pl.ds(pl.multiple_of(base + start, LANES), LANES)
    results = [
        lax.dot_general(
            spans[g],
            filter_rows_of(start // GROUP_CH + g),
            NT,
            preferred_element_type=jnp.float32,
        )
        for g in range(BLOCKS)
    ]
    for m in range(BLOCKS):
        rows = rows_of(results, m)
        for slot in range(slots):
            place = pl.ds(slot * STRETCH + m * GROUP_CH, GROUP_CH)
            tile = rows[slot * GROUP_CH : (slot + 1) * GROUP_CH]
            if slot == slots - 1:
                tile = tile + term[pl.ds(m * GROUP_CH, GROUP_CH), columns]
            gates = query[place, columns].astype(jnp.float32)
            result[place, :] = (gates * tile).astype(jnp.bfloat16)
    store = pltpu.make_async_copy(result, out.at[:, columns], sem)
    store.start()
    return store


def part_base(step, size, width):
    me = lax.axis_index("seq")
    return pl.multiple_of((me ^ step if size > 1 else 0) * width, width)


def scratch(count, row_count):
    return [
        pltpu.VMEM((count, row_count, LANES), jnp.bfloat16),
        pltpu.VMEM((count, BLOCKS, LANES, SENT * SPAN), jnp.bfloat16),
        pltpu.SemaphoreType.DMA((count + 1,)),
    ]


def open_kernel(size, first, meta_in, last, pieces, query, *refs):
    filters = refs[:-9]
    shifted, term, out, reverse, meta, last_spans, result, spans, sems = refs[-9:]
    slots = query.shape[0] // STRETCH
    width = pieces.shape[1]
    scalars = pltpu.make_async_copy(meta_in, meta, sems.at[width // LANES])
    scalars.start()
    build_shifted(size, first, filters, reverse, shifted)
    scalars.wait()
    last_term(slots, meta, last, shifted, term, last_spans)
    base = part_base(0, out.shape[1] // width, width)
    stores = []
    for index, start in enumerate(range(0, width, LANES)):
        spread_part(pieces, start, spans.at[index])
        stores.append(
            conv_part(
                lambda group: filter_rows(meta, shifted, base // GROUP_CH + group, slots),
                base,
                start,
                term,
                query,
                out,
                result.at[index],
                spans.at[index],
                sems.at[index],
            )
        )
    for store in stores:
        store.wait()


def open_conv(size, first, meta, last, pieces, query_proj, group_count, lag_count, filters):
    row_count, channels = query_proj.shape
    padded = lag_count + SPAN
    return pl.pallas_call(
        functools.partial(open_kernel, size, first),
        in_specs=[ANY_SPEC] + [VMEM_SPEC] * (3 + len(filters)),
        out_specs=[VMEM_SPEC, VMEM_SPEC, HBM_SPEC],
        out_shape=[
            jax.ShapeDtypeStruct((group_count, GROUP_CH, padded), jnp.bfloat16),
            jax.ShapeDtypeStruct((STRETCH, channels), jnp.float32),
            jax.ShapeDtypeStruct((row_count, channels), jnp.bfloat16),
        ],
        scratch_shapes=[
            pltpu.VMEM((group_count, padded), jnp.float32),
            pltpu.SMEM(meta.shape, jnp.int32),
            pltpu.VMEM((2, BLOCKS, LANES, SPAN), jnp.bfloat16),
            *scratch(pieces.shape[1] // LANES, row_count),
        ],
        compiler_params=params(),
        name="open_conv",
    )(meta, last, pieces, query_proj, *filters)


def near_kernel(size, steps, next_step, meta_in, shifted, term, query, before, *refs):
    parts = refs[: len(steps)]
    out, ready, meta, result, spans, sems = refs[len(steps) :]
    slots = query.shape[0] // STRETCH
    width = parts[0].shape[1]
    places = [(index, start) for index in range(len(steps)) for start in range(0, width, LANES)]
    scalars = pltpu.make_async_copy(meta_in, meta, sems.at[len(places)])
    scalars.start()
    for number, (index, start) in enumerate(places[: len(places) // 2]):
        spread_part(parts[index], start, spans.at[number])
    scalars.wait()
    stores = []
    for number, (index, start) in enumerate(places):
        if number >= len(places) // 2:
            spread_part(parts[index], start, spans.at[number])
        base = part_base(steps[index], size, width)
        stores.append(
            conv_part(
                lambda group, base=base: filter_rows(meta, shifted, base // GROUP_CH + group, slots),
                base,
                start,
                term,
                query,
                out,
                result.at[number],
                spans.at[number],
                sems.at[number],
            )
        )
    base = part_base(next_step, size, width)
    for group in range(width // GROUP_CH):
        ready[group] = filter_rows(meta, shifted, base // GROUP_CH + group, slots)
    for store in stores:
        store.wait()


def near_conv(size, steps, next_step, meta, parts, shifted, term, query_proj, before):
    row_count, channels = query_proj.shape
    width = channels // size
    slots = row_count // STRETCH
    return pl.pallas_call(
        functools.partial(near_kernel, size, steps, next_step),
        in_specs=[ANY_SPEC] + [VMEM_SPEC] * 3 + [HBM_SPEC] + [VMEM_SPEC] * len(parts),
        out_specs=[HBM_SPEC, VMEM_SPEC],
        out_shape=[
            jax.ShapeDtypeStruct((row_count, channels), jnp.bfloat16),
            jax.ShapeDtypeStruct((width // GROUP_CH, slots * GROUP_CH, SENT * SPAN), jnp.bfloat16),
        ],
        input_output_aliases={4: 0},
        scratch_shapes=[
            pltpu.SMEM(meta.shape, jnp.int32),
            *scratch(len(parts) * width // LANES, row_count),
        ],
        compiler_params=params(),
        name="near_conv",
    )(meta, shifted, term, query_proj, before, *parts)


def far_kernel(size, step, pieces, ready, term, query, before, out, result, spans, sems):
    width = pieces.shape[1]
    base = part_base(step, size, width)
    stores = []
    for index, start in enumerate(range(0, width, LANES)):
        spread_part(pieces, start, spans.at[index])
        stores.append(
            conv_part(
                lambda group: ready[group],
                base,
                start,
                term,
                query,
                out,
                result.at[index],
                spans.at[index],
                sems.at[index],
            )
        )
    for store in stores:
        store.wait()


def far_conv(size, step, pieces, ready, term, query_proj, before):
    row_count, channels = query_proj.shape
    return pl.pallas_call(
        functools.partial(far_kernel, size, step),
        in_specs=[VMEM_SPEC] * 4 + [HBM_SPEC],
        out_specs=HBM_SPEC,
        out_shape=jax.ShapeDtypeStruct((row_count, channels), jnp.bfloat16),
        input_output_aliases={4: 0},
        scratch_shapes=scratch(pieces.shape[1] // LANES, row_count),
        compiler_params=params(),
        name="far_conv",
    )(pieces, ready, term, query_proj, before)


def shards(size, key_proj, value_proj, query_proj, filters, sources, owner):
    row_count, channels = key_proj.shape
    group_count, part = filters.shape
    lag_count = size * part
    tiles = part // LANES
    by_parts = size == 4 and channels % (size * LANES) == 0
    block = group_count * tiles
    filter_rows = [0, block, block, 0] if by_parts else [block]
    parts = len(filter_rows)
    width = channels // parts
    sends, extra, meta = gate(filter_rows, sources, owner, key_proj, value_proj, filters)
    last = last_rows(key_proj, value_proj)
    first = SLOTS * width
    if not by_parts:
        blocks = lax.all_gather(sends[0][first:], "seq")
        held = jnp.concatenate([sends[0][:first].reshape(SLOTS, width, LANES), extra])
        mine = (meta[:SENT] == lax.axis_index("seq"))[:, None, None]
        pieces = lax.psum(jnp.where(mine, held[meta[PLACE:MANY]], jnp.zeros_like(held)), "seq")
        return open_conv(
            size, tiles, meta, last, pieces, query_proj, group_count, lag_count, [blocks]
        )[2]

    def exchange(value, step):
        return lax.ppermute(value, "seq", [(z, z ^ step) for z in range(size)])

    far, near, cross = (exchange(sends[step], step) for step in STEPS[1:])
    cross_filters = exchange(pick(first, far), 1)
    last, cross_filters, cross = lax.optimization_barrier((last, cross_filters, cross))
    received = [sends[0], far, near, cross]

    def merge_more(meta, received, extra):
        more = [extra[0]] + [exchange(extra[step], step) for step in STEPS[1:]]
        return merge(width, meta, received, more)

    def merge_plain(meta, received, extra):
        return merge(width, meta, received)

    merged = lax.cond(meta[MANY] > 0, merge_more, merge_plain, meta, received, extra)
    far_part, near_part = exchange(merged, 2), exchange(merged, 1)
    shifted, term, out = open_conv(
        size,
        first,
        meta,
        last,
        merged,
        query_proj,
        group_count,
        lag_count,
        [filters, far, near, cross_filters],
    )
    far_part, out = lax.optimization_barrier((far_part, out))
    last_part = exchange(far_part, 1)
    out, ready = near_conv(
        size, (1, 2), 3, meta, [near_part, far_part], shifted, term, query_proj, out
    )
    return far_conv(size, 3, last_part, ready, term, query_proj, out)


def solution(mesh):
    return jax.shard_map(
        functools.partial(shards, mesh.shape["seq"]),
        mesh=mesh,
        in_specs=(
            P(("rep", "seq"), "ch"),
            P(("rep", "seq"), "ch"),
            P(("rep", "seq"), "ch"),
            P("ch", "seq"),
            P("rep"),
            P("rep"),
        ),
        out_specs=P(("rep", "seq"), "ch"),
        check_vma=False,
    )
```

```python
import functools

import jax
import jax.numpy as jnp
from jax import lax
from jax.experimental import pallas as pl
from jax.experimental.pallas import tpu as pltpu
from jax.sharding import PartitionSpec as P

GROUP_CH = 16
STRETCH = 128
WIN = 4
SENT = WIN - 1
LANES = 128
BLOCKS = LANES // GROUP_CH
SPAN = 2 * STRETCH
VMEM_LIMIT = 16 * 1024 * 1024

SMEM_SPEC = pl.BlockSpec(memory_space=pltpu.SMEM)
ANY_SPEC = pl.BlockSpec(memory_space=pl.ANY)
HBM_SPEC = pl.BlockSpec(memory_space=pltpu.HBM)
VMEM_SPEC = pl.BlockSpec(memory_space=pltpu.VMEM)
NT = (((1,), (1,)), ((), ()))


def params():
    return pltpu.CompilerParams(vmem_limit_bytes=VMEM_LIMIT)


STEPS = (0, 2, 1, 3)


PLACE = SENT
MANY = 2 * SENT
WINDOWS = MANY + 1
SLOTS = 2


def product(key, value, start, columns):
    rows = pl.ds(start, STRETCH)
    rows_k = key[rows, columns].astype(jnp.float32)
    rows_v = value[rows, columns].astype(jnp.float32)
    return (rows_k * rows_v).astype(jnp.bfloat16).T


def gate_kernel(parts, sources_in, owner_in, key_in, value_in, filters_in, *refs):
    sends = refs[:parts]
    extra, meta, sources, owner, key, value, filters, sems = refs[parts:]
    stretch_count = owner.shape[0]
    channels = key.shape[1]
    width = channels // parts
    me = lax.axis_index("seq")
    copies = [
        pltpu.make_async_copy(sources_in, sources, sems.at[0]),
        pltpu.make_async_copy(owner_in, owner, sems.at[1]),
        pltpu.make_async_copy(filters_in, filters, sems.at[2]),
    ]
    for start in range(0, key.shape[0], STRETCH):
        rows = pl.ds(start, STRETCH)
        for number, (held, array) in enumerate(((key_in, key), (value_in, value))):
            sem = sems.at[3 + start // STRETCH * 2 + number]
            copies.append(pltpu.make_async_copy(held.at[rows], array.at[rows], sem))
    for copy in copies:
        copy.start()
    for copy in copies[:2]:
        copy.wait()

    def target(k, slot):
        mine = owner[k] == me

        @pl.when(mine)
        def _():
            for w in range(WIN):
                lag_block = jnp.maximum(k - sources[w], -1)
                meta[WINDOWS + slot * WIN + w] = (stretch_count - 1 - lag_block) * STRETCH

        return slot + jnp.where(mine, 1, 0)

    lax.fori_loop(0, stretch_count, target, 0)
    copies[2].wait()
    group_count = filters.shape[0]
    for tile in range(filters.shape[1] // LANES):
        piece = filters[:, pl.ds(tile * LANES, LANES)]
        for send in sends:
            if send.shape[0] > SLOTS * width:
                send[pl.ds(SLOTS * width + tile * group_count, group_count), :] = piece
    for copy in copies[3:]:
        copy.wait()
    holders = [owner[sources[w]] for w in range(SENT)]
    many = 0
    for w, holder in enumerate(holders):
        place = sum([jnp.where(other == holder, 1, 0) for other in holders[:w]], 0)
        meta[w] = holder
        meta[PLACE + w] = place
        many = many + jnp.where(place >= SLOTS, 1, 0)

        @pl.when(holder == me)
        def _(w=w, holder=holder, place=place):
            def count(k, total):
                return total + jnp.where(owner[k] == holder, 1, 0)

            slot = lax.fori_loop(0, sources[w], count, 0)
            first = pl.multiple_of(slot * STRETCH, STRETCH)
            for step in range(parts):
                part = me ^ step if parts > 1 else 0
                base = part * width

                def fill(target, offset, base=base):
                    for start in range(0, width, LANES):
                        columns = pl.ds(pl.multiple_of(base + start, LANES), LANES)
                        target[pl.ds(offset + start, LANES), :] = product(key, value, first, columns)

                if w < SLOTS:
                    fill(sends[step], pl.multiple_of(place * width, LANES))
                else:

                    @pl.when(place < SLOTS)
                    def _(step=step, fill=fill):
                        fill(sends[step], pl.multiple_of(place * width, LANES))

                    @pl.when(place >= SLOTS)
                    def _(step=step, fill=fill):
                        fill(extra.at[step], 0)

    meta[MANY] = many


def gate(filter_rows, sources, owner, key_proj, value_proj, filters):
    row_count, channels = key_proj.shape
    slots = row_count // STRETCH
    parts = len(filter_rows)
    width = channels // parts
    operands = [
        pltpu.with_memory_space_constraint(operand, pltpu.HBM)
        for operand in (sources, owner, key_proj, value_proj, filters)
    ]
    *sends, extra, meta = pl.pallas_call(
        functools.partial(gate_kernel, parts),
        in_specs=[HBM_SPEC] * 5,
        out_specs=[VMEM_SPEC] * (parts + 1) + [SMEM_SPEC],
        out_shape=[
            jax.ShapeDtypeStruct((SLOTS * width + rows, LANES), jnp.bfloat16) for rows in filter_rows
        ]
        + [
            jax.ShapeDtypeStruct((parts, width, LANES), jnp.bfloat16),
            jax.ShapeDtypeStruct((WINDOWS + slots * WIN,), jnp.int32),
        ],
        scratch_shapes=[
            pltpu.SMEM(sources.shape, jnp.int32),
            pltpu.SMEM(owner.shape, jnp.int32),
            pltpu.VMEM(key_proj.shape, key_proj.dtype),
            pltpu.VMEM(value_proj.shape, value_proj.dtype),
            pltpu.VMEM(filters.shape, filters.dtype),
            pltpu.SemaphoreType.DMA((3 + 2 * slots,)),
        ],
        compiler_params=params(),
        name="gate",
    )(*operands)
    return sends, extra, meta


def merge_kernel(width, meta, *refs):
    received, extras, out = refs[: len(STEPS)], refs[len(STEPS) : -1], refs[-1]
    me = lax.axis_index("seq")

    for w in range(SENT):
        place = meta[PLACE + w]
        rows = pl.ds(pl.multiple_of(jnp.minimum(place, SLOTS - 1) * width, LANES), width)
        for block, step in zip(received, STEPS):

            @pl.when(me ^ step == meta[w])
            def _(w=w, block=block, rows=rows):
                out[w] = block[rows, :]

    for w in range(SLOTS, SENT):
        for extra, step in zip(extras, STEPS):

            @pl.when((me ^ step == meta[w]) & (meta[PLACE + w] >= SLOTS))
            def _(w=w, extra=extra):
                out[w] = extra[...]


def merge(width, meta, received, extras=()):
    return pl.pallas_call(
        functools.partial(merge_kernel, width),
        in_specs=[SMEM_SPEC] + [VMEM_SPEC] * (len(received) + len(extras)),
        out_specs=VMEM_SPEC,
        out_shape=jax.ShapeDtypeStruct((SENT, width, LANES), received[0].dtype),
        compiler_params=params(),
        name="merge",
    )(meta, *received, *extras)


def pick_kernel(first, received, out):
    out[...] = received[pl.ds(first, out.shape[0]), :]


def pick(first, received):
    return pl.pallas_call(
        functools.partial(pick_kernel, first),
        in_specs=[VMEM_SPEC],
        out_specs=VMEM_SPEC,
        out_shape=jax.ShapeDtypeStruct((received.shape[0] - first, LANES), received.dtype),
        compiler_params=params(),
        name="pick",
    )(received)


def lag_tiles(size, first, filters):
    if len(filters) == 1:
        blocks = filters[0]
        group_count = blocks.shape[1] // first
        for shard in range(size):
            for tile in range(first):
                rows = pl.ds(tile * group_count, group_count)
                yield shard * first + tile, blocks[shard, rows, :]
        return
    own, far, near, cross = filters
    me = lax.axis_index("seq")
    group_count = own.shape[0]
    tiles = own.shape[1] // LANES
    for tile in range(tiles):
        yield me * tiles + tile, own[:, pl.ds(tile * LANES, LANES)]
        for block, start, step in ((far, first, 2), (near, first, 1), (cross, 0, 3)):
            rows = pl.ds(start + tile * group_count, group_count)
            yield (me ^ step) * tiles + tile, block[rows, :]


def build_shifted(size, first, filters, reverse, shifted):
    group_count, padded = reverse.shape
    lag_count = padded - SPAN
    row = lax.broadcasted_iota(jnp.int32, (LANES, LANES), 0)
    column = lax.broadcasted_iota(jnp.int32, (LANES, LANES), 1)
    flip = jnp.where(row + column == LANES - 1, 1.0, 0.0).astype(jnp.bfloat16)
    for number, values in lag_tiles(size, first, filters):
        start = lag_count - LANES - number * LANES
        if not isinstance(start, int):
            start = pl.multiple_of(start, LANES)
        reverse[:, pl.ds(start, LANES)] = jnp.dot(
            values, flip, preferred_element_type=jnp.float32
        )
    reverse[:, pl.ds(lag_count, SPAN)] = jnp.zeros((group_count, SPAN), jnp.float32)
    inside = (
        lax.broadcasted_iota(jnp.int32, (GROUP_CH, LANES), 1)
        > lax.broadcasted_iota(jnp.int32, (GROUP_CH, LANES), 0)
    )

    @pl.loop(0, group_count // BLOCKS)
    def _(block):
        tile_rows = pl.ds(pl.multiple_of(block * BLOCKS, BLOCKS), BLOCKS)
        before = [jnp.zeros((GROUP_CH, LANES), jnp.float32)] * BLOCKS
        for start in range(0, padded, LANES):
            tile = reverse[tile_rows, pl.ds(start, LANES)]
            for g in range(BLOCKS):
                spread = jnp.broadcast_to(tile[g : g + 1, :], (GROUP_CH, LANES))
                rolled = pltpu.roll(spread, 1, 1, stride=1, stride_axis=0)
                shifted[block * BLOCKS + g, :, pl.ds(start, LANES)] = jnp.where(
                    inside, rolled, before[g]
                ).astype(jnp.bfloat16)
                before[g] = rolled


def spread_rows(tile, spans, base):
    lane = lax.broadcasted_iota(jnp.int16, tile.shape, 1)
    zero = jnp.zeros(tile.shape, tile.dtype)
    for i1 in range(BLOCKS):
        shift = GROUP_CH * i1
        if i1 == 0:
            low, high = zero, tile
        else:
            moved = pltpu.roll(tile, LANES - shift, 1)
            early = lane < LANES - shift
            low, high = jnp.where(early, zero, moved), jnp.where(early, moved, zero)
        rows = pl.ds(shift, GROUP_CH)
        for g in range(BLOCKS):
            part = slice(g * GROUP_CH, (g + 1) * GROUP_CH)
            spans[g, rows, pl.ds(base, LANES)] = low[part]
            spans[g, rows, pl.ds(base + LANES, LANES)] = high[part]


def window(meta, shifted, group, slot, w):
    start = pl.multiple_of(meta[WINDOWS + slot * WIN + w], STRETCH)
    return shifted[group, :, pl.ds(start, SPAN)]


def filter_rows(meta, shifted, group, slots):
    return jnp.concatenate(
        [
            jnp.concatenate([window(meta, shifted, group, slot, w) for w in range(SENT)], axis=1)
            for slot in range(slots)
        ],
        axis=0,
    )


def rows_of(results, block):
    part = slice(block * GROUP_CH, (block + 1) * GROUP_CH)
    return jnp.concatenate([result[part] for result in results], axis=0).T


def last_rows_kernel(key, value, out):
    for start in range(0, out.shape[0], LANES):
        out[pl.ds(start, LANES), :] = product(key, value, 0, pl.ds(start, LANES))


def last_rows(key_proj, value_proj):
    row_count, channels = key_proj.shape
    block = pl.BlockSpec((STRETCH, channels), lambda i: (row_count // STRETCH - 1, 0))
    operands = [pltpu.with_memory_space_constraint(x, pltpu.HBM) for x in (key_proj, value_proj)]
    return pl.pallas_call(
        last_rows_kernel,
        grid=(1,),
        in_specs=[block, block],
        out_specs=pl.BlockSpec((channels, STRETCH), lambda i: (0, 0)),
        out_shape=jax.ShapeDtypeStruct((channels, STRETCH), jnp.bfloat16),
        compiler_params=params(),
        name="last_rows",
    )(*operands)


def last_term(slots, meta, last, shifted, term, spans):
    for start in range(0, last.shape[0], LANES):
        held = spans.at[start // LANES % 2]
        spread_rows(last[pl.ds(start, LANES), :], held, 0)
        results = [
            lax.dot_general(
                held[g],
                window(meta, shifted, start // GROUP_CH + g, slots - 1, SENT),
                NT,
                preferred_element_type=jnp.float32,
            )
            for g in range(BLOCKS)
        ]
        for m in range(BLOCKS):
            term[pl.ds(m * GROUP_CH, GROUP_CH), pl.ds(start, LANES)] = rows_of(results, m)


def spread_part(pieces, start, spans):
    for w in range(SENT):
        spread_rows(pieces[w, pl.ds(start, LANES), :], spans, w * SPAN)


def conv_part(filter_rows_of, base, start, term, query, out, result, spans, sem):
    slots = query.shape[0] // STRETCH
    columns = pl.ds(pl.multiple_of(base + start, LANES), LANES)
    results = [
        lax.dot_general(
            spans[g],
            filter_rows_of(start // GROUP_CH + g),
            NT,
            preferred_element_type=jnp.float32,
        )
        for g in range(BLOCKS)
    ]
    for m in range(BLOCKS):
        rows = rows_of(results, m)
        for slot in range(slots):
            place = pl.ds(slot * STRETCH + m * GROUP_CH, GROUP_CH)
            tile = rows[slot * GROUP_CH : (slot + 1) * GROUP_CH]
            if slot == slots - 1:
                tile = tile + term[pl.ds(m * GROUP_CH, GROUP_CH), columns]
            gates = query[place, columns].astype(jnp.float32)
            result[place, :] = (gates * tile).astype(jnp.bfloat16)
    stores = []
    for slot in range(slots):
        place = pl.ds(slot * STRETCH, STRETCH)
        store = pltpu.make_async_copy(result.at[place], out.at[place, columns], sem.at[slot])
        store.start()
        stores.append(store)
    return stores


def part_base(step, size, width):
    me = lax.axis_index("seq")
    return pl.multiple_of((me ^ step if size > 1 else 0) * width, width)


def scratch(count, row_count):
    return [
        pltpu.VMEM((count, row_count, LANES), jnp.bfloat16),
        pltpu.VMEM((count, BLOCKS, LANES, SENT * SPAN), jnp.bfloat16),
        pltpu.SemaphoreType.DMA((count + 1, row_count // STRETCH)),
    ]


def open_kernel(size, first, meta_in, last, pieces, query, *refs):
    filters = refs[:-9]
    shifted, term, out, reverse, meta, last_spans, result, spans, sems = refs[-9:]
    slots = query.shape[0] // STRETCH
    width = pieces.shape[1]
    scalars = pltpu.make_async_copy(meta_in, meta, sems.at[width // LANES, 0])
    scalars.start()
    build_shifted(size, first, filters, reverse, shifted)
    scalars.wait()
    last_term(slots, meta, last, shifted, term, last_spans)
    base = part_base(0, out.shape[1] // width, width)
    stores = []
    for index, start in enumerate(range(0, width, LANES)):
        spread_part(pieces, start, spans.at[index])
        stores.extend(
            conv_part(
                lambda group: filter_rows(meta, shifted, base // GROUP_CH + group, slots),
                base,
                start,
                term,
                query,
                out,
                result.at[index],
                spans.at[index],
                sems.at[index],
            )
        )
    for store in stores:
        store.wait()


def open_conv(size, first, meta, last, pieces, query_proj, group_count, lag_count, filters):
    row_count, channels = query_proj.shape
    padded = lag_count + SPAN
    return pl.pallas_call(
        functools.partial(open_kernel, size, first),
        in_specs=[ANY_SPEC] + [VMEM_SPEC] * (3 + len(filters)),
        out_specs=[VMEM_SPEC, VMEM_SPEC, HBM_SPEC],
        out_shape=[
            jax.ShapeDtypeStruct((group_count, GROUP_CH, padded), jnp.bfloat16),
            jax.ShapeDtypeStruct((STRETCH, channels), jnp.float32),
            jax.ShapeDtypeStruct((row_count, channels), jnp.bfloat16),
        ],
        scratch_shapes=[
            pltpu.VMEM((group_count, padded), jnp.float32),
            pltpu.SMEM(meta.shape, jnp.int32),
            pltpu.VMEM((2, BLOCKS, LANES, SPAN), jnp.bfloat16),
            *scratch(pieces.shape[1] // LANES, row_count),
        ],
        compiler_params=params(),
        name="open_conv",
    )(meta, last, pieces, query_proj, *filters)


def near_kernel(size, steps, next_step, meta_in, shifted, term, query, before, *refs):
    parts = refs[: len(steps)]
    out, ready, meta, result, spans, sems = refs[len(steps) :]
    slots = query.shape[0] // STRETCH
    width = parts[0].shape[1]
    places = [(index, start) for index in range(len(steps)) for start in range(0, width, LANES)]
    scalars = pltpu.make_async_copy(meta_in, meta, sems.at[len(places), 0])
    scalars.start()
    for number, (index, start) in enumerate(places[: len(places) // 2]):
        spread_part(parts[index], start, spans.at[number])
    scalars.wait()
    stores = []
    for number, (index, start) in enumerate(places):
        if number >= len(places) // 2:
            spread_part(parts[index], start, spans.at[number])
        base = part_base(steps[index], size, width)
        stores.extend(
            conv_part(
                lambda group, base=base: filter_rows(meta, shifted, base // GROUP_CH + group, slots),
                base,
                start,
                term,
                query,
                out,
                result.at[number],
                spans.at[number],
                sems.at[number],
            )
        )
    base = part_base(next_step, size, width)
    for group in range(width // GROUP_CH):
        ready[group] = filter_rows(meta, shifted, base // GROUP_CH + group, slots)
    for store in stores:
        store.wait()


def near_conv(size, steps, next_step, meta, parts, shifted, term, query_proj, before):
    row_count, channels = query_proj.shape
    width = channels // size
    slots = row_count // STRETCH
    return pl.pallas_call(
        functools.partial(near_kernel, size, steps, next_step),
        in_specs=[ANY_SPEC] + [VMEM_SPEC] * 3 + [HBM_SPEC] + [VMEM_SPEC] * len(parts),
        out_specs=[HBM_SPEC, VMEM_SPEC],
        out_shape=[
            jax.ShapeDtypeStruct((row_count, channels), jnp.bfloat16),
            jax.ShapeDtypeStruct((width // GROUP_CH, slots * GROUP_CH, SENT * SPAN), jnp.bfloat16),
        ],
        input_output_aliases={4: 0},
        scratch_shapes=[
            pltpu.SMEM(meta.shape, jnp.int32),
            *scratch(len(parts) * width // LANES, row_count),
        ],
        compiler_params=params(),
        name="near_conv",
    )(meta, shifted, term, query_proj, before, *parts)


def far_kernel(size, step, pieces, ready, term, query, before, out, result, spans, sems):
    width = pieces.shape[1]
    base = part_base(step, size, width)
    stores = []
    for index, start in enumerate(range(0, width, LANES)):
        spread_part(pieces, start, spans.at[index])
        stores.extend(
            conv_part(
                lambda group: ready[group],
                base,
                start,
                term,
                query,
                out,
                result.at[index],
                spans.at[index],
                sems.at[index],
            )
        )
    for store in stores:
        store.wait()


def far_conv(size, step, pieces, ready, term, query_proj, before):
    row_count, channels = query_proj.shape
    return pl.pallas_call(
        functools.partial(far_kernel, size, step),
        in_specs=[VMEM_SPEC] * 4 + [HBM_SPEC],
        out_specs=HBM_SPEC,
        out_shape=jax.ShapeDtypeStruct((row_count, channels), jnp.bfloat16),
        input_output_aliases={4: 0},
        scratch_shapes=scratch(pieces.shape[1] // LANES, row_count),
        compiler_params=params(),
        name="far_conv",
    )(pieces, ready, term, query_proj, before)


def shards(size, key_proj, value_proj, query_proj, filters, sources, owner):
    row_count, channels = key_proj.shape
    group_count, part = filters.shape
    lag_count = size * part
    tiles = part // LANES
    by_parts = size == 4 and channels % (size * LANES) == 0
    block = group_count * tiles
    filter_rows = [0, block, block, 0] if by_parts else [block]
    parts = len(filter_rows)
    width = channels // parts
    operands = [
        pltpu.with_memory_space_constraint(operand, pltpu.HBM)
        for operand in (sources, owner, key_proj, value_proj, filters)
    ]
    *sends, extra, meta = pl.pallas_call(
        functools.partial(gate_kernel, parts),
        in_specs=[HBM_SPEC] * 5,
        out_specs=[VMEM_SPEC] * (parts + 1) + [SMEM_SPEC],
        out_shape=[
            jax.ShapeDtypeStruct((SLOTS * width + rows, LANES), jnp.bfloat16) for rows in filter_rows
        ]
        + [
            jax.ShapeDtypeStruct((parts, width, LANES), jnp.bfloat16),
            jax.ShapeDtypeStruct((WINDOWS + slots * WIN,), jnp.int32),
        ],
        scratch_shapes=[
            pltpu.SMEM(sources.shape, jnp.int32),
            pltpu.SMEM(owner.shape, jnp.int32),
            pltpu.VMEM(key_proj.shape, key_proj.dtype),
            pltpu.VMEM(value_proj.shape, value_proj.dtype),
            pltpu.VMEM(filters.shape, filters.dtype),
            pltpu.SemaphoreType.DMA((3 + 2 * slots,)),
        ],
        compiler_params=params(),
        name="gate",
    )(*operands)
    return sends, extra, meta


def merge_kernel(width, meta, *refs):
    received, extras, out = refs[: len(STEPS)], refs[len(STEPS) : -1], refs[-1]
    me = lax.axis_index("seq")

    for w in range(SENT):
        place = meta[PLACE + w]
        rows = pl.ds(pl.multiple_of(jnp.minimum(place, SLOTS - 1) * width, LANES), width)
        for block, step in zip(received, STEPS):

            @pl.when(me ^ step == meta[w])
            def _(w=w, block=block, rows=rows):
                out[w] = block[rows, :]

    for w in range(SLOTS, SENT):
        for extra, step in zip(extras, STEPS):

            @pl.when((me ^ step == meta[w]) & (meta[PLACE + w] >= SLOTS))
            def _(w=w, extra=extra):
                out[w] = extra[...]


def merge(width, meta, received, extras=()):
    return pl.pallas_call(
        functools.partial(merge_kernel, width),
        in_specs=[SMEM_SPEC] + [VMEM_SPEC] * (len(received) + len(extras)),
        out_specs=VMEM_SPEC,
        out_shape=jax.ShapeDtypeStruct((SENT, width, LANES), received[0].dtype),
        compiler_params=params(),
        name="merge",
    )(meta, *received, *extras)


def pick_kernel(first, received, out):
    out[...] = received[pl.ds(first, out.shape[0]), :]


def pick(first, received):
    return pl.pallas_call(
        functools.partial(pick_kernel, first),
        in_specs=[VMEM_SPEC],
        out_specs=VMEM_SPEC,
        out_shape=jax.ShapeDtypeStruct((received.shape[0] - first, LANES), received.dtype),
        compiler_params=params(),
        name="pick",
    )(received)


def lag_tiles(size, first, filters):
    if len(filters) == 1:
        blocks = filters[0]
        group_count = blocks.shape[1] // first
        for shard in range(size):
            for tile in range(first):
                rows = pl.ds(tile * group_count, group_count)
                yield shard * first + tile, blocks[shard, rows, :]
        return
    own, far, near, cross = filters
    me = lax.axis_index("seq")
    group_count = own.shape[0]
    tiles = own.shape[1] // LANES
    for tile in range(tiles):
        yield me * tiles + tile, own[:, pl.ds(tile * LANES, LANES)]
        for block, start, step in ((far, first, 2), (near, first, 1), (cross, 0, 3)):
            rows = pl.ds(start + tile * group_count, group_count)
            yield (me ^ step) * tiles + tile, block[rows, :]


def build_shifted(size, first, filters, reverse, shifted):
    group_count, padded = reverse.shape
    lag_count = padded - SPAN
    row = lax.broadcasted_iota(jnp.int32, (LANES, LANES), 0)
    column = lax.broadcasted_iota(jnp.int32, (LANES, LANES), 1)
    flip = jnp.where(row + column == LANES - 1, 1.0, 0.0).astype(jnp.bfloat16)
    for number, values in lag_tiles(size, first, filters):
        start = lag_count - LANES - number * LANES
        if not isinstance(start, int):
            start = pl.multiple_of(start, LANES)
        reverse[:, pl.ds(start, LANES)] = jnp.dot(
            values, flip, preferred_element_type=jnp.float32
        )
    reverse[:, pl.ds(lag_count, SPAN)] = jnp.zeros((group_count, SPAN), jnp.float32)
    inside = (
        lax.broadcasted_iota(jnp.int32, (GROUP_CH, LANES), 1)
        > lax.broadcasted_iota(jnp.int32, (GROUP_CH, LANES), 0)
    )

    @pl.loop(0, group_count // BLOCKS)
    def _(block):
        tile_rows = pl.ds(pl.multiple_of(block * BLOCKS, BLOCKS), BLOCKS)
        before = [jnp.zeros((GROUP_CH, LANES), jnp.float32)] * BLOCKS
        for start in range(0, padded, LANES):
            tile = reverse[tile_rows, pl.ds(start, LANES)]
            for g in range(BLOCKS):
                spread = jnp.broadcast_to(tile[g : g + 1, :], (GROUP_CH, LANES))
                rolled = pltpu.roll(spread, 1, 1, stride=1, stride_axis=0)
                shifted[block * BLOCKS + g, :, pl.ds(start, LANES)] = jnp.where(
                    inside, rolled, before[g]
                ).astype(jnp.bfloat16)
                before[g] = rolled


def spread_rows(tile, spans, base):
    lane = lax.broadcasted_iota(jnp.int16, tile.shape, 1)
    zero = jnp.zeros(tile.shape, tile.dtype)
    for i1 in range(BLOCKS):
        shift = GROUP_CH * i1
        if i1 == 0:
            low, high = zero, tile
        else:
            moved = pltpu.roll(tile, LANES - shift, 1)
            early = lane < LANES - shift
            low, high = jnp.where(early, zero, moved), jnp.where(early, moved, zero)
        rows = pl.ds(shift, GROUP_CH)
        for g in range(BLOCKS):
            part = slice(g * GROUP_CH, (g + 1) * GROUP_CH)
            spans[g, rows, pl.ds(base, LANES)] = low[part]
            spans[g, rows, pl.ds(base + LANES, LANES)] = high[part]


def window(meta, shifted, group, slot, w):
    start = pl.multiple_of(meta[WINDOWS + slot * WIN + w], STRETCH)
    return shifted[group, :, pl.ds(start, SPAN)]


def filter_rows(meta, shifted, group, slots):
    return jnp.concatenate(
        [
            jnp.concatenate([window(meta, shifted, group, slot, w) for w in range(SENT)], axis=1)
            for slot in range(slots)
        ],
        axis=0,
    )


def rows_of(results, block):
    part = slice(block * GROUP_CH, (block + 1) * GROUP_CH)
    return jnp.concatenate([result[part] for result in results], axis=0).T


def last_rows_kernel(key, value, out):
    for start in range(0, out.shape[0], LANES):
        out[pl.ds(start, LANES), :] = product(key, value, 0, pl.ds(start, LANES))


def last_rows(key_proj, value_proj):
    row_count, channels = key_proj.shape
    block = pl.BlockSpec((STRETCH, channels), lambda i: (row_count // STRETCH - 1, 0))
    operands = [pltpu.with_memory_space_constraint(x, pltpu.HBM) for x in (key_proj, value_proj)]
    return pl.pallas_call(
        last_rows_kernel,
        grid=(1,),
        in_specs=[block, block],
        out_specs=pl.BlockSpec((channels, STRETCH), lambda i: (0, 0)),
        out_shape=jax.ShapeDtypeStruct((channels, STRETCH), jnp.bfloat16),
        compiler_params=params(),
        name="last_rows",
    )(*operands)


def last_term(slots, meta, last, shifted, term, spans):
    for start in range(0, last.shape[0], LANES):
        held = spans.at[start // LANES % 2]
        spread_rows(last[pl.ds(start, LANES), :], held, 0)
        results = [
            lax.dot_general(
                held[g],
                window(meta, shifted, start // GROUP_CH + g, slots - 1, SENT),
                NT,
                preferred_element_type=jnp.float32,
            )
            for g in range(BLOCKS)
        ]
        for m in range(BLOCKS):
            term[pl.ds(m * GROUP_CH, GROUP_CH), pl.ds(start, LANES)] = rows_of(results, m)


def spread_part(pieces, start, spans):
    for w in range(SENT):
        spread_rows(pieces[w, pl.ds(start, LANES), :], spans, w * SPAN)


def conv_part(filter_rows_of, base, start, term, query, out, result, spans, sem):
    slots = query.shape[0] // STRETCH
    columns = pl.ds(pl.multiple_of(base + start, LANES), LANES)
    results = [
        lax.dot_general(
            spans[g],
            filter_rows_of(start // GROUP_CH + g),
            NT,
            preferred_element_type=jnp.float32,
        )
        for g in range(BLOCKS)
    ]
    for m in range(BLOCKS):
        rows = rows_of(results, m)
        for slot in range(slots):
            place = pl.ds(slot * STRETCH + m * GROUP_CH, GROUP_CH)
            tile = rows[slot * GROUP_CH : (slot + 1) * GROUP_CH]
            if slot == slots - 1:
                tile = tile + term[pl.ds(m * GROUP_CH, GROUP_CH), columns]
            gates = query[place, columns].astype(jnp.float32)
            result[place, :] = (gates * tile).astype(jnp.bfloat16)
    stores = []
    for slot in range(slots):
        place = pl.ds(slot * STRETCH, STRETCH)
        store = pltpu.make_async_copy(result.at[place], out.at[place, columns], sem.at[slot])
        store.start()
        stores.append(store)
    return stores


def part_base(step, size, width):
    me = lax.axis_index("seq")
    return pl.multiple_of((me ^ step if size > 1 else 0) * width, width)


def scratch(count, row_count):
    return [
        pltpu.VMEM((count, row_count, LANES), jnp.bfloat16),
        pltpu.VMEM((count, BLOCKS, LANES, SENT * SPAN), jnp.bfloat16),
        pltpu.SemaphoreType.DMA((count + 1, row_count // STRETCH)),
    ]


def open_kernel(size, first, meta_in, last, pieces, query, *refs):
    filters = refs[:-9]
    shifted, term, out, reverse, meta, last_spans, result, spans, sems = refs[-9:]
    slots = query.shape[0] // STRETCH
    width = pieces.shape[1]
    scalars = pltpu.make_async_copy(meta_in, meta, sems.at[width // LANES, 0])
    scalars.start()
    build_shifted(size, first, filters, reverse, shifted)
    scalars.wait()
    last_term(slots, meta, last, shifted, term, last_spans)
    base = part_base(0, out.shape[1] // width, width)
    stores = []
    for index, start in enumerate(range(0, width, LANES)):
        spread_part(pieces, start, spans.at[index])
        stores.extend(
            conv_part(
                lambda group: filter_rows(meta, shifted, base // GROUP_CH + group, slots),
                base,
                start,
                term,
                query,
                out,
                result.at[index],
                spans.at[index],
                sems.at[index],
            )
        )
    for store in stores:
        store.wait()


def open_conv(size, first, meta, last, pieces, query_proj, group_count, lag_count, filters):
    row_count, channels = query_proj.shape
    padded = lag_count + SPAN
    return pl.pallas_call(
        functools.partial(open_kernel, size, first),
        in_specs=[ANY_SPEC] + [VMEM_SPEC] * (3 + len(filters)),
        out_specs=[VMEM_SPEC, VMEM_SPEC, HBM_SPEC],
        out_shape=[
            jax.ShapeDtypeStruct((group_count, GROUP_CH, padded), jnp.bfloat16),
            jax.ShapeDtypeStruct((STRETCH, channels), jnp.float32),
            jax.ShapeDtypeStruct((row_count, channels), jnp.bfloat16),
        ],
        scratch_shapes=[
            pltpu.VMEM((group_count, padded), jnp.float32),
            pltpu.SMEM(meta.shape, jnp.int32),
            pltpu.VMEM((2, BLOCKS, LANES, SPAN), jnp.bfloat16),
            *scratch(pieces.shape[1] // LANES, row_count),
        ],
        compiler_params=params(),
        name="open_conv",
    )(meta, last, pieces, query_proj, *filters)


def near_kernel(size, steps, next_step, meta_in, shifted, term, query, before, *refs):
    parts = refs[: len(steps)]
    out, ready, meta, result, spans, sems = refs[len(steps) :]
    slots = query.shape[0] // STRETCH
    width = parts[0].shape[1]
    places = [(index, start) for index in range(len(steps)) for start in range(0, width, LANES)]
    scalars = pltpu.make_async_copy(meta_in, meta, sems.at[len(places), 0])
    scalars.start()
    for number, (index, start) in enumerate(places[: len(places) // 2]):
        spread_part(parts[index], start, spans.at[number])
    scalars.wait()
    stores = []
    for number, (index, start) in enumerate(places):
        if number >= len(places) // 2:
            spread_part(parts[index], start, spans.at[number])
        base = part_base(steps[index], size, width)
        stores.extend(
            conv_part(
                lambda group, base=base: filter_rows(meta, shifted, base // GROUP_CH + group, slots),
                base,
                start,
                term,
                query,
                out,
                result.at[number],
                spans.at[number],
                sems.at[number],
            )
        )
    base = part_base(next_step, size, width)
    for group in range(width // GROUP_CH):
        ready[group] = filter_rows(meta, shifted, base // GROUP_CH + group, slots)
    for store in stores:
        store.wait()


def near_conv(size, steps, next_step, meta, parts, shifted, term, query_proj, before):
    row_count, channels = query_proj.shape
    width = channels // size
    slots = row_count // STRETCH
    return pl.pallas_call(
        functools.partial(near_kernel, size, steps, next_step),
        in_specs=[ANY_SPEC] + [VMEM_SPEC] * 3 + [HBM_SPEC] + [VMEM_SPEC] * len(parts),
        out_specs=[HBM_SPEC, VMEM_SPEC],
        out_shape=[
            jax.ShapeDtypeStruct((row_count, channels), jnp.bfloat16),
            jax.ShapeDtypeStruct((width // GROUP_CH, slots * GROUP_CH, SENT * SPAN), jnp.bfloat16),
        ],
        input_output_aliases={4: 0},
        scratch_shapes=[
            pltpu.SMEM(meta.shape, jnp.int32),
            *scratch(len(parts) * width // LANES, row_count),
        ],
        compiler_params=params(),
        name="near_conv",
    )(meta, shifted, term, query_proj, before, *parts)


def far_kernel(size, step, pieces, ready, term, query, before, out, result, spans, sems):
    width = pieces.shape[1]
    base = part_base(step, size, width)
    stores = []
    for index, start in enumerate(range(0, width, LANES)):
        spread_part(pieces, start, spans.at[index])
        stores.extend(
            conv_part(
                lambda group: ready[group],
                base,
                start,
                term,
                query,
                out,
                result.at[index],
                spans.at[index],
                sems.at[index],
            )
        )
    for store in stores:
        store.wait()


def far_conv(size, step, pieces, ready, term, query_proj, before):
    row_count, channels = query_proj.shape
    return pl.pallas_call(
        functools.partial(far_kernel, size, step),
        in_specs=[VMEM_SPEC] * 4 + [HBM_SPEC],
        out_specs=HBM_SPEC,
        out_shape=jax.ShapeDtypeStruct((row_count, channels), jnp.bfloat16),
        input_output_aliases={4: 0},
        scratch_shapes=scratch(pieces.shape[1] // LANES, row_count),
        compiler_params=params(),
        name="far_conv",
    )(pieces, ready, term, query_proj, before)


def shards(size, key_proj, value_proj, query_proj, filters, sources, owner):
    row_count, channels = key_proj.shape
    group_count, part = filters.shape
    lag_count = size * part
    tiles = part // LANES
    by_parts = size == 4 and channels % (size * LANES) == 0
    block = group_count * tiles
    filter_rows = [0, block, block, 0] if by_parts else [block]
    parts = len(filter_rows)
    width = channels // parts
    sends, extra, meta = gate(filter_rows, sources, owner, key_proj, value_proj, filters)
    last = last_rows(key_proj, value_proj)
    first = SLOTS * width
    if not by_parts:
        blocks = lax.all_gather(sends[0][first:], "seq")
        held = jnp.concatenate([sends[0][:first].reshape(SLOTS, width, LANES), extra])
        mine = (meta[:SENT] == lax.axis_index("seq"))[:, None, None]
        pieces = lax.psum(jnp.where(mine, held[meta[PLACE:MANY]], jnp.zeros_like(held)), "seq")
        return open_conv(
            size, tiles, meta, last, pieces, query_proj, group_count, lag_count, [blocks]
        )[2]

    def exchange(value, step):
        return lax.ppermute(value, "seq", [(z, z ^ step) for z in range(size)])

    far, near, cross = (exchange(sends[step], step) for step in STEPS[1:])
    cross_filters = exchange(pick(first, far), 1)
    last, cross_filters, cross = lax.optimization_barrier((last, cross_filters, cross))
    received = [sends[0], far, near, cross]

    def merge_more(meta, received, extra):
        more = [extra[0]] + [exchange(extra[step], step) for step in STEPS[1:]]
        return merge(width, meta, received, more)

    def merge_plain(meta, received, extra):
        return merge(width, meta, received)

    merged = lax.cond(meta[MANY] > 0, merge_more, merge_plain, meta, received, extra)
    far_part, near_part = exchange(merged, 2), exchange(merged, 1)
    shifted, term, out = open_conv(
        size,
        first,
        meta,
        last,
        merged,
        query_proj,
        group_count,
        lag_count,
        [filters, far, near, cross_filters],
    )
    far_part, out = lax.optimization_barrier((far_part, out))
    last_part = exchange(far_part, 1)
    out, ready = near_conv(
        size, (1, 2), 3, meta, [near_part, far_part], shifted, term, query_proj, out
    )
    return far_conv(size, 3, last_part, ready, term, query_proj, out)


def solution(mesh):
    return jax.shard_map(
        functools.partial(shards, mesh.shape["seq"]),
        mesh=mesh,
        in_specs=(
            P(("rep", "seq"), "ch"),
            P(("rep", "seq"), "ch"),
            P(("rep", "seq"), "ch"),
            P("ch", "seq"),
            P("rep"),
            P("rep"),
        ),
        out_specs=P(("rep", "seq"), "ch"),
        check_vma=False,
    )
```

```python
import functools

import jax
import jax.numpy as jnp
from jax import lax
from jax.experimental import pallas as pl
from jax.experimental.pallas import tpu as pltpu
from jax.sharding import PartitionSpec as P

GROUP_CH = 16
STRETCH = 128
WIN = 4
SENT = WIN - 1
LANES = 128
BLOCKS = LANES // GROUP_CH
SPAN = 2 * STRETCH
VMEM_LIMIT = 16 * 1024 * 1024

SMEM_SPEC = pl.BlockSpec(memory_space=pltpu.SMEM)
ANY_SPEC = pl.BlockSpec(memory_space=pl.ANY)
HBM_SPEC = pl.BlockSpec(memory_space=pltpu.HBM)
VMEM_SPEC = pl.BlockSpec(memory_space=pltpu.VMEM)
NT = (((1,), (1,)), ((), ()))


def params():
    return pltpu.CompilerParams(vmem_limit_bytes=VMEM_LIMIT)


STEPS = (0, 2, 1, 3)


PLACE = SENT
MANY = 2 * SENT
WINDOWS = MANY + 1
SLOTS = 2


def product(key, value, start, columns):
    rows = pl.ds(start, STRETCH)
    rows_k = key[rows, columns].astype(jnp.float32)
    rows_v = value[rows, columns].astype(jnp.float32)
    return (rows_k * rows_v).astype(jnp.bfloat16).T


def gate_kernel(parts, sources_in, owner_in, key_in, value_in, filters_in, *refs):
    sends = refs[:parts]
    extra, meta, sources, owner, key, value, filters, sems = refs[parts:]
    stretch_count = owner.shape[0]
    channels = key.shape[1]
    width = channels // parts
    me = lax.axis_index("seq")
    copies = [
        pltpu.make_async_copy(sources_in, sources, sems.at[0]),
        pltpu.make_async_copy(owner_in, owner, sems.at[1]),
        pltpu.make_async_copy(key_in, key, sems.at[2]),
        pltpu.make_async_copy(value_in, value, sems.at[3]),
        pltpu.make_async_copy(filters_in, filters, sems.at[4]),
    ]
    for copy in copies:
        copy.start()

    for copy in copies[:2]:
        copy.wait()

    def target(k, slot):
        mine = owner[k] == me

        @pl.when(mine)
        def _():
            for w in range(WIN):
                lag_block = jnp.maximum(k - sources[w], -1)
                meta[WINDOWS + slot * WIN + w] = (stretch_count - 1 - lag_block) * STRETCH

        return slot + jnp.where(mine, 1, 0)

    lax.fori_loop(0, stretch_count, target, 0)
    for copy in copies[2:]:
        copy.wait()
    holders = [owner[sources[w]] for w in range(SENT)]
    many = 0
    for w, holder in enumerate(holders):
        place = sum([jnp.where(other == holder, 1, 0) for other in holders[:w]], 0)
        meta[w] = holder
        meta[PLACE + w] = place
        many = many + jnp.where(place >= SLOTS, 1, 0)

        @pl.when(holder == me)
        def _(w=w, holder=holder, place=place):
            def count(k, total):
                return total + jnp.where(owner[k] == holder, 1, 0)

            slot = lax.fori_loop(0, sources[w], count, 0)
            first = pl.multiple_of(slot * STRETCH, STRETCH)
            for step in range(parts):
                part = me ^ step if parts > 1 else 0
                base = part * width

                def fill(target, offset, base=base):
                    for start in range(0, width, LANES):
                        columns = pl.ds(pl.multiple_of(base + start, LANES), LANES)
                        target[pl.ds(offset + start, LANES), :] = product(key, value, first, columns)

                if w < SLOTS:
                    fill(sends[step], pl.multiple_of(place * width, LANES))
                else:

                    @pl.when(place < SLOTS)
                    def _(step=step, fill=fill):
                        fill(sends[step], pl.multiple_of(place * width, LANES))

                    @pl.when(place >= SLOTS)
                    def _(step=step, fill=fill):
                        fill(extra.at[step], 0)

    meta[MANY] = many
    group_count = filters.shape[0]
    for tile in range(filters.shape[1] // LANES):
        piece = filters[:, pl.ds(tile * LANES, LANES)]
        for send in sends:
            if send.shape[0] > SLOTS * width:
                send[pl.ds(SLOTS * width + tile * group_count, group_count), :] = piece


def gate(filter_rows, sources, owner, key_proj, value_proj, filters):
    row_count, channels = key_proj.shape
    slots = row_count // STRETCH
    parts = len(filter_rows)
    width = channels // parts
    operands = [
        pltpu.with_memory_space_constraint(operand, pltpu.HBM)
        for operand in (sources, owner, key_proj, value_proj, filters)
    ]
    *sends, extra, meta = pl.pallas_call(
        functools.partial(gate_kernel, parts),
        in_specs=[HBM_SPEC] * 5,
        out_specs=[VMEM_SPEC] * (parts + 1) + [SMEM_SPEC],
        out_shape=[
            jax.ShapeDtypeStruct((SLOTS * width + rows, LANES), jnp.bfloat16) for rows in filter_rows
        ]
        + [
            jax.ShapeDtypeStruct((parts, width, LANES), jnp.bfloat16),
            jax.ShapeDtypeStruct((WINDOWS + slots * WIN,), jnp.int32),
        ],
        scratch_shapes=[
            pltpu.SMEM(sources.shape, jnp.int32),
            pltpu.SMEM(owner.shape, jnp.int32),
            pltpu.VMEM(key_proj.shape, key_proj.dtype),
            pltpu.VMEM(value_proj.shape, value_proj.dtype),
            pltpu.VMEM(filters.shape, filters.dtype),
            pltpu.SemaphoreType.DMA((5,)),
        ],
        compiler_params=params(),
        name="gate",
    )(*operands)
    return sends, extra, meta


def merge_kernel(width, meta, *refs):
    received, extras, out = refs[: len(STEPS)], refs[len(STEPS) : -1], refs[-1]
    me = lax.axis_index("seq")

    for w in range(SENT):
        place = meta[PLACE + w]
        rows = pl.ds(pl.multiple_of(jnp.minimum(place, SLOTS - 1) * width, LANES), width)
        for block, step in zip(received, STEPS):

            @pl.when(me ^ step == meta[w])
            def _(w=w, block=block, rows=rows):
                out[w] = block[rows, :]

    for w in range(SLOTS, SENT):
        for extra, step in zip(extras, STEPS):

            @pl.when((me ^ step == meta[w]) & (meta[PLACE + w] >= SLOTS))
            def _(w=w, extra=extra):
                out[w] = extra[...]


def merge(width, meta, received, extras=()):
    return pl.pallas_call(
        functools.partial(merge_kernel, width),
        in_specs=[SMEM_SPEC] + [VMEM_SPEC] * (len(received) + len(extras)),
        out_specs=VMEM_SPEC,
        out_shape=jax.ShapeDtypeStruct((SENT, width, LANES), received[0].dtype),
        compiler_params=params(),
        name="merge",
    )(meta, *received, *extras)


def pick_kernel(first, received, out):
    out[...] = received[pl.ds(first, out.shape[0]), :]


def pick(first, received):
    return pl.pallas_call(
        functools.partial(pick_kernel, first),
        in_specs=[VMEM_SPEC],
        out_specs=VMEM_SPEC,
        out_shape=jax.ShapeDtypeStruct((received.shape[0] - first, LANES), received.dtype),
        compiler_params=params(),
        name="pick",
    )(received)


def lag_tiles(size, first, filters):
    if len(filters) == 1:
        blocks = filters[0]
        group_count = blocks.shape[1] // first
        for shard in range(size):
            for tile in range(first):
                rows = pl.ds(tile * group_count, group_count)
                yield shard * first + tile, blocks[shard, rows, :]
        return
    own, far, near, cross = filters
    me = lax.axis_index("seq")
    group_count = own.shape[0]
    tiles = own.shape[1] // LANES
    for tile in range(tiles):
        yield me * tiles + tile, own[:, pl.ds(tile * LANES, LANES)]
        for block, start, step in ((far, first, 2), (near, first, 1), (cross, 0, 3)):
            rows = pl.ds(start + tile * group_count, group_count)
            yield (me ^ step) * tiles + tile, block[rows, :]


def build_shifted(size, first, filters, reverse, shifted):
    group_count, padded = reverse.shape
    lag_count = padded - SPAN
    row = lax.broadcasted_iota(jnp.int32, (LANES, LANES), 0)
    column = lax.broadcasted_iota(jnp.int32, (LANES, LANES), 1)
    flip = jnp.where(row + column == LANES - 1, 1.0, 0.0).astype(jnp.bfloat16)
    for number, values in lag_tiles(size, first, filters):
        start = lag_count - LANES - number * LANES
        if not isinstance(start, int):
            start = pl.multiple_of(start, LANES)
        reverse[:, pl.ds(start, LANES)] = jnp.dot(
            values, flip, preferred_element_type=jnp.float32
        )
    reverse[:, pl.ds(lag_count, SPAN)] = jnp.zeros((group_count, SPAN), jnp.float32)
    inside = (
        lax.broadcasted_iota(jnp.int32, (GROUP_CH, LANES), 1)
        > lax.broadcasted_iota(jnp.int32, (GROUP_CH, LANES), 0)
    )

    @pl.loop(0, group_count // BLOCKS)
    def _(block):
        tile_rows = pl.ds(pl.multiple_of(block * BLOCKS, BLOCKS), BLOCKS)
        before = [jnp.zeros((GROUP_CH, LANES), jnp.float32)] * BLOCKS
        for start in range(0, padded, LANES):
            tile = reverse[tile_rows, pl.ds(start, LANES)]
            for g in range(BLOCKS):
                spread = jnp.broadcast_to(tile[g : g + 1, :], (GROUP_CH, LANES))
                rolled = pltpu.roll(spread, 1, 1, stride=1, stride_axis=0)
                shifted[block * BLOCKS + g, :, pl.ds(start, LANES)] = jnp.where(
                    inside, rolled, before[g]
                ).astype(jnp.bfloat16)
                before[g] = rolled


def spread_rows(tile, spans, base):
    lane = lax.broadcasted_iota(jnp.int16, tile.shape, 1)
    zero = jnp.zeros(tile.shape, tile.dtype)
    for i1 in range(BLOCKS):
        shift = GROUP_CH * i1
        if i1 == 0:
            low, high = zero, tile
        else:
            moved = pltpu.roll(tile, LANES - shift, 1)
            early = lane < LANES - shift
            low, high = jnp.where(early, zero, moved), jnp.where(early, moved, zero)
        rows = pl.ds(shift, GROUP_CH)
        for g in range(BLOCKS):
            part = slice(g * GROUP_CH, (g + 1) * GROUP_CH)
            spans[g, rows, pl.ds(base, LANES)] = low[part]
            spans[g, rows, pl.ds(base + LANES, LANES)] = high[part]


def window(meta, shifted, group, slot, w):
    start = pl.multiple_of(meta[WINDOWS + slot * WIN + w], STRETCH)
    return shifted[group, :, pl.ds(start, SPAN)]


def filter_rows(meta, shifted, group, slots):
    return jnp.concatenate(
        [
            jnp.concatenate([window(meta, shifted, group, slot, w) for w in range(SENT)], axis=1)
            for slot in range(slots)
        ],
        axis=0,
    )


def rows_of(results, block):
    part = slice(block * GROUP_CH, (block + 1) * GROUP_CH)
    return jnp.concatenate([result[part] for result in results], axis=0).T


def last_rows_kernel(key, value, out):
    for start in range(0, out.shape[0], LANES):
        out[pl.ds(start, LANES), :] = product(key, value, 0, pl.ds(start, LANES))


def last_rows(key_proj, value_proj):
    row_count, channels = key_proj.shape
    block = pl.BlockSpec((STRETCH, channels), lambda i: (row_count // STRETCH - 1, 0))
    operands = [pltpu.with_memory_space_constraint(x, pltpu.HBM) for x in (key_proj, value_proj)]
    return pl.pallas_call(
        last_rows_kernel,
        grid=(1,),
        in_specs=[block, block],
        out_specs=pl.BlockSpec((channels, STRETCH), lambda i: (0, 0)),
        out_shape=jax.ShapeDtypeStruct((channels, STRETCH), jnp.bfloat16),
        compiler_params=params(),
        name="last_rows",
    )(*operands)


def last_term(slots, meta, last, shifted, term, spans):
    for start in range(0, last.shape[0], LANES):
        held = spans.at[start // LANES % 2]
        spread_rows(last[pl.ds(start, LANES), :], held, 0)
        results = [
            lax.dot_general(
                held[g],
                window(meta, shifted, start // GROUP_CH + g, slots - 1, SENT),
                NT,
                preferred_element_type=jnp.float32,
            )
            for g in range(BLOCKS)
        ]
        for m in range(BLOCKS):
            term[pl.ds(m * GROUP_CH, GROUP_CH), pl.ds(start, LANES)] = rows_of(results, m)


def spread_part(pieces, start, spans):
    for w in range(SENT):
        spread_rows(pieces[w, pl.ds(start, LANES), :], spans, w * SPAN)


def conv_part(filter_rows_of, base, start, term, query, out, result, spans, sem):
    slots = query.shape[0] // STRETCH
    columns = pl.ds(pl.multiple_of(base + start, LANES), LANES)
    results = [
        lax.dot_general(
            spans[g],
            filter_rows_of(start // GROUP_CH + g),
            NT,
            preferred_element_type=jnp.float32,
        )
        for g in range(BLOCKS)
    ]
    for m in range(BLOCKS):
        rows = rows_of(results, m)
        for slot in range(slots):
            place = pl.ds(slot * STRETCH + m * GROUP_CH, GROUP_CH)
            tile = rows[slot * GROUP_CH : (slot + 1) * GROUP_CH]
            if slot == slots - 1:
                tile = tile + term[pl.ds(m * GROUP_CH, GROUP_CH), columns]
            gates = query[place, columns].astype(jnp.float32)
            result[place, :] = (gates * tile).astype(jnp.bfloat16)
    store = pltpu.make_async_copy(result, out.at[:, columns], sem)
    store.start()
    return store


def part_base(step, size, width):
    me = lax.axis_index("seq")
    return pl.multiple_of((me ^ step if size > 1 else 0) * width, width)


def scratch(count, row_count):
    return [
        pltpu.VMEM((count, row_count, LANES), jnp.bfloat16),
        pltpu.VMEM((count, BLOCKS, LANES, SENT * SPAN), jnp.bfloat16),
        pltpu.SemaphoreType.DMA((count + 1,)),
    ]


def open_kernel(size, first, meta_in, last, pieces, query, *refs):
    filters = refs[:-9]
    shifted, term, out, reverse, meta, last_spans, result, spans, sems = refs[-9:]
    slots = query.shape[0] // STRETCH
    width = pieces.shape[1]
    scalars = pltpu.make_async_copy(meta_in, meta, sems.at[width // LANES])
    scalars.start()
    build_shifted(size, first, filters, reverse, shifted)
    scalars.wait()
    last_term(slots, meta, last, shifted, term, last_spans)
    base = part_base(0, out.shape[1] // width, width)
    stores = []
    for index, start in enumerate(range(0, width, LANES)):
        spread_part(pieces, start, spans.at[index])
        stores.append(
            conv_part(
                lambda group: filter_rows(meta, shifted, base // GROUP_CH + group, slots),
                base,
                start,
                term,
                query,
                out,
                result.at[index],
                spans.at[index],
                sems.at[index],
            )
        )
    for store in stores:
        store.wait()


def open_conv(size, first, meta, last, pieces, query_proj, group_count, lag_count, filters):
    row_count, channels = query_proj.shape
    padded = lag_count + SPAN
    return pl.pallas_call(
        functools.partial(open_kernel, size, first),
        in_specs=[ANY_SPEC] + [VMEM_SPEC] * (3 + len(filters)),
        out_specs=[VMEM_SPEC, VMEM_SPEC, HBM_SPEC],
        out_shape=[
            jax.ShapeDtypeStruct((group_count, GROUP_CH, padded), jnp.bfloat16),
            jax.ShapeDtypeStruct((STRETCH, channels), jnp.float32),
            jax.ShapeDtypeStruct((row_count, channels), jnp.bfloat16),
        ],
        scratch_shapes=[
            pltpu.VMEM((group_count, padded), jnp.float32),
            pltpu.SMEM(meta.shape, jnp.int32),
            pltpu.VMEM((2, BLOCKS, LANES, SPAN), jnp.bfloat16),
            *scratch(pieces.shape[1] // LANES, row_count),
        ],
        compiler_params=params(),
        name="open_conv",
    )(meta, last, pieces, query_proj, *filters)


def near_kernel(size, steps, next_step, meta_in, shifted, term, query, before, *refs):
    parts = refs[: len(steps)]
    out, ready, meta, result, spans, sems = refs[len(steps) :]
    slots = query.shape[0] // STRETCH
    width = parts[0].shape[1]
    places = [(index, start) for index in range(len(steps)) for start in range(0, width, LANES)]
    scalars = pltpu.make_async_copy(meta_in, meta, sems.at[len(places)])
    scalars.start()
    for number, (index, start) in enumerate(places[: len(places) // 2]):
        spread_part(parts[index], start, spans.at[number])
    scalars.wait()
    stores = []
    for number, (index, start) in enumerate(places):
        if number >= len(places) // 2:
            spread_part(parts[index], start, spans.at[number])
        base = part_base(steps[index], size, width)
        stores.append(
            conv_part(
                lambda group, base=base: filter_rows(meta, shifted, base // GROUP_CH + group, slots),
                base,
                start,
                term,
                query,
                out,
                result.at[number],
                spans.at[number],
                sems.at[number],
            )
        )
    base = part_base(next_step, size, width)
    for group in range(width // GROUP_CH):
        ready[group] = filter_rows(meta, shifted, base // GROUP_CH + group, slots)
    for store in stores:
        store.wait()


def near_conv(size, steps, next_step, meta, parts, shifted, term, query_proj, before):
    row_count, channels = query_proj.shape
    width = channels // size
    slots = row_count // STRETCH
    return pl.pallas_call(
        functools.partial(near_kernel, size, steps, next_step),
        in_specs=[ANY_SPEC] + [VMEM_SPEC] * 3 + [HBM_SPEC] + [VMEM_SPEC] * len(parts),
        out_specs=[HBM_SPEC, VMEM_SPEC],
        out_shape=[
            jax.ShapeDtypeStruct((row_count, channels), jnp.bfloat16),
            jax.ShapeDtypeStruct((width // GROUP_CH, slots * GROUP_CH, SENT * SPAN), jnp.bfloat16),
        ],
        input_output_aliases={4: 0},
        scratch_shapes=[
            pltpu.SMEM(meta.shape, jnp.int32),
            *scratch(len(parts) * width // LANES, row_count),
        ],
        compiler_params=params(),
        name="near_conv",
    )(meta, shifted, term, query_proj, before, *parts)


def far_kernel(size, step, pieces, ready, term, query, before, out, result, spans, sems):
    width = pieces.shape[1]
    base = part_base(step, size, width)
    stores = []
    for index, start in enumerate(range(0, width, LANES)):
        spread_part(pieces, start, spans.at[index])
        stores.append(
            conv_part(
                lambda group: ready[group],
                base,
                start,
                term,
                query,
                out,
                result.at[index],
                spans.at[index],
                sems.at[index],
            )
        )
    for store in stores:
        store.wait()


def far_conv(size, step, pieces, ready, term, query_proj, before):
    row_count, channels = query_proj.shape
    return pl.pallas_call(
        functools.partial(far_kernel, size, step),
        in_specs=[VMEM_SPEC] * 4 + [HBM_SPEC],
        out_specs=HBM_SPEC,
        out_shape=jax.ShapeDtypeStruct((row_count, channels), jnp.bfloat16),
        input_output_aliases={4: 0},
        scratch_shapes=scratch(pieces.shape[1] // LANES, row_count),
        compiler_params=params(),
        name="far_conv",
    )(pieces, ready, term, query_proj, before)


def shards(size, key_proj, value_proj, query_proj, filters, sources, owner):
    row_count, channels = key_proj.shape
    group_count, part = filters.shape
    lag_count = size * part
    tiles = part // LANES
    by_parts = size == 4 and channels % (size * LANES) == 0
    block = group_count * tiles
    filter_rows = [0, block, block, 0] if by_parts else [block]
    parts = len(filter_rows)
    width = channels // parts
    operands = [
        pltpu.with_memory_space_constraint(operand, pltpu.HBM)
        for operand in (sources, owner, key_proj, value_proj, filters)
    ]
    *sends, extra, meta = pl.pallas_call(
        functools.partial(gate_kernel, parts),
        in_specs=[HBM_SPEC] * 5,
        out_specs=[VMEM_SPEC] * (parts + 1) + [SMEM_SPEC],
        out_shape=[
            jax.ShapeDtypeStruct((SLOTS * width + rows, LANES), jnp.bfloat16) for rows in filter_rows
        ]
        + [
            jax.ShapeDtypeStruct((parts, width, LANES), jnp.bfloat16),
            jax.ShapeDtypeStruct((WINDOWS + slots * WIN,), jnp.int32),
        ],
        scratch_shapes=[
            pltpu.SMEM(sources.shape, jnp.int32),
            pltpu.SMEM(owner.shape, jnp.int32),
            pltpu.VMEM(key_proj.shape, key_proj.dtype),
            pltpu.VMEM(value_proj.shape, value_proj.dtype),
            pltpu.VMEM(filters.shape, filters.dtype),
            pltpu.SemaphoreType.DMA((5,)),
        ],
        compiler_params=params(),
        name="gate",
    )(*operands)
    return sends, extra, meta


def merge_kernel(width, meta, *refs):
    received, extras, out = refs[: len(STEPS)], refs[len(STEPS) : -1], refs[-1]
    me = lax.axis_index("seq")

    for w in range(SENT):
        place = meta[PLACE + w]
        rows = pl.ds(pl.multiple_of(jnp.minimum(place, SLOTS - 1) * width, LANES), width)
        for block, step in zip(received, STEPS):

            @pl.when(me ^ step == meta[w])
            def _(w=w, block=block, rows=rows):
                out[w] = block[rows, :]

    for w in range(SLOTS, SENT):
        for extra, step in zip(extras, STEPS):

            @pl.when((me ^ step == meta[w]) & (meta[PLACE + w] >= SLOTS))
            def _(w=w, extra=extra):
                out[w] = extra[...]


def merge(width, meta, received, extras=()):
    return pl.pallas_call(
        functools.partial(merge_kernel, width),
        in_specs=[SMEM_SPEC] + [VMEM_SPEC] * (len(received) + len(extras)),
        out_specs=VMEM_SPEC,
        out_shape=jax.ShapeDtypeStruct((SENT, width, LANES), received[0].dtype),
        compiler_params=params(),
        name="merge",
    )(meta, *received, *extras)


def pick_kernel(first, received, out):
    out[...] = received[pl.ds(first, out.shape[0]), :]


def pick(first, received):
    return pl.pallas_call(
        functools.partial(pick_kernel, first),
        in_specs=[VMEM_SPEC],
        out_specs=VMEM_SPEC,
        out_shape=jax.ShapeDtypeStruct((received.shape[0] - first, LANES), received.dtype),
        compiler_params=params(),
        name="pick",
    )(received)


def lag_tiles(size, first, filters):
    if len(filters) == 1:
        blocks = filters[0]
        group_count = blocks.shape[1] // first
        for shard in range(size):
            for tile in range(first):
                rows = pl.ds(tile * group_count, group_count)
                yield shard * first + tile, blocks[shard, rows, :]
        return
    own, far, near, cross = filters
    me = lax.axis_index("seq")
    group_count = own.shape[0]
    tiles = own.shape[1] // LANES
    for tile in range(tiles):
        yield me * tiles + tile, own[:, pl.ds(tile * LANES, LANES)]
        for block, start, step in ((far, first, 2), (near, first, 1), (cross, 0, 3)):
            rows = pl.ds(start + tile * group_count, group_count)
            yield (me ^ step) * tiles + tile, block[rows, :]


def build_shifted(size, first, filters, reverse, shifted):
    group_count, padded = reverse.shape
    lag_count = padded - SPAN
    row = lax.broadcasted_iota(jnp.int32, (LANES, LANES), 0)
    column = lax.broadcasted_iota(jnp.int32, (LANES, LANES), 1)
    flip = jnp.where(row + column == LANES - 1, 1.0, 0.0).astype(jnp.bfloat16)
    for number, values in lag_tiles(size, first, filters):
        start = lag_count - LANES - number * LANES
        if not isinstance(start, int):
            start = pl.multiple_of(start, LANES)
        reverse[:, pl.ds(start, LANES)] = jnp.dot(
            values, flip, preferred_element_type=jnp.float32
        )
    reverse[:, pl.ds(lag_count, SPAN)] = jnp.zeros((group_count, SPAN), jnp.float32)
    inside = (
        lax.broadcasted_iota(jnp.int32, (GROUP_CH, LANES), 1)
        > lax.broadcasted_iota(jnp.int32, (GROUP_CH, LANES), 0)
    )

    @pl.loop(0, group_count // BLOCKS)
    def _(block):
        tile_rows = pl.ds(pl.multiple_of(block * BLOCKS, BLOCKS), BLOCKS)
        before = [jnp.zeros((GROUP_CH, LANES), jnp.float32)] * BLOCKS
        for start in range(0, padded, LANES):
            tile = reverse[tile_rows, pl.ds(start, LANES)]
            for g in range(BLOCKS):
                spread = jnp.broadcast_to(tile[g : g + 1, :], (GROUP_CH, LANES))
                rolled = pltpu.roll(spread, 1, 1, stride=1, stride_axis=0)
                shifted[block * BLOCKS + g, :, pl.ds(start, LANES)] = jnp.where(
                    inside, rolled, before[g]
                ).astype(jnp.bfloat16)
                before[g] = rolled


def spread_rows(tile, spans, base):
    lane = lax.broadcasted_iota(jnp.int16, tile.shape, 1)
    zero = jnp.zeros(tile.shape, tile.dtype)
    for i1 in range(BLOCKS):
        shift = GROUP_CH * i1
        if i1 == 0:
            low, high = zero, tile
        else:
            moved = pltpu.roll(tile, LANES - shift, 1)
            early = lane < LANES - shift
            low, high = jnp.where(early, zero, moved), jnp.where(early, moved, zero)
        rows = pl.ds(shift, GROUP_CH)
        for g in range(BLOCKS):
            part = slice(g * GROUP_CH, (g + 1) * GROUP_CH)
            spans[g, rows, pl.ds(base, LANES)] = low[part]
            spans[g, rows, pl.ds(base + LANES, LANES)] = high[part]


def window(meta, shifted, group, slot, w):
    start = pl.multiple_of(meta[WINDOWS + slot * WIN + w], STRETCH)
    return shifted[group, :, pl.ds(start, SPAN)]


def filter_rows(meta, shifted, group, slots):
    return jnp.concatenate(
        [
            jnp.concatenate([window(meta, shifted, group, slot, w) for w in range(SENT)], axis=1)
            for slot in range(slots)
        ],
        axis=0,
    )


def rows_of(results, block):
    part = slice(block * GROUP_CH, (block + 1) * GROUP_CH)
    return jnp.concatenate([result[part] for result in results], axis=0).T


def last_rows_kernel(key, value, out):
    for start in range(0, out.shape[0], LANES):
        out[pl.ds(start, LANES), :] = product(key, value, 0, pl.ds(start, LANES))


def last_rows(key_proj, value_proj):
    row_count, channels = key_proj.shape
    block = pl.BlockSpec((STRETCH, channels), lambda i: (row_count // STRETCH - 1, 0))
    operands = [pltpu.with_memory_space_constraint(x, pltpu.HBM) for x in (key_proj, value_proj)]
    return pl.pallas_call(
        last_rows_kernel,
        grid=(1,),
        in_specs=[block, block],
        out_specs=pl.BlockSpec((channels, STRETCH), lambda i: (0, 0)),
        out_shape=jax.ShapeDtypeStruct((channels, STRETCH), jnp.bfloat16),
        compiler_params=params(),
        name="last_rows",
    )(*operands)


def last_term(slots, meta, last, shifted, term, spans):
    for start in range(0, last.shape[0], LANES):
        held = spans.at[start // LANES % 2]
        spread_rows(last[pl.ds(start, LANES), :], held, 0)
        results = [
            lax.dot_general(
                held[g],
                window(meta, shifted, start // GROUP_CH + g, slots - 1, SENT),
                NT,
                preferred_element_type=jnp.float32,
            )
            for g in range(BLOCKS)
        ]
        for m in range(BLOCKS):
            term[pl.ds(m * GROUP_CH, GROUP_CH), pl.ds(start, LANES)] = rows_of(results, m)


def spread_part(pieces, start, spans):
    for w in range(SENT):
        spread_rows(pieces[w, pl.ds(start, LANES), :], spans, w * SPAN)


def conv_part(filter_rows_of, base, start, term, query, out, result, spans, sem):
    slots = query.shape[0] // STRETCH
    columns = pl.ds(pl.multiple_of(base + start, LANES), LANES)
    results = [
        lax.dot_general(
            spans[g],
            filter_rows_of(start // GROUP_CH + g),
            NT,
            preferred_element_type=jnp.float32,
        )
        for g in range(BLOCKS)
    ]
    for m in range(BLOCKS):
        rows = rows_of(results, m)
        for slot in range(slots):
            place = pl.ds(slot * STRETCH + m * GROUP_CH, GROUP_CH)
            tile = rows[slot * GROUP_CH : (slot + 1) * GROUP_CH]
            if slot == slots - 1:
                tile = tile + term[pl.ds(m * GROUP_CH, GROUP_CH), columns]
            gates = query[place, columns].astype(jnp.float32)
            result[place, :] = (gates * tile).astype(jnp.bfloat16)
    store = pltpu.make_async_copy(result, out.at[:, columns], sem)
    store.start()
    return store


def part_base(step, size, width):
    me = lax.axis_index("seq")
    return pl.multiple_of((me ^ step if size > 1 else 0) * width, width)


def scratch(count, row_count):
    return [
        pltpu.VMEM((count, row_count, LANES), jnp.bfloat16),
        pltpu.VMEM((count, BLOCKS, LANES, SENT * SPAN), jnp.bfloat16),
        pltpu.SemaphoreType.DMA((count + 1,)),
    ]


def open_kernel(size, first, meta_in, last, pieces, query, *refs):
    filters = refs[:-9]
    shifted, term, out, reverse, meta, last_spans, result, spans, sems = refs[-9:]
    slots = query.shape[0] // STRETCH
    width = pieces.shape[1]
    scalars = pltpu.make_async_copy(meta_in, meta, sems.at[width // LANES])
    scalars.start()
    build_shifted(size, first, filters, reverse, shifted)
    scalars.wait()
    last_term(slots, meta, last, shifted, term, last_spans)
    base = part_base(0, out.shape[1] // width, width)
    stores = []
    for index, start in enumerate(range(0, width, LANES)):
        spread_part(pieces, start, spans.at[index])
        stores.append(
            conv_part(
                lambda group: filter_rows(meta, shifted, base // GROUP_CH + group, slots),
                base,
                start,
                term,
                query,
                out,
                result.at[index],
                spans.at[index],
                sems.at[index],
            )
        )
    for store in stores:
        store.wait()


def open_conv(size, first, meta, last, pieces, query_proj, group_count, lag_count, filters):
    row_count, channels = query_proj.shape
    padded = lag_count + SPAN
    return pl.pallas_call(
        functools.partial(open_kernel, size, first),
        in_specs=[ANY_SPEC] + [VMEM_SPEC] * (3 + len(filters)),
        out_specs=[VMEM_SPEC, VMEM_SPEC, HBM_SPEC],
        out_shape=[
            jax.ShapeDtypeStruct((group_count, GROUP_CH, padded), jnp.bfloat16),
            jax.ShapeDtypeStruct((STRETCH, channels), jnp.float32),
            jax.ShapeDtypeStruct((row_count, channels), jnp.bfloat16),
        ],
        scratch_shapes=[
            pltpu.VMEM((group_count, padded), jnp.float32),
            pltpu.SMEM(meta.shape, jnp.int32),
            pltpu.VMEM((2, BLOCKS, LANES, SPAN), jnp.bfloat16),
            *scratch(pieces.shape[1] // LANES, row_count),
        ],
        compiler_params=params(),
        name="open_conv",
    )(meta, last, pieces, query_proj, *filters)


def near_kernel(size, steps, next_step, meta_in, shifted, term, query, before, *refs):
    parts = refs[: len(steps)]
    out, ready, meta, result, spans, sems = refs[len(steps) :]
    slots = query.shape[0] // STRETCH
    width = parts[0].shape[1]
    places = [(index, start) for index in range(len(steps)) for start in range(0, width, LANES)]
    scalars = pltpu.make_async_copy(meta_in, meta, sems.at[len(places)])
    scalars.start()
    for number, (index, start) in enumerate(places[: len(places) // 2]):
        spread_part(parts[index], start, spans.at[number])
    scalars.wait()
    stores = []
    for number, (index, start) in enumerate(places):
        if number >= len(places) // 2:
            spread_part(parts[index], start, spans.at[number])
        base = part_base(steps[index], size, width)
        stores.append(
            conv_part(
                lambda group, base=base: filter_rows(meta, shifted, base // GROUP_CH + group, slots),
                base,
                start,
                term,
                query,
                out,
                result.at[number],
                spans.at[number],
                sems.at[number],
            )
        )
    base = part_base(next_step, size, width)
    for group in range(width // GROUP_CH):
        ready[group] = filter_rows(meta, shifted, base // GROUP_CH + group, slots)
    for store in stores:
        store.wait()


def near_conv(size, steps, next_step, meta, parts, shifted, term, query_proj, before):
    row_count, channels = query_proj.shape
    width = channels // size
    slots = row_count // STRETCH
    return pl.pallas_call(
        functools.partial(near_kernel, size, steps, next_step),
        in_specs=[ANY_SPEC] + [VMEM_SPEC] * 3 + [HBM_SPEC] + [VMEM_SPEC] * len(parts),
        out_specs=[HBM_SPEC, VMEM_SPEC],
        out_shape=[
            jax.ShapeDtypeStruct((row_count, channels), jnp.bfloat16),
            jax.ShapeDtypeStruct((width // GROUP_CH, slots * GROUP_CH, SENT * SPAN), jnp.bfloat16),
        ],
        input_output_aliases={4: 0},
        scratch_shapes=[
            pltpu.SMEM(meta.shape, jnp.int32),
            *scratch(len(parts) * width // LANES, row_count),
        ],
        compiler_params=params(),
        name="near_conv",
    )(meta, shifted, term, query_proj, before, *parts)


def far_kernel(size, step, pieces, ready, term, query, before, out, result, spans, sems):
    width = pieces.shape[1]
    base = part_base(step, size, width)
    stores = []
    for index, start in enumerate(range(0, width, LANES)):
        spread_part(pieces, start, spans.at[index])
        stores.append(
            conv_part(
                lambda group: ready[group],
                base,
                start,
                term,
                query,
                out,
                result.at[index],
                spans.at[index],
                sems.at[index],
            )
        )
    for store in stores:
        store.wait()


def far_conv(size, step, pieces, ready, term, query_proj, before):
    row_count, channels = query_proj.shape
    return pl.pallas_call(
        functools.partial(far_kernel, size, step),
        in_specs=[VMEM_SPEC] * 4 + [HBM_SPEC],
        out_specs=HBM_SPEC,
        out_shape=jax.ShapeDtypeStruct((row_count, channels), jnp.bfloat16),
        input_output_aliases={4: 0},
        scratch_shapes=scratch(pieces.shape[1] // LANES, row_count),
        compiler_params=params(),
        name="far_conv",
    )(pieces, ready, term, query_proj, before)


def shards(size, key_proj, value_proj, query_proj, filters, sources, owner):
    row_count, channels = key_proj.shape
    group_count, part = filters.shape
    lag_count = size * part
    tiles = part // LANES
    by_parts = size == 4 and channels % (size * LANES) == 0
    block = group_count * tiles
    filter_rows = [0, block, block, 0] if by_parts else [block]
    parts = len(filter_rows)
    width = channels // parts
    sends, extra, meta = gate(filter_rows, sources, owner, key_proj, value_proj, filters)
    last = last_rows(key_proj, value_proj)
    first = SLOTS * width
    if not by_parts:
        blocks = lax.all_gather(sends[0][first:], "seq")
        held = jnp.concatenate([sends[0][:first].reshape(SLOTS, width, LANES), extra])
        mine = (meta[:SENT] == lax.axis_index("seq"))[:, None, None]
        pieces = lax.psum(jnp.where(mine, held[meta[PLACE:MANY]], jnp.zeros_like(held)), "seq")
        return open_conv(
            size, tiles, meta, last, pieces, query_proj, group_count, lag_count, [blocks]
        )[2]

    def exchange(value, step):
        return lax.ppermute(value, "seq", [(z, z ^ step) for z in range(size)])

    far, near, cross = (exchange(sends[step], step) for step in STEPS[1:])
    cross_filters = exchange(pick(first, far), 1)

    def more(extra):
        return [extra[0]] + [exchange(extra[step], step) for step in STEPS[1:]]

    def none(extra):
        return [extra[step] for step in STEPS]

    extras = lax.cond(meta[MANY] > 0, more, none, extra)
    last, cross_filters, extras, cross = lax.optimization_barrier(
        (last, cross_filters, extras, cross)
    )
    merged = merge(width, meta, [sends[0], far, near, cross], extras)
    far_part, near_part = exchange(merged, 2), exchange(merged, 1)
    shifted, term, out = open_conv(
        size,
        first,
        meta,
        last,
        merged,
        query_proj,
        group_count,
        lag_count,
        [filters, far, near, cross_filters],
    )
    far_part, out = lax.optimization_barrier((far_part, out))
    last_part = exchange(far_part, 1)
    out, ready = near_conv(
        size, (1, 2), 3, meta, [near_part, far_part], shifted, term, query_proj, out
    )
    return far_conv(size, 3, last_part, ready, term, query_proj, out)


def solution(mesh):
    return jax.shard_map(
        functools.partial(shards, mesh.shape["seq"]),
        mesh=mesh,
        in_specs=(
            P(("rep", "seq"), "ch"),
            P(("rep", "seq"), "ch"),
            P(("rep", "seq"), "ch"),
            P("ch", "seq"),
            P("rep"),
            P("rep"),
        ),
        out_specs=P(("rep", "seq"), "ch"),
        check_vma=False,
    )
```

```python
import functools

import jax
import jax.numpy as jnp
from jax import lax
from jax.experimental import pallas as pl
from jax.experimental.pallas import tpu as pltpu
from jax.sharding import PartitionSpec as P

GROUP_CH = 16
STRETCH = 128
WIN = 4
SENT = WIN - 1
LANES = 128
BLOCKS = LANES // GROUP_CH
SPAN = 2 * STRETCH
VMEM_LIMIT = 16 * 1024 * 1024

SMEM_SPEC = pl.BlockSpec(memory_space=pltpu.SMEM)
ANY_SPEC = pl.BlockSpec(memory_space=pl.ANY)
HBM_SPEC = pl.BlockSpec(memory_space=pltpu.HBM)
VMEM_SPEC = pl.BlockSpec(memory_space=pltpu.VMEM)
NT = (((1,), (1,)), ((), ()))


def params():
    return pltpu.CompilerParams(vmem_limit_bytes=VMEM_LIMIT)


STEPS = (0, 2, 1, 3)


PLACE = SENT
MANY = 2 * SENT
WINDOWS = MANY + 1
SLOTS = 2


def product(key, value, start, columns):
    rows = pl.ds(start, STRETCH)
    rows_k = key[rows, columns].astype(jnp.float32)
    rows_v = value[rows, columns].astype(jnp.float32)
    return (rows_k * rows_v).astype(jnp.bfloat16).T


def gate_kernel(parts, sources_in, owner_in, key_in, value_in, filters_in, *refs):
    sends = refs[:parts]
    extra, meta, sources, owner, key, value, filters, sems = refs[parts:]
    stretch_count = owner.shape[0]
    channels = key.shape[1]
    width = channels // parts
    me = lax.axis_index("seq")
    copies = [
        pltpu.make_async_copy(sources_in, sources, sems.at[0]),
        pltpu.make_async_copy(owner_in, owner, sems.at[1]),
        pltpu.make_async_copy(key_in, key, sems.at[2]),
        pltpu.make_async_copy(value_in, value, sems.at[3]),
        pltpu.make_async_copy(filters_in, filters, sems.at[4]),
    ]
    for copy in copies:
        copy.start()

    for copy in copies[:2]:
        copy.wait()

    def target(k, slot):
        mine = owner[k] == me

        @pl.when(mine)
        def _():
            for w in range(WIN):
                lag_block = jnp.maximum(k - sources[w], -1)
                meta[WINDOWS + slot * WIN + w] = (stretch_count - 1 - lag_block) * STRETCH

        return slot + jnp.where(mine, 1, 0)

    lax.fori_loop(0, stretch_count, target, 0)
    for copy in copies[2:]:
        copy.wait()
    holders = [owner[sources[w]] for w in range(SENT)]
    many = 0
    for w, holder in enumerate(holders):
        place = sum([jnp.where(other == holder, 1, 0) for other in holders[:w]], 0)
        meta[w] = holder
        meta[PLACE + w] = place
        many = many + jnp.where(place >= SLOTS, 1, 0)

        @pl.when(holder == me)
        def _(w=w, holder=holder, place=place):
            def count(k, total):
                return total + jnp.where(owner[k] == holder, 1, 0)

            slot = lax.fori_loop(0, sources[w], count, 0)
            first = pl.multiple_of(slot * STRETCH, STRETCH)
            for step in range(parts):
                part = me ^ step if parts > 1 else 0
                base = part * width

                def fill(target, offset, base=base):
                    for start in range(0, width, LANES):
                        columns = pl.ds(pl.multiple_of(base + start, LANES), LANES)
                        target[pl.ds(offset + start, LANES), :] = product(key, value, first, columns)

                if w < SLOTS:
                    fill(sends[step], pl.multiple_of(place * width, LANES))
                else:

                    @pl.when(place < SLOTS)
                    def _(step=step, fill=fill):
                        fill(sends[step], pl.multiple_of(place * width, LANES))

                    @pl.when(place >= SLOTS)
                    def _(step=step, fill=fill):
                        fill(extra.at[step], 0)

    meta[MANY] = many
    group_count = filters.shape[0]
    for tile in range(filters.shape[1] // LANES):
        piece = filters[:, pl.ds(tile * LANES, LANES)]
        for send in sends:
            if send.shape[0] > SLOTS * width:
                send[pl.ds(SLOTS * width + tile * group_count, group_count), :] = piece


def gate(filter_rows, sources, owner, key_proj, value_proj, filters):
    row_count, channels = key_proj.shape
    slots = row_count // STRETCH
    parts = len(filter_rows)
    width = channels // parts
    operands = [
        pltpu.with_memory_space_constraint(operand, pltpu.HBM)
        for operand in (sources, owner, key_proj, value_proj, filters)
    ]
    *sends, extra, meta = pl.pallas_call(
        functools.partial(gate_kernel, parts),
        in_specs=[HBM_SPEC] * 5,
        out_specs=[VMEM_SPEC] * (parts + 1) + [SMEM_SPEC],
        out_shape=[
            jax.ShapeDtypeStruct((SLOTS * width + rows, LANES), jnp.bfloat16) for rows in filter_rows
        ]
        + [
            jax.ShapeDtypeStruct((parts, width, LANES), jnp.bfloat16),
            jax.ShapeDtypeStruct((WINDOWS + slots * WIN,), jnp.int32),
        ],
        scratch_shapes=[
            pltpu.SMEM(sources.shape, jnp.int32),
            pltpu.SMEM(owner.shape, jnp.int32),
            pltpu.VMEM(key_proj.shape, key_proj.dtype),
            pltpu.VMEM(value_proj.shape, value_proj.dtype),
            pltpu.VMEM(filters.shape, filters.dtype),
            pltpu.SemaphoreType.DMA((5,)),
        ],
        compiler_params=params(),
        name="gate",
    )(*operands)
    return sends, extra, meta


def third_kernel(meta, *refs):
    arrived, out = refs[:-1], refs[-1]
    me = lax.axis_index("seq")
    for block, step in zip(arrived, STEPS):

        @pl.when(me ^ step == meta[SENT - 1])
        def _(block=block):
            out[...] = block[...]


def third(meta, arrived):
    return pl.pallas_call(
        third_kernel,
        in_specs=[SMEM_SPEC] + [VMEM_SPEC] * len(arrived),
        out_specs=VMEM_SPEC,
        out_shape=jax.ShapeDtypeStruct(arrived[0].shape, arrived[0].dtype),
        compiler_params=params(),
        name="third",
    )(meta, *arrived)


def merge_kernel(width, meta, late, *refs):
    received, out = refs[:-1], refs[-1]
    me = lax.axis_index("seq")
    for w in range(SENT):
        place = meta[PLACE + w]
        rows = pl.ds(pl.multiple_of(jnp.minimum(place, SLOTS - 1) * width, LANES), width)
        for block, step in zip(received, STEPS):

            @pl.when(me ^ step == meta[w])
            def _(w=w, block=block, rows=rows):
                out[w] = block[rows, :]

    @pl.when(meta[PLACE + SENT - 1] >= SLOTS)
    def _():
        out[SENT - 1] = late[...]


def merge(width, meta, received, late):
    return pl.pallas_call(
        functools.partial(merge_kernel, width),
        in_specs=[SMEM_SPEC] + [VMEM_SPEC] * (1 + len(received)),
        out_specs=VMEM_SPEC,
        out_shape=jax.ShapeDtypeStruct((SENT, width, LANES), received[0].dtype),
        compiler_params=params(),
        name="merge",
    )(meta, late, *received)


def pick_kernel(first, received, out):
    out[...] = received[pl.ds(first, out.shape[0]), :]


def pick(first, received):
    return pl.pallas_call(
        functools.partial(pick_kernel, first),
        in_specs=[VMEM_SPEC],
        out_specs=VMEM_SPEC,
        out_shape=jax.ShapeDtypeStruct((received.shape[0] - first, LANES), received.dtype),
        compiler_params=params(),
        name="pick",
    )(received)


def lag_tiles(size, first, filters):
    if len(filters) == 1:
        blocks = filters[0]
        group_count = blocks.shape[1] // first
        for shard in range(size):
            for tile in range(first):
                rows = pl.ds(tile * group_count, group_count)
                yield shard * first + tile, blocks[shard, rows, :]
        return
    own, far, near, cross = filters
    me = lax.axis_index("seq")
    group_count = own.shape[0]
    tiles = own.shape[1] // LANES
    for tile in range(tiles):
        yield me * tiles + tile, own[:, pl.ds(tile * LANES, LANES)]
        for block, start, step in ((far, first, 2), (near, first, 1), (cross, 0, 3)):
            rows = pl.ds(start + tile * group_count, group_count)
            yield (me ^ step) * tiles + tile, block[rows, :]


def build_shifted(size, first, filters, reverse, shifted):
    group_count, padded = reverse.shape
    lag_count = padded - SPAN
    row = lax.broadcasted_iota(jnp.int32, (LANES, LANES), 0)
    column = lax.broadcasted_iota(jnp.int32, (LANES, LANES), 1)
    flip = jnp.where(row + column == LANES - 1, 1.0, 0.0).astype(jnp.bfloat16)
    for number, values in lag_tiles(size, first, filters):
        start = lag_count - LANES - number * LANES
        if not isinstance(start, int):
            start = pl.multiple_of(start, LANES)
        reverse[:, pl.ds(start, LANES)] = jnp.dot(
            values, flip, preferred_element_type=jnp.float32
        )
    reverse[:, pl.ds(lag_count, SPAN)] = jnp.zeros((group_count, SPAN), jnp.float32)
    inside = (
        lax.broadcasted_iota(jnp.int32, (GROUP_CH, LANES), 1)
        > lax.broadcasted_iota(jnp.int32, (GROUP_CH, LANES), 0)
    )

    @pl.loop(0, group_count // BLOCKS)
    def _(block):
        tile_rows = pl.ds(pl.multiple_of(block * BLOCKS, BLOCKS), BLOCKS)
        before = [jnp.zeros((GROUP_CH, LANES), jnp.float32)] * BLOCKS
        for start in range(0, padded, LANES):
            tile = reverse[tile_rows, pl.ds(start, LANES)]
            for g in range(BLOCKS):
                spread = jnp.broadcast_to(tile[g : g + 1, :], (GROUP_CH, LANES))
                rolled = pltpu.roll(spread, 1, 1, stride=1, stride_axis=0)
                shifted[block * BLOCKS + g, :, pl.ds(start, LANES)] = jnp.where(
                    inside, rolled, before[g]
                ).astype(jnp.bfloat16)
                before[g] = rolled


def spread_rows(tile, spans, base):
    lane = lax.broadcasted_iota(jnp.int16, tile.shape, 1)
    zero = jnp.zeros(tile.shape, tile.dtype)
    for i1 in range(BLOCKS):
        shift = GROUP_CH * i1
        if i1 == 0:
            low, high = zero, tile
        else:
            moved = pltpu.roll(tile, LANES - shift, 1)
            early = lane < LANES - shift
            low, high = jnp.where(early, zero, moved), jnp.where(early, moved, zero)
        rows = pl.ds(shift, GROUP_CH)
        for g in range(BLOCKS):
            part = slice(g * GROUP_CH, (g + 1) * GROUP_CH)
            spans[g, rows, pl.ds(base, LANES)] = low[part]
            spans[g, rows, pl.ds(base + LANES, LANES)] = high[part]


def window(meta, shifted, group, slot, w):
    start = pl.multiple_of(meta[WINDOWS + slot * WIN + w], STRETCH)
    return shifted[group, :, pl.ds(start, SPAN)]


def filter_rows(meta, shifted, group, slots):
    return jnp.concatenate(
        [
            jnp.concatenate([window(meta, shifted, group, slot, w) for w in range(SENT)], axis=1)
            for slot in range(slots)
        ],
        axis=0,
    )


def rows_of(results, block):
    part = slice(block * GROUP_CH, (block + 1) * GROUP_CH)
    return jnp.concatenate([result[part] for result in results], axis=0).T


def last_rows_kernel(key, value, out):
    for start in range(0, out.shape[0], LANES):
        out[pl.ds(start, LANES), :] = product(key, value, 0, pl.ds(start, LANES))


def last_rows(key_proj, value_proj):
    row_count, channels = key_proj.shape
    block = pl.BlockSpec((STRETCH, channels), lambda i: (row_count // STRETCH - 1, 0))
    operands = [pltpu.with_memory_space_constraint(x, pltpu.HBM) for x in (key_proj, value_proj)]
    return pl.pallas_call(
        last_rows_kernel,
        grid=(1,),
        in_specs=[block, block],
        out_specs=pl.BlockSpec((channels, STRETCH), lambda i: (0, 0)),
        out_shape=jax.ShapeDtypeStruct((channels, STRETCH), jnp.bfloat16),
        compiler_params=params(),
        name="last_rows",
    )(*operands)


def last_term(slots, meta, last, shifted, term, spans):
    for start in range(0, last.shape[0], LANES):
        held = spans.at[start // LANES % 2]
        spread_rows(last[pl.ds(start, LANES), :], held, 0)
        results = [
            lax.dot_general(
                held[g],
                window(meta, shifted, start // GROUP_CH + g, slots - 1, SENT),
                NT,
                preferred_element_type=jnp.float32,
            )
            for g in range(BLOCKS)
        ]
        for m in range(BLOCKS):
            term[pl.ds(m * GROUP_CH, GROUP_CH), pl.ds(start, LANES)] = rows_of(results, m)


def spread_part(pieces, start, spans):
    for w in range(SENT):
        spread_rows(pieces[w, pl.ds(start, LANES), :], spans, w * SPAN)


def conv_part(filter_rows_of, base, start, term, query, out, result, spans, sem):
    slots = query.shape[0] // STRETCH
    columns = pl.ds(pl.multiple_of(base + start, LANES), LANES)
    results = [
        lax.dot_general(
            spans[g],
            filter_rows_of(start // GROUP_CH + g),
            NT,
            preferred_element_type=jnp.float32,
        )
        for g in range(BLOCKS)
    ]
    for m in range(BLOCKS):
        rows = rows_of(results, m)
        for slot in range(slots):
            place = pl.ds(slot * STRETCH + m * GROUP_CH, GROUP_CH)
            tile = rows[slot * GROUP_CH : (slot + 1) * GROUP_CH]
            if slot == slots - 1:
                tile = tile + term[pl.ds(m * GROUP_CH, GROUP_CH), columns]
            gates = query[place, columns].astype(jnp.float32)
            result[place, :] = (gates * tile).astype(jnp.bfloat16)
    store = pltpu.make_async_copy(result, out.at[:, columns], sem)
    store.start()
    return store


def part_base(step, size, width):
    me = lax.axis_index("seq")
    return pl.multiple_of((me ^ step if size > 1 else 0) * width, width)


def scratch(count, row_count):
    return [
        pltpu.VMEM((count, row_count, LANES), jnp.bfloat16),
        pltpu.VMEM((count, BLOCKS, LANES, SENT * SPAN), jnp.bfloat16),
        pltpu.SemaphoreType.DMA((count + 1,)),
    ]


def open_kernel(size, first, meta_in, last, pieces, query, *refs):
    filters = refs[:-9]
    shifted, term, out, reverse, meta, last_spans, result, spans, sems = refs[-9:]
    slots = query.shape[0] // STRETCH
    width = pieces.shape[1]
    scalars = pltpu.make_async_copy(meta_in, meta, sems.at[width // LANES])
    scalars.start()
    build_shifted(size, first, filters, reverse, shifted)
    scalars.wait()
    last_term(slots, meta, last, shifted, term, last_spans)
    base = part_base(0, out.shape[1] // width, width)
    stores = []
    for index, start in enumerate(range(0, width, LANES)):
        spread_part(pieces, start, spans.at[index])
        stores.append(
            conv_part(
                lambda group: filter_rows(meta, shifted, base // GROUP_CH + group, slots),
                base,
                start,
                term,
                query,
                out,
                result.at[index],
                spans.at[index],
                sems.at[index],
            )
        )
    for store in stores:
        store.wait()


def open_conv(size, first, meta, last, pieces, query_proj, group_count, lag_count, filters):
    row_count, channels = query_proj.shape
    padded = lag_count + SPAN
    return pl.pallas_call(
        functools.partial(open_kernel, size, first),
        in_specs=[ANY_SPEC] + [VMEM_SPEC] * (3 + len(filters)),
        out_specs=[VMEM_SPEC, VMEM_SPEC, HBM_SPEC],
        out_shape=[
            jax.ShapeDtypeStruct((group_count, GROUP_CH, padded), jnp.bfloat16),
            jax.ShapeDtypeStruct((STRETCH, channels), jnp.float32),
            jax.ShapeDtypeStruct((row_count, channels), jnp.bfloat16),
        ],
        scratch_shapes=[
            pltpu.VMEM((group_count, padded), jnp.float32),
            pltpu.SMEM(meta.shape, jnp.int32),
            pltpu.VMEM((2, BLOCKS, LANES, SPAN), jnp.bfloat16),
            *scratch(pieces.shape[1] // LANES, row_count),
        ],
        compiler_params=params(),
        name="open_conv",
    )(meta, last, pieces, query_proj, *filters)


def near_kernel(size, steps, next_step, meta_in, shifted, term, query, before, *refs):
    parts = refs[: len(steps)]
    out, ready, meta, result, spans, sems = refs[len(steps) :]
    slots = query.shape[0] // STRETCH
    width = parts[0].shape[1]
    places = [(index, start) for index in range(len(steps)) for start in range(0, width, LANES)]
    scalars = pltpu.make_async_copy(meta_in, meta, sems.at[len(places)])
    scalars.start()
    for number, (index, start) in enumerate(places[: len(places) // 2]):
        spread_part(parts[index], start, spans.at[number])
    scalars.wait()
    stores = []
    for number, (index, start) in enumerate(places):
        if number >= len(places) // 2:
            spread_part(parts[index], start, spans.at[number])
        base = part_base(steps[index], size, width)
        stores.append(
            conv_part(
                lambda group, base=base: filter_rows(meta, shifted, base // GROUP_CH + group, slots),
                base,
                start,
                term,
                query,
                out,
                result.at[number],
                spans.at[number],
                sems.at[number],
            )
        )
    base = part_base(next_step, size, width)
    for group in range(width // GROUP_CH):
        ready[group] = filter_rows(meta, shifted, base // GROUP_CH + group, slots)
    for store in stores:
        store.wait()


def near_conv(size, steps, next_step, meta, parts, shifted, term, query_proj, before):
    row_count, channels = query_proj.shape
    width = channels // size
    slots = row_count // STRETCH
    return pl.pallas_call(
        functools.partial(near_kernel, size, steps, next_step),
        in_specs=[ANY_SPEC] + [VMEM_SPEC] * 3 + [HBM_SPEC] + [VMEM_SPEC] * len(parts),
        out_specs=[HBM_SPEC, VMEM_SPEC],
        out_shape=[
            jax.ShapeDtypeStruct((row_count, channels), jnp.bfloat16),
            jax.ShapeDtypeStruct((width // GROUP_CH, slots * GROUP_CH, SENT * SPAN), jnp.bfloat16),
        ],
        input_output_aliases={4: 0},
        scratch_shapes=[
            pltpu.SMEM(meta.shape, jnp.int32),
            *scratch(len(parts) * width // LANES, row_count),
        ],
        compiler_params=params(),
        name="near_conv",
    )(meta, shifted, term, query_proj, before, *parts)


def far_kernel(size, step, pieces, ready, term, query, before, out, result, spans, sems):
    width = pieces.shape[1]
    base = part_base(step, size, width)
    stores = []
    for index, start in enumerate(range(0, width, LANES)):
        spread_part(pieces, start, spans.at[index])
        stores.append(
            conv_part(
                lambda group: ready[group],
                base,
                start,
                term,
                query,
                out,
                result.at[index],
                spans.at[index],
                sems.at[index],
            )
        )
    for store in stores:
        store.wait()


def far_conv(size, step, pieces, ready, term, query_proj, before):
    row_count, channels = query_proj.shape
    return pl.pallas_call(
        functools.partial(far_kernel, size, step),
        in_specs=[VMEM_SPEC] * 4 + [HBM_SPEC],
        out_specs=HBM_SPEC,
        out_shape=jax.ShapeDtypeStruct((row_count, channels), jnp.bfloat16),
        input_output_aliases={4: 0},
        scratch_shapes=scratch(pieces.shape[1] // LANES, row_count),
        compiler_params=params(),
        name="far_conv",
    )(pieces, ready, term, query_proj, before)


def shards(size, key_proj, value_proj, query_proj, filters, sources, owner):
    row_count, channels = key_proj.shape
    group_count, part = filters.shape
    lag_count = size * part
    tiles = part // LANES
    by_parts = size == 4 and channels % (size * LANES) == 0
    block = group_count * tiles
    filter_rows = [0, block, block, 0] if by_parts else [block]
    parts = len(filter_rows)
    width = channels // parts
    sends, extra, meta = gate(filter_rows, sources, owner, key_proj, value_proj, filters)
    last = last_rows(key_proj, value_proj)
    first = SLOTS * width
    if not by_parts:
        blocks = lax.all_gather(sends[0][first:], "seq")
        held = jnp.concatenate([sends[0][:first].reshape(SLOTS, width, LANES), extra])
        mine = (meta[:SENT] == lax.axis_index("seq"))[:, None, None]
        pieces = lax.psum(jnp.where(mine, held[meta[PLACE:MANY]], jnp.zeros_like(held)), "seq")
        return open_conv(
            size, tiles, meta, last, pieces, query_proj, group_count, lag_count, [blocks]
        )[2]

    def exchange(value, step):
        return lax.ppermute(value, "seq", [(z, z ^ step) for z in range(size)])

    far, near, cross = (exchange(sends[step], step) for step in STEPS[1:])
    cross_filters = exchange(pick(first, far), 1)

    def more(meta, extra):
        arrived = [extra[0]] + [exchange(extra[step], step) for step in STEPS[1:]]
        return third(meta, arrived)

    def none(meta, extra):
        return extra[0]

    extra, far = lax.optimization_barrier((extra, far))
    late = lax.cond(meta[MANY] > 0, more, none, meta, extra)
    last, cross_filters, late, cross = lax.optimization_barrier((last, cross_filters, late, cross))
    merged = merge(width, meta, [sends[0], far, near, cross], late)
    far_part, near_part = exchange(merged, 2), exchange(merged, 1)
    shifted, term, out = open_conv(
        size,
        first,
        meta,
        last,
        merged,
        query_proj,
        group_count,
        lag_count,
        [filters, far, near, cross_filters],
    )
    far_part, out = lax.optimization_barrier((far_part, out))
    last_part = exchange(far_part, 1)
    out, ready = near_conv(
        size, (1, 2), 3, meta, [near_part, far_part], shifted, term, query_proj, out
    )
    return far_conv(size, 3, last_part, ready, term, query_proj, out)


def solution(mesh):
    return jax.shard_map(
        functools.partial(shards, mesh.shape["seq"]),
        mesh=mesh,
        in_specs=(
            P(("rep", "seq"), "ch"),
            P(("rep", "seq"), "ch"),
            P(("rep", "seq"), "ch"),
            P("ch", "seq"),
            P("rep"),
            P("rep"),
        ),
        out_specs=P(("rep", "seq"), "ch"),
        check_vma=False,
    )
```

```python
import functools

import jax
import jax.numpy as jnp
from jax import lax
from jax.experimental import pallas as pl
from jax.experimental.pallas import tpu as pltpu
from jax.sharding import PartitionSpec as P

GROUP_CH = 16
STRETCH = 128
WIN = 4
SENT = WIN - 1
LANES = 128
BLOCKS = LANES // GROUP_CH
SPAN = 2 * STRETCH
VMEM_LIMIT = 16 * 1024 * 1024

SMEM_SPEC = pl.BlockSpec(memory_space=pltpu.SMEM)
ANY_SPEC = pl.BlockSpec(memory_space=pl.ANY)
HBM_SPEC = pl.BlockSpec(memory_space=pltpu.HBM)
VMEM_SPEC = pl.BlockSpec(memory_space=pltpu.VMEM)
NT = (((1,), (1,)), ((), ()))


def params():
    return pltpu.CompilerParams(vmem_limit_bytes=VMEM_LIMIT)


STEPS = (0, 2, 1, 3)


PLACE = SENT
MANY = 2 * SENT
WINDOWS = MANY + 1
SLOTS = 2


def product(key, value, start, columns):
    rows = pl.ds(start, STRETCH)
    rows_k = key[rows, columns].astype(jnp.float32)
    rows_v = value[rows, columns].astype(jnp.float32)
    return (rows_k * rows_v).astype(jnp.bfloat16).T


def gate_kernel(parts, sources_in, owner_in, key_in, value_in, filters_in, *refs):
    sends = refs[:parts]
    extra, meta, sources, owner, key, value, filters, sems = refs[parts:]
    stretch_count = owner.shape[0]
    channels = key.shape[1]
    width = channels // parts
    me = lax.axis_index("seq")
    copies = [
        pltpu.make_async_copy(sources_in, sources, sems.at[0]),
        pltpu.make_async_copy(owner_in, owner, sems.at[1]),
        pltpu.make_async_copy(key_in, key, sems.at[2]),
        pltpu.make_async_copy(value_in, value, sems.at[3]),
        pltpu.make_async_copy(filters_in, filters, sems.at[4]),
    ]
    for copy in copies:
        copy.start()

    for copy in copies[:2]:
        copy.wait()

    def target(k, slot):
        mine = owner[k] == me

        @pl.when(mine)
        def _():
            for w in range(WIN):
                lag_block = jnp.maximum(k - sources[w], -1)
                meta[WINDOWS + slot * WIN + w] = (stretch_count - 1 - lag_block) * STRETCH

        return slot + jnp.where(mine, 1, 0)

    lax.fori_loop(0, stretch_count, target, 0)
    for copy in copies[2:]:
        copy.wait()
    holders = [owner[sources[w]] for w in range(SENT)]
    many = 0
    for w, holder in enumerate(holders):
        place = sum([jnp.where(other == holder, 1, 0) for other in holders[:w]], 0)
        meta[w] = holder
        meta[PLACE + w] = place
        many = many + jnp.where(place >= SLOTS, 1, 0)

        @pl.when(holder == me)
        def _(w=w, holder=holder, place=place):
            def count(k, total):
                return total + jnp.where(owner[k] == holder, 1, 0)

            slot = lax.fori_loop(0, sources[w], count, 0)
            first = pl.multiple_of(slot * STRETCH, STRETCH)
            for step in range(parts):
                part = me ^ step if parts > 1 else 0
                base = part * width

                def fill(target, offset, base=base):
                    for start in range(0, width, LANES):
                        columns = pl.ds(pl.multiple_of(base + start, LANES), LANES)
                        target[pl.ds(offset + start, LANES), :] = product(key, value, first, columns)

                if w < SLOTS:
                    fill(sends[step], pl.multiple_of(place * width, LANES))
                else:

                    @pl.when(place < SLOTS)
                    def _(step=step, fill=fill):
                        fill(sends[step], pl.multiple_of(place * width, LANES))

                    @pl.when(place >= SLOTS)
                    def _(step=step, fill=fill):
                        fill(extra.at[step], 0)

    meta[MANY] = many
    group_count = filters.shape[0]
    for tile in range(filters.shape[1] // LANES):
        piece = filters[:, pl.ds(tile * LANES, LANES)]
        for send in sends:
            if send.shape[0] > SLOTS * width:
                send[pl.ds(SLOTS * width + tile * group_count, group_count), :] = piece


def gate(filter_rows, sources, owner, key_proj, value_proj, filters):
    row_count, channels = key_proj.shape
    slots = row_count // STRETCH
    parts = len(filter_rows)
    width = channels // parts
    operands = [
        pltpu.with_memory_space_constraint(operand, pltpu.HBM)
        for operand in (sources, owner, key_proj, value_proj, filters)
    ]
    *sends, extra, meta = pl.pallas_call(
        functools.partial(gate_kernel, parts),
        in_specs=[HBM_SPEC] * 5,
        out_specs=[VMEM_SPEC] * (parts + 1) + [SMEM_SPEC],
        out_shape=[
            jax.ShapeDtypeStruct((SLOTS * width + rows, LANES), jnp.bfloat16) for rows in filter_rows
        ]
        + [
            jax.ShapeDtypeStruct((parts, width, LANES), jnp.bfloat16),
            jax.ShapeDtypeStruct((WINDOWS + slots * WIN,), jnp.int32),
        ],
        scratch_shapes=[
            pltpu.SMEM(sources.shape, jnp.int32),
            pltpu.SMEM(owner.shape, jnp.int32),
            pltpu.VMEM(key_proj.shape, key_proj.dtype),
            pltpu.VMEM(value_proj.shape, value_proj.dtype),
            pltpu.VMEM(filters.shape, filters.dtype),
            pltpu.SemaphoreType.DMA((5,)),
        ],
        compiler_params=params(),
        name="gate",
    )(*operands)
    return sends, extra, meta


def third_kernel(meta, *refs):
    arrived, out = refs[:-1], refs[-1]
    me = lax.axis_index("seq")
    for block, step in zip(arrived, STEPS):

        @pl.when(me ^ step == meta[SENT - 1])
        def _(block=block):
            out[...] = block[...]


def third(meta, arrived):
    return pl.pallas_call(
        third_kernel,
        in_specs=[SMEM_SPEC] + [VMEM_SPEC] * len(arrived),
        out_specs=VMEM_SPEC,
        out_shape=jax.ShapeDtypeStruct(arrived[0].shape, arrived[0].dtype),
        compiler_params=params(),
        name="third",
    )(meta, *arrived)


def merge_kernel(width, meta, late, *refs):
    received, out = refs[:-1], refs[-1]
    me = lax.axis_index("seq")
    for w in range(SENT):
        place = meta[PLACE + w]
        rows = pl.ds(pl.multiple_of(jnp.minimum(place, SLOTS - 1) * width, LANES), width)
        for block, step in zip(received, STEPS):

            @pl.when(me ^ step == meta[w])
            def _(w=w, block=block, rows=rows):
                out[w] = block[rows, :]

    @pl.when(meta[PLACE + SENT - 1] >= SLOTS)
    def _():
        out[SENT - 1] = late[...]


def merge(width, meta, received, late):
    return pl.pallas_call(
        functools.partial(merge_kernel, width),
        in_specs=[SMEM_SPEC] + [VMEM_SPEC] * (1 + len(received)),
        out_specs=VMEM_SPEC,
        out_shape=jax.ShapeDtypeStruct((SENT, width, LANES), received[0].dtype),
        compiler_params=params(),
        name="merge",
    )(meta, late, *received)


def pick_kernel(first, received, out):
    out[...] = received[pl.ds(first, out.shape[0]), :]


def pick(first, received):
    return pl.pallas_call(
        functools.partial(pick_kernel, first),
        in_specs=[VMEM_SPEC],
        out_specs=VMEM_SPEC,
        out_shape=jax.ShapeDtypeStruct((received.shape[0] - first, LANES), received.dtype),
        compiler_params=params(),
        name="pick",
    )(received)


def lag_tiles(size, first, filters):
    if len(filters) == 1:
        blocks = filters[0]
        group_count = blocks.shape[1] // first
        for shard in range(size):
            for tile in range(first):
                rows = pl.ds(tile * group_count, group_count)
                yield shard * first + tile, blocks[shard, rows, :]
        return
    own, far, near, cross = filters
    me = lax.axis_index("seq")
    group_count = own.shape[0]
    tiles = own.shape[1] // LANES
    for tile in range(tiles):
        yield me * tiles + tile, own[:, pl.ds(tile * LANES, LANES)]
        for block, start, step in ((far, first, 2), (near, first, 1), (cross, 0, 3)):
            rows = pl.ds(start + tile * group_count, group_count)
            yield (me ^ step) * tiles + tile, block[rows, :]


def build_shifted(size, first, filters, reverse, shifted):
    group_count, padded = reverse.shape
    lag_count = padded - SPAN
    row = lax.broadcasted_iota(jnp.int32, (LANES, LANES), 0)
    column = lax.broadcasted_iota(jnp.int32, (LANES, LANES), 1)
    flip = jnp.where(row + column == LANES - 1, 1.0, 0.0).astype(jnp.bfloat16)
    for number, values in lag_tiles(size, first, filters):
        start = lag_count - LANES - number * LANES
        if not isinstance(start, int):
            start = pl.multiple_of(start, LANES)
        reverse[:, pl.ds(start, LANES)] = jnp.dot(
            values, flip, preferred_element_type=jnp.float32
        )
    reverse[:, pl.ds(lag_count, SPAN)] = jnp.zeros((group_count, SPAN), jnp.float32)
    inside = (
        lax.broadcasted_iota(jnp.int32, (GROUP_CH, LANES), 1)
        > lax.broadcasted_iota(jnp.int32, (GROUP_CH, LANES), 0)
    )

    @pl.loop(0, group_count // BLOCKS)
    def _(block):
        tile_rows = pl.ds(pl.multiple_of(block * BLOCKS, BLOCKS), BLOCKS)
        before = [jnp.zeros((GROUP_CH, LANES), jnp.float32)] * BLOCKS
        for start in range(0, padded, LANES):
            tile = reverse[tile_rows, pl.ds(start, LANES)]
            for g in range(BLOCKS):
                spread = jnp.broadcast_to(tile[g : g + 1, :], (GROUP_CH, LANES))
                rolled = pltpu.roll(spread, 1, 1, stride=1, stride_axis=0)
                shifted[block * BLOCKS + g, :, pl.ds(start, LANES)] = jnp.where(
                    inside, rolled, before[g]
                ).astype(jnp.bfloat16)
                before[g] = rolled


def spread_rows(tile, spans, base):
    lane = lax.broadcasted_iota(jnp.int16, tile.shape, 1)
    zero = jnp.zeros(tile.shape, tile.dtype)
    for i1 in range(BLOCKS):
        shift = GROUP_CH * i1
        if i1 == 0:
            low, high = zero, tile
        else:
            moved = pltpu.roll(tile, LANES - shift, 1)
            early = lane < LANES - shift
            low, high = jnp.where(early, zero, moved), jnp.where(early, moved, zero)
        rows = pl.ds(shift, GROUP_CH)
        for g in range(BLOCKS):
            part = slice(g * GROUP_CH, (g + 1) * GROUP_CH)
            spans[g, rows, pl.ds(base, LANES)] = low[part]
            spans[g, rows, pl.ds(base + LANES, LANES)] = high[part]


def window(meta, shifted, group, slot, w):
    start = pl.multiple_of(meta[WINDOWS + slot * WIN + w], STRETCH)
    return shifted[group, :, pl.ds(start, SPAN)]


def filter_rows(meta, shifted, group, slots):
    return jnp.concatenate(
        [
            jnp.concatenate([window(meta, shifted, group, slot, w) for w in range(SENT)], axis=1)
            for slot in range(slots)
        ],
        axis=0,
    )


def rows_of(results, block):
    part = slice(block * GROUP_CH, (block + 1) * GROUP_CH)
    return jnp.concatenate([result[part] for result in results], axis=0).T


def last_rows_kernel(key, value, out):
    for start in range(0, out.shape[0], LANES):
        out[pl.ds(start, LANES), :] = product(key, value, 0, pl.ds(start, LANES))


def last_rows(key_proj, value_proj):
    row_count, channels = key_proj.shape
    block = pl.BlockSpec((STRETCH, channels), lambda i: (row_count // STRETCH - 1, 0))
    operands = [pltpu.with_memory_space_constraint(x, pltpu.HBM) for x in (key_proj, value_proj)]
    return pl.pallas_call(
        last_rows_kernel,
        grid=(1,),
        in_specs=[block, block],
        out_specs=pl.BlockSpec((channels, STRETCH), lambda i: (0, 0)),
        out_shape=jax.ShapeDtypeStruct((channels, STRETCH), jnp.bfloat16),
        compiler_params=params(),
        name="last_rows",
    )(*operands)


def last_term(slots, meta, last, shifted, term, spans):
    for start in range(0, last.shape[0], LANES):
        held = spans.at[start // LANES % 2]
        spread_rows(last[pl.ds(start, LANES), :], held, 0)
        results = [
            lax.dot_general(
                held[g],
                window(meta, shifted, start // GROUP_CH + g, slots - 1, SENT),
                NT,
                preferred_element_type=jnp.float32,
            )
            for g in range(BLOCKS)
        ]
        for m in range(BLOCKS):
            term[pl.ds(m * GROUP_CH, GROUP_CH), pl.ds(start, LANES)] = rows_of(results, m)


def spread_part(pieces, start, spans):
    for w in range(SENT):
        spread_rows(pieces[w, pl.ds(start, LANES), :], spans, w * SPAN)


def conv_part(filter_rows_of, base, start, term, query, out, result, spans, sem):
    slots = query.shape[0] // STRETCH
    columns = pl.ds(pl.multiple_of(base + start, LANES), LANES)
    results = [
        lax.dot_general(
            spans[g],
            filter_rows_of(start // GROUP_CH + g),
            NT,
            preferred_element_type=jnp.float32,
        )
        for g in range(BLOCKS)
    ]
    for m in range(BLOCKS):
        rows = rows_of(results, m)
        for slot in range(slots):
            place = pl.ds(slot * STRETCH + m * GROUP_CH, GROUP_CH)
            tile = rows[slot * GROUP_CH : (slot + 1) * GROUP_CH]
            if slot == slots - 1:
                tile = tile + term[pl.ds(m * GROUP_CH, GROUP_CH), columns]
            gates = query[place, columns].astype(jnp.float32)
            result[place, :] = (gates * tile).astype(jnp.bfloat16)
    store = pltpu.make_async_copy(result, out.at[:, columns], sem)
    store.start()
    return store


def part_base(step, size, width):
    me = lax.axis_index("seq")
    return pl.multiple_of((me ^ step if size > 1 else 0) * width, width)


def scratch(count, row_count):
    return [
        pltpu.VMEM((count, row_count, LANES), jnp.bfloat16),
        pltpu.VMEM((count, BLOCKS, LANES, SENT * SPAN), jnp.bfloat16),
        pltpu.SemaphoreType.DMA((count + 1,)),
    ]


def open_kernel(size, first, meta_in, last, pieces, query, *refs):
    filters = refs[:-9]
    shifted, term, out, reverse, meta, last_spans, result, spans, sems = refs[-9:]
    slots = query.shape[0] // STRETCH
    width = pieces.shape[1]
    scalars = pltpu.make_async_copy(meta_in, meta, sems.at[width // LANES])
    scalars.start()
    build_shifted(size, first, filters, reverse, shifted)
    scalars.wait()
    last_term(slots, meta, last, shifted, term, last_spans)
    base = part_base(0, out.shape[1] // width, width)
    stores = []
    for index, start in enumerate(range(0, width, LANES)):
        spread_part(pieces, start, spans.at[index])
        stores.append(
            conv_part(
                lambda group: filter_rows(meta, shifted, base // GROUP_CH + group, slots),
                base,
                start,
                term,
                query,
                out,
                result.at[index],
                spans.at[index],
                sems.at[index],
            )
        )
    for store in stores:
        store.wait()


def open_conv(size, first, meta, last, pieces, query_proj, group_count, lag_count, filters):
    row_count, channels = query_proj.shape
    padded = lag_count + SPAN
    return pl.pallas_call(
        functools.partial(open_kernel, size, first),
        in_specs=[ANY_SPEC] + [VMEM_SPEC] * (3 + len(filters)),
        out_specs=[VMEM_SPEC, VMEM_SPEC, HBM_SPEC],
        out_shape=[
            jax.ShapeDtypeStruct((group_count, GROUP_CH, padded), jnp.bfloat16),
            jax.ShapeDtypeStruct((STRETCH, channels), jnp.float32),
            jax.ShapeDtypeStruct((row_count, channels), jnp.bfloat16),
        ],
        scratch_shapes=[
            pltpu.VMEM((group_count, padded), jnp.float32),
            pltpu.SMEM(meta.shape, jnp.int32),
            pltpu.VMEM((2, BLOCKS, LANES, SPAN), jnp.bfloat16),
            *scratch(pieces.shape[1] // LANES, row_count),
        ],
        compiler_params=params(),
        name="open_conv",
    )(meta, last, pieces, query_proj, *filters)


def near_kernel(size, steps, next_step, meta_in, shifted, term, query, before, *refs):
    parts = refs[: len(steps)]
    out, ready, meta, result, spans, sems = refs[len(steps) :]
    slots = query.shape[0] // STRETCH
    width = parts[0].shape[1]
    places = [(index, start) for index in range(len(steps)) for start in range(0, width, LANES)]
    scalars = pltpu.make_async_copy(meta_in, meta, sems.at[len(places)])
    scalars.start()
    for number, (index, start) in enumerate(places[: len(places) // 2]):
        spread_part(parts[index], start, spans.at[number])
    scalars.wait()
    stores = []
    for number, (index, start) in enumerate(places):
        if number >= len(places) // 2:
            spread_part(parts[index], start, spans.at[number])
        base = part_base(steps[index], size, width)
        stores.append(
            conv_part(
                lambda group, base=base: filter_rows(meta, shifted, base // GROUP_CH + group, slots),
                base,
                start,
                term,
                query,
                out,
                result.at[number],
                spans.at[number],
                sems.at[number],
            )
        )
    base = part_base(next_step, size, width)
    for group in range(width // GROUP_CH):
        ready[group] = filter_rows(meta, shifted, base // GROUP_CH + group, slots)
    for store in stores:
        store.wait()


def near_conv(size, steps, next_step, meta, parts, shifted, term, query_proj, before):
    row_count, channels = query_proj.shape
    width = channels // size
    slots = row_count // STRETCH
    return pl.pallas_call(
        functools.partial(near_kernel, size, steps, next_step),
        in_specs=[ANY_SPEC] + [VMEM_SPEC] * 3 + [HBM_SPEC] + [VMEM_SPEC] * len(parts),
        out_specs=[HBM_SPEC, VMEM_SPEC],
        out_shape=[
            jax.ShapeDtypeStruct((row_count, channels), jnp.bfloat16),
            jax.ShapeDtypeStruct((width // GROUP_CH, slots * GROUP_CH, SENT * SPAN), jnp.bfloat16),
        ],
        input_output_aliases={4: 0},
        scratch_shapes=[
            pltpu.SMEM(meta.shape, jnp.int32),
            *scratch(len(parts) * width // LANES, row_count),
        ],
        compiler_params=params(),
        name="near_conv",
    )(meta, shifted, term, query_proj, before, *parts)


def far_kernel(size, step, pieces, ready, term, query, before, out, result, spans, sems):
    width = pieces.shape[1]
    base = part_base(step, size, width)
    stores = []
    for index, start in enumerate(range(0, width, LANES)):
        spread_part(pieces, start, spans.at[index])
        stores.append(
            conv_part(
                lambda group: ready[group],
                base,
                start,
                term,
                query,
                out,
                result.at[index],
                spans.at[index],
                sems.at[index],
            )
        )
    for store in stores:
        store.wait()


def far_conv(size, step, pieces, ready, term, query_proj, before):
    row_count, channels = query_proj.shape
    return pl.pallas_call(
        functools.partial(far_kernel, size, step),
        in_specs=[VMEM_SPEC] * 4 + [HBM_SPEC],
        out_specs=HBM_SPEC,
        out_shape=jax.ShapeDtypeStruct((row_count, channels), jnp.bfloat16),
        input_output_aliases={4: 0},
        scratch_shapes=scratch(pieces.shape[1] // LANES, row_count),
        compiler_params=params(),
        name="far_conv",
    )(pieces, ready, term, query_proj, before)


def shards(size, key_proj, value_proj, query_proj, filters, sources, owner):
    row_count, channels = key_proj.shape
    group_count, part = filters.shape
    lag_count = size * part
    tiles = part // LANES
    by_parts = size == 4 and channels % (size * LANES) == 0
    block = group_count * tiles
    filter_rows = [0, block, block, 0] if by_parts else [block]
    parts = len(filter_rows)
    width = channels // parts
    sends, extra, meta = gate(filter_rows, sources, owner, key_proj, value_proj, filters)
    last = last_rows(key_proj, value_proj)
    first = SLOTS * width
    if not by_parts:
        blocks = lax.all_gather(sends[0][first:], "seq")
        held = jnp.concatenate([sends[0][:first].reshape(SLOTS, width, LANES), extra])
        mine = (meta[:SENT] == lax.axis_index("seq"))[:, None, None]
        pieces = lax.psum(jnp.where(mine, held[meta[PLACE:MANY]], jnp.zeros_like(held)), "seq")
        return open_conv(
            size, tiles, meta, last, pieces, query_proj, group_count, lag_count, [blocks]
        )[2]

    def exchange(value, step):
        return lax.ppermute(value, "seq", [(z, z ^ step) for z in range(size)])

    far, near, cross = (exchange(sends[step], step) for step in STEPS[1:])
    cross_filters = exchange(pick(first, far), 1)

    def more(meta, extra):
        arrived = [extra[0]] + [exchange(extra[step], step) for step in STEPS[1:]]
        return third(meta, arrived)

    def none(meta, extra):
        return extra[0]

    extra, far = lax.optimization_barrier((extra, far))
    late = lax.cond(meta[MANY] > 0, more, none, meta, extra)
    last, late, cross = lax.optimization_barrier((last, late, cross))
    merged = merge(width, meta, [sends[0], far, near, cross], late)
    far_part, near_part = exchange(merged, 2), exchange(merged, 1)
    shifted, term, out = open_conv(
        size,
        first,
        meta,
        last,
        merged,
        query_proj,
        group_count,
        lag_count,
        [filters, far, near, cross_filters],
    )
    far_part, out = lax.optimization_barrier((far_part, out))
    last_part = exchange(far_part, 1)
    out, ready = near_conv(
        size, (1, 2), 3, meta, [near_part, far_part], shifted, term, query_proj, out
    )
    return far_conv(size, 3, last_part, ready, term, query_proj, out)


def solution(mesh):
    return jax.shard_map(
        functools.partial(shards, mesh.shape["seq"]),
        mesh=mesh,
        in_specs=(
            P(("rep", "seq"), "ch"),
            P(("rep", "seq"), "ch"),
            P(("rep", "seq"), "ch"),
            P("ch", "seq"),
            P("rep"),
            P("rep"),
        ),
        out_specs=P(("rep", "seq"), "ch"),
        check_vma=False,
    )
```

```python
import functools

import jax
import jax.numpy as jnp
from jax import lax
from jax.experimental import pallas as pl
from jax.experimental.pallas import tpu as pltpu
from jax.sharding import PartitionSpec as P

GROUP_CH = 16
STRETCH = 128
WIN = 4
SENT = WIN - 1
LANES = 128
BLOCKS = LANES // GROUP_CH
SPAN = 2 * STRETCH
VMEM_LIMIT = 16 * 1024 * 1024

SMEM_SPEC = pl.BlockSpec(memory_space=pltpu.SMEM)
ANY_SPEC = pl.BlockSpec(memory_space=pl.ANY)
HBM_SPEC = pl.BlockSpec(memory_space=pltpu.HBM)
VMEM_SPEC = pl.BlockSpec(memory_space=pltpu.VMEM)
NT = (((1,), (1,)), ((), ()))


def params():
    return pltpu.CompilerParams(vmem_limit_bytes=VMEM_LIMIT)


STEPS = (0, 2, 1, 3)


PLACE = SENT
MANY = 2 * SENT
WINDOWS = MANY + 1
SLOTS = 2
CHOICES = SENT * len(STEPS) * SLOTS


def product(key, value, start, columns):
    rows = pl.ds(start, STRETCH)
    rows_k = key[rows, columns].astype(jnp.float32)
    rows_v = value[rows, columns].astype(jnp.float32)
    return (rows_k * rows_v).astype(jnp.bfloat16).T


def gate_kernel(parts, sources_in, owner_in, key_in, value_in, filters_in, *refs):
    sends = refs[:parts]
    extra, choice, meta, sources, owner, key, value, filters, sems = refs[parts:]
    stretch_count = owner.shape[0]
    channels = key.shape[1]
    width = channels // parts
    me = lax.axis_index("seq")
    copies = [
        pltpu.make_async_copy(sources_in, sources, sems.at[0]),
        pltpu.make_async_copy(owner_in, owner, sems.at[1]),
        pltpu.make_async_copy(key_in, key, sems.at[2]),
        pltpu.make_async_copy(value_in, value, sems.at[3]),
        pltpu.make_async_copy(filters_in, filters, sems.at[4]),
    ]
    for copy in copies:
        copy.start()

    for copy in copies[:2]:
        copy.wait()

    def target(k, slot):
        mine = owner[k] == me

        @pl.when(mine)
        def _():
            for w in range(WIN):
                lag_block = jnp.maximum(k - sources[w], -1)
                meta[WINDOWS + slot * WIN + w] = (stretch_count - 1 - lag_block) * STRETCH

        return slot + jnp.where(mine, 1, 0)

    lax.fori_loop(0, stretch_count, target, 0)
    for copy in copies[2:]:
        copy.wait()
    holders = [owner[sources[w]] for w in range(SENT)]
    many = 0
    for w, holder in enumerate(holders):
        place = sum([jnp.where(other == holder, 1, 0) for other in holders[:w]], 0)
        meta[w] = holder
        meta[PLACE + w] = place
        many = many + jnp.where(place >= SLOTS, 1, 0)
        for index, step in enumerate(STEPS):
            for packed in range(SLOTS):
                here = jnp.where((holder == me ^ step) & (place == packed), 1, 0)
                mask = jnp.broadcast_to(here, choice.shape[1:]).astype(jnp.int16)
                choice[(w * len(STEPS) + index) * SLOTS + packed] = mask

        @pl.when(holder == me)
        def _(w=w, holder=holder, place=place):
            def count(k, total):
                return total + jnp.where(owner[k] == holder, 1, 0)

            slot = lax.fori_loop(0, sources[w], count, 0)
            first = pl.multiple_of(slot * STRETCH, STRETCH)
            for step in range(parts):
                part = me ^ step if parts > 1 else 0
                base = part * width

                def fill(target, offset, base=base):
                    for start in range(0, width, LANES):
                        columns = pl.ds(pl.multiple_of(base + start, LANES), LANES)
                        target[pl.ds(offset + start, LANES), :] = product(key, value, first, columns)

                if w < SLOTS:
                    fill(sends[step], pl.multiple_of(place * width, LANES))
                else:

                    @pl.when(place < SLOTS)
                    def _(step=step, fill=fill):
                        fill(sends[step], pl.multiple_of(place * width, LANES))

                    @pl.when(place >= SLOTS)
                    def _(step=step, fill=fill):
                        fill(extra.at[step], 0)

    meta[MANY] = many
    group_count = filters.shape[0]
    for tile in range(filters.shape[1] // LANES):
        piece = filters[:, pl.ds(tile * LANES, LANES)]
        for send in sends:
            if send.shape[0] > SLOTS * width:
                send[pl.ds(SLOTS * width + tile * group_count, group_count), :] = piece


def gate(filter_rows, sources, owner, key_proj, value_proj, filters):
    row_count, channels = key_proj.shape
    slots = row_count // STRETCH
    parts = len(filter_rows)
    width = channels // parts
    operands = [
        pltpu.with_memory_space_constraint(operand, pltpu.HBM)
        for operand in (sources, owner, key_proj, value_proj, filters)
    ]
    *sends, extra, choice, meta = pl.pallas_call(
        functools.partial(gate_kernel, parts),
        in_specs=[HBM_SPEC] * 5,
        out_specs=[VMEM_SPEC] * (parts + 2) + [SMEM_SPEC],
        out_shape=[
            jax.ShapeDtypeStruct((SLOTS * width + rows, LANES), jnp.bfloat16) for rows in filter_rows
        ]
        + [
            jax.ShapeDtypeStruct((parts, width, LANES), jnp.bfloat16),
            jax.ShapeDtypeStruct((CHOICES, GROUP_CH, LANES), jnp.int16),
            jax.ShapeDtypeStruct((WINDOWS + slots * WIN,), jnp.int32),
        ],
        scratch_shapes=[
            pltpu.SMEM(sources.shape, jnp.int32),
            pltpu.SMEM(owner.shape, jnp.int32),
            pltpu.VMEM(key_proj.shape, key_proj.dtype),
            pltpu.VMEM(value_proj.shape, value_proj.dtype),
            pltpu.VMEM(filters.shape, filters.dtype),
            pltpu.SemaphoreType.DMA((5,)),
        ],
        compiler_params=params(),
        name="gate",
    )(*operands)
    return sends, extra, choice, meta


def third_kernel(meta, *refs):
    arrived, out = refs[:-1], refs[-1]
    me = lax.axis_index("seq")
    for block, step in zip(arrived, STEPS):

        @pl.when(me ^ step == meta[SENT - 1])
        def _(block=block):
            out[...] = block[...]


def third(meta, arrived):
    return pl.pallas_call(
        third_kernel,
        in_specs=[SMEM_SPEC] + [VMEM_SPEC] * len(arrived),
        out_specs=VMEM_SPEC,
        out_shape=jax.ShapeDtypeStruct(arrived[0].shape, arrived[0].dtype),
        compiler_params=params(),
        name="third",
    )(meta, *arrived)


def merge_kernel(width, choice, late, *refs):
    received, out = refs[:-1], refs[-1]
    for w in range(SENT):
        masks = [choice[w * len(STEPS) * SLOTS + number] != 0 for number in range(len(STEPS) * SLOTS)]
        for start in range(0, width, GROUP_CH):
            tile = late[pl.ds(start, GROUP_CH), :]
            for number, mask in enumerate(masks):
                rows = pl.ds(number % SLOTS * width + start, GROUP_CH)
                tile = jnp.where(mask, received[number // SLOTS][rows, :], tile)
            out[w, pl.ds(start, GROUP_CH), :] = tile


def merge(width, choice, received, late):
    return pl.pallas_call(
        functools.partial(merge_kernel, width),
        in_specs=[VMEM_SPEC] * (2 + len(received)),
        out_specs=VMEM_SPEC,
        out_shape=jax.ShapeDtypeStruct((SENT, width, LANES), received[0].dtype),
        compiler_params=params(),
        name="merge",
    )(choice, late, *received)


def pick_kernel(first, received, out):
    out[...] = received[pl.ds(first, out.shape[0]), :]


def pick(first, received):
    return pl.pallas_call(
        functools.partial(pick_kernel, first),
        in_specs=[VMEM_SPEC],
        out_specs=VMEM_SPEC,
        out_shape=jax.ShapeDtypeStruct((received.shape[0] - first, LANES), received.dtype),
        compiler_params=params(),
        name="pick",
    )(received)


def lag_tiles(size, first, filters):
    if len(filters) == 1:
        blocks = filters[0]
        group_count = blocks.shape[1] // first
        for shard in range(size):
            for tile in range(first):
                rows = pl.ds(tile * group_count, group_count)
                yield shard * first + tile, blocks[shard, rows, :]
        return
    own, far, near, cross = filters
    me = lax.axis_index("seq")
    group_count = own.shape[0]
    tiles = own.shape[1] // LANES
    for tile in range(tiles):
        yield me * tiles + tile, own[:, pl.ds(tile * LANES, LANES)]
        for block, start, step in ((far, first, 2), (near, first, 1), (cross, 0, 3)):
            rows = pl.ds(start + tile * group_count, group_count)
            yield (me ^ step) * tiles + tile, block[rows, :]


def build_shifted(size, first, filters, reverse, shifted):
    group_count, padded = reverse.shape
    lag_count = padded - SPAN
    row = lax.broadcasted_iota(jnp.int32, (LANES, LANES), 0)
    column = lax.broadcasted_iota(jnp.int32, (LANES, LANES), 1)
    flip = jnp.where(row + column == LANES - 1, 1.0, 0.0).astype(jnp.bfloat16)
    for number, values in lag_tiles(size, first, filters):
        start = lag_count - LANES - number * LANES
        if not isinstance(start, int):
            start = pl.multiple_of(start, LANES)
        reverse[:, pl.ds(start, LANES)] = jnp.dot(
            values, flip, preferred_element_type=jnp.float32
        )
    reverse[:, pl.ds(lag_count, SPAN)] = jnp.zeros((group_count, SPAN), jnp.float32)
    inside = (
        lax.broadcasted_iota(jnp.int32, (GROUP_CH, LANES), 1)
        > lax.broadcasted_iota(jnp.int32, (GROUP_CH, LANES), 0)
    )

    @pl.loop(0, group_count // BLOCKS)
    def _(block):
        tile_rows = pl.ds(pl.multiple_of(block * BLOCKS, BLOCKS), BLOCKS)
        before = [jnp.zeros((GROUP_CH, LANES), jnp.float32)] * BLOCKS
        for start in range(0, padded, LANES):
            tile = reverse[tile_rows, pl.ds(start, LANES)]
            for g in range(BLOCKS):
                spread = jnp.broadcast_to(tile[g : g + 1, :], (GROUP_CH, LANES))
                rolled = pltpu.roll(spread, 1, 1, stride=1, stride_axis=0)
                shifted[block * BLOCKS + g, :, pl.ds(start, LANES)] = jnp.where(
                    inside, rolled, before[g]
                ).astype(jnp.bfloat16)
                before[g] = rolled


def spread_rows(tile, spans, base):
    lane = lax.broadcasted_iota(jnp.int16, tile.shape, 1)
    zero = jnp.zeros(tile.shape, tile.dtype)
    for i1 in range(BLOCKS):
        shift = GROUP_CH * i1
        if i1 == 0:
            low, high = zero, tile
        else:
            moved = pltpu.roll(tile, LANES - shift, 1)
            early = lane < LANES - shift
            low, high = jnp.where(early, zero, moved), jnp.where(early, moved, zero)
        rows = pl.ds(shift, GROUP_CH)
        for g in range(BLOCKS):
            part = slice(g * GROUP_CH, (g + 1) * GROUP_CH)
            spans[g, rows, pl.ds(base, LANES)] = low[part]
            spans[g, rows, pl.ds(base + LANES, LANES)] = high[part]


def window(meta, shifted, group, slot, w):
    start = pl.multiple_of(meta[WINDOWS + slot * WIN + w], STRETCH)
    return shifted[group, :, pl.ds(start, SPAN)]


def filter_rows(meta, shifted, group, slots):
    return jnp.concatenate(
        [
            jnp.concatenate([window(meta, shifted, group, slot, w) for w in range(SENT)], axis=1)
            for slot in range(slots)
        ],
        axis=0,
    )


def rows_of(results, block):
    part = slice(block * GROUP_CH, (block + 1) * GROUP_CH)
    return jnp.concatenate([result[part] for result in results], axis=0).T


def last_rows_kernel(key, value, out):
    for start in range(0, out.shape[0], LANES):
        out[pl.ds(start, LANES), :] = product(key, value, 0, pl.ds(start, LANES))


def last_rows(key_proj, value_proj):
    row_count, channels = key_proj.shape
    block = pl.BlockSpec((STRETCH, channels), lambda i: (row_count // STRETCH - 1, 0))
    operands = [pltpu.with_memory_space_constraint(x, pltpu.HBM) for x in (key_proj, value_proj)]
    return pl.pallas_call(
        last_rows_kernel,
        grid=(1,),
        in_specs=[block, block],
        out_specs=pl.BlockSpec((channels, STRETCH), lambda i: (0, 0)),
        out_shape=jax.ShapeDtypeStruct((channels, STRETCH), jnp.bfloat16),
        compiler_params=params(),
        name="last_rows",
    )(*operands)


def last_term(slots, meta, last, shifted, term, spans):
    for start in range(0, last.shape[0], LANES):
        held = spans.at[start // LANES % 2]
        spread_rows(last[pl.ds(start, LANES), :], held, 0)
        results = [
            lax.dot_general(
                held[g],
                window(meta, shifted, start // GROUP_CH + g, slots - 1, SENT),
                NT,
                preferred_element_type=jnp.float32,
            )
            for g in range(BLOCKS)
        ]
        for m in range(BLOCKS):
            term[pl.ds(m * GROUP_CH, GROUP_CH), pl.ds(start, LANES)] = rows_of(results, m)


def spread_part(pieces, start, spans):
    for w in range(SENT):
        spread_rows(pieces[w, pl.ds(start, LANES), :], spans, w * SPAN)


def conv_part(filter_rows_of, base, start, term, query, out, result, spans, sem):
    slots = query.shape[0] // STRETCH
    columns = pl.ds(pl.multiple_of(base + start, LANES), LANES)
    results = [
        lax.dot_general(
            spans[g],
            filter_rows_of(start // GROUP_CH + g),
            NT,
            preferred_element_type=jnp.float32,
        )
        for g in range(BLOCKS)
    ]
    for m in range(BLOCKS):
        rows = rows_of(results, m)
        for slot in range(slots):
            place = pl.ds(slot * STRETCH + m * GROUP_CH, GROUP_CH)
            tile = rows[slot * GROUP_CH : (slot + 1) * GROUP_CH]
            if slot == slots - 1:
                tile = tile + term[pl.ds(m * GROUP_CH, GROUP_CH), columns]
            gates = query[place, columns].astype(jnp.float32)
            result[place, :] = (gates * tile).astype(jnp.bfloat16)
    store = pltpu.make_async_copy(result, out.at[:, columns], sem)
    store.start()
    return store


def part_base(step, size, width):
    me = lax.axis_index("seq")
    return pl.multiple_of((me ^ step if size > 1 else 0) * width, width)


def scratch(count, row_count):
    return [
        pltpu.VMEM((count, row_count, LANES), jnp.bfloat16),
        pltpu.VMEM((count, BLOCKS, LANES, SENT * SPAN), jnp.bfloat16),
        pltpu.SemaphoreType.DMA((count + 1,)),
    ]


def open_kernel(size, first, meta_in, last, pieces, query, *refs):
    filters = refs[:-9]
    shifted, term, out, reverse, meta, last_spans, result, spans, sems = refs[-9:]
    slots = query.shape[0] // STRETCH
    width = pieces.shape[1]
    scalars = pltpu.make_async_copy(meta_in, meta, sems.at[width // LANES])
    scalars.start()
    build_shifted(size, first, filters, reverse, shifted)
    scalars.wait()
    last_term(slots, meta, last, shifted, term, last_spans)
    base = part_base(0, out.shape[1] // width, width)
    stores = []
    for index, start in enumerate(range(0, width, LANES)):
        spread_part(pieces, start, spans.at[index])
        stores.append(
            conv_part(
                lambda group: filter_rows(meta, shifted, base // GROUP_CH + group, slots),
                base,
                start,
                term,
                query,
                out,
                result.at[index],
                spans.at[index],
                sems.at[index],
            )
        )
    for store in stores:
        store.wait()


def open_conv(size, first, meta, last, pieces, query_proj, group_count, lag_count, filters):
    row_count, channels = query_proj.shape
    padded = lag_count + SPAN
    return pl.pallas_call(
        functools.partial(open_kernel, size, first),
        in_specs=[ANY_SPEC] + [VMEM_SPEC] * (3 + len(filters)),
        out_specs=[VMEM_SPEC, VMEM_SPEC, HBM_SPEC],
        out_shape=[
            jax.ShapeDtypeStruct((group_count, GROUP_CH, padded), jnp.bfloat16),
            jax.ShapeDtypeStruct((STRETCH, channels), jnp.float32),
            jax.ShapeDtypeStruct((row_count, channels), jnp.bfloat16),
        ],
        scratch_shapes=[
            pltpu.VMEM((group_count, padded), jnp.float32),
            pltpu.SMEM(meta.shape, jnp.int32),
            pltpu.VMEM((2, BLOCKS, LANES, SPAN), jnp.bfloat16),
            *scratch(pieces.shape[1] // LANES, row_count),
        ],
        compiler_params=params(),
        name="open_conv",
    )(meta, last, pieces, query_proj, *filters)


def near_kernel(size, steps, next_step, meta_in, shifted, term, query, before, *refs):
    parts = refs[: len(steps)]
    out, ready, meta, result, spans, sems = refs[len(steps) :]
    slots = query.shape[0] // STRETCH
    width = parts[0].shape[1]
    places = [(index, start) for index in range(len(steps)) for start in range(0, width, LANES)]
    scalars = pltpu.make_async_copy(meta_in, meta, sems.at[len(places)])
    scalars.start()
    for number, (index, start) in enumerate(places[: len(places) // 2]):
        spread_part(parts[index], start, spans.at[number])
    scalars.wait()
    stores = []
    for number, (index, start) in enumerate(places):
        if number >= len(places) // 2:
            spread_part(parts[index], start, spans.at[number])
        base = part_base(steps[index], size, width)
        stores.append(
            conv_part(
                lambda group, base=base: filter_rows(meta, shifted, base // GROUP_CH + group, slots),
                base,
                start,
                term,
                query,
                out,
                result.at[number],
                spans.at[number],
                sems.at[number],
            )
        )
    base = part_base(next_step, size, width)
    for group in range(width // GROUP_CH):
        ready[group] = filter_rows(meta, shifted, base // GROUP_CH + group, slots)
    for store in stores:
        store.wait()


def near_conv(size, steps, next_step, meta, parts, shifted, term, query_proj, before):
    row_count, channels = query_proj.shape
    width = channels // size
    slots = row_count // STRETCH
    return pl.pallas_call(
        functools.partial(near_kernel, size, steps, next_step),
        in_specs=[ANY_SPEC] + [VMEM_SPEC] * 3 + [HBM_SPEC] + [VMEM_SPEC] * len(parts),
        out_specs=[HBM_SPEC, VMEM_SPEC],
        out_shape=[
            jax.ShapeDtypeStruct((row_count, channels), jnp.bfloat16),
            jax.ShapeDtypeStruct((width // GROUP_CH, slots * GROUP_CH, SENT * SPAN), jnp.bfloat16),
        ],
        input_output_aliases={4: 0},
        scratch_shapes=[
            pltpu.SMEM(meta.shape, jnp.int32),
            *scratch(len(parts) * width // LANES, row_count),
        ],
        compiler_params=params(),
        name="near_conv",
    )(meta, shifted, term, query_proj, before, *parts)


def far_kernel(size, step, pieces, ready, term, query, before, out, result, spans, sems):
    width = pieces.shape[1]
    base = part_base(step, size, width)
    stores = []
    for index, start in enumerate(range(0, width, LANES)):
        spread_part(pieces, start, spans.at[index])
        stores.append(
            conv_part(
                lambda group: ready[group],
                base,
                start,
                term,
                query,
                out,
                result.at[index],
                spans.at[index],
                sems.at[index],
            )
        )
    for store in stores:
        store.wait()


def far_conv(size, step, pieces, ready, term, query_proj, before):
    row_count, channels = query_proj.shape
    return pl.pallas_call(
        functools.partial(far_kernel, size, step),
        in_specs=[VMEM_SPEC] * 4 + [HBM_SPEC],
        out_specs=HBM_SPEC,
        out_shape=jax.ShapeDtypeStruct((row_count, channels), jnp.bfloat16),
        input_output_aliases={4: 0},
        scratch_shapes=scratch(pieces.shape[1] // LANES, row_count),
        compiler_params=params(),
        name="far_conv",
    )(pieces, ready, term, query_proj, before)


def shards(size, key_proj, value_proj, query_proj, filters, sources, owner):
    row_count, channels = key_proj.shape
    group_count, part = filters.shape
    lag_count = size * part
    tiles = part // LANES
    by_parts = size == 4 and channels % (size * LANES) == 0
    block = group_count * tiles
    filter_rows = [0, block, block, 0] if by_parts else [block]
    parts = len(filter_rows)
    width = channels // parts
    sends, extra, choice, meta = gate(filter_rows, sources, owner, key_proj, value_proj, filters)
    last = last_rows(key_proj, value_proj)
    first = SLOTS * width
    if not by_parts:
        blocks = lax.all_gather(sends[0][first:], "seq")
        held = jnp.concatenate([sends[0][:first].reshape(SLOTS, width, LANES), extra])
        mine = (meta[:SENT] == lax.axis_index("seq"))[:, None, None]
        pieces = lax.psum(jnp.where(mine, held[meta[PLACE:MANY]], jnp.zeros_like(held)), "seq")
        return open_conv(
            size, tiles, meta, last, pieces, query_proj, group_count, lag_count, [blocks]
        )[2]

    def exchange(value, step):
        return lax.ppermute(value, "seq", [(z, z ^ step) for z in range(size)])

    far, near, cross = (exchange(sends[step], step) for step in STEPS[1:])
    cross_filters = exchange(pick(first, far), 1)

    def more(meta, extra):
        arrived = [extra[0]] + [exchange(extra[step], step) for step in STEPS[1:]]
        return third(meta, arrived)

    def none(meta, extra):
        return extra[0]

    extra, far = lax.optimization_barrier((extra, far))
    late = lax.cond(meta[MANY] > 0, more, none, meta, extra)
    last, cross_filters, late, cross = lax.optimization_barrier((last, cross_filters, late, cross))
    merged = merge(width, choice, [sends[0], far, near, cross], late)
    far_part, near_part = exchange(merged, 2), exchange(merged, 1)
    shifted, term, out = open_conv(
        size,
        first,
        meta,
        last,
        merged,
        query_proj,
        group_count,
        lag_count,
        [filters, far, near, cross_filters],
    )
    far_part, out = lax.optimization_barrier((far_part, out))
    last_part = exchange(far_part, 1)
    out, ready = near_conv(
        size, (1, 2), 3, meta, [near_part, far_part], shifted, term, query_proj, out
    )
    return far_conv(size, 3, last_part, ready, term, query_proj, out)


def solution(mesh):
    return jax.shard_map(
        functools.partial(shards, mesh.shape["seq"]),
        mesh=mesh,
        in_specs=(
            P(("rep", "seq"), "ch"),
            P(("rep", "seq"), "ch"),
            P(("rep", "seq"), "ch"),
            P("ch", "seq"),
            P("rep"),
            P("rep"),
        ),
        out_specs=P(("rep", "seq"), "ch"),
        check_vma=False,
    )
```
